32 devices in a mesh: dp: 8 (over y, x, core), mp: 4 (over z).
Axes of the slice: x: 2, y: 2, z: 4, core: 2. Of those that a mesh axis runs over, the one named last changes fastest.
Arguments:
- inputs: bfloat16 [8, 1024, 1024], P('dp'), may hold values from -6 to 6
- encoder: bfloat16 [8, 2048, 1024], P('dp'), may hold values from -6 to 6
- prefix: int32 [8], P('dp'), may hold values from 102 to 512, as said below
- cotangent: bfloat16 [8, 1024, 1024], P('dp'), may hold values from -6 to 6
- inner_weights: float32 [2, 3, 1024, 1024], P(None, None, 'dp', 'mp')
- inner_first: float32 [2, 3, 1024, 1024], P(None, None, 'dp', 'mp')
- inner_second: float32 [2, 3, 1024, 1024], P(None, None, 'dp', 'mp'), may hold values from 4423.68 to 17694.72
- outer_weights: float32 [2, 1024, 1024], P(None, 'mp', 'dp')
- outer_first: float32 [2, 1024, 1024], P(None, 'mp', 'dp')
- outer_second: float32 [2, 1024, 1024], P(None, 'mp', 'dp')
- expand_weights: float32 [1024, 4096], P('dp', 'mp')
- expand_first: float32 [1024, 4096], P('dp', 'mp')
- expand_second: float32 [1024, 4096], P('dp', 'mp'), may hold values from 630.784 to 2539.52
- shrink_weights: float32 [4096, 1024], P('mp', 'dp')
- shrink_first: float32 [4096, 1024], P('mp', 'dp')
- shrink_second: float32 [4096, 1024], P('mp', 'dp'), may hold values from 3522.56 to 13926.4
- norm_params: float32 [2, 3, 1024], P(None, None, 'dp')
- norm_first: float32 [2, 3, 1024], P(None, None, 'dp')
- norm_second: float32 [2, 3, 1024], P(None, None, 'dp'), may hold values from 5464.064 to 21848.064
Outputs:
- layer_out: float32 [8, 1024, 1024], P('dp')
- input_grad: float32 [8, 1024, 1024], P('dp')
- encoder_grad: float32 [8, 2048, 1024], P('dp')
- inner_new: float32 [2, 3, 1024, 1024], P(None, None, 'dp', 'mp')
- outer_new: float32 [2, 1024, 1024], P(None, 'mp', 'dp')
- expand_new: float32 [1024, 4096], P('dp', 'mp')
- shrink_new: float32 [4096, 1024], P('mp', 'dp')
- norm_new: float32 [2, 3, 1024], P(None, None, 'dp')
- inner_first_new: float32 [2, 3, 1024, 1024], P(None, None, 'dp', 'mp')
- outer_first_new: float32 [2, 1024, 1024], P(None, 'mp', 'dp')
- expand_first_new: float32 [1024, 4096], P('dp', 'mp')
- shrink_first_new: float32 [4096, 1024], P('mp', 'dp')
- norm_first_new: float32 [2, 3, 1024], P(None, None, 'dp')
- inner_second_new: float32 [2, 3, 1024, 1024], P(None, None, 'dp', 'mp')
- outer_second_new: float32 [2, 1024, 1024], P(None, 'mp', 'dp')
- expand_second_new: float32 [1024, 4096], P('dp', 'mp')
- shrink_second_new: float32 [4096, 1024], P('mp', 'dp')
- norm_second_new: float32 [2, 3, 1024], P(None, None, 'dp')
- trust_table: float32 [3, 16], replicated
The draws below stay inside these ranges and needn't reach their ends.
Inputs may be any that keep to these rules, and one draw needn't show every extreme that they name: `prefix`: prefix lengths; in every draw one sequence has exactly 102 and one exactly 512.
All inputs are finite; a program needn't handle non-finite values.
Results may differ from the reference program's by a relative error of at most 0.034.
Values may be sent and summed in bfloat16 or wider, within the bound.
A program may use at most 192 MiB of HBM per device.

```python
import math
import jax
import jax.numpy as jnp
from jax import lax

D = 1024
H = 16
HEAD = 64
FF = 4096
LEN = 1024
ENC = 2048
STEP = 5
SEQS = 8
TOKENS = 8192
N_MP = 4


def rising(key, shape, axis, factor, top):
    normal_part = jax.random.normal(key, shape, jnp.float32)
    noise = normal_part
    ramp = 1.0 + (top - 1.0) * lax.broadcasted_iota(jnp.float32, shape, axis) / (shape[axis] - 1)
    return noise * ramp * factor


def spread_log(key, shape, lowest, highest):
    unit = jax.random.uniform(key, shape, jnp.float32, 0.0, 1.0)
    return lowest * jnp.exp(unit * math.log(highest / lowest))


def draw_inner_weights(key, part):
    key = jax.random.fold_in(key, 11)
    return rising(key, (2, 3, D, D), 2, 0.75 * D ** (-0.5), 1.8)


def draw_inner_first(key, part):
    key = jax.random.fold_in(key, 21)
    top = 3.0
    return rising(key, (2, 3, D, D), 2, 1.8 * TOKENS ** 0.5 / (1.0 + top), top)


def draw_outer_weights(key, part):
    key = jax.random.fold_in(key, 12)
    self_factor = (LEN / (5.0 * D)) ** 0.5
    cross_factor = (ENC / (3.0 * D)) ** 0.5
    top = 1.8
    first_part = rising(jax.random.fold_in(key, 1), (D, D), 1, self_factor, top)
    second_part = rising(jax.random.fold_in(key, 2), (D, D), 1, cross_factor, top)
    return jnp.stack([first_part, second_part])


def draw_outer_first(key, part):
    key = jax.random.fold_in(key, 17)
    top = 3.0
    self_part = rising(jax.random.fold_in(key, 1), (D, D), 1, 3.72 * SEQS ** 0.5 / (1.0 + top), top)
    cross_part = rising(jax.random.fold_in(key, 2), (D, D), 1, 1.86 * SEQS ** 0.5 / (1.0 + top), top)
    return jnp.stack([self_part, cross_part])


def draw_outer_second(key, part):
    key = jax.random.fold_in(key, 18)
    self_part = spread_log(jax.random.fold_in(key, 1), (D, D), 2.3 * SEQS, 9.2 * SEQS)
    cross_part = spread_log(jax.random.fold_in(key, 2), (D, D), 0.58 * SEQS, 2.3 * SEQS)
    return jnp.stack([self_part, cross_part])


def draw_expand_weights(key, part):
    key = jax.random.fold_in(key, 13)
    return rising(key, (D, FF), 0, D ** (-0.5), 1.8)


def draw_expand_first(key, part):
    key = jax.random.fold_in(key, 22)
    top = 3.0
    return rising(key, (D, FF), 0, 0.68 * TOKENS ** 0.5 / (1.0 + top), top)


def draw_shrink_weights(key, part):
    key = jax.random.fold_in(key, 14)
    return rising(key, (FF, D), 1, FF ** (-0.5), 1.8)


def draw_shrink_first(key, part):
    key = jax.random.fold_in(key, 23)
    top = 3.0
    return rising(key, (FF, D), 1, 1.6 * TOKENS ** 0.5 / (1.0 + top), top)


def draw_norm_params(key, part):
    key = jax.random.fold_in(key, 15)
    top = 1.8
    ramp = 1.0 + (top - 1.0) * lax.broadcasted_iota(jnp.float32, (3, D), 1) / (D - 1)
    gains = 0.7 * ramp + rising(jax.random.fold_in(key, 1), (3, D), 1, 0.07, top)
    biases = rising(jax.random.fold_in(key, 2), (3, D), 1, 0.3, top)
    return jnp.stack([gains, biases])


def draw_norm_first(key, part):
    key = jax.random.fold_in(key, 24)
    top = 3.0
    return rising(key, (2, 3, D), 2, 2.0 * TOKENS ** 0.5 / (1.0 + top), top)


def draw_prefix(key, part):
    key = jax.random.fold_in(key, 16)
    lowest = LEN // 10
    highest = LEN // 2
    values = jax.random.randint(jax.random.fold_in(key, 1), (SEQS,), lowest, highest + 1)
    where_high = jax.random.randint(jax.random.fold_in(key, 2), (), 0, SEQS)
    values = values.at[where_high].set(highest)
    values = values.at[(where_high + 1) % SEQS].set(lowest)
    return values.astype(jnp.int32)


def shard_levels(key, dims, cuts, low, largest):
    loudness, own = 1.0, jax.random.fold_in(key, 6)
    for position, shards_of in cuts:
        steps = jnp.exp(jax.random.uniform(jax.random.fold_in(own, position), (shards_of,), jnp.float32, low / len(cuts), largest / len(cuts)))
        loudness = loudness * jnp.repeat(steps, dims[position] // shards_of).reshape([-1 if axis == position else 1 for axis in range(len(dims))])
    return loudness


def scatter_about(stream_key, dims, width, limit, shards=(), held_as=jnp.bfloat16):
    result = jax.random.normal(stream_key, dims, jnp.float32) * width
    if len(shards) > 0:
        result = shard_levels(stream_key, dims, shards, -0.22, 0.18) * result
    return jnp.clip(result, min=-limit, max=limit).astype(held_as)


def setup_inputs(seed: int = 0) -> dict:
    key_list = jax.random.split(jax.random.key(seed), 20)
    inputs = scatter_about(key_list[0], (SEQS, LEN, D), 1.0, 6.0, ((0, 8),))
    encoder = scatter_about(key_list[1], (SEQS, ENC, D), 1.0, 6.0, ((0, 8),))
    prefix = draw_prefix(jax.random.fold_in(key_list[19], 71), 0)
    cotangent = scatter_about(key_list[3], (SEQS, LEN, D), 1.0, 6.0, ((0, 8),))
    inner_weights = draw_inner_weights(jax.random.fold_in(key_list[19], 71), 0)
    inner_first = draw_inner_first(jax.random.fold_in(key_list[19], 71), 0)
    inner_second = jnp.clip(jnp.exp(math.log(17694.72) - 1.3862944 * jax.random.uniform(key_list[6], (2, 3, D, D), jnp.float32) ** shard_levels(key_list[6], (2, 3, D, D), ((2, 8), (3, 4)), -0.2, 0.2)), 4423.68, 17694.72)
    outer_weights = draw_outer_weights(jax.random.fold_in(key_list[19], 71), 0)
    outer_first = draw_outer_first(jax.random.fold_in(key_list[19], 71), 0)
    outer_second = draw_outer_second(jax.random.fold_in(key_list[19], 71), 0)
    expand_weights = draw_expand_weights(jax.random.fold_in(key_list[19], 71), 0)
    expand_first = draw_expand_first(jax.random.fold_in(key_list[19], 71), 0)
    expand_second = jnp.clip(jnp.exp(math.log(2539.52) - 1.39276689 * jax.random.uniform(key_list[12], (D, FF), jnp.float32) ** shard_levels(key_list[12], (D, FF), ((0, 8), (1, 4)), -0.2, 0.2)), 630.784, 2539.52)
    shrink_weights = draw_shrink_weights(jax.random.fold_in(key_list[19], 71), 0)
    shrink_first = draw_shrink_first(jax.random.fold_in(key_list[19], 71), 0)
    shrink_second = jnp.clip(jnp.exp(math.log(13926.4) - 1.37459833 * jax.random.uniform(key_list[15], (FF, D), jnp.float32) ** shard_levels(key_list[15], (FF, D), ((0, 4), (1, 8)), -0.2, 0.2)), 3522.56, 13926.4)
    norm_params = draw_norm_params(jax.random.fold_in(key_list[19], 71), 0)
    norm_first = draw_norm_first(jax.random.fold_in(key_list[19], 71), 0)
    norm_second = jnp.clip(jnp.exp(math.log(21848.064) - 1.3859195 * jax.random.uniform(key_list[18], (2, 3, D), jnp.float32) ** shard_levels(key_list[18], (2, 3, D), ((2, 8),), -0.2, 0.2)), 5464.064, 21848.064)
    return dict(inputs=inputs, encoder=encoder, prefix=prefix, cotangent=cotangent, inner_weights=inner_weights, inner_first=inner_first, inner_second=inner_second, outer_weights=outer_weights, outer_first=outer_first, outer_second=outer_second, expand_weights=expand_weights, expand_first=expand_first, expand_second=expand_second, shrink_weights=shrink_weights, shrink_first=shrink_first, shrink_second=shrink_second, norm_params=norm_params, norm_first=norm_first, norm_second=norm_second)


@jax.custom_vjp
def low(v):
    return lax.optimization_barrier(v.astype(jnp.bfloat16)).astype(jnp.float32)

@jax.custom_vjp
def low_back(v):
    return v

def low_keep(v):
    return (low(v), None)

def low_pass(kept, grad):
    return (grad,)

def back_keep(v):
    return (v, None)

def back_low(kept, grad):
    return (low(grad),)
low.defvjp(low_keep, low_pass)
low_back.defvjp(back_keep, back_low)
first_decay = 0.5
second_decay = 0.6
learn_rate = 0.5
weight_decay = 0.01
epsilon = 1e-06
norm_eps = 1e-05
mask_fill = -1000000000.0

def product(form, left, right):
    return jnp.einsum(form, left, right, precision=lax.Precision.HIGHEST)

def layer_norm(values, gain_row, bias_row):
    center = values - lax.optimization_barrier(jnp.mean(values, axis=-1, keepdims=True))
    spread = lax.optimization_barrier(jnp.mean(center * center, axis=-1, keepdims=True))
    return center * lax.rsqrt(spread + norm_eps) * gain_row + bias_row

def spread_groups(values):
    return jnp.broadcast_to(values[None], (N_MP,) + values.shape)

def to_heads(grouped):
    row_count = grouped.shape[1]
    return grouped.reshape(N_MP, row_count, H // N_MP, HEAD).transpose(0, 2, 1, 3).reshape(H, row_count, HEAD)

def from_heads(headed):
    row_count = headed.shape[1]
    return headed.reshape(N_MP, H // N_MP, row_count, HEAD).transpose(0, 2, 1, 3).reshape(N_MP, row_count, D // N_MP)

def by_groups(matrix):
    return matrix.reshape(matrix.shape[0], N_MP, matrix.shape[1] // N_MP).transpose(1, 0, 2)

def project(grouped, matrix):
    return to_heads(low_back(low(product('gtd,gdm->gtm', grouped, by_groups(matrix)))))

def attention(query_in, source_in, weights, outer, allowed):
    query = project(query_in, weights[0])
    key_rows = project(source_in, weights[1])
    value_rows = project(source_in, weights[2])
    scores = low_back(product('hqd,hkd->hqk', query, key_rows) * HEAD ** (-0.5))
    if allowed is not None:
        scores = jnp.where(allowed[None], scores, mask_fill)
    attn_probs = low(jax.nn.softmax(scores, axis=-1))
    mixed_out = low_back(low(product('hqk,hkd->hqd', attn_probs, value_rows)))
    parts = product('gtm,gmd->gtd', from_heads(mixed_out), outer.reshape(N_MP, D // N_MP, D))
    return low_back(lax.optimization_barrier(jnp.sum(parts, axis=0)))

def one_sequence(params, tokens, states, prefix_len):
    inner, outer, expand, shrink, norms = params
    row_ids = lax.broadcasted_iota(jnp.int32, (LEN, LEN), 0)
    col_ids = lax.broadcasted_iota(jnp.int32, (LEN, LEN), 1)
    allowed = (col_ids <= row_ids) | (col_ids < prefix_len)
    token_groups = spread_groups(low(tokens))
    branch = attention(token_groups, token_groups, inner[0], outer[0], allowed)
    hidden_one = layer_norm(tokens + branch, norms[0, 0], norms[1, 0])
    cross = attention(spread_groups(low(hidden_one)), spread_groups(low(states)), inner[1], outer[1], None)
    hidden_two = layer_norm(hidden_one + cross, norms[0, 1], norms[1, 1])
    pre_act = low_back(product('gtd,gdf->gtf', spread_groups(low(hidden_two)), by_groups(expand)))
    activation = low(jax.nn.gelu(pre_act, approximate=False))
    parts = product('gtf,gfd->gtd', activation, shrink.reshape(N_MP, FF // N_MP, D))
    return layer_norm(hidden_two + low_back(lax.optimization_barrier(jnp.sum(parts, axis=0))), norms[0, 2], norms[1, 2])

def moments(grad, first_moment, second_moment, master, decay):
    first_new = first_decay * first_moment + (1.0 - first_decay) * grad
    second_new = second_decay * second_moment + (1.0 - second_decay) * grad * grad
    direction = first_new / (1.0 - first_decay ** STEP) / (jnp.sqrt(second_new / (1.0 - second_decay ** STEP)) + epsilon) + decay * master
    return (first_new, second_new, direction)

def squares(inner, outer, expand, shrink, norms, norm_share):
    return jnp.concatenate([lax.optimization_barrier(jnp.sum(inner * inner, axis=(2, 3))).reshape(6), lax.optimization_barrier(jnp.sum(outer * outer, axis=(1, 2))), jnp.sum(expand * expand)[None], jnp.sum(shrink * shrink)[None], lax.optimization_barrier(jnp.sum(norms * norms, axis=2)).reshape(6) * norm_share])

def entry_counts():
    return jnp.array([D * D] * 8 + [D * FF] * 2 + [D] * 6, dtype=jnp.float32)

def reference(inputs, encoder, prefix, cotangent, inner_weights, inner_first, inner_second, outer_weights, outer_first, outer_second, expand_weights, expand_first, expand_second, shrink_weights, shrink_first, shrink_second, norm_params, norm_first, norm_second):
    working = tuple((master.astype(jnp.bfloat16).astype(jnp.float32) for master in (inner_weights, outer_weights, expand_weights, shrink_weights, norm_params)))

    def forward(tokens, states, inner, outer, expand, shrink, norms):

        def step(running, member):
            return (running, one_sequence((inner, outer, expand, shrink, norms), member[0], member[1], member[2]))
        return lax.scan(jax.checkpoint(step), None, (tokens, states, prefix))[1]
    layer, pull = jax.vjp(forward, inputs.astype(jnp.float32), encoder.astype(jnp.float32), *working)
    grads = pull(cotangent.astype(jnp.float32))
    inner_f, inner_s, inner_d = moments(grads[2], inner_first, inner_second, inner_weights, weight_decay)
    outer_f, outer_s, outer_d = moments(grads[3], outer_first, outer_second, outer_weights, weight_decay)
    expand_f, expand_s, expand_d = moments(grads[4], expand_first, expand_second, expand_weights, weight_decay)
    shrink_f, shrink_s, shrink_d = moments(grads[5], shrink_first, shrink_second, shrink_weights, weight_decay)
    norm_f, norm_s, norm_d = moments(grads[6], norm_first, norm_second, norm_params, 0.0)
    counts_all = entry_counts()
    weight_norm = jnp.sqrt(squares(inner_weights, outer_weights, expand_weights, shrink_weights, norm_params, 1.0) / counts_all)
    update_norm = jnp.sqrt(squares(inner_d, outer_d, expand_d, shrink_d, norm_d, 1.0) / counts_all)
    trust = weight_norm / (update_norm + epsilon)
    inner_new = inner_weights - learn_rate * trust[0:6].reshape(2, 3, 1, 1) * inner_d
    outer_new = outer_weights - learn_rate * trust[6:8].reshape(2, 1, 1) * outer_d
    expand_new = expand_weights - learn_rate * trust[8] * expand_d
    shrink_new = shrink_weights - learn_rate * trust[9] * shrink_d
    norm_new = norm_params - learn_rate * trust[10:16].reshape(2, 3, 1) * norm_d
    table = jnp.stack([weight_norm, update_norm, trust])
    return (layer, grads[0], grads[1], inner_new, outer_new, expand_new, shrink_new, norm_new, inner_f, outer_f, expand_f, shrink_f, norm_f, inner_s, outer_s, expand_s, shrink_s, norm_s, table)
```

```python
from functools import partial

import jax
import jax.numpy as jnp
from jax import lax
from jax.experimental import pallas as pl
from jax.experimental.pallas import tpu as pltpu
from jax.sharding import PartitionSpec as P

D = 1024
HEAD = 64
FF = 4096
STEP = 5

first_decay = 0.5
second_decay = 0.6
learn_rate = 0.5
weight_decay = 0.01
epsilon = 1e-06
norm_eps = 1e-05
mask_fill = -1000000000.0

MESH = pl.DeviceIdType.MESH
ANYWHERE = pl.BlockSpec(memory_space=pl.ANY)
IN_VMEM = pl.BlockSpec(memory_space=pltpu.VMEM)
NN = (((1,), (0,)), ((), ()))
NT = (((1,), (1,)), ((), ()))
TN = (((0,), (0,)), ((), ()))
VMEM_LIMIT = 58 << 20


def dot(left, right, dims=NN):
    return lax.dot_general(left, right, dims, preferred_element_type=jnp.float32)


def bf16(values):
    return values.astype(jnp.bfloat16)


def f32(values):
    return values.astype(jnp.float32)


def layer_norm(values, gain_row, bias_row):
    center = values - jnp.mean(values, axis=-1, keepdims=True)
    spread = jnp.mean(center * center, axis=-1, keepdims=True)
    inverse = lax.rsqrt(spread + norm_eps)
    normed = center * inverse
    return (normed * gain_row + bias_row, normed, inverse)


def norm_back(upstream, normed, inverse, gain_row):
    scaled = upstream * gain_row
    inner = (
        scaled
        - jnp.mean(scaled, axis=-1, keepdims=True)
        - normed * jnp.mean(scaled * normed, axis=-1, keepdims=True)
    )
    return (
        inner * inverse,
        jnp.sum(upstream * normed, axis=0, keepdims=True),
        jnp.sum(upstream, axis=0, keepdims=True),
    )


def sizes_of(total, block, limit):
    groups = {}
    for index in range(total // block):
        groups.setdefault(limit(index), []).append(index)
    return groups.items()


def forward_kernel(masked, block, prefix_ref, q_ref, k_ref, v_ref, mixed_ref, sums_ref):
    width = q_ref.shape[1]
    heads = width // HEAD
    keys_total = k_ref.shape[0]
    step = pl.program_id(0)
    lane = lax.broadcasted_iota(jnp.int32, (block, width), 1) // HEAD

    def run(keys, start):
        query = q_ref[...] * jnp.bfloat16(HEAD**-0.5)
        key_rows = k_ref[:keys, :]
        value_rows = v_ref[:keys, :]
        if masked:
            rows = start + lax.broadcasted_iota(jnp.int32, (block, keys), 0)
            cols = lax.broadcasted_iota(jnp.int32, (block, keys), 1)
            allowed = (cols <= rows) | (cols < prefix_ref[0])
        mixed = jnp.zeros((block, width), jnp.float32)
        slot = lax.broadcasted_iota(jnp.int32, (block, 128), 1)
        table = jnp.zeros((block, 128), jnp.float32)
        for head in range(heads):
            scores = dot(jnp.where(lane == head, query, jnp.bfloat16(0)), key_rows, NT)
            if masked:
                scores = jnp.where(allowed, scores, mask_fill)
            row_max = jnp.max(scores, axis=1, keepdims=True)
            powered = jnp.exp(scores - row_max)
            totals = jnp.sum(powered, axis=1, keepdims=True)
            part = dot(bf16(powered), value_rows) * (1.0 / totals)
            mixed = jnp.where(lane == head, part, mixed)
            table = jnp.where(slot == head, row_max + jnp.log(totals), table)
        mixed_ref[...] = bf16(mixed)
        sums_ref[...] = table.T[:8, :]

    if masked:
        limit = lambda index: max(keys_total // 2, (index + 1) * block)
        for keys, blocks in sizes_of(keys_total, block, limit):

            @pl.when((step >= blocks[0]) & (step <= blocks[-1]))
            def _(keys=keys):
                run(keys, step * block)
    else:
        run(keys_total, 0)


def attend_forward(query, key_rows, value_rows, prefix, masked, block=512):
    total, width = query.shape
    keys = key_rows.shape[0]
    block = min(block, total)
    whole = pl.BlockSpec((keys, width), lambda i, p: (0, 0))
    return pl.pallas_call(
        partial(forward_kernel, masked, block),
        grid_spec=pltpu.PrefetchScalarGridSpec(
            num_scalar_prefetch=1,
            grid=(total // block,),
            in_specs=[pl.BlockSpec((block, width), lambda i, p: (i, 0)), whole, whole],
            out_specs=[
                pl.BlockSpec((block, width), lambda i, p: (i, 0)),
                pl.BlockSpec((8, block), lambda i, p: (0, i)),
            ],
        ),
        out_shape=[
            jax.ShapeDtypeStruct((total, width), jnp.bfloat16),
            jax.ShapeDtypeStruct((8, total), jnp.float32),
        ],
        compiler_params=pltpu.CompilerParams(vmem_limit_bytes=VMEM_LIMIT),
        cost_estimate=pl.CostEstimate(
            flops=16 * total * keys * width, bytes_accessed=4 * keys * width, transcendentals=0
        ),
        name="attend_forward",
    )(prefix, query, key_rows, value_rows)


def backward_kernel(
    masked, block, prefix_ref, q_ref, k_ref, v_ref, do_ref, o_ref, sums_ref,
    dq_ref, dk_ref, dv_ref, acc, delta,
):
    width = q_ref.shape[1]
    heads = width // HEAD
    total = q_ref.shape[0]
    step = pl.program_id(0)
    factor = HEAD**-0.5

    @pl.when(step == 0)
    def _():
        product = f32(do_ref[...]) * f32(o_ref[...])
        row = lax.broadcasted_iota(jnp.int32, (8, width), 0)
        col = lax.broadcasted_iota(jnp.int32, (8, width), 1) // HEAD
        pick = jnp.where(row == col, 1.0, 0.0).astype(jnp.float32)
        delta[...] = lax.dot_general(
            pick, product, NT, precision=lax.Precision.HIGHEST, preferred_element_type=jnp.float32
        )
        acc[...] = jnp.zeros_like(acc)

    lane = lax.broadcasted_iota(jnp.int32, (block, width), 1) // HEAD

    def run(first):
        count = total - first
        query = q_ref[first:, :]
        grad_rows = do_ref[first:, :]
        scaled_keys = k_ref[...] * jnp.bfloat16(factor)
        value_rows = v_ref[...]
        if masked:
            rows = first + lax.broadcasted_iota(jnp.int32, (block, count), 1)
            cols = step * block + lax.broadcasted_iota(jnp.int32, (block, count), 0)
            allowed = (cols <= rows) | (cols < prefix_ref[0])
        key_grad = jnp.zeros((block, width), jnp.float32)
        value_grad = jnp.zeros((block, width), jnp.float32)
        query_grad = jnp.zeros((count, width), jnp.float32)
        for head in range(heads):
            own_keys = jnp.where(lane == head, scaled_keys, jnp.bfloat16(0))
            scores = dot(own_keys, query, NT)
            if masked:
                scores = jnp.where(allowed, scores, mask_fill)
            probs = jnp.exp(scores - sums_ref[head : head + 1, first:])
            prob_grad = dot(jnp.where(lane == head, value_rows, jnp.bfloat16(0)), grad_rows, NT)
            score_grad = bf16(probs * (prob_grad - delta[head : head + 1, first:]))
            value_grad = jnp.where(lane == head, dot(bf16(probs), grad_rows), value_grad)
            key_grad = jnp.where(lane == head, dot(score_grad, query), key_grad)
            query_grad = query_grad + dot(score_grad, own_keys, TN)
        acc[first:, :] += query_grad
        dk_ref[...] = bf16(key_grad * factor)
        dv_ref[...] = bf16(value_grad)

    if masked:
        limit = lambda index: 0 if index * block < total // 2 else index * block
        for first, blocks in sizes_of(total, block, limit):

            @pl.when((step >= blocks[0]) & (step <= blocks[-1]))
            def _(first=first):
                run(first)
    else:
        run(0)

    @pl.when(step == pl.num_programs(0) - 1)
    def _():
        dq_ref[...] = bf16(acc[...])


def attend_backward(query, key_rows, value_rows, grad_out, mixed, sums, prefix, masked, block=512):
    total, width = query.shape
    keys = key_rows.shape[0]
    whole = pl.BlockSpec((total, width), lambda i, p: (0, 0))
    part = pl.BlockSpec((block, width), lambda i, p: (i, 0))
    return pl.pallas_call(
        partial(backward_kernel, masked, block),
        grid_spec=pltpu.PrefetchScalarGridSpec(
            num_scalar_prefetch=1,
            grid=(keys // block,),
            in_specs=[
                whole, part, part, whole, whole, pl.BlockSpec((8, total), lambda i, p: (0, 0)),
            ],
            out_specs=[whole, part, part],
            scratch_shapes=[
                pltpu.VMEM((total, width), jnp.float32),
                pltpu.VMEM((8, total), jnp.float32),
            ],
        ),
        out_shape=[jax.ShapeDtypeStruct((total, width), jnp.bfloat16)]
        + [jax.ShapeDtypeStruct((keys, width), jnp.bfloat16)] * 2,
        compiler_params=pltpu.CompilerParams(vmem_limit_bytes=VMEM_LIMIT),
        cost_estimate=pl.CostEstimate(
            flops=40 * total * keys * width, bytes_accessed=4 * keys * width, transcendentals=0
        ),
        name="attend_backward",
    )(prefix, query, key_rows, value_rows, grad_out, mixed, sums)


def greet(n):
    me = lax.axis_index("mp")
    barrier = pltpu.get_barrier_semaphore()
    for distance in range(1, n):
        pl.semaphore_signal(
            barrier, inc=1, device_id={"mp": lax.rem(me + distance, n)}, device_id_type=MESH
        )
    pl.semaphore_wait(barrier, n - 1)


def push(source, target, send_sem, recv_sem, to):
    copy = pltpu.make_async_remote_copy(
        source, target, send_sem, recv_sem, device_id={"mp": to}, device_id_type=MESH
    )
    copy.start()
    return copy


def rows_at(index, size):
    return pl.ds(pl.multiple_of(index * size, size), size)


def heads_to_tokens(n, source, slots, send_sems, recv_sems):
    me = lax.axis_index("mp")
    size = source.shape[0] // n
    copies = []
    for distance in range(1, n):
        to = lax.rem(me + distance, n)
        copies.append(
            push(
                source.at[rows_at(to, size)], slots.at[me],
                send_sems.at[distance - 1], recv_sems.at[distance - 1], to,
            )
        )
    return copies


def tokens_to_heads(n, make, block, target, send_sems, recv_sems, local_sem):
    me = lax.axis_index("mp")
    size, width = block.shape[0], block.shape[1] // n
    copies = []
    for distance in (*range(1, n), 0):
        to = lax.rem(me + distance, n)
        cols = rows_at(to, width)
        block[:, cols] = bf16(make(cols))
        place = target.at[rows_at(me, size)]
        if distance:
            copies.append(
                push(
                    block.at[:, cols], place,
                    send_sems.at[distance - 1], recv_sems.at[distance - 1], to,
                )
            )
        else:
            copy = pltpu.make_async_copy(block.at[:, cols], place, local_sem)
            copy.start()
            copies.append(copy)
    return copies


def merge_heads(n, local, slots, copies, weights_of, start):
    me = lax.axis_index("mp")
    total = start + weights_of(local, me)
    for distance in range(1, n):
        origin = lax.rem(me + n - distance, n)
        copies[distance - 1].wait_recv()
        total = total + weights_of(slots[origin], origin)
    for copy in copies:
        copy.wait_send()
    return total


def self_to_cross_kernel(
    n, mixed_ref, wo_ref, wq_ref, x_ref, gain_ref, bias_ref,
    hidden_ref, normed_ref, inverse_ref, slots_ref, q_ref,
    wo, wq, x_rows, block, wo_sem, wq_sem, x_sem, own_sem, send_in, recv_in, send_out, recv_out,
):
    me = lax.axis_index("mp")
    size = x_rows.shape[0]
    loads = [
        pltpu.make_async_copy(mixed_ref.at[rows_at(me, size)], slots_ref.at[me], own_sem),
        pltpu.make_async_copy(wo_ref, wo, wo_sem),
        pltpu.make_async_copy(x_ref.at[rows_at(me, size)], x_rows, x_sem),
        pltpu.make_async_copy(wq_ref, wq, wq_sem),
    ]
    for load in loads:
        load.start()
    greet(n)
    copies = heads_to_tokens(n, mixed_ref, slots_ref, send_in, recv_in)
    for load in loads:
        load.wait()
    width = mixed_ref.shape[1]
    branch = merge_heads(
        n, slots_ref[me], slots_ref, copies,
        lambda part, group: dot(part, wo[rows_at(group, width), :]), f32(x_rows[...]),
    )
    hidden, normed, inverse = layer_norm(branch, gain_ref[0:1, :], bias_ref[0:1, :])
    hidden_ref[...] = hidden
    normed_ref[...] = normed
    inverse_ref[...] = jnp.broadcast_to(inverse, inverse_ref.shape)
    low = bf16(hidden)
    sent = tokens_to_heads(
        n, lambda cols: dot(low, wq[:, cols]), block, q_ref, send_out, recv_out, own_sem
    )
    for copy in sent:
        copy.wait()


def self_to_cross(n, mixed, wo, wq, tokens, gains, biases):
    total, width = mixed.shape
    size, model = total // n, tokens.shape[1]
    shape = jax.ShapeDtypeStruct
    dma = pltpu.SemaphoreType.DMA
    return pl.pallas_call(
        partial(self_to_cross_kernel, n),
        out_shape=[
            shape((size, model), jnp.float32),
            shape((size, model), jnp.float32),
            shape((size, 128), jnp.float32),
            shape((n, size, width), jnp.bfloat16),
            shape((total, width), jnp.bfloat16),
        ],
        in_specs=[ANYWHERE] * 4 + [IN_VMEM] * 2,
        out_specs=[IN_VMEM] * 4 + [ANYWHERE],
        scratch_shapes=[
            pltpu.VMEM((model, model), jnp.bfloat16),
            pltpu.VMEM((model, model), jnp.bfloat16),
            pltpu.VMEM((size, model), jnp.bfloat16),
            pltpu.VMEM((size, model), jnp.bfloat16),
            dma, dma, dma, dma,
            dma((n - 1,)), dma((n - 1,)), dma((n - 1,)), dma((n - 1,)),
        ],
        compiler_params=pltpu.CompilerParams(
            collective_id=1, has_side_effects=True, vmem_limit_bytes=VMEM_LIMIT
        ),
        cost_estimate=pl.CostEstimate(
            flops=30 * 10**9, bytes_accessed=8 * total * width, transcendentals=0
        ),
        name="self_to_cross",
    )(mixed, wo, wq, tokens, gains, biases)


def feed_kernel(
    n, mixed_ref, wo_ref, expand_ref, shrink_ref, hidden_one_ref, cot_ref, gain_ref, bias_ref,
    out_ref, second_ref, dmix_ref, shrink_grad_ref, expand_grad_ref, wo_grad_ref, norm_grad_ref,
    wo, expand, shrink, slots, hidden_two, normed_two, low_two, low_three, act, slope,
    y_own, y_send, y_recv, d_send, d_recv, cot, block,
    load_sems, own_sem, send_in, recv_in, send_out, recv_out, pair_send, pair_recv,
):
    me = lax.axis_index("mp")
    mate = me + 1 - 2 * lax.rem(me, 2)
    size = cot.shape[0]
    half = size // 2
    width = mixed_ref.shape[1]
    hidden_units = act.shape[1]
    chunk = min(512, hidden_units)
    loads = [
        pltpu.make_async_copy(mixed_ref.at[rows_at(me, size)], slots.at[me], load_sems.at[0]),
        pltpu.make_async_copy(wo_ref, wo, load_sems.at[1]),
        pltpu.make_async_copy(expand_ref, expand, load_sems.at[2]),
        pltpu.make_async_copy(shrink_ref, shrink, load_sems.at[3]),
        pltpu.make_async_copy(cot_ref.at[rows_at(me, size)], cot, load_sems.at[4]),
    ]
    for load in loads:
        load.start()
    greet(n)
    copies = heads_to_tokens(n, mixed_ref, slots, send_in, recv_in)
    loads[0].wait()
    loads[1].wait()
    branch = merge_heads(
        n, slots[me], slots, copies,
        lambda part, group: dot(part, wo[rows_at(group, width), :]), hidden_one_ref[...],
    )
    hidden, normed, inverse_two = layer_norm(branch, gain_ref[1:2, :], bias_ref[1:2, :])
    hidden_two[...] = hidden
    normed_two[...] = normed
    low_two[:size, :] = bf16(hidden)
    own, other = pl.ds(0, size), pl.ds(size, size)
    pair = []

    def to_mate(source, target):
        index = len(pair)
        pair.append(push(source, target, pair_send.at[index], pair_recv.at[index], mate))
        return pair[-1]

    hidden_copy = to_mate(low_two.at[own], low_two.at[other])
    loads[2].wait()

    def expand_rows(start, count):
        rows = low_two[start : start + count, :]
        for first in range(0, hidden_units, chunk):
            pre = dot(rows, expand[:, first : first + chunk])
            cdf = 0.5 + 0.5 * lax.erf(pre * 0.7071067811865476)
            act[start : start + count, first : first + chunk] = bf16(pre * cdf)
            slope[start : start + count, first : first + chunk] = bf16(
                cdf + pre * jnp.exp(-0.5 * pre * pre) * 0.3989422804014327
            )

    expand_rows(0, size)
    loads[3].wait()
    hidden_copy.wait_recv()
    y_copies = []
    for start in (0, half):
        expand_rows(size + start, half)
        y_send[start : start + half, :] = bf16(
            dot(act[size + start : size + start + half, :], shrink[...])
        )
        y_copies.append(to_mate(y_send.at[pl.ds(start, half)], y_recv.at[pl.ds(start, half)]))
    y_own[...] = dot(act[:size, :], shrink[...])
    for copy in y_copies:
        copy.wait_recv()
    output, normed, inverse = layer_norm(
        hidden_two[...] + y_own[...] + f32(y_recv[...]), gain_ref[2:3, :], bias_ref[2:3, :]
    )
    out_ref[...] = bf16(output)
    loads[4].wait()
    third, gain_three, bias_three = norm_back(f32(cot[...]), normed, inverse, gain_ref[2:3, :])
    low_three[:size, :] = bf16(third)
    grad_copy = to_mate(low_three.at[own], low_three.at[other])

    def back_rows(start, count):
        rows = low_three[start : start + count, :]
        for first in range(0, hidden_units, chunk):
            grad = dot(rows, shrink[first : first + chunk, :], NT)
            spot = (slice(start, start + count), slice(first, first + chunk))
            slope[spot] = bf16(grad * f32(slope[spot]))

    back_rows(0, size)
    grad_copy.wait_recv()
    d_copies = []
    for start in (0, half):
        back_rows(size + start, half)
        d_send[start : start + half, :] = bf16(
            dot(slope[size + start : size + start + half, :], expand[...], NT)
        )
        d_copies.append(to_mate(d_send.at[pl.ds(start, half)], d_recv.at[pl.ds(start, half)]))
    y_own[...] = third + dot(slope[:size, :], expand[...], NT)
    for copy in d_copies:
        copy.wait_recv()
    second, gain_two, bias_two = norm_back(
        y_own[...] + f32(d_recv[...]), normed_two[...], inverse_two, gain_ref[1:2, :]
    )
    second_ref[...] = second
    low = bf16(second)
    sent = tokens_to_heads(
        n, lambda cols: dot(low, wo[cols, :], NT), block, dmix_ref, send_out, recv_out, own_sem
    )
    norm_grad_ref[...] = jnp.concatenate(
        [gain_two, gain_three, bias_two, bias_three, jnp.zeros((4, norm_grad_ref.shape[1]))], axis=0
    )
    for first in range(0, hidden_units, chunk):
        shrink_grad_ref[first : first + chunk, :] = bf16(
            dot(act[:, first : first + chunk], low_three[...], TN)
        )
    for first in range(0, low_two.shape[1], 256):
        expand_grad_ref[first : first + 256, :] = bf16(
            dot(low_two[:, first : first + 256], slope[...], TN)
        )
    for group in range(n):
        wo_grad_ref[group * width : (group + 1) * width, :] = bf16(dot(slots[group], low, TN))
    for copy in sent:
        copy.wait()
    for copy in pair:
        copy.wait_send()


def feed(n, mixed, wo, expand, shrink, hidden_one, cotangent, gains, biases):
    total, width = mixed.shape
    model, units = expand.shape
    size = total // n
    shape = jax.ShapeDtypeStruct
    dma = pltpu.SemaphoreType.DMA
    low, wide = jnp.bfloat16, jnp.float32
    return pl.pallas_call(
        partial(feed_kernel, n),
        out_shape=[
            shape((size, model), low),
            shape((size, model), wide),
            shape((total, width), low),
            shape((units, model), low),
            shape((model, units), low),
            shape((model, model), low),
            shape((8, model), wide),
        ],
        in_specs=[ANYWHERE] * 4 + [IN_VMEM, ANYWHERE] + [IN_VMEM] * 2,
        out_specs=[IN_VMEM] * 2 + [ANYWHERE] + [IN_VMEM] * 4,
        scratch_shapes=[
            pltpu.VMEM((model, model), low),
            pltpu.VMEM((model, units), low),
            pltpu.VMEM((units, model), low),
            pltpu.VMEM((n, size, width), low),
            pltpu.VMEM((size, model), wide),
            pltpu.VMEM((size, model), wide),
            pltpu.VMEM((2 * size, model), low),
            pltpu.VMEM((2 * size, model), low),
            pltpu.VMEM((2 * size, units), low),
            pltpu.VMEM((2 * size, units), low),
            pltpu.VMEM((size, model), wide),
            pltpu.VMEM((size, model), low),
            pltpu.VMEM((size, model), low),
            pltpu.VMEM((size, model), low),
            pltpu.VMEM((size, model), low),
            pltpu.VMEM((size, model), low),
            pltpu.VMEM((size, model), low),
            dma((5,)), dma,
            dma((n - 1,)), dma((n - 1,)), dma((n - 1,)), dma((n - 1,)),
            dma((6,)), dma((6,)),
        ],
        compiler_params=pltpu.CompilerParams(
            collective_id=2, has_side_effects=True, vmem_limit_bytes=VMEM_LIMIT
        ),
        cost_estimate=pl.CostEstimate(
            flops=80 * 10**9, bytes_accessed=8 * total * width, transcendentals=0
        ),
        name="feed",
    )(mixed, wo, expand, shrink, hidden_one, cotangent, gains, biases)


def cross_to_self_kernel(
    n, dq_ref, wo_ref, wq_ref, second_ref, hidden_ref, normed_ref, inverse_ref, mixed_ref, gain_ref,
    first_ref, dmix_ref, wq_grad_ref, wo_grad_ref, norm_grad_ref,
    wo, wq, slots, block, wo_sem, wq_sem, own_sem, send_in, recv_in, send_out, recv_out,
):
    me = lax.axis_index("mp")
    size, model = block.shape
    width = dq_ref.shape[1]
    loads = [
        pltpu.make_async_copy(dq_ref.at[rows_at(me, size)], slots.at[me], own_sem),
        pltpu.make_async_copy(wq_ref, wq, wq_sem),
        pltpu.make_async_copy(wo_ref, wo, wo_sem),
    ]
    for load in loads:
        load.start()
    greet(n)
    copies = heads_to_tokens(n, dq_ref, slots, send_in, recv_in)
    for load in loads:
        load.wait()
    upstream = merge_heads(
        n, slots[me], slots, copies,
        lambda part, group: dot(part, wq[:, rows_at(group, width)], NT), second_ref[...],
    )
    first, gain_one, bias_one = norm_back(
        upstream, normed_ref[...], inverse_ref[:, 0:1], gain_ref[0:1, :]
    )
    first_ref[...] = first
    low = bf16(first)
    sent = tokens_to_heads(
        n, lambda cols: dot(low, wo[cols, :], NT), block, dmix_ref, send_out, recv_out, own_sem
    )
    norm_grad_ref[...] = jnp.concatenate(
        [gain_one, bias_one, jnp.zeros((6, model), jnp.float32)], axis=0
    )
    hidden_low = bf16(hidden_ref[...])
    for group in range(n):
        cols = slice(group * width, (group + 1) * width)
        wq_grad_ref[:, cols] = bf16(dot(hidden_low, slots[group], TN))
        wo_grad_ref[cols, :] = bf16(dot(mixed_ref[group], low, TN))
    for copy in sent:
        copy.wait()


def cross_to_self(n, dq, wo, wq, second, hidden, normed, inverse, slots, gains):
    total, width = dq.shape
    size, model = second.shape
    shape = jax.ShapeDtypeStruct
    dma = pltpu.SemaphoreType.DMA
    return pl.pallas_call(
        partial(cross_to_self_kernel, n),
        out_shape=[
            shape((size, model), jnp.float32),
            shape((total, width), jnp.bfloat16),
            shape((model, model), jnp.bfloat16),
            shape((model, model), jnp.bfloat16),
            shape((8, model), jnp.float32),
        ],
        in_specs=[ANYWHERE] * 3 + [IN_VMEM] * 6,
        out_specs=[IN_VMEM, ANYWHERE] + [IN_VMEM] * 3,
        scratch_shapes=[
            pltpu.VMEM((model, model), jnp.bfloat16),
            pltpu.VMEM((model, model), jnp.bfloat16),
            pltpu.VMEM((n, size, width), jnp.bfloat16),
            pltpu.VMEM((size, model), jnp.bfloat16),
            dma, dma, dma,
            dma((n - 1,)), dma((n - 1,)), dma((n - 1,)), dma((n - 1,)),
        ],
        compiler_params=pltpu.CompilerParams(
            collective_id=3, has_side_effects=True, vmem_limit_bytes=VMEM_LIMIT
        ),
        cost_estimate=pl.CostEstimate(
            flops=30 * 10**9, bytes_accessed=8 * total * width, transcendentals=0
        ),
        name="cross_to_self",
    )(dq, wo, wq, second, hidden, normed, inverse, slots, gains)


def sum_all_kernel(n_dp, n_mp, mine_ref, total_ref, slots, send_sems, recv_sems):
    n = n_dp * n_mp
    me = lax.axis_index("dp") * n_mp + lax.axis_index("mp")
    barrier = pltpu.get_barrier_semaphore()

    def place(distance):
        to = lax.rem(me + distance, n)
        return {"dp": to // n_mp, "mp": lax.rem(to, n_mp)}

    def signal(distance, carry):
        pl.semaphore_signal(barrier, inc=1, device_id=place(distance), device_id_type=MESH)
        return carry

    lax.fori_loop(1, n, signal, 0)
    pl.semaphore_wait(barrier, n - 1)

    def copy(distance):
        return pltpu.make_async_remote_copy(
            mine_ref, slots.at[me], send_sems.at[distance - 1], recv_sems.at[distance - 1],
            device_id=place(distance), device_id_type=MESH,
        )

    def start(distance, carry):
        copy(distance).start()
        return carry

    def finish(distance, carry):
        copy(distance).wait()
        return carry

    slots[me] = mine_ref[...]
    lax.fori_loop(1, n, start, 0)
    lax.fori_loop(1, n, finish, 0)
    total_ref[...] = jnp.sum(slots[...], axis=0)


def sum_all(n_dp, n_mp, block):
    n = n_dp * n_mp
    dma = pltpu.SemaphoreType.DMA
    return pl.pallas_call(
        partial(sum_all_kernel, n_dp, n_mp),
        out_shape=jax.ShapeDtypeStruct(block.shape, jnp.float32),
        in_specs=[IN_VMEM],
        out_specs=IN_VMEM,
        scratch_shapes=[
            pltpu.VMEM((n,) + block.shape, jnp.float32), dma((n - 1,)), dma((n - 1,)),
        ],
        compiler_params=pltpu.CompilerParams(collective_id=4, has_side_effects=True),
        name="sum_all",
    )(block)


def moments(upstream, first_moment, second_moment, master, decay):
    first_new = first_decay * first_moment + (1.0 - first_decay) * upstream
    second_new = second_decay * second_moment + (1.0 - second_decay) * upstream * upstream
    direction = (
        first_new
        / (1.0 - first_decay**STEP)
        / (jnp.sqrt(second_new / (1.0 - second_decay**STEP)) + epsilon)
        + decay * master
    )
    return (first_new, second_new, direction)


def squares(inner, outer, expand, shrink, norms, norm_share):
    return jnp.concatenate(
        [
            jnp.sum(inner * inner, axis=(2, 3)).reshape(6),
            jnp.sum(outer * outer, axis=(1, 2)),
            jnp.sum(expand * expand)[None],
            jnp.sum(shrink * shrink)[None],
            jnp.sum(norms * norms, axis=2).reshape(6) * norm_share,
        ]
    )


def entry_counts():
    return jnp.array([D * D] * 8 + [D * FF] * 2 + [D] * 6, dtype=jnp.float32)


def swap_far(values, n):
    return lax.ppermute(values, "mp", [(i, (i + n // 2) % n) for i in range(n)])


def on_device(
    inputs,
    encoder,
    prefix,
    cotangent,
    inner_weights,
    inner_first,
    inner_second,
    outer_weights,
    outer_first,
    outer_second,
    expand_weights,
    expand_first,
    expand_second,
    shrink_weights,
    shrink_first,
    shrink_second,
    norm_params,
    norm_first,
    norm_second,
):
    n_dp, n_mp = lax.axis_size("dp"), lax.axis_size("mp")
    seq_count, seq_len, model = inputs.shape
    tokens = inputs.reshape(seq_len, model)
    states = encoder.reshape(-1, model)
    inner_low, outer_low = bf16(inner_weights), bf16(outer_weights)
    expand_low, shrink_low = bf16(expand_weights), bf16(shrink_weights)

    self_weights = lax.all_gather(inner_low[0], "dp", axis=1, tiled=True)
    norm_all = f32(lax.all_gather(bf16(norm_params), "dp", axis=2, tiled=True))
    gains, biases = norm_all[0], norm_all[1]
    outer_all = (
        lax.all_gather(outer_low, ("dp", "mp"))
        .reshape((n_dp, n_mp) + outer_low.shape)
        .transpose(2, 1, 3, 0, 4)
        .reshape(2, model, model)
    )
    query_all = (
        lax.all_gather(inner_low[1, 0], ("dp", "mp"))
        .reshape((n_dp, n_mp) + inner_low.shape[2:])
        .transpose(0, 2, 1, 3)
        .reshape(model, model)
    )
    source_weights = lax.all_gather(inner_low[1, 1:], "dp", axis=1, tiled=True)
    expand_two = lax.all_gather(
        jnp.concatenate([expand_low, swap_far(expand_low, n_mp)], axis=1), "dp", axis=0, tiled=True
    )
    shrink_two = lax.all_gather(
        jnp.concatenate([shrink_low, swap_far(shrink_low, n_mp)], axis=0), "dp", axis=1, tiled=True
    )

    project = lambda rows, weights: bf16(
        jnp.einsum("td,cdm->ctm", rows, weights, preferred_element_type=jnp.float32)
    )
    self_proj = project(tokens, self_weights)
    self_mixed, self_sums = attend_forward(self_proj[0], self_proj[1], self_proj[2], prefix, True)
    hidden_one, normed_one, inverse_one, self_slots, cross_query = self_to_cross(
        n_mp, self_mixed, outer_all[0], query_all, tokens, gains, biases
    )
    source = project(states, source_weights)
    cross_mixed, cross_sums = attend_forward(cross_query, source[0], source[1], prefix, False)
    out_rows, grad_second, cross_dmix, shrink_grad, expand_grad, cross_wo_grad, norm_rows = feed(
        n_mp, cross_mixed, outer_all[1], expand_two, shrink_two, hidden_one,
        cotangent.reshape(seq_len, model), gains, biases,
    )
    layer_out = f32(lax.all_gather(out_rows, "mp", axis=0, tiled=True))
    cross_dq, cross_dk, cross_dv = attend_backward(
        cross_query, source[0], source[1], cross_dmix, cross_mixed, cross_sums, prefix, False
    )
    state_part = dot(cross_dk, source_weights[0], NT) + dot(cross_dv, source_weights[1], NT)
    encoder_grad = f32(lax.psum(bf16(state_part), "mp"))
    source_grad = jnp.stack([dot(states, cross_dk, TN), dot(states, cross_dv, TN)])
    grad_first, self_dmix, query_grad, self_wo_grad, norm_one = cross_to_self(
        n_mp, cross_dq, outer_all[0], query_all, grad_second, hidden_one, normed_one, inverse_one,
        self_slots, gains,
    )
    self_grads = jnp.stack(
        attend_backward(
            self_proj[0], self_proj[1], self_proj[2], self_dmix, self_mixed, self_sums, prefix, True
        )
    )
    self_inner_grad = jnp.einsum(
        "td,ctm->cdm", tokens, self_grads, preferred_element_type=jnp.float32
    )
    input_part = jnp.einsum(
        "ctm,cdm->td", self_grads, self_weights, preferred_element_type=jnp.float32
    )
    input_rows = grad_first + f32(
        lax.psum_scatter(bf16(input_part), "mp", scatter_dimension=0, tiled=True)
    )
    input_grad = f32(lax.all_gather(bf16(input_rows), "mp", axis=0, tiled=True))

    scatter = lambda values, axis, dim: lax.psum_scatter(
        bf16(values), axis, scatter_dimension=dim, tiled=True
    )
    shrink_both = scatter(shrink_grad, "dp", 1)
    expand_both = scatter(expand_grad, "dp", 0)
    units = shrink_low.shape[0]
    shrink_grad = f32(shrink_both[:units]) + f32(swap_far(shrink_both[units:], n_mp))
    expand_grad = f32(expand_both[:, :units]) + f32(swap_far(expand_both[:, units:], n_mp))
    outer_grad = f32(
        scatter(scatter(jnp.stack([self_wo_grad, cross_wo_grad]), "dp", 2), "mp", 1)
    )
    query_grad = f32(scatter(scatter(query_grad, "dp", 0), "mp", 1))
    inner_grad = jnp.stack(
        [
            f32(scatter(self_inner_grad, "dp", 1)),
            jnp.concatenate([query_grad[None], f32(scatter(source_grad, "dp", 1))]),
        ]
    )
    norm_grad = jnp.stack(
        [
            jnp.stack([norm_one[0], norm_rows[0], norm_rows[1]]),
            jnp.stack([norm_one[1], norm_rows[2], norm_rows[3]]),
        ]
    )
    norm_grad = lax.psum(
        lax.psum_scatter(norm_grad, "dp", scatter_dimension=2, tiled=True), "mp"
    )
    inner_f, inner_s, inner_d = moments(
        inner_grad, inner_first, inner_second, inner_weights, weight_decay
    )
    outer_f, outer_s, outer_d = moments(
        outer_grad, outer_first, outer_second, outer_weights, weight_decay
    )
    expand_f, expand_s, expand_d = moments(
        expand_grad, expand_first, expand_second, expand_weights, weight_decay
    )
    shrink_f, shrink_s, shrink_d = moments(
        shrink_grad, shrink_first, shrink_second, shrink_weights, weight_decay
    )
    norm_f, norm_s, norm_d = moments(norm_grad, norm_first, norm_second, norm_params, 0.0)
    norm_share = 1.0 / n_mp
    weight_local = squares(
        inner_weights, outer_weights, expand_weights, shrink_weights, norm_params, norm_share
    )
    update_local = squares(inner_d, outer_d, expand_d, shrink_d, norm_d, norm_share)
    both = jnp.concatenate([weight_local, update_local])
    totals = sum_all(n_dp, n_mp, jnp.zeros((8, 128), jnp.float32).at[0, :32].set(both))
    counts_all = entry_counts()
    weight_norm = jnp.sqrt(totals[0, 0:16] / counts_all)
    update_norm = jnp.sqrt(totals[0, 16:32] / counts_all)
    trust = weight_norm / (update_norm + epsilon)
    inner_new = inner_weights - learn_rate * trust[0:6].reshape(2, 3, 1, 1) * inner_d
    outer_new = outer_weights - learn_rate * trust[6:8].reshape(2, 1, 1) * outer_d
    expand_new = expand_weights - learn_rate * trust[8] * expand_d
    shrink_new = shrink_weights - learn_rate * trust[9] * shrink_d
    norm_new = norm_params - learn_rate * trust[10:16].reshape(2, 3, 1) * norm_d
    table = jnp.stack([weight_norm, update_norm, trust])
    return (
        layer_out.reshape(seq_count, seq_len, model),
        input_grad.reshape(seq_count, seq_len, model),
        encoder_grad.reshape(seq_count, -1, model),
        inner_new,
        outer_new,
        expand_new,
        shrink_new,
        norm_new,
        inner_f,
        outer_f,
        expand_f,
        shrink_f,
        norm_f,
        inner_s,
        outer_s,
        expand_s,
        shrink_s,
        norm_s,
        table,
    )


def solution(mesh):
    placed = (
        P("dp", None, None),
        P("dp", None, None),
        P("dp"),
        P("dp", None, None),
        P(None, None, "dp", "mp"),
        P(None, None, "dp", "mp"),
        P(None, None, "dp", "mp"),
        P(None, "mp", "dp"),
        P(None, "mp", "dp"),
        P(None, "mp", "dp"),
        P("dp", "mp"),
        P("dp", "mp"),
        P("dp", "mp"),
        P("mp", "dp"),
        P("mp", "dp"),
        P("mp", "dp"),
        P(None, None, "dp"),
        P(None, None, "dp"),
        P(None, None, "dp"),
    )
    return jax.shard_map(
        on_device,
        mesh=mesh,
        in_specs=placed,
        out_specs=(
            P("dp", None, None),
            P("dp", None, None),
            P("dp", None, None),
            P(None, None, "dp", "mp"),
            P(None, "mp", "dp"),
            P("dp", "mp"),
            P("mp", "dp"),
            P(None, None, "dp"),
            P(None, None, "dp", "mp"),
            P(None, "mp", "dp"),
            P("dp", "mp"),
            P("mp", "dp"),
            P(None, None, "dp"),
            P(None, None, "dp", "mp"),
            P(None, "mp", "dp"),
            P("dp", "mp"),
            P("mp", "dp"),
            P(None, None, "dp"),
            P(),
        ),
        check_vma=False,
    )
```

```python
from functools import partial

import jax
import jax.numpy as jnp
from jax import lax
from jax.experimental import pallas as pl
from jax.experimental.pallas import tpu as pltpu
from jax.sharding import PartitionSpec as P

D = 1024
HEAD = 64
FF = 4096
STEP = 5

first_decay = 0.5
second_decay = 0.6
learn_rate = 0.5
weight_decay = 0.01
epsilon = 1e-06
norm_eps = 1e-05
mask_fill = -1000000000.0

MESH = pl.DeviceIdType.MESH
ANYWHERE = pl.BlockSpec(memory_space=pl.ANY)
IN_VMEM = pl.BlockSpec(memory_space=pltpu.VMEM)
NN = (((1,), (0,)), ((), ()))
NT = (((1,), (1,)), ((), ()))
TN = (((0,), (0,)), ((), ()))
VMEM_LIMIT = 54 << 20


def dot(left, right, dims=NN):
    return lax.dot_general(left, right, dims, preferred_element_type=jnp.float32)


def bf16(values):
    return values.astype(jnp.bfloat16)


def f32(values):
    return values.astype(jnp.float32)


def layer_norm(values, gain_row, bias_row):
    center = values - jnp.mean(values, axis=-1, keepdims=True)
    spread = jnp.mean(center * center, axis=-1, keepdims=True)
    inverse = lax.rsqrt(spread + norm_eps)
    normed = center * inverse
    return (normed * gain_row + bias_row, normed, inverse)


def norm_back(upstream, normed, inverse, gain_row):
    scaled = upstream * gain_row
    inner = (
        scaled
        - jnp.mean(scaled, axis=-1, keepdims=True)
        - normed * jnp.mean(scaled * normed, axis=-1, keepdims=True)
    )
    return (
        inner * inverse,
        jnp.sum(upstream * normed, axis=0, keepdims=True),
        jnp.sum(upstream, axis=0, keepdims=True),
    )


class Place:
    def __init__(self, n_mp, side):
        self.n, self.side = n_mp, side
        self.z = lax.axis_index("mp")
        dp = lax.axis_index("dp")
        self.core = lax.rem(dp, 2)
        self.x = lax.rem(dp // 2, side)
        self.y = dp // (2 * side)

    def at(self, y, x, core):
        return {"dp": (y * self.side + x) * 2 + core}

    def x_peer(self, distance):
        other = lax.rem(self.x + distance, self.side)
        return other, self.at(self.y, other, self.core)

    def y_peer(self, distance):
        other = lax.rem(self.y + distance, self.side)
        return other, self.at(other, self.x, self.core)

    def sibling(self):
        return self.at(self.y, self.x, 1 - self.core)

    def line(self):
        return [{"mp": lax.rem(self.z + distance, self.n)} for distance in range(1, self.n)]

    def plane(self):
        steps = range(1, self.side)
        return (
            [self.x_peer(step)[1] for step in steps]
            + [self.y_peer(step)[1] for step in steps]
            + [self.sibling()]
        )


def greet(others):
    barrier = pltpu.get_barrier_semaphore()
    for other in others:
        pl.semaphore_signal(barrier, inc=1, device_id=other, device_id_type=MESH)
    pl.semaphore_wait(barrier, len(others))


def push(source, target, send_sem, recv_sem, to):
    copy = pltpu.make_async_remote_copy(
        source, target, send_sem, recv_sem, device_id=to, device_id_type=MESH
    )
    copy.start()
    return copy


def rows_at(index, size):
    return pl.ds(pl.multiple_of(index * size, size), size)


def heads_to_tokens(n, source, slots, send_sems, recv_sems):
    me = lax.axis_index("mp")
    size = source.shape[0] // n
    copies = []
    for distance in range(1, n):
        to = lax.rem(me + distance, n)
        copies.append(
            push(
                source.at[rows_at(to, size)], slots.at[me],
                send_sems.at[distance - 1], recv_sems.at[distance - 1], {"mp": to},
            )
        )
    return copies


def tokens_to_heads(n, make, blocks, target, send_sems, recv_sems, local_sem):
    me = lax.axis_index("mp")
    size = blocks.shape[1]
    copies = []
    for distance in (*range(1, n), 0):
        to = lax.rem(me + distance, n)
        blocks[to] = bf16(make(to))
        place = target.at[rows_at(me, size)]
        if distance:
            copies.append(
                push(
                    blocks.at[to], place,
                    send_sems.at[distance - 1], recv_sems.at[distance - 1], {"mp": to},
                )
            )
        else:
            copy = pltpu.make_async_copy(blocks.at[to], place, local_sem)
            copy.start()
            copies.append(copy)
    return copies


def merge_heads(n, slots, copies, part_of, start):
    me = lax.axis_index("mp")
    total = start + part_of(slots[me], me)
    for distance in range(1, n):
        origin = lax.rem(me + n - distance, n)
        copies[distance - 1].wait_recv()
        total = total + part_of(slots[origin], origin)
    for copy in copies:
        copy.wait_send()
    return total


def load_groups(n, bundle, first, width, target, sems):
    return [
        pltpu.make_async_copy(
            bundle.at[:, pl.ds(group * 3 * width + first, width)], target.at[group], sems.at[group]
        )
        for group in range(n)
    ]


class Give:
    def __init__(self, place, out, sems):
        self.place, self.n, self.me, self.out = place, place.n, place.z, out
        self.sems = {"right": sems[0:2], "left": sems[2:4]}

    @staticmethod
    def sems(n):
        return [pltpu.SemaphoreType.DMA((max(n - 1, 1),))] * 4

    def _copy(self, way, step):
        ahead = 1 if way == "right" else -1
        chunk = lax.rem(self.me - ahead * step + self.n, self.n)
        return pltpu.make_async_remote_copy(
            self.out.at[chunk], self.out.at[chunk],
            self.sems[way][0].at[step], self.sems[way][1].at[step],
            device_id={"mp": lax.rem(self.me + ahead + self.n, self.n)}, device_id_type=MESH,
        )

    def _spots(self):
        return (("right", self.me), ("left", self.n - 1 - self.me))

    def step(self, step):
        for way, spot in self._spots():

            @pl.when((spot >= step) & (spot < self.n - 1))
            def _():
                if step > 0:
                    self._copy(way, step - 1).wait_recv()
                self._copy(way, step).start()

    def finish(self):
        for way, spot in self._spots():

            @pl.when(spot == self.n - 1)
            def _():
                for step in range(self.n - 1):
                    self._copy(way, step).wait_recv()

            for step in range(self.n - 1):

                @pl.when((spot >= step) & (spot < self.n - 1))
                def _():
                    self._copy(way, step).wait_send()


def sizes_of(total, block, limit):
    groups = {}
    for index in range(total // block):
        groups.setdefault(limit(index), []).append(index)
    return groups.items()


def forward_kernel(masked, block, prefix_ref, q_ref, k_ref, v_ref, mixed_ref, sums_ref):
    width = q_ref.shape[1]
    heads = width // HEAD
    keys_total = k_ref.shape[0]
    step = pl.program_id(0)
    lane = lax.broadcasted_iota(jnp.int32, (block, width), 1) // HEAD

    def run(keys, start):
        query = q_ref[...] * jnp.bfloat16(HEAD**-0.5)
        key_rows = k_ref[:keys, :]
        value_rows = v_ref[:keys, :]
        if masked:
            rows = start + lax.broadcasted_iota(jnp.int32, (block, keys), 0)
            cols = lax.broadcasted_iota(jnp.int32, (block, keys), 1)
            allowed = (cols <= rows) | (cols < prefix_ref[0])
        mixed = jnp.zeros((block, width), jnp.float32)
        slot = lax.broadcasted_iota(jnp.int32, (block, 128), 1)
        table = jnp.zeros((block, 128), jnp.float32)
        for head in range(heads):
            scores = dot(jnp.where(lane == head, query, jnp.bfloat16(0)), key_rows, NT)
            if masked:
                scores = jnp.where(allowed, scores, mask_fill)
            row_max = jnp.max(scores, axis=1, keepdims=True)
            powered = jnp.exp(scores - row_max)
            totals = jnp.sum(powered, axis=1, keepdims=True)
            part = dot(bf16(powered), value_rows) * (1.0 / totals)
            mixed = jnp.where(lane == head, part, mixed)
            table = jnp.where(slot == head, row_max + jnp.log(totals), table)
        mixed_ref[...] = bf16(mixed)
        sums_ref[...] = table.T[:8, :]

    if masked:
        limit = lambda index: max(keys_total // 2, (index + 1) * block)
        for keys, blocks in sizes_of(keys_total, block, limit):

            @pl.when((step >= blocks[0]) & (step <= blocks[-1]))
            def _(keys=keys):
                run(keys, step * block)
    else:
        run(keys_total, 0)


def attend_forward(query, key_rows, value_rows, prefix, masked, block=512):
    total, width = query.shape
    keys = key_rows.shape[0]
    block = min(block, total)
    whole = pl.BlockSpec((keys, width), lambda i, p: (0, 0))
    return pl.pallas_call(
        partial(forward_kernel, masked, block),
        grid_spec=pltpu.PrefetchScalarGridSpec(
            num_scalar_prefetch=1,
            grid=(total // block,),
            in_specs=[pl.BlockSpec((block, width), lambda i, p: (i, 0)), whole, whole],
            out_specs=[
                pl.BlockSpec((block, width), lambda i, p: (i, 0)),
                pl.BlockSpec((8, block), lambda i, p: (0, i)),
            ],
        ),
        out_shape=[
            jax.ShapeDtypeStruct((total, width), jnp.bfloat16),
            jax.ShapeDtypeStruct((8, total), jnp.float32),
        ],
        compiler_params=pltpu.CompilerParams(vmem_limit_bytes=VMEM_LIMIT),
        cost_estimate=pl.CostEstimate(
            flops=16 * total * keys * width, bytes_accessed=4 * keys * width, transcendentals=0
        ),
        name="attend_forward",
    )(prefix, query, key_rows, value_rows)


def backward_kernel(
    masked, block, n, prefix_ref, q_ref, k_ref, v_ref, do_ref, o_ref, sums_ref, *refs,
):
    if n:
        mine_ref, states_ref, dq_ref, dk_ref, dv_ref, all_ref, source_ref, *refs = refs
        acc, delta, source, own_sem, *sems = refs
        give = Give(Place(n, 1), all_ref, sems)
    else:
        dq_ref, dk_ref, dv_ref, acc, delta = refs
    width = q_ref.shape[1]
    heads = width // HEAD
    total = q_ref.shape[0]
    step = pl.program_id(0)
    factor = HEAD**-0.5

    @pl.when(step == 0)
    def _():
        if n:
            source[...] = jnp.zeros_like(source)
            own = pltpu.make_async_copy(mine_ref, all_ref.at[give.me], own_sem)
            own.start()
            greet(give.place.line())
            own.wait()
            give.step(0)
        product = f32(do_ref[...]) * f32(o_ref[...])
        row = lax.broadcasted_iota(jnp.int32, (8, width), 0)
        col = lax.broadcasted_iota(jnp.int32, (8, width), 1) // HEAD
        pick = jnp.where(row == col, 1.0, 0.0).astype(jnp.float32)
        delta[...] = lax.dot_general(
            pick, product, NT, precision=lax.Precision.HIGHEST, preferred_element_type=jnp.float32
        )
        acc[...] = jnp.zeros_like(acc)

    if n:
        steps = pl.num_programs(0)
        for later in range(1, n - 1):

            @pl.when(step == (later + 1) * steps // n)
            def _():
                give.step(later)

    lane = lax.broadcasted_iota(jnp.int32, (block, width), 1) // HEAD

    def run(first):
        count = total - first
        query = q_ref[first:, :]
        grad_rows = do_ref[first:, :]
        scaled_keys = k_ref[...] * jnp.bfloat16(factor)
        value_rows = v_ref[...]
        if masked:
            rows = first + lax.broadcasted_iota(jnp.int32, (block, count), 1)
            cols = step * block + lax.broadcasted_iota(jnp.int32, (block, count), 0)
            allowed = (cols <= rows) | (cols < prefix_ref[0])
        key_grad = jnp.zeros((block, width), jnp.float32)
        value_grad = jnp.zeros((block, width), jnp.float32)
        query_grad = jnp.zeros((count, width), jnp.float32)
        for head in range(heads):
            own_keys = jnp.where(lane == head, scaled_keys, jnp.bfloat16(0))
            scores = dot(own_keys, query, NT)
            if masked:
                scores = jnp.where(allowed, scores, mask_fill)
            probs = jnp.exp(scores - sums_ref[head : head + 1, first:])
            prob_grad = dot(jnp.where(lane == head, value_rows, jnp.bfloat16(0)), grad_rows, NT)
            score_grad = bf16(probs * (prob_grad - delta[head : head + 1, first:]))
            value_grad = jnp.where(lane == head, dot(bf16(probs), grad_rows), value_grad)
            key_grad = jnp.where(lane == head, dot(score_grad, query), key_grad)
            query_grad = query_grad + dot(score_grad, own_keys, TN)
        acc[first:, :] += query_grad
        dk_ref[...] = bf16(key_grad * factor)
        dv_ref[...] = bf16(value_grad)
        if n:
            source[:, :width] += dot(states_ref[...], dk_ref[...], TN)
            source[:, width:] += dot(states_ref[...], dv_ref[...], TN)

    if masked:
        limit = lambda index: 0 if index * block < total // 2 else index * block
        for first, blocks in sizes_of(total, block, limit):

            @pl.when((step >= blocks[0]) & (step <= blocks[-1]))
            def _(first=first):
                run(first)
    else:
        run(0)

    @pl.when(step == pl.num_programs(0) - 1)
    def _():
        dq_ref[...] = bf16(acc[...])
        if n:
            source_ref[...] = bf16(source[...])
            give.finish()


def attend_backward(
    query, key_rows, value_rows, grad_out, mixed, sums, prefix, masked, n=0, mine=(), states=(), block=512
):
    total, width = query.shape
    keys = key_rows.shape[0]
    whole = pl.BlockSpec((total, width), lambda i, p: (0, 0))
    part = pl.BlockSpec((block, width), lambda i, p: (i, 0))
    return pl.pallas_call(
        partial(backward_kernel, masked, block, n),
        grid_spec=pltpu.PrefetchScalarGridSpec(
            num_scalar_prefetch=1,
            grid=(keys // block,),
            in_specs=[
                whole, part, part, whole, whole, pl.BlockSpec((8, total), lambda i, p: (0, 0)),
            ]
            + [pl.BlockSpec(rows.shape, lambda i, p: (0, 0)) for rows in mine]
            + [pl.BlockSpec((block, rows.shape[1]), lambda i, p: (i, 0)) for rows in states],
            out_specs=[whole, part, part]
            + [ANYWHERE] * len(mine)
            + [pl.BlockSpec((rows.shape[1], 2 * width), lambda i, p: (0, 0)) for rows in states],
            scratch_shapes=[
                pltpu.VMEM((total, width), jnp.float32),
                pltpu.VMEM((8, total), jnp.float32),
            ]
            + [pltpu.VMEM((rows.shape[1], 2 * width), jnp.float32) for rows in states]
            + [pltpu.SemaphoreType.DMA] * len(mine)
            + Give.sems(n) * len(mine),
        ),
        out_shape=[jax.ShapeDtypeStruct((total, width), jnp.bfloat16)]
        + [jax.ShapeDtypeStruct((keys, width), jnp.bfloat16)] * 2
        + [jax.ShapeDtypeStruct((n,) + rows.shape, rows.dtype) for rows in mine]
        + [jax.ShapeDtypeStruct((rows.shape[1], 2 * width), rows.dtype) for rows in states],
        compiler_params=pltpu.CompilerParams(
            vmem_limit_bytes=VMEM_LIMIT,
            **(dict(collective_id=6, has_side_effects=True) if n else {}),
        ),
        cost_estimate=pl.CostEstimate(
            flops=4 * total * keys * width, bytes_accessed=4 * keys * width, transcendentals=0
        ),
        name="attend_backward",
    )(prefix, query, key_rows, value_rows, grad_out, mixed, sums, *mine, *states)


class Spread:
    def __init__(self, place, home, send_sems, recv_sems):
        self.place, self.home, self.send, self.recv = place, home, send_sems, recv_sems
        self.half = home.shape[3] // 2
        self.copies = {"first": [], "second": [], "core": []}
        self.index = 0

    def _push(self, stage, block, to):
        spot = self.index
        self.index += 1
        self.copies[stage].append(push(block, block, self.send.at[spot], self.recv.at[spot], to))

    def first(self):
        p, half = self.place, self.half
        for step in range(1, p.side):
            own = self.home.at[p.y, p.x, p.core]
            self._push("first", own.at[pl.ds(0, half)], p.x_peer(step)[1])
            self._push("first", own.at[pl.ds(half, half)], p.y_peer(step)[1])

    def second(self):
        p, half = self.place, self.half
        for copy in self.copies["first"]:
            copy.wait_recv()
        for step in range(1, p.side):
            self._push(
                "second", self.home.at[p.y, :, p.core, pl.ds(0, half)], p.y_peer(step)[1]
            )
            self._push(
                "second", self.home.at[:, p.x, p.core, pl.ds(half, half)], p.x_peer(step)[1]
            )

    def core(self):
        for copy in self.copies["second"]:
            copy.wait_recv()
        self._push("core", self.home.at[:, :, self.place.core], self.place.sibling())

    def finish(self):
        for copy in self.copies["core"] or self.copies["second"]:
            copy.wait_recv()
        for stage in self.copies.values():
            for copy in stage:
                copy.wait_send()

    @staticmethod
    def sems(side):
        return pltpu.SemaphoreType.DMA((4 * (side - 1) + 1,))


def front_kernel(
    n, side, inner_ref, outer_ref, norm_ref, expand_ref, shrink_ref, home_self, home_rest, feed_ref,
    self_sems_send, self_sems_recv, rest_send, rest_recv, line_send, line_recv,
    block_self, block_line, block_rest, own_sems, far_send, far_recv,
):
    p = Place(n, side)
    width = inner_ref.shape[3]
    for index in range(3):
        block_self[:, index * width : (index + 1) * width] = bf16(inner_ref[0, index])
    block_line[:, :width] = bf16(inner_ref[1, 0])
    for index in range(2):
        block_line[:, (index + 1) * width : (index + 2) * width] = outer_ref[index]
        block_rest[:, index * width : (index + 1) * width] = bf16(inner_ref[1, index + 1])
    block_rest[:, 2 * width :] = norm_ref[...]
    units = expand_ref.shape[1]
    feed_ref[:, :units] = bf16(expand_ref[...])
    feed_ref[:, 2 * units : 3 * units] = shrink_ref[...]
    whole = 3 * width
    line_cols = pl.ds(pl.multiple_of(p.z * whole, whole), whole)
    spot = home_rest.at[p.y, p.x, p.core]
    own = [
        pltpu.make_async_copy(block_self, home_self.at[p.y, p.x, p.core], own_sems.at[0]),
        pltpu.make_async_copy(block_line, spot.at[:, line_cols], own_sems.at[1]),
        pltpu.make_async_copy(
            block_rest, spot.at[:, pl.ds(n * whole, block_rest.shape[1])], own_sems.at[2]
        ),
    ]
    for copy in own:
        copy.start()
    greet(p.line() + p.plane())
    line = [
        push(block_line, spot.at[:, line_cols], line_send.at[index], line_recv.at[index], other)
        for index, other in enumerate(p.line())
    ]
    far = {"mp": lax.rem(p.z + n // 2, n)}
    far_copies = [
        push(
            feed_ref.at[:, pl.ds(2 * index * units, units)],
            feed_ref.at[:, pl.ds((2 * index + 1) * units, units)],
            far_send.at[index], far_recv.at[index], far,
        )
        for index in range(2)
    ]
    for copy in own:
        copy.wait()
    near = Spread(p, home_self, self_sems_send, self_sems_recv)
    rest = Spread(p, home_rest, rest_send, rest_recv)
    near.first()
    near.second()
    near.core()
    for copy in line:
        copy.wait_recv()
    rest.first()
    near.finish()
    rest.second()
    rest.core()
    rest.finish()
    for copy in line:
        copy.wait_send()
    for copy in far_copies:
        copy.wait()


def front(n_dp, n_mp, inner, outer_t, norm_t, expand, shrink_t):
    rows, width = inner.shape[2:]
    side = round((n_dp // 2) ** 0.5)
    whole = 3 * width
    columns = n_mp * whole + 2 * width + norm_t.shape[1]
    low = jnp.bfloat16
    dma = pltpu.SemaphoreType.DMA
    near, rest, feed_block = pl.pallas_call(
        partial(front_kernel, n_mp, side),
        out_shape=[
            jax.ShapeDtypeStruct((side, side, 2, rows, whole), low),
            jax.ShapeDtypeStruct((side, side, 2, rows, columns), low),
            jax.ShapeDtypeStruct((rows, 4 * expand.shape[1]), low),
        ],
        in_specs=[IN_VMEM] * 5,
        out_specs=[ANYWHERE, ANYWHERE, IN_VMEM],
        scratch_shapes=[
            Spread.sems(side), Spread.sems(side), Spread.sems(side), Spread.sems(side),
            dma((n_mp - 1,)), dma((n_mp - 1,)),
            pltpu.VMEM((rows, whole), low),
            pltpu.VMEM((rows, whole), low),
            pltpu.VMEM((rows, 2 * width + norm_t.shape[1]), low),
            dma((3,)), dma((2,)), dma((2,)),
        ],
        compiler_params=pltpu.CompilerParams(
            collective_id=0, has_side_effects=True, vmem_limit_bytes=VMEM_LIMIT
        ),
        cost_estimate=pl.CostEstimate(flops=40 * 10**9, bytes_accessed=1 << 20, transcendentals=0),
        name="front",
    )(inner, outer_t, norm_t, expand, shrink_t)
    return near.reshape(n_dp * rows, whole), rest.reshape(n_dp * rows, columns), feed_block


def self_to_cross_kernel(
    n, side, mixed_ref, bundle_ref, x_ref, feed_ref, gain_ref, bias_ref,
    hidden_ref, normed_ref, inverse_ref, slots_ref, q_ref, home_ref,
    wo, wq, x_rows, blocks, wo_sems, wq_sems, x_sem, own_sem, send_in, recv_in, send_out, recv_out,
    feed_block, feed_sem, feed_send, feed_recv,
):
    p = Place(n, side)
    me = p.z
    size = x_rows.shape[0]
    width = mixed_ref.shape[1]
    loads = [
        pltpu.make_async_copy(mixed_ref.at[rows_at(me, size)], slots_ref.at[me], own_sem),
        pltpu.make_async_copy(x_ref.at[rows_at(me, size)], x_rows, x_sem),
        *load_groups(n, bundle_ref, width, width, wo, wo_sems),
        *load_groups(n, bundle_ref, 0, width, wq, wq_sems),
    ]
    feed_load = pltpu.make_async_copy(feed_ref, feed_block, feed_sem)
    feed_load.start()
    for load in loads:
        load.start()
    greet(p.line() + p.plane())
    copies = heads_to_tokens(n, mixed_ref, slots_ref, send_in, recv_in)
    feed_load.wait()
    home_copy = pltpu.make_async_copy(feed_block, home_ref.at[p.y, p.x, p.core], feed_sem)
    home_copy.start()
    home_copy.wait()
    spread = Spread(p, home_ref, feed_send, feed_recv)
    spread.first()
    for load in loads:
        load.wait()
    branch = merge_heads(
        n, slots_ref, copies, lambda part, group: dot(part, wo[group], NT), f32(x_rows[...])
    )
    hidden, normed, inverse = layer_norm(branch, gain_ref[0:1, :], bias_ref[0:1, :])
    hidden_ref[...] = hidden
    normed_ref[...] = normed
    inverse_ref[...] = jnp.broadcast_to(inverse, inverse_ref.shape)
    low = bf16(hidden)
    sent = tokens_to_heads(
        n, lambda group: dot(low, wq[group]), blocks, q_ref, send_out, recv_out, own_sem
    )
    spread.second()
    for copy in sent:
        copy.wait()
    spread.finish()


def self_to_cross(n_dp, n, mixed, bundle, tokens, feed_block, gains, biases):
    side = round((n_dp // 2) ** 0.5)
    total, width = mixed.shape
    size, model = total // n, tokens.shape[1]
    shape = jax.ShapeDtypeStruct
    dma = pltpu.SemaphoreType.DMA
    return pl.pallas_call(
        partial(self_to_cross_kernel, n, side),
        out_shape=[
            shape((size, model), jnp.float32),
            shape((size, model), jnp.float32),
            shape((size, 128), jnp.float32),
            shape((n, size, width), jnp.bfloat16),
            shape((total, width), jnp.bfloat16),
            shape((side, side, 2) + feed_block.shape, jnp.bfloat16),
        ],
        in_specs=[ANYWHERE] * 4 + [IN_VMEM] * 2,
        out_specs=[IN_VMEM] * 4 + [ANYWHERE] * 2,
        scratch_shapes=[
            pltpu.VMEM((n, model, width), jnp.bfloat16),
            pltpu.VMEM((n, model, width), jnp.bfloat16),
            pltpu.VMEM((size, model), jnp.bfloat16),
            pltpu.VMEM((n, size, width), jnp.bfloat16),
            dma((n,)), dma((n,)), dma, dma,
            dma((n - 1,)), dma((n - 1,)), dma((n - 1,)), dma((n - 1,)),
            pltpu.VMEM(feed_block.shape, jnp.bfloat16),
            dma, Spread.sems(side), Spread.sems(side),
        ],
        compiler_params=pltpu.CompilerParams(
            collective_id=1, has_side_effects=True, vmem_limit_bytes=VMEM_LIMIT
        ),
        cost_estimate=pl.CostEstimate(
            flops=10**9, bytes_accessed=8 * total * width, transcendentals=0
        ),
        name="self_to_cross",
    )(mixed, bundle, tokens, feed_block, gains, biases)


def feed_kernel(
    n, side, mixed_ref, bundle_ref, home_ref, hidden_one_ref, cot_ref, gain_ref, bias_ref,
    out_ref, second_ref, dmix_ref, shrink_grad_ref, expand_grad_ref, wo_grad_ref, norm_grad_ref,
    wo, weights, slots, hidden_two, normed_two, low_two, low_three, act, slope,
    y_own, y_send, y_recv, d_send, d_recv, cot, blocks,
    load_sems, wo_sems, own_sem, send_in, recv_in, send_out, recv_out, pair_send, pair_recv,
    home_sems, home_send, home_recv,
):
    p = Place(n, side)
    me = p.z
    mate = {"mp": me + 1 - 2 * lax.rem(me, 2)}
    size = cot.shape[0]
    half = size // 2
    width = mixed_ref.shape[1]
    hidden_units = act.shape[1]
    chunk = min(512, hidden_units)
    loads = [
        pltpu.make_async_copy(mixed_ref.at[rows_at(me, size)], slots.at[me], load_sems.at[0]),
        *load_groups(n, bundle_ref, 2 * width, width, wo, wo_sems),
        pltpu.make_async_copy(cot_ref.at[rows_at(me, size)], cot, load_sems.at[1]),
    ]
    rows = home_ref.shape[3]
    places = [(y, x) for y in range(side) for x in range(side)]
    spots = [rows_at((y * side + x) * 2 + p.core, rows) for y, x in places]
    homes = [
        pltpu.make_async_copy(home_ref.at[y, x, p.core], weights.at[spot], home_sems.at[index])
        for index, ((y, x), spot) in enumerate(zip(places, spots))
    ]
    for load in loads + homes:
        load.start()
    greet(p.line() + [p.sibling()])
    copies = heads_to_tokens(n, mixed_ref, slots, send_in, recv_in)
    home_copies = [
        push(
            home_ref.at[y, x, p.core], weights.at[spot],
            home_send.at[index], home_recv.at[index], p.sibling(),
        )
        for index, ((y, x), spot) in enumerate(zip(places, spots))
    ]
    for load in loads[: n + 1]:
        load.wait()
    branch = merge_heads(
        n, slots, copies, lambda part, group: dot(part, wo[group], NT), hidden_one_ref[...]
    )
    hidden, normed, inverse_two = layer_norm(branch, gain_ref[1:2, :], bias_ref[1:2, :])
    hidden_two[...] = hidden
    normed_two[...] = normed
    low_two[:size, :] = bf16(hidden)
    own, other = pl.ds(0, size), pl.ds(size, size)
    pair = []

    def to_mate(source, target):
        index = len(pair)
        pair.append(push(source, target, pair_send.at[index], pair_recv.at[index], mate))
        return pair[-1]

    hidden_copy = to_mate(low_two.at[own], low_two.at[other])
    for copy in homes:
        copy.wait()
    for copy in home_copies:
        copy.wait_recv()
    expand = weights.at[:, pl.ds(0, hidden_units)]
    shrink = weights.at[:, pl.ds(hidden_units, hidden_units)]

    def expand_rows(start, count):
        rows = low_two[start : start + count, :]
        for first in range(0, hidden_units, chunk):
            pre = dot(rows, expand[:, first : first + chunk])
            cdf = 0.5 + 0.5 * lax.erf(pre * 0.7071067811865476)
            act[start : start + count, first : first + chunk] = bf16(pre * cdf)
            slope[start : start + count, first : first + chunk] = bf16(
                cdf + pre * jnp.exp(-0.5 * pre * pre) * 0.3989422804014327
            )

    expand_rows(0, size)
    hidden_copy.wait_recv()
    y_copies = []
    for start in (0, half):
        expand_rows(size + start, half)
        y_send[start : start + half, :] = bf16(
            dot(act[size + start : size + start + half, :], shrink[...], NT)
        )
        y_copies.append(to_mate(y_send.at[pl.ds(start, half)], y_recv.at[pl.ds(start, half)]))
    y_own[...] = dot(act[:size, :], shrink[...], NT)
    for copy in y_copies:
        copy.wait_recv()
    output, normed, inverse = layer_norm(
        hidden_two[...] + y_own[...] + f32(y_recv[...]), gain_ref[2:3, :], bias_ref[2:3, :]
    )
    out_ref[...] = bf16(output)
    loads[n + 1].wait()
    third, gain_three, bias_three = norm_back(f32(cot[...]), normed, inverse, gain_ref[2:3, :])
    low_three[:size, :] = bf16(third)
    grad_copy = to_mate(low_three.at[own], low_three.at[other])

    def back_rows(start, count):
        rows = low_three[start : start + count, :]
        for first in range(0, hidden_units, chunk):
            grad = dot(rows, shrink[:, first : first + chunk])
            spot = (slice(start, start + count), slice(first, first + chunk))
            slope[spot] = bf16(grad * f32(slope[spot]))

    back_rows(0, size)
    grad_copy.wait_recv()
    d_copies = []
    for start in (0, half):
        back_rows(size + start, half)
        d_send[start : start + half, :] = bf16(
            dot(slope[size + start : size + start + half, :], expand[...], NT)
        )
        d_copies.append(to_mate(d_send.at[pl.ds(start, half)], d_recv.at[pl.ds(start, half)]))
    y_own[...] = third + dot(slope[:size, :], expand[...], NT)
    for copy in d_copies:
        copy.wait_recv()
    second, gain_two, bias_two = norm_back(
        y_own[...] + f32(d_recv[...]), normed_two[...], inverse_two, gain_ref[1:2, :]
    )
    second_ref[...] = second
    low = bf16(second)
    sent = tokens_to_heads(
        n, lambda group: dot(low, wo[group]), blocks, dmix_ref, send_out, recv_out, own_sem
    )
    norm_grad_ref[...] = jnp.concatenate(
        [gain_two, gain_three, bias_two, bias_three, jnp.zeros((4, norm_grad_ref.shape[1]))], axis=0
    )
    for first in range(0, low_two.shape[1], 256):
        rows = slice(first, first + 256)
        shrink_grad_ref[rows, :] = bf16(dot(low_three[:, rows], act[...], TN))
        expand_grad_ref[rows, :] = bf16(dot(low_two[:, rows], slope[...], TN))
    for group in range(n):
        wo_grad_ref[:, group * width : (group + 1) * width] = bf16(dot(low, slots[group], TN))
    for copy in sent:
        copy.wait()
    for copy in pair + home_copies:
        copy.wait_send()


def feed(n, mixed, bundle, home, hidden_one, cotangent, gains, biases):
    total, width = mixed.shape
    side, model, units = home.shape[0], hidden_one.shape[1], home.shape[4] // 2
    size = total // n
    shape = jax.ShapeDtypeStruct
    dma = pltpu.SemaphoreType.DMA
    low, wide = jnp.bfloat16, jnp.float32
    return pl.pallas_call(
        partial(feed_kernel, n, side),
        out_shape=[
            shape((size, model), low),
            shape((size, model), wide),
            shape((total, width), low),
            shape((model, units), low),
            shape((model, units), low),
            shape((model, model), low),
            shape((8, model), wide),
        ],
        in_specs=[ANYWHERE] * 3 + [IN_VMEM, ANYWHERE] + [IN_VMEM] * 2,
        out_specs=[IN_VMEM] * 2 + [ANYWHERE] + [IN_VMEM] * 4,
        scratch_shapes=[
            pltpu.VMEM((n, model, width), low),
            pltpu.VMEM((model, 2 * units), low),
            pltpu.VMEM((n, size, width), low),
            pltpu.VMEM((size, model), wide),
            pltpu.VMEM((size, model), wide),
            pltpu.VMEM((2 * size, model), low),
            pltpu.VMEM((2 * size, model), low),
            pltpu.VMEM((2 * size, units), low),
            pltpu.VMEM((2 * size, units), low),
            pltpu.VMEM((size, model), wide),
            pltpu.VMEM((size, model), low),
            pltpu.VMEM((size, model), low),
            pltpu.VMEM((size, model), low),
            pltpu.VMEM((size, model), low),
            pltpu.VMEM((size, model), low),
            pltpu.VMEM((n, size, width), low),
            dma((2,)), dma((n,)), dma,
            dma((n - 1,)), dma((n - 1,)), dma((n - 1,)), dma((n - 1,)),
            dma((6,)), dma((6,)),
            dma((side * side,)), dma((side * side,)), dma((side * side,)),
        ],
        compiler_params=pltpu.CompilerParams(
            collective_id=2, has_side_effects=True, vmem_limit_bytes=VMEM_LIMIT
        ),
        cost_estimate=pl.CostEstimate(
            flops=80 * 10**9, bytes_accessed=8 * total * width, transcendentals=0
        ),
        name="feed",
    )(mixed, bundle, home, hidden_one, cotangent, gains, biases)


def cross_to_self_kernel(
    n, dq_ref, bundle_ref, second_ref, hidden_ref, normed_ref, inverse_ref, mixed_ref, gain_ref, norm_ref,
    first_ref, dmix_ref, weight_grad_ref, norm_grad_ref,
    wo, wq, slots, blocks, wo_sems, wq_sems, own_sem, send_in, recv_in, send_out, recv_out,
):
    p = Place(n, 1)
    me = p.z
    size, model = second_ref.shape
    width = dq_ref.shape[1]
    loads = [
        pltpu.make_async_copy(dq_ref.at[rows_at(me, size)], slots.at[me], own_sem),
        *load_groups(n, bundle_ref, 0, width, wq, wq_sems),
        *load_groups(n, bundle_ref, width, width, wo, wo_sems),
    ]
    for load in loads:
        load.start()
    greet(p.line())
    copies = heads_to_tokens(n, dq_ref, slots, send_in, recv_in)
    for load in loads:
        load.wait()
    upstream = merge_heads(
        n, slots, copies, lambda part, group: dot(part, wq[group], NT), second_ref[...]
    )
    first, gain_one, bias_one = norm_back(
        upstream, normed_ref[...], inverse_ref[:, 0:1], gain_ref[0:1, :]
    )
    first_ref[...] = first
    low = bf16(first)
    sent = tokens_to_heads(
        n, lambda group: dot(low, wo[group]), blocks, dmix_ref, send_out, recv_out, own_sem
    )
    hidden_low = bf16(hidden_ref[...])
    for group in range(n):
        cols = 2 * group * width
        weight_grad_ref[:, cols : cols + width] = bf16(dot(hidden_low, slots[group], TN))
        weight_grad_ref[:, cols + width : cols + 2 * width] = bf16(dot(low, mixed_ref[group], TN))
    rows = jnp.concatenate(
        [
            gain_one, norm_ref[0:2, :], bias_one, norm_ref[2:4, :],
            jnp.zeros((122, model), jnp.float32),
        ],
        axis=0,
    )
    norm_grad_ref[...] = bf16(rows.T)
    for copy in sent:
        copy.wait()


def cross_to_self(n, dq, bundle, second, hidden, normed, inverse, slots, gains, norm_rows):
    total, width = dq.shape
    size, model = second.shape
    shape = jax.ShapeDtypeStruct
    dma = pltpu.SemaphoreType.DMA
    return pl.pallas_call(
        partial(cross_to_self_kernel, n),
        out_shape=[
            shape((size, model), jnp.float32),
            shape((total, width), jnp.bfloat16),
            shape((model, 2 * model), jnp.bfloat16),
            shape((model, 128), jnp.bfloat16),
        ],
        in_specs=[ANYWHERE] * 2 + [IN_VMEM] * 7,
        out_specs=[IN_VMEM, ANYWHERE, IN_VMEM, IN_VMEM],
        scratch_shapes=[
            pltpu.VMEM((n, model, width), jnp.bfloat16),
            pltpu.VMEM((n, model, width), jnp.bfloat16),
            pltpu.VMEM((n, size, width), jnp.bfloat16),
            pltpu.VMEM((n, size, width), jnp.bfloat16),
            dma((n,)), dma((n,)), dma,
            dma((n - 1,)), dma((n - 1,)), dma((n - 1,)), dma((n - 1,)),
        ],
        compiler_params=pltpu.CompilerParams(
            collective_id=3, has_side_effects=True, vmem_limit_bytes=VMEM_LIMIT
        ),
        cost_estimate=pl.CostEstimate(
            flops=10**9, bytes_accessed=8 * total * width, transcendentals=0
        ),
        name="cross_to_self",
    )(dq, bundle, second, hidden, normed, inverse, slots, gains, norm_rows)


class Reduce:
    def __init__(self, place, sources, scratch):
        self.place, self.sources = place, sources
        (
            self.keep, self.first_a, self.first_b, self.second_a, self.second_b,
            self.local, self.send, self.recv,
        ) = scratch
        self.half = self.keep.shape[2] // 2
        self.copies = {"core": [], "first": [], "second": []}
        self.index = 0

    @staticmethod
    def scratch(side, rows, columns, sources):
        low, dma = jnp.bfloat16, pltpu.SemaphoreType.DMA
        block = pltpu.VMEM((side, side, rows, columns), low)
        first = pltpu.VMEM((side - 1, side, rows // 2, columns), low)
        second = pltpu.VMEM((side - 1, rows // 2, columns), low)
        count = sources + 4 * (side - 1)
        return [
            block, first, first, second, second, dma((2, sources)), dma((count,)), dma((count,)),
        ]

    def _push(self, stage, source, target, to):
        spot = self.index
        self.index += 1
        self.copies[stage].append(push(source, target, self.send.at[spot], self.recv.at[spot], to))

    def core_start(self):
        p, column = self.place, 0
        for source in self.sources:
            cols = pl.ds(column, source.shape[4])
            column += source.shape[4]
            self._push(
                "core", source.at[:, :, 1 - p.core], self.keep.at[:, :, :, cols], p.sibling()
            )

    def _load(self, stage, index):
        y, x = index // self.place.side, index % self.place.side
        column, loads = 0, []
        for spot, source in enumerate(self.sources):
            cols = pl.ds(column, source.shape[4])
            column += source.shape[4]
            loads.append(
                pltpu.make_async_copy(
                    source.at[y, x, self.place.core], stage.at[index % 2, :, cols],
                    self.local.at[index % 2, spot],
                )
            )
        return loads

    def core_finish(self, stage):
        side, keep, columns = self.place.side, self.keep, self.keep.shape[3]
        for load in self._load(stage, 0):
            load.start()
        for copy in self.copies["core"]:
            copy.wait_recv()
        for index in range(side * side):
            if index + 1 < side * side:
                for load in self._load(stage, index + 1):
                    load.start()
            for load in self._load(stage, index):
                load.wait()
            y, x = index // side, index % side
            keep[y, x] = bf16(f32(keep[y, x]) + f32(stage[index % 2, :, :columns]))

    def first_start(self):
        p, half = self.place, self.half
        top, bottom = pl.ds(0, half), pl.ds(half, half)
        for step in range(1, p.side):
            other, to = p.x_peer(step)
            self._push("first", self.keep.at[:, other, top], self.first_a.at[step - 1], to)
            other, to = p.y_peer(step)
            self._push("first", self.keep.at[other, :, bottom], self.first_b.at[step - 1], to)

    def first_finish(self):
        p, half, keep = self.place, self.half, self.keep
        for copy in self.copies["first"]:
            copy.wait_recv()

        def add(index, carry):
            total = f32(keep[index, p.x, :half, :])
            for step in range(p.side - 1):
                total = total + f32(self.first_a[step, index])
            keep[index, p.x, :half, :] = bf16(total)
            total = f32(keep[p.y, index, half:, :])
            for step in range(p.side - 1):
                total = total + f32(self.first_b[step, index])
            keep[p.y, index, half:, :] = bf16(total)
            return carry

        lax.fori_loop(0, p.side, add, 0)

    def second_start(self):
        p, half = self.place, self.half
        top, bottom = pl.ds(0, half), pl.ds(half, half)
        for step in range(1, p.side):
            other, to = p.y_peer(step)
            self._push("second", self.keep.at[other, p.x, top], self.second_a.at[step - 1], to)
            other, to = p.x_peer(step)
            self._push("second", self.keep.at[p.y, other, bottom], self.second_b.at[step - 1], to)

    def second_wait(self):
        for copy in self.copies["second"]:
            copy.wait_recv()

    def total(self, cols):
        p, half = self.place, self.half
        top, bottom = f32(self.keep[p.y, p.x, :half, cols]), f32(self.keep[p.y, p.x, half:, cols])
        for step in range(p.side - 1):
            top = top + f32(self.second_a[step, :, cols])
            bottom = bottom + f32(self.second_b[step, :, cols])
        return jnp.concatenate([top, bottom], axis=0)

    def finish(self):
        for stage in self.copies.values():
            for copy in stage:
                copy.wait_send()


class Fold:
    def __init__(self, place, make, out, scratch):
        self.n, self.me, self.make, self.out = place.n, place.z, make, out
        self.parts, self.held, self.down_send, self.down_recv, self.back_send, self.back_recv, self.own = scratch
        self.chunks = self.held.shape[1]
        self.ring = self.parts.shape[1]
        self.ticks = self.chunks + 2 * (self.n - 1) - 1

    @staticmethod
    def scratch(chunks, rows, columns, ring=6):
        low, dma = jnp.bfloat16, pltpu.SemaphoreType.DMA((2, chunks))
        return [
            pltpu.VMEM((2, ring, rows, columns), low), pltpu.VMEM((2, chunks, rows, columns), low),
            dma, dma, dma, dma, dma,
        ]

    def _flows(self):
        n, me = self.n, self.me
        return (
            (0, me, lax.rem(me + 1, n), lax.rem(me + n - 1, n)),
            (1, n - 1 - me, lax.rem(me + n - 1, n), lax.rem(me + 1, n)),
        )

    def _down(self, flow, chunk, to, first):
        source = self.parts.at[flow, lax.rem(chunk, self.ring)] if first else self.held.at[flow, chunk]
        return pltpu.make_async_remote_copy(
            source, self.held.at[flow, chunk],
            self.down_send.at[flow, chunk], self.down_recv.at[flow, chunk],
            device_id={"mp": to}, device_id_type=MESH,
        )

    def _back(self, flow, chunk, to, first):
        source = (self.held if first else self.out).at[flow, chunk]
        return pltpu.make_async_remote_copy(
            source, self.out.at[flow, chunk],
            self.back_send.at[flow, chunk], self.back_recv.at[flow, chunk],
            device_id={"mp": to}, device_id_type=MESH,
        )

    def _keep(self, flow, chunk):
        return pltpu.make_async_copy(
            self.held.at[flow, chunk], self.out.at[flow, chunk], self.own.at[flow, chunk]
        )

    def tick(self, tick):
        last = self.n - 1
        for flow, spot, ahead, behind in self._flows():
            if tick < self.chunks:
                if tick >= self.ring:

                    @pl.when(spot == 0)
                    def _():
                        self._down(flow, tick - self.ring, ahead, True).wait_send()

                self.parts[flow, tick % self.ring] = bf16(self.make(flow, tick))

                @pl.when(spot == 0)
                def _():
                    self._down(flow, tick, ahead, True).start()

            chunk = tick - spot

            @pl.when((spot > 0) & (chunk >= 0) & (chunk < self.chunks))
            def _():
                self._down(flow, chunk, ahead, False).wait_recv()
                self.held[flow, chunk] = bf16(
                    f32(self.held[flow, chunk]) + f32(self.parts[flow, lax.rem(chunk, self.ring)])
                )

                @pl.when(spot < last)
                def _():
                    self._down(flow, chunk, ahead, False).start()

                @pl.when(spot == last)
                def _():
                    self._back(flow, chunk, behind, True).start()
                    self._keep(flow, chunk).start()

            given = tick - 2 * last + spot

            @pl.when((spot > 0) & (spot < last) & (given >= 0) & (given < self.chunks))
            def _():
                self._back(flow, given, behind, False).wait_recv()
                self._back(flow, given, behind, False).start()

    def finish(self):
        last = self.n - 1
        for flow, spot, ahead, behind in self._flows():

            @pl.when(spot == 0)
            def _():
                def wait(chunk, carry):
                    self._back(flow, chunk, behind, False).wait_recv()
                    return carry

                lax.fori_loop(0, self.chunks, wait, 0)

                def sent(chunk, carry):
                    self._down(flow, chunk, ahead, True).wait_send()
                    return carry

                lax.fori_loop(max(self.chunks - self.ring, 0), self.chunks, sent, 0)

            @pl.when((spot > 0) & (spot < last))
            def _():
                def sent(chunk, carry):
                    self._down(flow, chunk, ahead, False).wait_send()
                    self._back(flow, chunk, behind, False).wait_send()
                    return carry

                lax.fori_loop(0, self.chunks, sent, 0)

            @pl.when(spot == last)
            def _():
                def sent(chunk, carry):
                    self._back(flow, chunk, behind, True).wait_send()
                    self._keep(flow, chunk).wait()
                    return carry

                lax.fori_loop(0, self.chunks, sent, 0)


class Everyone:
    def __init__(self, n_dp, n_mp, mine, slots, send_sems, recv_sems):
        self.n, self.n_mp = n_dp * n_mp, n_mp
        self.me = lax.axis_index("dp") * n_mp + lax.axis_index("mp")
        self.mine, self.slots, self.send, self.recv = mine, slots, send_sems, recv_sems

    def _to(self, distance):
        to = lax.rem(self.me + distance, self.n)
        return {"dp": to // self.n_mp, "mp": lax.rem(to, self.n_mp)}

    def _copy(self, distance):
        return pltpu.make_async_remote_copy(
            self.mine, self.slots.at[self.me], self.send.at[distance - 1], self.recv.at[distance - 1],
            device_id=self._to(distance), device_id_type=MESH,
        )

    def greet(self):
        barrier = pltpu.get_barrier_semaphore()

        def signal(distance, carry):
            pl.semaphore_signal(barrier, inc=1, device_id=self._to(distance), device_id_type=MESH)
            return carry

        lax.fori_loop(1, self.n, signal, 0)
        pl.semaphore_wait(barrier, self.n - 1)

    def total(self):
        def start(distance, carry):
            self._copy(distance).start()
            return carry

        def wait(distance, carry):
            self._copy(distance).wait()
            return carry

        self.slots[self.me] = self.mine[...]
        lax.fori_loop(1, self.n, start, 0)
        lax.fori_loop(1, self.n, wait, 0)
        return jnp.sum(self.slots[...], axis=0)


def moments(upstream, first_moment, second_moment, master, decay):
    first_new = first_decay * first_moment + (1.0 - first_decay) * upstream
    second_new = second_decay * second_moment + (1.0 - second_decay) * upstream * upstream
    direction = (
        first_new
        / (1.0 - first_decay**STEP)
        / (jnp.sqrt(second_new / (1.0 - second_decay**STEP)) + epsilon)
        + decay * master
    )
    return (first_new, second_new, direction)


def tensors(inner, outer, expand, shrink, norms):
    found = [inner.at[a, c] for a in range(2) for c in range(3)]
    found += [outer.at[0], outer.at[1], expand, shrink]
    found += [norms.at[pl.ds(row, 1)] for row in range(6)]
    return list(zip(found, [weight_decay] * 10 + [0.0] * 6))


def square_row(squares, share):
    lane = lax.broadcasted_iota(jnp.int32, (1, 128), 1)
    row = jnp.zeros((1, 128), jnp.float32)
    for index, values in enumerate(squares):
        total = jnp.sum(jnp.sum(values, axis=0, keepdims=True), axis=1, keepdims=True)
        row = jnp.where(lane == index, total * share if index >= 10 else total, row)
    return row


def update_kernel(*refs):
    (
        sums_ref, grads, weights, firsts, seconds, table_ref,
        new_weights, new_firsts, new_seconds,
    ) = refs[0], refs[1:6], refs[6:11], refs[11:16], refs[16:21], refs[21], refs[22:27], refs[27:32], refs[32:37]
    lane = lax.broadcasted_iota(jnp.int32, (1, 128), 1)
    counts = jnp.where(lane < 8, float(D * D), jnp.where(lane < 10, float(D * FF), float(D)))
    weight_norm = jnp.sqrt(sums_ref[0:1, :] / counts)
    update_norm = jnp.sqrt(sums_ref[1:2, :] / counts)
    trust = weight_norm / (update_norm + epsilon)
    table_ref[...] = jnp.concatenate([weight_norm, update_norm, trust], axis=0)[:, :16]
    groups = [tensors(*group) for group in (grads, weights, firsts, seconds, new_weights, new_firsts, new_seconds)]
    for index, parts in enumerate(zip(*groups)):
        grad, weight, first, second, new_weight, new_first, new_second = [part[0] for part in parts]
        ratio = jnp.sum(jnp.where(lane == index, trust, 0.0), axis=1, keepdims=True)
        master = weight[...]
        first_new, second_new, direction = moments(
            grad[...], first[...], second[...], master, parts[0][1]
        )
        new_first[...] = first_new
        new_second[...] = second_new
        new_weight[...] = master - learn_rate * ratio * direction


def update(sums, grads, weights, firsts, seconds):
    shape = lambda values: jax.ShapeDtypeStruct(values.shape, jnp.float32)
    results = [shape(values) for values in weights]
    return pl.pallas_call(
        update_kernel,
        out_shape=[jax.ShapeDtypeStruct((3, 16), jnp.float32)] + results * 3,
        compiler_params=pltpu.CompilerParams(vmem_limit_bytes=VMEM_LIMIT),
        name="update",
    )(sums, *grads, *weights, *firsts, *seconds)


def finish_kernel(
    n, side, units, width, dq_ref, dk_ref, dv_ref, near_ref, x_ref, first_ref,
    cross_dk_ref, cross_dv_ref, source_ref,
    shrink_ref, expand_ref, cross_wo_ref, weight_ref, norm_ref, source_grad_ref, *refs,
):
    states, refs = refs[:15], refs[15:]
    out_ref, sums_ref, grads, refs = refs[0], refs[1], refs[2:7], refs[7:]
    masters, refs = refs[:15], refs[15:]
    (
        master_sems, inner, stage, far_send, far_recv, group_send, group_recv,
        far_send_sem, far_recv_sem, group_send_sems, group_recv_sems,
        mine, slots, everyone_send, everyone_recv, *scratch,
    ) = refs
    n_dp = 2 * side * side
    p = Place(n, side)
    everyone = Everyone(n_dp, n, mine, slots, everyone_send, everyone_recv)
    master_loads = [
        pltpu.make_async_copy(source, target, master_sems.at[index])
        for index, (source, target) in enumerate(zip(states, masters))
    ]
    me = p.z
    own_heads = (dq_ref, dk_ref, dv_ref)
    size, model = first_ref.shape
    rows = inner.shape[3]
    chunk_rows = out_ref.shape[2]
    source_chunks = cross_dk_ref.shape[0] // (2 * chunk_rows)

    def make(flow, chunk):
        if chunk < source_chunks:
            spot = pl.ds((flow * source_chunks + chunk) * chunk_rows, chunk_rows)
            return dot(cross_dk_ref[spot, :], source_ref[:, :width], NT) + dot(
                cross_dv_ref[spot, :], source_ref[:, width:], NT
            )
        tokens = x_ref.shape[0]
        start = flow * (tokens // 2) + (chunk - source_chunks) * chunk_rows
        spot = pl.ds(start, chunk_rows)
        total = jnp.zeros((chunk_rows, model), jnp.float32)
        for index, own in enumerate(own_heads):
            total = total + dot(own[spot, :], near_ref[:, index * width : (index + 1) * width], NT)
        here = first_ref[start % size : start % size + chunk_rows, :]
        return total + jnp.where(me == start // size, here, 0.0)

    fold = Fold(p, make, out_ref, scratch[:7])
    feed_sum = Reduce(p, [shrink_ref, expand_ref], scratch[7:15])
    group_sum = Reduce(p, [cross_wo_ref, weight_ref, norm_ref, source_grad_ref], scratch[15:23])
    inner_sum = Reduce(p, [inner], scratch[23:31])

    everyone.greet()
    feed_sum.core_start()
    group_sum.core_start()

    ticks = iter(range(fold.ticks))

    def advance(count):
        for _ in range(count):
            fold.tick(next(ticks))

    advance(2)
    for load in master_loads:
        load.start()

    per = 256
    for start in range(0, model, per):
        turned = x_ref[:, start : start + per]
        for index, own in enumerate(own_heads):
            block = bf16(dot(turned, own[...], TN))
            for row in range(0, per, rows):
                flat = (start + row) // rows
                y, x, core = flat // (2 * side), flat // 2 % side, flat % 2
                inner[y, x, core, :, index * width : (index + 1) * width] = block[row : row + rows]
    inner_sum.core_start()
    for load in master_loads:
        load.wait()
    weights, firsts, seconds = (tensors(*masters[index : index + 5]) for index in (0, 5, 10))
    share = 1.0 / n
    mine[...] = jnp.zeros(mine.shape, jnp.float32)
    mine[0:1, :] = square_row([ref[...] * ref[...] for ref, _ in weights], share)
    feed_sum.core_finish(stage)
    feed_sum.first_start()
    advance(1)
    inner_sum.core_finish(stage)
    group_sum.core_finish(stage)
    group_sum.first_start()
    inner_sum.first_start()
    advance(2)
    feed_sum.first_finish()
    feed_sum.second_start()
    advance(2)
    feed_sum.second_wait()
    far = {"mp": lax.rem(me + n // 2, n)}
    far_send[:, :units] = bf16(feed_sum.total(slice(units, 2 * units)))
    far_send[:, units:] = bf16(feed_sum.total(slice(3 * units, 4 * units)))
    far_copy = push(far_send, far_recv, far_send_sem, far_recv_sem, far)
    group_sum.first_finish()
    inner_sum.first_finish()
    group_sum.second_start()
    inner_sum.second_start()
    advance(2)
    group_sum.second_wait()
    whole = n * width
    for group in range(n):
        group_send[group, :, :width] = bf16(
            group_sum.total(slice(group * width, (group + 1) * width))
        )
        start = whole + 2 * group * width
        group_send[group, :, width : 3 * width] = bf16(
            group_sum.total(slice(start, start + 2 * width))
        )
        group_send[group, :, 3 * width :] = bf16(
            group_sum.total(slice(3 * whole, 3 * whole + norm_ref.shape[4]))
        )
    group_copies = []
    for distance in range(1, n):
        to = lax.rem(me + distance, n)
        group_copies.append(
            push(
                group_send.at[to], group_recv.at[distance - 1],
                group_send_sems.at[distance - 1], group_recv_sems.at[distance - 1], {"mp": to},
            )
        )
    grad_inner, grad_outer, grad_expand, grad_shrink, grad_norms = grads
    advance(1)
    inner_sum.second_wait()
    for index in range(3):
        grad_inner[0, index] = inner_sum.total(slice(index * width, (index + 1) * width))
    start = 3 * whole + norm_ref.shape[4]
    for index in range(2):
        grad_inner[1, index + 1] = group_sum.total(
            slice(start + index * width, start + (index + 1) * width)
        )
    advance(2)
    far_copy.wait_recv()
    grad_shrink[...] = (feed_sum.total(slice(0, units)) + f32(far_recv[:, :units])).T
    grad_expand[...] = feed_sum.total(slice(2 * units, 3 * units)) + f32(far_recv[:, units:])

    def direction_square(index):
        (grad, decay), first, second, weight = [group[index] for group in (found, firsts, seconds, weights)]
        step = moments(grad[...], first[0][...], second[0][...], weight[0][...], decay)[2]
        return step * step

    found = tensors(*grads)
    early = {index: direction_square(index) for index in (0, 1, 2, 4, 5, 8, 9)}
    advance(1)
    for distance in range(1, n):
        group_copies[distance - 1].wait_recv()
    received = lambda cols: sum(
        [f32(group_recv[distance - 1, :, cols]) for distance in range(1, n)], f32(group_send[me, :, cols])
    )
    grad_outer[1] = received(slice(0, width)).T
    grad_inner[1, 0] = received(slice(width, 2 * width))
    grad_outer[0] = received(slice(2 * width, 3 * width)).T
    grad_norms[...] = received(slice(3 * width, 3 * width + norm_ref.shape[4])).T[:6, :]
    advance(1)
    mine[1:2, :] = square_row(
        [early[index] if index in early else direction_square(index) for index in range(16)], share
    )
    sums_ref[...] = everyone.total()
    for tick in ticks:
        fold.tick(tick)
    fold.finish()
    for copy in (far_copy, *group_copies):
        copy.wait_send()
    for batch in (feed_sum, group_sum, inner_sum):
        batch.finish()


def finish(
    n_dp, n_mp, own_heads, near, tokens, first, source_heads, source_weights,
    shrink, expand, cross_wo, weights, norms, source_grad, states,
):
    side = round((n_dp // 2) ** 0.5)
    total, width = own_heads[0].shape
    size, model = first.shape
    units = expand.shape[1] // 2
    rows = model // n_dp
    low, wide = jnp.bfloat16, jnp.float32
    shape = jax.ShapeDtypeStruct
    dma = pltpu.SemaphoreType.DMA
    by_place = lambda values: values.reshape(side, side, 2, rows, values.shape[1])
    early = [by_place(values) for values in (shrink, expand, cross_wo, weights, norms, source_grad)]
    columns = [sum(values.shape[4] for values in group) for group in (early[:2], early[2:])]
    bundle = 3 * width + norms.shape[1]
    devices = n_dp * n_mp
    chunk_rows = min(128, size // 2)
    chunks = (total + source_heads[0].shape[0]) // (2 * chunk_rows)
    both, sums, *grads = pl.pallas_call(
        partial(finish_kernel, n_mp, side, units, width),
        out_shape=[shape((2, chunks, chunk_rows, model), low), shape((8, 128), wide)]
        + [shape(values.shape, wide) for values in states[:5]],
        in_specs=[IN_VMEM] * 9 + [ANYWHERE] * (6 + len(states)),
        out_specs=[ANYWHERE] + [IN_VMEM] * 6,
        scratch_shapes=[
            *[pltpu.VMEM(values.shape, wide) for values in states],
            dma((len(states),)),
            pltpu.VMEM((side, side, 2, rows, 3 * width), low),
            pltpu.VMEM((2, rows, max(columns)), low),
            pltpu.VMEM((rows, 2 * units), low),
            pltpu.VMEM((rows, 2 * units), low),
            pltpu.VMEM((n_mp, rows, bundle), low),
            pltpu.VMEM((n_mp - 1, rows, bundle), low),
            dma, dma, dma((n_mp - 1,)), dma((n_mp - 1,)),
            pltpu.VMEM((8, 128), wide),
            pltpu.VMEM((devices, 8, 128), wide),
            dma((devices - 1,)), dma((devices - 1,)),
            *Fold.scratch(chunks, chunk_rows, model),
            *Reduce.scratch(side, rows, columns[0], 2),
            *Reduce.scratch(side, rows, columns[1], 4),
            *Reduce.scratch(side, rows, 3 * width, 1),
        ],
        compiler_params=pltpu.CompilerParams(
            collective_id=5, has_side_effects=True, vmem_limit_bytes=VMEM_LIMIT
        ),
        cost_estimate=pl.CostEstimate(flops=10**9, bytes_accessed=1 << 20, transcendentals=0),
        name="finish",
    )(*own_heads, near, tokens, first, *source_heads, source_weights, *early, *states)
    split = source_heads[0].shape[0] // (2 * chunk_rows)
    return both[:, :split], both[:, split:], sums, grads


def on_device(
    inputs,
    encoder,
    prefix,
    cotangent,
    inner_weights,
    inner_first,
    inner_second,
    outer_weights,
    outer_first,
    outer_second,
    expand_weights,
    expand_first,
    expand_second,
    shrink_weights,
    shrink_first,
    shrink_second,
    norm_params,
    norm_first,
    norm_second,
):
    n_dp, n_mp = lax.axis_size("dp"), lax.axis_size("mp")
    seq_count, seq_len, model = inputs.shape
    tokens = inputs.reshape(seq_len, model)
    states = encoder.reshape(-1, model)
    rows, width = inner_weights.shape[2:]
    units = expand_weights.shape[1]

    norm_t = jnp.pad(bf16(norm_params).reshape(6, rows).T, ((0, 0), (0, 122)))
    near, bundle, feed_block = front(
        n_dp, n_mp, inner_weights, bf16(jnp.swapaxes(outer_weights, 1, 2)), norm_t,
        expand_weights, bf16(shrink_weights.T),
    )
    last = n_mp * 3 * width
    source_weights = bundle[:, last : last + 2 * width]
    norm_all = f32(bundle[:, last + 2 * width :].T)
    gains, biases = norm_all[0:3], norm_all[3:6]

    self_proj = bf16(dot(tokens, near))
    split = lambda values, count: [
        values[:, index * width : (index + 1) * width] for index in range(count)
    ]
    self_q, self_k, self_v = split(self_proj, 3)
    self_mixed, self_sums = attend_forward(self_q, self_k, self_v, prefix, True)
    hidden_one, normed_one, inverse_one, self_slots, cross_query, home = self_to_cross(
        n_dp, n_mp, self_mixed, bundle, tokens, feed_block, gains, biases
    )
    cross_k, cross_v = split(bf16(dot(states, source_weights)), 2)
    cross_mixed, cross_sums = attend_forward(cross_query, cross_k, cross_v, prefix, False)
    out_rows, grad_second, cross_dmix, shrink_grad, expand_grad, cross_wo_grad, norm_rows = feed(
        n_mp, cross_mixed, bundle, home, hidden_one, cotangent.reshape(seq_len, model), gains, biases,
    )
    cross_dq, cross_dk, cross_dv, layer_low, source_grad = attend_backward(
        cross_query, cross_k, cross_v, cross_dmix, cross_mixed, cross_sums, prefix, False,
        n_mp, (out_rows,), (states,),
    )
    grad_first, self_dmix, weight_grad, norm_grad = cross_to_self(
        n_mp, cross_dq, bundle, grad_second, hidden_one, normed_one, inverse_one,
        self_slots, gains, norm_rows,
    )
    self_grads = attend_backward(
        self_q, self_k, self_v, self_dmix, self_mixed, self_sums, prefix, True
    )
    flat = lambda values: values.reshape(6, rows)
    weights = [inner_weights, outer_weights, expand_weights, shrink_weights, flat(norm_params)]
    firsts = [inner_first, outer_first, expand_first, shrink_first, flat(norm_first)]
    seconds = [inner_second, outer_second, expand_second, shrink_second, flat(norm_second)]
    encoder_low, input_low, sums, grads = finish(
        n_dp, n_mp, self_grads, near, tokens, grad_first, (cross_dk, cross_dv), source_weights,
        shrink_grad, expand_grad, cross_wo_grad, weight_grad, norm_grad, source_grad,
        weights + firsts + seconds,
    )
    table, *results = update(sums, grads, weights, firsts, seconds)
    for index in (4, 9, 14):
        results[index] = results[index].reshape(2, 3, rows)
    return (
        f32(layer_low).reshape(seq_count, seq_len, model),
        f32(input_low).reshape(seq_count, seq_len, model),
        f32(encoder_low).reshape(seq_count, -1, model),
        *results,
        table,
    )


def solution(mesh):
    placed = (
        P("dp", None, None),
        P("dp", None, None),
        P("dp"),
        P("dp", None, None),
        P(None, None, "dp", "mp"),
        P(None, None, "dp", "mp"),
        P(None, None, "dp", "mp"),
        P(None, "mp", "dp"),
        P(None, "mp", "dp"),
        P(None, "mp", "dp"),
        P("dp", "mp"),
        P("dp", "mp"),
        P("dp", "mp"),
        P("mp", "dp"),
        P("mp", "dp"),
        P("mp", "dp"),
        P(None, None, "dp"),
        P(None, None, "dp"),
        P(None, None, "dp"),
    )
    return jax.shard_map(
        on_device,
        mesh=mesh,
        in_specs=placed,
        out_specs=(
            P("dp", None, None),
            P("dp", None, None),
            P("dp", None, None),
            P(None, None, "dp", "mp"),
            P(None, "mp", "dp"),
            P("dp", "mp"),
            P("mp", "dp"),
            P(None, None, "dp"),
            P(None, None, "dp", "mp"),
            P(None, "mp", "dp"),
            P("dp", "mp"),
            P("mp", "dp"),
            P(None, None, "dp"),
            P(None, None, "dp", "mp"),
            P(None, "mp", "dp"),
            P("dp", "mp"),
            P("mp", "dp"),
            P(None, None, "dp"),
            P(),
        ),
        check_vma=False,
    )
```

```python
from functools import partial

import jax
import jax.numpy as jnp
from jax import lax
from jax.experimental import pallas as pl
from jax.experimental.pallas import tpu as pltpu
from jax.sharding import PartitionSpec as P

D = 1024
HEAD = 64
FF = 4096
STEP = 5

first_decay = 0.5
second_decay = 0.6
learn_rate = 0.5
weight_decay = 0.01
epsilon = 1e-06
norm_eps = 1e-05
mask_fill = -1000000000.0

MESH = pl.DeviceIdType.MESH
ANYWHERE = pl.BlockSpec(memory_space=pl.ANY)
IN_VMEM = pl.BlockSpec(memory_space=pltpu.VMEM)
NN = (((1,), (0,)), ((), ()))
NT = (((1,), (1,)), ((), ()))
TN = (((0,), (0,)), ((), ()))
VMEM_LIMIT = 52 << 20


def dot(left, right, dims=NN):
    return lax.dot_general(left, right, dims, preferred_element_type=jnp.float32)


def bf16(values):
    return values.astype(jnp.bfloat16)


def f32(values):
    return values.astype(jnp.float32)


def layer_norm(values, gain_row, bias_row):
    center = values - jnp.mean(values, axis=-1, keepdims=True)
    spread = jnp.mean(center * center, axis=-1, keepdims=True)
    inverse = lax.rsqrt(spread + norm_eps)
    normed = center * inverse
    return (normed * gain_row + bias_row, normed, inverse)


def norm_back(upstream, normed, inverse, gain_row):
    scaled = upstream * gain_row
    inner = (
        scaled
        - jnp.mean(scaled, axis=-1, keepdims=True)
        - normed * jnp.mean(scaled * normed, axis=-1, keepdims=True)
    )
    return (
        inner * inverse,
        jnp.sum(upstream * normed, axis=0, keepdims=True),
        jnp.sum(upstream, axis=0, keepdims=True),
    )


class Place:
    def __init__(self, n_mp, side):
        self.n, self.side = n_mp, side
        self.z = lax.axis_index("mp")
        dp = lax.axis_index("dp")
        self.core = lax.rem(dp, 2)
        self.x = lax.rem(dp // 2, side)
        self.y = dp // (2 * side)

    def at(self, y, x, core):
        return {"dp": (y * self.side + x) * 2 + core}

    def x_peer(self, distance):
        other = lax.rem(self.x + distance, self.side)
        return other, self.at(self.y, other, self.core)

    def y_peer(self, distance):
        other = lax.rem(self.y + distance, self.side)
        return other, self.at(other, self.x, self.core)

    def sibling(self):
        return self.at(self.y, self.x, 1 - self.core)

    def line(self):
        return [{"mp": lax.rem(self.z + distance, self.n)} for distance in range(1, self.n)]

    def plane(self):
        steps = range(1, self.side)
        return (
            [self.x_peer(step)[1] for step in steps]
            + [self.y_peer(step)[1] for step in steps]
            + [self.sibling()]
        )


def greet(others):
    barrier = pltpu.get_barrier_semaphore()
    for other in others:
        pl.semaphore_signal(barrier, inc=1, device_id=other, device_id_type=MESH)
    pl.semaphore_wait(barrier, len(others))


def push(source, target, send_sem, recv_sem, to):
    copy = pltpu.make_async_remote_copy(
        source, target, send_sem, recv_sem, device_id=to, device_id_type=MESH
    )
    copy.start()
    return copy


def rows_at(index, size):
    return pl.ds(pl.multiple_of(index * size, size), size)


def heads_to_tokens(n, source, slots, send_sems, recv_sems):
    me = lax.axis_index("mp")
    size = source.shape[0] // n
    copies = []
    for distance in range(1, n):
        to = lax.rem(me + distance, n)
        copies.append(
            push(
                source.at[rows_at(to, size)], slots.at[me],
                send_sems.at[distance - 1], recv_sems.at[distance - 1], {"mp": to},
            )
        )
    return copies


def tokens_to_heads(n, make, blocks, target, send_sems, recv_sems, local_sem):
    me = lax.axis_index("mp")
    size = blocks.shape[1]
    copies = []
    for distance in (*range(1, n), 0):
        to = lax.rem(me + distance, n)
        blocks[to] = bf16(make(to))
        place = target.at[rows_at(me, size)]
        if distance:
            copies.append(
                push(
                    blocks.at[to], place,
                    send_sems.at[distance - 1], recv_sems.at[distance - 1], {"mp": to},
                )
            )
        else:
            copy = pltpu.make_async_copy(blocks.at[to], place, local_sem)
            copy.start()
            copies.append(copy)
    return copies


def merge_heads(n, slots, copies, part_of, start):
    me = lax.axis_index("mp")
    total = start + part_of(slots[me], me)
    for distance in range(1, n):
        origin = lax.rem(me + n - distance, n)
        copies[distance - 1].wait_recv()
        total = total + part_of(slots[origin], origin)
    for copy in copies:
        copy.wait_send()
    return total


def load_groups(n, bundle, stride, first, width, target, sems):
    return [
        pltpu.make_async_copy(
            bundle.at[:, pl.ds(group * stride + first, width)], target.at[group], sems.at[group]
        )
        for group in range(n)
    ]


class Give:
    def __init__(self, place, out, sems):
        self.place, self.n, self.me, self.out = place, place.n, place.z, out
        self.sems = {"right": sems[0:2], "left": sems[2:4]}

    @staticmethod
    def sems(n):
        return [pltpu.SemaphoreType.DMA((max(n - 1, 1),))] * 4

    def _copy(self, way, step):
        ahead = 1 if way == "right" else -1
        chunk = lax.rem(self.me - ahead * step + self.n, self.n)
        return pltpu.make_async_remote_copy(
            self.out.at[chunk], self.out.at[chunk],
            self.sems[way][0].at[step], self.sems[way][1].at[step],
            device_id={"mp": lax.rem(self.me + ahead + self.n, self.n)}, device_id_type=MESH,
        )

    def _spots(self):
        return (("right", self.me), ("left", self.n - 1 - self.me))

    def step(self, step):
        for way, spot in self._spots():

            @pl.when((spot >= step) & (spot < self.n - 1))
            def _():
                if step > 0:
                    self._copy(way, step - 1).wait_recv()
                self._copy(way, step).start()

    def finish(self):
        for way, spot in self._spots():

            @pl.when(spot == self.n - 1)
            def _():
                for step in range(self.n - 1):
                    self._copy(way, step).wait_recv()

            for step in range(self.n - 1):

                @pl.when((spot >= step) & (spot < self.n - 1))
                def _():
                    self._copy(way, step).wait_send()


class Spread:
    def __init__(self, place, home, send_sems, recv_sems):
        self.place, self.home, self.send, self.recv = place, home, send_sems, recv_sems
        self.half = home.shape[3] // 2
        self.copies = {"first": [], "second": [], "core": []}
        self.index = 0

    def _push(self, stage, block, to):
        spot = self.index
        self.index += 1
        self.copies[stage].append(push(block, block, self.send.at[spot], self.recv.at[spot], to))

    def first(self):
        p, half = self.place, self.half
        for step in range(1, p.side):
            own = self.home.at[p.y, p.x, p.core]
            self._push("first", own.at[pl.ds(0, half)], p.x_peer(step)[1])
            self._push("first", own.at[pl.ds(half, half)], p.y_peer(step)[1])

    def second(self):
        p, half = self.place, self.half
        for copy in self.copies["first"]:
            copy.wait_recv()
        for step in range(1, p.side):
            self._push(
                "second", self.home.at[p.y, :, p.core, pl.ds(0, half)], p.y_peer(step)[1]
            )
            self._push(
                "second", self.home.at[:, p.x, p.core, pl.ds(half, half)], p.x_peer(step)[1]
            )

    def core(self):
        for copy in self.copies["second"]:
            copy.wait_recv()
        self._push("core", self.home.at[:, :, self.place.core], self.place.sibling())

    def finish(self):
        for copy in self.copies["core"] or self.copies["second"] or self.copies["first"]:
            copy.wait_recv()
        for stage in self.copies.values():
            for copy in stage:
                copy.wait_send()

    @staticmethod
    def sems(side):
        return pltpu.SemaphoreType.DMA((4 * (side - 1) + 1,))


class Reduce:
    def __init__(self, place, sources, scratch):
        self.place, self.sources = place, sources
        self.keep, self.first_a, self.first_b, *rest = scratch
        *rest, self.local, self.send, self.recv = rest
        if rest:
            self.second_a, self.second_b = rest
        self.half = self.keep.shape[2] // 2
        self.copies = {"core": [], "first": [], "second": []}
        self.index = 0

    @staticmethod
    def scratch(side, rows, columns, sources, second=True):
        low, dma = jnp.bfloat16, pltpu.SemaphoreType.DMA
        block = pltpu.VMEM((side, side, rows, columns), low)
        first = pltpu.VMEM((side - 1, side, rows // 2, columns), low)
        rest = pltpu.VMEM((side - 1, rows // 2, columns), low)
        count = sources + 4 * (side - 1)
        seconds = [rest, rest] if second else []
        return [
            block, first, first, *seconds, dma((2, sources)), dma((count,)), dma((count,)),
        ]

    def _push(self, stage, source, target, to, begin=True):
        copy = pltpu.make_async_remote_copy(
            source, target, self.send.at[self.index], self.recv.at[self.index],
            device_id=to, device_id_type=MESH,
        )
        self.index += 1
        self.copies[stage].append(copy)
        if begin:
            copy.start()

    def core_start(self, begin=True):
        p, column = self.place, 0
        self.index, self.copies["core"] = 0, []
        for source in self.sources:
            cols = pl.ds(column, source.shape[4])
            column += source.shape[4]
            self._push(
                "core", source.at[:, :, 1 - p.core], self.keep.at[:, :, :, cols], p.sibling(), begin
            )

    def _load(self, stage, index):
        y, x = index // self.place.side, index % self.place.side
        column, loads = 0, []
        for spot, source in enumerate(self.sources):
            cols = pl.ds(column, source.shape[4])
            column += source.shape[4]
            loads.append(
                pltpu.make_async_copy(
                    source.at[y, x, self.place.core], stage.at[index % 2, :, cols],
                    self.local.at[index % 2, spot],
                )
            )
        return loads

    def core_finish(self, stage):
        side, keep, columns = self.place.side, self.keep, self.keep.shape[3]
        for load in self._load(stage, 0):
            load.start()
        for copy in self.copies["core"]:
            copy.wait_recv()
        for index in range(side * side):
            if index + 1 < side * side:
                for load in self._load(stage, index + 1):
                    load.start()
            for load in self._load(stage, index):
                load.wait()
            y, x = index // side, index % side
            keep[y, x] = bf16(f32(keep[y, x]) + f32(stage[index % 2, :, :columns]))

    def first_start(self, begin=True):
        p, half = self.place, self.half
        self.index, self.copies["first"] = len(self.sources), []
        top, bottom = pl.ds(0, half), pl.ds(half, half)
        for step in range(1, p.side):
            other, to = p.x_peer(step)
            self._push("first", self.keep.at[:, other, top], self.first_a.at[step - 1], to, begin)
            other, to = p.y_peer(step)
            self._push("first", self.keep.at[other, :, bottom], self.first_b.at[step - 1], to, begin)

    def first_finish(self):
        p, half, keep = self.place, self.half, self.keep
        for copy in self.copies["first"]:
            copy.wait_recv()

        def add(index, carry):
            total = f32(keep[index, p.x, :half, :])
            for step in range(p.side - 1):
                total = total + f32(self.first_a[step, index])
            keep[index, p.x, :half, :] = bf16(total)
            total = f32(keep[p.y, index, half:, :])
            for step in range(p.side - 1):
                total = total + f32(self.first_b[step, index])
            keep[p.y, index, half:, :] = bf16(total)
            return carry

        lax.fori_loop(0, p.side, add, 0)

    def halves(self, out_a, out_b):
        p, half, keep = self.place, self.half, self.keep
        for index in range(p.side):
            out_a[index] = keep[index, p.x, :half, :]
            out_b[index] = keep[p.y, index, half:, :]

    def second_start(self):
        p, half = self.place, self.half
        top, bottom = pl.ds(0, half), pl.ds(half, half)
        for step in range(1, p.side):
            other, to = p.y_peer(step)
            self._push("second", self.keep.at[other, p.x, top], self.second_a.at[step - 1], to)
            other, to = p.x_peer(step)
            self._push("second", self.keep.at[p.y, other, bottom], self.second_b.at[step - 1], to)

    def second_wait(self):
        for copy in self.copies["second"]:
            copy.wait_recv()

    def total(self, cols):
        p, half = self.place, self.half
        top, bottom = f32(self.keep[p.y, p.x, :half, cols]), f32(self.keep[p.y, p.x, half:, cols])
        for step in range(p.side - 1):
            top = top + f32(self.second_a[step, :, cols])
            bottom = bottom + f32(self.second_b[step, :, cols])
        return jnp.concatenate([top, bottom], axis=0)

    def finish(self):
        for stage in self.copies.values():
            for copy in stage:
                copy.wait_send()


class Halves:
    def __init__(self, place, part_a, part_b, scratch):
        self.place, self.parts = place, (part_a, part_b)
        self.landed, (self.send, self.recv) = scratch[:2], scratch[2:]

    @staticmethod
    def scratch(side, half, columns):
        dma = pltpu.SemaphoreType.DMA((2 * (side - 1),))
        return [pltpu.VMEM((side - 1, half, columns), jnp.bfloat16)] * 2 + [dma, dma]

    def start(self):
        p = self.place
        self.copies = []
        for step in range(1, p.side):
            for index, (other, to) in enumerate((p.y_peer(step), p.x_peer(step))):
                spot = 2 * (step - 1) + index
                self.copies.append(
                    push(
                        self.parts[index].at[other], self.landed[index].at[step - 1],
                        self.send.at[spot], self.recv.at[spot], to,
                    )
                )

    def total(self):
        for copy in self.copies:
            copy.wait()
        sums = []
        for index, mine in enumerate((self.place.y, self.place.x)):
            total = f32(self.parts[index][mine])
            for step in range(self.place.side - 1):
                total = total + f32(self.landed[index][step])
            sums.append(total)
        return jnp.concatenate(sums, axis=0)


def forward_rows(masked, start, block, prefix_ref, q_ref, k_ref, v_ref, mixed_ref, sums_ref):
    width = q_ref.shape[1]
    keys = k_ref.shape[0]
    if masked:
        keys = max(keys // 2, start + block)
    lane = lax.broadcasted_iota(jnp.int32, (block, width), 1) // HEAD
    span = slice(start, start + block)
    query = q_ref[span, :] * jnp.bfloat16(HEAD**-0.5)
    key_rows, value_rows = k_ref[:keys, :], v_ref[:keys, :]
    if masked:
        query_ids = start + lax.broadcasted_iota(jnp.int32, (block, keys), 0)
        key_ids = lax.broadcasted_iota(jnp.int32, (block, keys), 1)
        allowed = (key_ids <= query_ids) | (key_ids < prefix_ref[0])
    mixed = jnp.zeros((block, width), jnp.float32)
    slot = lax.broadcasted_iota(jnp.int32, (block, 128), 1)
    table = jnp.zeros((block, 128), jnp.float32)
    for head in range(width // HEAD):
        scores = dot(jnp.where(lane == head, query, jnp.bfloat16(0)), key_rows, NT)
        if masked:
            scores = jnp.where(allowed, scores, mask_fill)
        row_max = jnp.max(scores, axis=1, keepdims=True)
        powered = jnp.exp(scores - row_max)
        totals = jnp.sum(powered, axis=1, keepdims=True)
        part = dot(bf16(powered), value_rows) * (1.0 / totals)
        mixed = jnp.where(lane == head, part, mixed)
        table = jnp.where(slot == head, row_max + jnp.log(totals), table)
    mixed_ref[span, :] = bf16(mixed)
    sums_ref[:, span] = table.T[:8, :]


def backward_delta(do_ref, o_ref, delta):
    width = do_ref.shape[1]
    product = f32(do_ref[...]) * f32(o_ref[...])
    row = lax.broadcasted_iota(jnp.int32, (8, width), 0)
    col = lax.broadcasted_iota(jnp.int32, (8, width), 1) // HEAD
    pick = jnp.where(row == col, 1.0, 0.0).astype(jnp.float32)
    delta[...] = lax.dot_general(
        pick, product, NT, precision=lax.Precision.HIGHEST, preferred_element_type=jnp.float32
    )


def backward_block(
    masked, block, index, heads, prefix_ref, q_ref, k_ref, v_ref, do_ref, sums_ref, delta, acc, dk_ref, dv_ref
):
    total, width = q_ref.shape
    factor = HEAD**-0.5
    rows = slice(index * block, (index + 1) * block)
    first = index * block if masked and index * block >= total // 2 else 0
    count = total - first
    lane = lax.broadcasted_iota(jnp.int32, (block, width), 1) // HEAD
    query, grad_rows = q_ref[first:, :], do_ref[first:, :]
    scaled_keys = k_ref[rows, :] * jnp.bfloat16(factor)
    value_rows = v_ref[rows, :]
    if masked:
        query_ids = first + lax.broadcasted_iota(jnp.int32, (block, count), 1)
        key_ids = index * block + lax.broadcasted_iota(jnp.int32, (block, count), 0)
        allowed = (key_ids <= query_ids) | (key_ids < prefix_ref[0])
    key_grad = jnp.zeros((block, width), jnp.float32)
    value_grad = jnp.zeros((block, width), jnp.float32)
    query_grad = jnp.zeros((count, width), jnp.float32)
    for head in heads:
        own_keys = jnp.where(lane == head, scaled_keys, jnp.bfloat16(0))
        scores = dot(own_keys, query, NT)
        if masked:
            scores = jnp.where(allowed, scores, mask_fill)
        probs = jnp.exp(scores - sums_ref[head : head + 1, first:])
        prob_grad = dot(jnp.where(lane == head, value_rows, jnp.bfloat16(0)), grad_rows, NT)
        score_grad = bf16(probs * (prob_grad - delta[head : head + 1, first:]))
        value_grad = jnp.where(lane == head, dot(bf16(probs), grad_rows), value_grad)
        key_grad = jnp.where(lane == head, dot(score_grad, query), key_grad)
        query_grad = query_grad + dot(score_grad, own_keys, TN)
    acc[first:, :] += query_grad
    mine = (lane >= heads[0]) & (lane <= heads[-1])
    key_grad, value_grad = bf16(key_grad * factor), bf16(value_grad)
    if heads[0] > 0:
        key_grad = jnp.where(mine, key_grad, dk_ref[rows, :])
        value_grad = jnp.where(mine, value_grad, dv_ref[rows, :])
    dk_ref[rows, :] = key_grad
    dv_ref[rows, :] = value_grad


def cross_backward_kernel(
    n, side, prefix_ref, q_ref, k_ref, v_ref, do_ref, o_ref, sums_ref, mine_ref, states_ref,
    shrink_ref, expand_ref, dq_ref, dk_ref, dv_ref, all_ref, source_ref, half_a_ref, half_b_ref,
    acc, delta, source, stage, own_sem, *scratch,
):
    p = Place(n, side)
    give = Give(p, all_ref, scratch[:4])
    feed_sum = Reduce(p, [shrink_ref, expand_ref], scratch[4:])
    width = q_ref.shape[1]
    step = pl.program_id(0)
    steps = pl.num_programs(0)

    @pl.when(step == 0)
    def _():
        own = pltpu.make_async_copy(mine_ref, all_ref.at[give.me], own_sem)
        own.start()
        greet(p.line() + p.plane())
        feed_sum.core_start()
        own.wait()
        give.step(0)
        backward_delta(do_ref, o_ref, delta)
        acc[...] = jnp.zeros_like(acc)
        source[...] = jnp.zeros_like(source)

    for later in range(1, n - 1):

        @pl.when(step == (later + 1) * steps // n)
        def _():
            give.step(later)

    @pl.when(step == 1)
    def _():
        feed_sum.core_start(False)
        feed_sum.core_finish(stage)
        feed_sum.first_start()

    backward_block(
        False, k_ref.shape[0], 0, tuple(range(width // HEAD)),
        prefix_ref, q_ref, k_ref, v_ref, do_ref, sums_ref, delta, acc, dk_ref, dv_ref,
    )
    source[:, :width] += dot(states_ref[...], dk_ref[...], TN)
    source[:, width:] += dot(states_ref[...], dv_ref[...], TN)

    @pl.when(step == steps - 1)
    def _():
        dq_ref[...] = bf16(acc[...])
        source_ref[...] = bf16(source[...])
        feed_sum.core_start(False)
        feed_sum.first_start(False)
        feed_sum.first_finish()
        feed_sum.halves(half_a_ref, half_b_ref)
        feed_sum.finish()
        give.finish()


def cross_backward(
    n_dp, n, query, key_rows, value_rows, grad_out, mixed, sums, prefix, mine, states, shrink, expand, block=512
):
    total, width = query.shape
    keys, model = states.shape
    side = round((n_dp // 2) ** 0.5)
    rows, columns = model // n_dp, shrink.shape[1] + expand.shape[1]
    half = (side, rows // 2, columns)
    by_place = lambda values: values.reshape(side, side, 2, rows, values.shape[1])
    low, wide = jnp.bfloat16, jnp.float32
    shape = jax.ShapeDtypeStruct
    whole = pl.BlockSpec((total, width), lambda i, p: (0, 0))
    part = pl.BlockSpec((block, width), lambda i, p: (i, 0))
    return pl.pallas_call(
        partial(cross_backward_kernel, n, side),
        grid_spec=pltpu.PrefetchScalarGridSpec(
            num_scalar_prefetch=1,
            grid=(keys // block,),
            in_specs=[
                whole, part, part, whole, whole,
                pl.BlockSpec((8, total), lambda i, p: (0, 0)),
                pl.BlockSpec(mine.shape, lambda i, p: (0, 0)),
                pl.BlockSpec((block, model), lambda i, p: (i, 0)),
                ANYWHERE, ANYWHERE,
            ],
            out_specs=[
                whole, part, part, ANYWHERE, pl.BlockSpec((model, 2 * width), lambda i, p: (0, 0)),
                pl.BlockSpec(half, lambda i, p: (0, 0, 0)), pl.BlockSpec(half, lambda i, p: (0, 0, 0)),
            ],
            scratch_shapes=[
                pltpu.VMEM((total, width), wide),
                pltpu.VMEM((8, total), wide),
                pltpu.VMEM((model, 2 * width), wide),
                pltpu.VMEM((2, rows, columns), low),
                pltpu.SemaphoreType.DMA,
                *Give.sems(n),
                *Reduce.scratch(side, rows, columns, 2, second=False),
            ],
        ),
        out_shape=[
            shape((total, width), low),
            shape((keys, width), low),
            shape((keys, width), low),
            shape((n,) + mine.shape, low),
            shape((model, 2 * width), low),
            shape(half, low),
            shape(half, low),
        ],
        compiler_params=pltpu.CompilerParams(
            vmem_limit_bytes=VMEM_LIMIT, collective_id=6, has_side_effects=True
        ),
        cost_estimate=pl.CostEstimate(
            flops=40 * total * keys * width, bytes_accessed=4 * keys * width, transcendentals=0
        ),
        name="cross_backward",
    )(
        prefix, query, key_rows, value_rows, grad_out, mixed, sums, mine, states,
        by_place(shrink), by_place(expand),
    )


def front_kernel(
    n, side, prefix_ref, inner_ref, outer_ref, norm_ref, expand_ref, shrink_ref, x_ref,
    near_ref, home_ref, later_ref, feed_ref, q_ref, k_ref, v_ref, mixed_ref, sums_ref,
    block_near, block_line, block_norm, own_sems, near_send, near_recv, home_send, home_recv,
    line_send, line_recv, far_send, far_recv,
):
    p = Place(n, side)
    width = inner_ref.shape[3]
    units = expand_ref.shape[1]
    for index in range(3):
        block_near[:, index * width : (index + 1) * width] = bf16(inner_ref[0, index])
    block_line[:, :width] = bf16(inner_ref[1, 0])
    block_line[:, width : 2 * width] = outer_ref[0]
    block_norm[...] = norm_ref[...]
    line_cols = pl.ds(pl.multiple_of(2 * width * p.z, 2 * width), 2 * width)
    later_cols = pl.ds(pl.multiple_of(width * p.z, width), width)
    spot = home_ref.at[p.y, p.x, p.core]
    near_ref[p.y, p.x, p.core] = block_near[...]
    own = [
        pltpu.make_async_copy(block_line, spot.at[:, line_cols], own_sems.at[0]),
        pltpu.make_async_copy(
            block_norm, spot.at[:, pl.ds(2 * n * width, block_norm.shape[1])], own_sems.at[1]
        ),
    ]
    for copy in own:
        copy.start()
    later_ref[:, later_cols] = outer_ref[1]
    for index in range(2):
        start = (n + index) * width
        later_ref[:, start : start + width] = bf16(inner_ref[1, index + 1])
    feed_ref[:, :units] = bf16(expand_ref[...])
    feed_ref[:, 2 * units : 3 * units] = shrink_ref[...]
    greet(p.line() + p.plane())
    near = Spread(p, near_ref, near_send, near_recv)
    rest = Spread(p, home_ref, home_send, home_recv)
    near.first()
    line = [
        push(block_line, spot.at[:, line_cols], line_send.at[index], line_recv.at[index], other)
        for index, other in enumerate(p.line())
    ]
    later = [
        push(
            later_ref.at[:, later_cols], later_ref.at[:, later_cols],
            line_send.at[n - 1 + index], line_recv.at[n - 1 + index], other,
        )
        for index, other in enumerate(p.line())
    ]
    far = {"mp": lax.rem(p.z + n // 2, n)}
    later += [
        push(
            feed_ref.at[:, pl.ds(2 * index * units, units)],
            feed_ref.at[:, pl.ds((2 * index + 1) * units, units)],
            far_send.at[index], far_recv.at[index], far,
        )
        for index in range(2)
    ]
    near.second()
    near.core()
    for copy in own:
        copy.wait()
    for copy in line:
        copy.wait_recv()
    rest.first()
    near.finish()
    model = x_ref.shape[1]
    weights = near_ref[...].reshape(model, 3 * width)
    for start in range(0, x_ref.shape[0], 256):
        rows = slice(start, start + 256)
        made = bf16(dot(x_ref[rows, :], weights))
        for index, target in enumerate((q_ref, k_ref, v_ref)):
            target[rows, :] = made[:, index * width : (index + 1) * width]
    rest.second()
    block = x_ref.shape[0] // 4
    for index in range(4):
        forward_rows(
            True, index * block, block, prefix_ref, q_ref, k_ref, v_ref, mixed_ref, sums_ref
        )
        if index == 2:
            rest.core()
    rest.finish()
    for copy in line:
        copy.wait_send()
    for copy in later:
        copy.wait()


def front(n_dp, n_mp, prefix, inner, outer_t, norm_t, expand, shrink_t, tokens):
    rows, width = inner.shape[2:]
    total = tokens.shape[0]
    side = round((n_dp // 2) ** 0.5)
    line = 2 * width
    columns = n_mp * line + norm_t.shape[1]
    low = jnp.bfloat16
    dma = pltpu.SemaphoreType.DMA
    shape = jax.ShapeDtypeStruct
    return pl.pallas_call(
        partial(front_kernel, n_mp, side),
        out_shape=[
            shape((side, side, 2, rows, 3 * width), low),
            shape((side, side, 2, rows, columns), low),
            shape((rows, (n_mp + 2) * width), low),
            shape((rows, 4 * expand.shape[1]), low),
            *[shape((total, width), low)] * 4,
            shape((8, total), jnp.float32),
        ],
        in_specs=[pl.BlockSpec(memory_space=pltpu.SMEM)] + [IN_VMEM] * 6,
        out_specs=[IN_VMEM, ANYWHERE] + [IN_VMEM] * 7,
        scratch_shapes=[
            pltpu.VMEM((rows, 3 * width), low),
            pltpu.VMEM((rows, line), low),
            pltpu.VMEM((rows, norm_t.shape[1]), low),
            dma((2,)),
            Spread.sems(side), Spread.sems(side), Spread.sems(side), Spread.sems(side),
            dma((2 * n_mp - 2,)), dma((2 * n_mp - 2,)), dma((2,)), dma((2,)),
        ],
        compiler_params=pltpu.CompilerParams(
            collective_id=0, has_side_effects=True, vmem_limit_bytes=VMEM_LIMIT
        ),
        cost_estimate=pl.CostEstimate(flops=40 * 10**9, bytes_accessed=1 << 20, transcendentals=0),
        name="front",
    )(prefix, inner, outer_t, norm_t, expand, shrink_t, tokens)


def self_to_cross_kernel(
    n, side, mixed_ref, bundle_ref, x_ref, feed_ref, later_ref,
    hidden_ref, normed_ref, inverse_ref, slots_ref, norm_ref, q_ref, home_ref, rest_ref,
    wo, wq, norm_columns, x_rows, blocks, wo_sems, wq_sems, x_sem, own_sem, send_in, recv_in, send_out, recv_out,
    feed_block, later_block, block_sems, feed_send, feed_recv, later_send, later_recv, norm_sem,
):
    p = Place(n, side)
    me = p.z
    size = x_rows.shape[0]
    width = mixed_ref.shape[1]
    loads = [
        pltpu.make_async_copy(mixed_ref.at[rows_at(me, size)], slots_ref.at[me], own_sem),
        pltpu.make_async_copy(x_ref.at[rows_at(me, size)], x_rows, x_sem),
        pltpu.make_async_copy(
            bundle_ref.at[:, pl.ds(2 * n * width, norm_columns.shape[1])], norm_columns, norm_sem
        ),
        *load_groups(n, bundle_ref, 2 * width, width, width, wo, wo_sems),
        *load_groups(n, bundle_ref, 2 * width, 0, width, wq, wq_sems),
    ]
    sources, blocks_here, homes = (later_ref, feed_ref), (later_block, feed_block), (rest_ref, home_ref)
    block_loads = [
        pltpu.make_async_copy(source, block, block_sems.at[index])
        for index, (source, block) in enumerate(zip(sources, blocks_here))
    ]
    for load in block_loads + loads:
        load.start()
    greet(p.line() + p.plane())
    copies = heads_to_tokens(n, mixed_ref, slots_ref, send_in, recv_in)
    for load in block_loads:
        load.wait()
    stores = [
        pltpu.make_async_copy(block, home.at[p.y, p.x, p.core], block_sems.at[index])
        for index, (block, home) in enumerate(zip(blocks_here, homes))
    ]
    for store in stores:
        store.start()
    rest = Spread(p, rest_ref, later_send, later_recv)
    spread = Spread(p, home_ref, feed_send, feed_recv)
    for store in stores:
        store.wait()
    rest.first()
    spread.first()
    for load in loads:
        load.wait()
    norms = f32(norm_columns[...]).T[:8, :]
    norm_ref[...] = norms
    branch = merge_heads(
        n, slots_ref, copies, lambda part, group: dot(part, wo[group], NT), f32(x_rows[...])
    )
    rest.second()
    hidden, normed, inverse = layer_norm(branch, norms[0:1, :], norms[3:4, :])
    hidden_ref[...] = hidden
    normed_ref[...] = normed
    inverse_ref[...] = jnp.broadcast_to(inverse, inverse_ref.shape)
    low = bf16(hidden)
    sent = tokens_to_heads(
        n, lambda group: dot(low, wq[group]), blocks, q_ref, send_out, recv_out, own_sem
    )
    rest.core()
    for copy in sent:
        copy.wait()
    rest.finish()
    spread.finish()


def self_to_cross(n_dp, n, mixed, bundle, tokens, feed_block, later_block):
    side = round((n_dp // 2) ** 0.5)
    total, width = mixed.shape
    size, model = total // n, tokens.shape[1]
    shape = jax.ShapeDtypeStruct
    dma = pltpu.SemaphoreType.DMA
    return pl.pallas_call(
        partial(self_to_cross_kernel, n, side),
        out_shape=[
            shape((size, model), jnp.float32),
            shape((size, model), jnp.float32),
            shape((size, 128), jnp.float32),
            shape((n, size, width), jnp.bfloat16),
            shape((8, model), jnp.float32),
            shape((total, width), jnp.bfloat16),
            shape((side, side, 2) + feed_block.shape, jnp.bfloat16),
            shape((side, side, 2) + later_block.shape, jnp.bfloat16),
        ],
        in_specs=[ANYWHERE] * 5,
        out_specs=[IN_VMEM] * 5 + [ANYWHERE] * 3,
        scratch_shapes=[
            pltpu.VMEM((n, model, width), jnp.bfloat16),
            pltpu.VMEM((n, model, width), jnp.bfloat16),
            pltpu.VMEM((model, bundle.shape[1] - 2 * n * width), jnp.bfloat16),
            pltpu.VMEM((size, model), jnp.bfloat16),
            pltpu.VMEM((n, size, width), jnp.bfloat16),
            dma((n,)), dma((n,)), dma, dma,
            dma((n - 1,)), dma((n - 1,)), dma((n - 1,)), dma((n - 1,)),
            pltpu.VMEM(feed_block.shape, jnp.bfloat16),
            pltpu.VMEM(later_block.shape, jnp.bfloat16),
            dma((2,)), Spread.sems(side), Spread.sems(side), Spread.sems(side), Spread.sems(side), dma,
        ],
        compiler_params=pltpu.CompilerParams(
            collective_id=1, has_side_effects=True, vmem_limit_bytes=VMEM_LIMIT
        ),
        cost_estimate=pl.CostEstimate(
            flops=10**9, bytes_accessed=8 * total * width, transcendentals=0
        ),
        name="self_to_cross",
    )(mixed, bundle, tokens, feed_block, later_block)


def cross_forward_kernel(
    side, n, q_ref, states_ref, rest_ref, home_in_ref, k_ref, v_ref, mixed_ref, sums_ref, home_ref,
    weights, weight_sem, feed_send, feed_recv,
):
    p = Place(n, side)
    width = q_ref.shape[1]
    load = pltpu.make_async_copy(
        rest_ref.at[:, pl.ds(n * width, 2 * width)], weights, weight_sem
    )
    load.start()
    greet(p.plane())
    spread = Spread(p, home_ref, feed_send, feed_recv)
    spread.second()
    load.wait()
    for start in range(0, states_ref.shape[0], 512):
        rows = slice(start, start + 512)
        made = bf16(dot(states_ref[rows, :], weights[...]))
        k_ref[rows, :] = made[:, :width]
        v_ref[rows, :] = made[:, width:]
    block = q_ref.shape[0] // 2
    for start in range(0, q_ref.shape[0], block):
        forward_rows(False, start, block, None, q_ref, k_ref, v_ref, mixed_ref, sums_ref)
    spread.finish()


def cross_forward(n, query, states, rest, home):
    total, width = query.shape
    keys, model = states.shape
    side = home.shape[0]
    shape = jax.ShapeDtypeStruct
    low = jnp.bfloat16
    return pl.pallas_call(
        partial(cross_forward_kernel, side, n),
        out_shape=[
            shape((keys, width), low),
            shape((keys, width), low),
            shape((total, width), low),
            shape((8, total), jnp.float32),
            shape(home.shape, low),
        ],
        in_specs=[IN_VMEM] * 2 + [ANYWHERE] * 2,
        out_specs=[IN_VMEM] * 4 + [ANYWHERE],
        input_output_aliases={3: 4},
        scratch_shapes=[
            pltpu.VMEM((model, 2 * width), low),
            pltpu.SemaphoreType.DMA,
            Spread.sems(side), Spread.sems(side),
        ],
        compiler_params=pltpu.CompilerParams(
            collective_id=7, has_side_effects=True, vmem_limit_bytes=VMEM_LIMIT
        ),
        cost_estimate=pl.CostEstimate(flops=10**10, bytes_accessed=1 << 20, transcendentals=0),
        name="cross_forward",
    )(query, states, rest, home)


def feed_kernel(
    n, side, mixed_ref, rest_ref, home_ref, hidden_one_ref, cot_ref, norm_ref,
    out_ref, second_ref, dmix_ref, shrink_grad_ref, expand_grad_ref, wo_grad_ref, norm_grad_ref,
    wo, weights, slots, hidden_two, normed_two, low_two, low_three, act, slope,
    y_own, y_send, y_recv, d_send, d_recv, cot, blocks,
    load_sems, wo_sems, own_sem, send_in, recv_in, send_out, recv_out, pair_send, pair_recv,
    home_sems, home_send, home_recv,
):
    p = Place(n, side)
    me = p.z
    mate = {"mp": me + 1 - 2 * lax.rem(me, 2)}
    size = cot.shape[0]
    half = size // 2
    width = mixed_ref.shape[1]
    hidden_units = act.shape[1]
    chunk = min(512, hidden_units)
    loads = [
        pltpu.make_async_copy(mixed_ref.at[rows_at(me, size)], slots.at[me], load_sems.at[0]),
        *load_groups(n, rest_ref, width, 0, width, wo, wo_sems),
        pltpu.make_async_copy(cot_ref.at[rows_at(me, size)], cot, load_sems.at[1]),
    ]
    rows = home_ref.shape[3]
    places = [(y, x) for y in range(side) for x in range(side)]
    spots = [rows_at((y * side + x) * 2 + p.core, rows) for y, x in places]
    homes = [
        pltpu.make_async_copy(home_ref.at[y, x, p.core], weights.at[spot], home_sems.at[index])
        for index, ((y, x), spot) in enumerate(zip(places, spots))
    ]
    for load in loads + homes:
        load.start()
    greet(p.line() + [p.sibling()])
    copies = heads_to_tokens(n, mixed_ref, slots, send_in, recv_in)
    home_copies = [
        push(
            home_ref.at[y, x, p.core], weights.at[spot],
            home_send.at[index], home_recv.at[index], p.sibling(),
        )
        for index, ((y, x), spot) in enumerate(zip(places, spots))
    ]
    for load in loads[: n + 1]:
        load.wait()
    branch = merge_heads(
        n, slots, copies, lambda part, group: dot(part, wo[group], NT), hidden_one_ref[...]
    )
    hidden, normed, inverse_two = layer_norm(branch, norm_ref[1:2, :], norm_ref[4:5, :])
    hidden_two[...] = hidden
    normed_two[...] = normed
    low_two[:size, :] = bf16(hidden)
    own, other = pl.ds(0, size), pl.ds(size, size)
    pair = []

    def to_mate(source, target):
        index = len(pair)
        pair.append(push(source, target, pair_send.at[index], pair_recv.at[index], mate))
        return pair[-1]

    hidden_copy = to_mate(low_two.at[own], low_two.at[other])
    for copy in homes:
        copy.wait()
    for copy in home_copies:
        copy.wait_recv()
    expand = weights.at[:, pl.ds(0, hidden_units)]
    shrink = weights.at[:, pl.ds(hidden_units, hidden_units)]

    def expand_rows(start, count):
        rows = low_two[start : start + count, :]
        for first in range(0, hidden_units, chunk):
            pre = dot(rows, expand[:, first : first + chunk])
            cdf = 0.5 + 0.5 * lax.erf(pre * 0.7071067811865476)
            act[start : start + count, first : first + chunk] = bf16(pre * cdf)
            slope[start : start + count, first : first + chunk] = bf16(
                cdf + pre * jnp.exp(-0.5 * pre * pre) * 0.3989422804014327
            )

    expand_rows(0, size)
    hidden_copy.wait_recv()
    y_copies = []
    for start in (0, half):
        expand_rows(size + start, half)
        y_send[start : start + half, :] = bf16(
            dot(act[size + start : size + start + half, :], shrink[...], NT)
        )
        y_copies.append(to_mate(y_send.at[pl.ds(start, half)], y_recv.at[pl.ds(start, half)]))
    y_own[...] = dot(act[:size, :], shrink[...], NT)
    for copy in y_copies:
        copy.wait_recv()
    output, normed, inverse = layer_norm(
        hidden_two[...] + y_own[...] + f32(y_recv[...]), norm_ref[2:3, :], norm_ref[5:6, :]
    )
    out_ref[...] = bf16(output)
    loads[n + 1].wait()
    third, gain_three, bias_three = norm_back(f32(cot[...]), normed, inverse, norm_ref[2:3, :])
    low_three[:size, :] = bf16(third)
    grad_copy = to_mate(low_three.at[own], low_three.at[other])

    def back_rows(start, count):
        rows = low_three[start : start + count, :]
        for first in range(0, hidden_units, chunk):
            grad = dot(rows, shrink[:, first : first + chunk])
            spot = (slice(start, start + count), slice(first, first + chunk))
            slope[spot] = bf16(grad * f32(slope[spot]))

    back_rows(0, size)
    grad_copy.wait_recv()
    d_copies = []
    for start in (0, half):
        back_rows(size + start, half)
        d_send[start : start + half, :] = bf16(
            dot(slope[size + start : size + start + half, :], expand[...], NT)
        )
        d_copies.append(to_mate(d_send.at[pl.ds(start, half)], d_recv.at[pl.ds(start, half)]))
    y_own[...] = third + dot(slope[:size, :], expand[...], NT)
    for copy in d_copies:
        copy.wait_recv()
    second, gain_two, bias_two = norm_back(
        y_own[...] + f32(d_recv[...]), normed_two[...], inverse_two, norm_ref[1:2, :]
    )
    second_ref[...] = second
    low = bf16(second)
    sent = tokens_to_heads(
        n, lambda group: dot(low, wo[group]), blocks, dmix_ref, send_out, recv_out, own_sem
    )
    norm_grad_ref[...] = jnp.concatenate(
        [gain_two, gain_three, bias_two, bias_three, jnp.zeros((4, norm_grad_ref.shape[1]))], axis=0
    )
    for first in range(0, low_two.shape[1], 256):
        rows = slice(first, first + 256)
        shrink_grad_ref[rows, :] = bf16(dot(low_three[:, rows], act[...], TN))
        expand_grad_ref[rows, :] = bf16(dot(low_two[:, rows], slope[...], TN))
    for group in range(n):
        wo_grad_ref[:, group * width : (group + 1) * width] = bf16(dot(low, slots[group], TN))
    for copy in sent:
        copy.wait()
    for copy in pair + home_copies:
        copy.wait_send()


def feed(n, mixed, rest, home, hidden_one, cotangent, norms):
    total, width = mixed.shape
    side, model, units = home.shape[0], hidden_one.shape[1], home.shape[4] // 2
    size = total // n
    shape = jax.ShapeDtypeStruct
    dma = pltpu.SemaphoreType.DMA
    low, wide = jnp.bfloat16, jnp.float32
    return pl.pallas_call(
        partial(feed_kernel, n, side),
        out_shape=[
            shape((size, model), low),
            shape((size, model), wide),
            shape((total, width), low),
            shape((model, units), low),
            shape((model, units), low),
            shape((model, model), low),
            shape((8, model), wide),
        ],
        in_specs=[ANYWHERE] * 3 + [IN_VMEM, ANYWHERE, IN_VMEM],
        out_specs=[IN_VMEM] * 2 + [ANYWHERE] + [IN_VMEM] * 4,
        scratch_shapes=[
            pltpu.VMEM((n, model, width), low),
            pltpu.VMEM((model, 2 * units), low),
            pltpu.VMEM((n, size, width), low),
            pltpu.VMEM((size, model), wide),
            pltpu.VMEM((size, model), wide),
            pltpu.VMEM((2 * size, model), low),
            pltpu.VMEM((2 * size, model), low),
            pltpu.VMEM((2 * size, units), low),
            pltpu.VMEM((2 * size, units), low),
            pltpu.VMEM((size, model), wide),
            pltpu.VMEM((size, model), low),
            pltpu.VMEM((size, model), low),
            pltpu.VMEM((size, model), low),
            pltpu.VMEM((size, model), low),
            pltpu.VMEM((size, model), low),
            pltpu.VMEM((n, size, width), low),
            dma((2,)), dma((n,)), dma,
            dma((n - 1,)), dma((n - 1,)), dma((n - 1,)), dma((n - 1,)),
            dma((6,)), dma((6,)),
            dma((side * side,)), dma((side * side,)), dma((side * side,)),
        ],
        compiler_params=pltpu.CompilerParams(
            collective_id=2, has_side_effects=True, vmem_limit_bytes=VMEM_LIMIT
        ),
        cost_estimate=pl.CostEstimate(
            flops=80 * 10**9, bytes_accessed=8 * total * width, transcendentals=0
        ),
        name="feed",
    )(mixed, rest, home, hidden_one, cotangent, norms)


def cross_to_self_kernel(
    n, side, dq_ref, bundle_ref, second_ref, hidden_ref, normed_ref, inverse_ref, mixed_ref, gain_ref, norm_ref,
    half_a_ref, half_b_ref, first_ref, dmix_ref, weight_grad_ref, norm_grad_ref, feed_ref,
    wo, wq, slots, blocks, wo_sems, wq_sems, own_sem, send_in, recv_in, send_out, recv_out, *scratch,
):
    p = Place(n, side)
    halves = Halves(p, half_a_ref, half_b_ref, scratch)
    me = p.z
    size, model = second_ref.shape
    width = dq_ref.shape[1]
    loads = [
        pltpu.make_async_copy(dq_ref.at[rows_at(me, size)], slots.at[me], own_sem),
        *load_groups(n, bundle_ref, 2 * width, 0, width, wq, wq_sems),
        *load_groups(n, bundle_ref, 2 * width, width, width, wo, wo_sems),
    ]
    for load in loads:
        load.start()
    greet(p.line() + p.plane())
    copies = heads_to_tokens(n, dq_ref, slots, send_in, recv_in)
    halves.start()
    for load in loads:
        load.wait()
    upstream = merge_heads(
        n, slots, copies, lambda part, group: dot(part, wq[group], NT), second_ref[...]
    )
    first, gain_one, bias_one = norm_back(
        upstream, normed_ref[...], inverse_ref[:, 0:1], gain_ref[0:1, :]
    )
    first_ref[...] = first
    low = bf16(first)
    sent = tokens_to_heads(
        n, lambda group: dot(low, wo[group]), blocks, dmix_ref, send_out, recv_out, own_sem
    )
    hidden_low = bf16(hidden_ref[...])
    for group in range(n):
        cols = 2 * group * width
        weight_grad_ref[:, cols : cols + width] = bf16(dot(hidden_low, slots[group], TN))
        weight_grad_ref[:, cols + width : cols + 2 * width] = bf16(dot(low, mixed_ref[group], TN))
    rows = jnp.concatenate(
        [
            gain_one, norm_ref[0:2, :], bias_one, norm_ref[2:4, :],
            jnp.zeros((122, model), jnp.float32),
        ],
        axis=0,
    )
    norm_grad_ref[...] = bf16(rows.T)
    feed_ref[...] = bf16(halves.total())
    for copy in sent:
        copy.wait()


def cross_to_self(n_dp, n, dq, bundle, second, hidden, normed, inverse, slots, gains, norm_rows, halves):
    side = round((n_dp // 2) ** 0.5)
    half, columns = halves[0].shape[1:]
    total, width = dq.shape
    size, model = second.shape
    shape = jax.ShapeDtypeStruct
    dma = pltpu.SemaphoreType.DMA
    return pl.pallas_call(
        partial(cross_to_self_kernel, n, side),
        out_shape=[
            shape((size, model), jnp.float32),
            shape((total, width), jnp.bfloat16),
            shape((model, 2 * model), jnp.bfloat16),
            shape((model, 128), jnp.bfloat16),
            shape((2 * half, columns), jnp.bfloat16),
        ],
        in_specs=[ANYWHERE] * 2 + [IN_VMEM] * 9,
        out_specs=[IN_VMEM, ANYWHERE, IN_VMEM, IN_VMEM, IN_VMEM],
        scratch_shapes=[
            pltpu.VMEM((n, model, width), jnp.bfloat16),
            pltpu.VMEM((n, model, width), jnp.bfloat16),
            pltpu.VMEM((n, size, width), jnp.bfloat16),
            pltpu.VMEM((n, size, width), jnp.bfloat16),
            dma((n,)), dma((n,)), dma,
            dma((n - 1,)), dma((n - 1,)), dma((n - 1,)), dma((n - 1,)),
            *Halves.scratch(side, half, columns),
        ],
        compiler_params=pltpu.CompilerParams(
            collective_id=3, has_side_effects=True, vmem_limit_bytes=VMEM_LIMIT
        ),
        cost_estimate=pl.CostEstimate(
            flops=10**9, bytes_accessed=8 * total * width, transcendentals=0
        ),
        name="cross_to_self",
    )(dq, bundle, second, hidden, normed, inverse, slots, gains, norm_rows, *halves)


class Fold:
    def __init__(self, place, make, out, scratch, group, slack=2):
        self.n, self.me, self.make, self.out = place.n, place.z, make, out
        self.parts, self.held, self.down_send, self.down_recv, self.back_send, self.back_recv, self.own = scratch
        self.chunks = self.held.shape[1]
        self.ring = self.parts.shape[1]
        self.group, self.slack = group, slack
        self.ticks = self.chunks + slack * (2 * (self.n - 1) - 1)

    @staticmethod
    def scratch(chunks, rows, columns, ring=12):
        low, dma = jnp.bfloat16, pltpu.SemaphoreType.DMA((2, chunks))
        return [
            pltpu.VMEM((2, ring, rows, columns), low), pltpu.VMEM((2, chunks, rows, columns), low),
            dma, dma, dma, dma, dma,
        ]

    def _flows(self):
        n, me = self.n, self.me
        return (
            (0, me, lax.rem(me + 1, n), lax.rem(me + n - 1, n)),
            (1, n - 1 - me, lax.rem(me + n - 1, n), lax.rem(me + 1, n)),
        )

    def _down(self, flow, chunk, to, first):
        source = self.parts.at[flow, lax.rem(chunk, self.ring)] if first else self.held.at[flow, chunk]
        return pltpu.make_async_remote_copy(
            source, self.held.at[flow, chunk],
            self.down_send.at[flow, chunk], self.down_recv.at[flow, chunk],
            device_id={"mp": to}, device_id_type=MESH,
        )

    def _back(self, flow, chunk, to, first):
        source = (self.held if first else self.out).at[flow, chunk]
        return pltpu.make_async_remote_copy(
            source, self.out.at[flow, chunk],
            self.back_send.at[flow, chunk], self.back_recv.at[flow, chunk],
            device_id={"mp": to}, device_id_type=MESH,
        )

    def _keep(self, flow, chunk):
        return pltpu.make_async_copy(
            self.held.at[flow, chunk], self.out.at[flow, chunk], self.own.at[flow, chunk]
        )

    def tick(self, tick):
        last = self.n - 1
        for flow, spot, ahead, behind in self._flows():
            if tick < self.chunks:
                if tick % self.group == 0:
                    whole = bf16(self.make(flow, tick // self.group))
                    rows = whole.shape[0] // self.group
                    for index in range(self.group):
                        if tick + index >= self.ring:

                            @pl.when(spot == 0)
                            def _():
                                self._down(flow, tick + index - self.ring, ahead, True).wait_send()

                        self.parts[flow, (tick + index) % self.ring] = whole[
                            index * rows : (index + 1) * rows
                        ]

                @pl.when(spot == 0)
                def _():
                    self._down(flow, tick, ahead, True).start()

            chunk = tick - self.slack * spot

            @pl.when((spot > 0) & (chunk >= 0) & (chunk < self.chunks))
            def _():
                self._down(flow, chunk, ahead, False).wait_recv()
                self.held[flow, chunk] = bf16(
                    f32(self.held[flow, chunk]) + f32(self.parts[flow, lax.rem(chunk, self.ring)])
                )

                @pl.when(spot < last)
                def _():
                    self._down(flow, chunk, ahead, False).start()

                @pl.when(spot == last)
                def _():
                    self._back(flow, chunk, behind, True).start()
                    self._keep(flow, chunk).start()

            given = tick - self.slack * (2 * last - spot)

            @pl.when((spot > 0) & (spot < last) & (given >= 0) & (given < self.chunks))
            def _():
                self._back(flow, given, behind, False).wait_recv()
                self._back(flow, given, behind, False).start()

    def finish(self):
        last = self.n - 1
        for flow, spot, ahead, behind in self._flows():

            @pl.when(spot == 0)
            def _():
                def wait(chunk, carry):
                    self._back(flow, chunk, behind, False).wait_recv()
                    return carry

                lax.fori_loop(0, self.chunks, wait, 0)

                def sent(chunk, carry):
                    self._down(flow, chunk, ahead, True).wait_send()
                    return carry

                lax.fori_loop(max(self.chunks - self.ring, 0), self.chunks, sent, 0)

            @pl.when((spot > 0) & (spot < last))
            def _():
                def sent(chunk, carry):
                    self._down(flow, chunk, ahead, False).wait_send()
                    self._back(flow, chunk, behind, False).wait_send()
                    return carry

                lax.fori_loop(0, self.chunks, sent, 0)

            @pl.when(spot == last)
            def _():
                def sent(chunk, carry):
                    self._back(flow, chunk, behind, True).wait_send()
                    self._keep(flow, chunk).wait()
                    return carry

                lax.fori_loop(0, self.chunks, sent, 0)


class Everyone:
    def __init__(self, n_dp, n_mp, mine, slots, send_sems, recv_sems):
        self.n, self.n_mp = n_dp * n_mp, n_mp
        self.me = lax.axis_index("dp") * n_mp + lax.axis_index("mp")
        self.mine, self.slots, self.send, self.recv = mine, slots, send_sems, recv_sems

    def _to(self, distance):
        to = lax.rem(self.me + distance, self.n)
        return {"dp": to // self.n_mp, "mp": lax.rem(to, self.n_mp)}

    def _copy(self, distance):
        return pltpu.make_async_remote_copy(
            self.mine, self.slots.at[self.me], self.send.at[distance - 1], self.recv.at[distance - 1],
            device_id=self._to(distance), device_id_type=MESH,
        )

    def greet(self):
        barrier = pltpu.get_barrier_semaphore()

        def signal(distance, carry):
            pl.semaphore_signal(barrier, inc=1, device_id=self._to(distance), device_id_type=MESH)
            return carry

        lax.fori_loop(1, self.n, signal, 0)
        pl.semaphore_wait(barrier, self.n - 1)

    def start(self):
        def start(distance, carry):
            self._copy(distance).start()
            return carry

        self.slots[self.me] = self.mine[...]
        lax.fori_loop(1, self.n, start, 0)

    def finish(self):
        def wait(distance, carry):
            self._copy(distance).wait()
            return carry

        lax.fori_loop(1, self.n, wait, 0)
        return jnp.sum(self.slots[...], axis=0)


def moments(upstream, first_moment, second_moment, master, decay):
    first_new = first_decay * first_moment + (1.0 - first_decay) * upstream
    second_new = second_decay * second_moment + (1.0 - second_decay) * upstream * upstream
    direction = (
        first_new
        / (1.0 - first_decay**STEP)
        / (jnp.sqrt(second_new / (1.0 - second_decay**STEP)) + epsilon)
        + decay * master
    )
    return (first_new, second_new, direction)


def tensors(inner, outer, expand, shrink, norms):
    found = [inner.at[a, c] for a in range(2) for c in range(3)]
    found += [outer.at[0], outer.at[1], expand, shrink]
    found += [norms.at[pl.ds(row, 1)] for row in range(6)]
    return list(zip(found, [weight_decay] * 10 + [0.0] * 6))


def square_row(squares, share):
    lane = lax.broadcasted_iota(jnp.int32, (1, 128), 1)
    row = jnp.zeros((1, 128), jnp.float32)
    for index, values in enumerate(squares):
        total = jnp.sum(jnp.sum(values, axis=0, keepdims=True), axis=1, keepdims=True)
        row = jnp.where(lane == index, total * share if index >= 10 else total, row)
    return row


def update_kernel(split, *refs):
    (
        both_ref, layer_ref, sums_ref, grads, weights, firsts, seconds,
        states_ref, input_ref, output_ref, table_ref, new_weights, new_firsts, new_seconds,
        both, layer, wide, loads, stores,
    ) = (
        *refs[:3], refs[3:8], refs[8:13], refs[13:18], refs[18:23],
        *refs[23:27], refs[27:32], refs[32:37], refs[37:42], *refs[42:],
    )
    size, columns = both.shape[2], both.shape[3]
    chunks = both.shape[1]
    pieces, row = [], 0
    for source, held, first, count, target, start in (
        (both_ref.at[0], both.at[0], 0, split, states_ref, 0),
        (both_ref.at[1], both.at[1], 0, split, states_ref, split * size),
        (both_ref.at[0], both.at[0], split, chunks - split, input_ref, 0),
        (both_ref.at[1], both.at[1], split, chunks - split, input_ref, (chunks - split) * size),
        (layer_ref, layer, 0, layer_ref.shape[0], output_ref, 0),
    ):
        span = pl.ds(first, count)
        length = count * source.shape[1]
        load = pltpu.make_async_copy(source.at[span], held.at[span], loads.at[len(pieces)])
        store = pltpu.make_async_copy(
            wide.at[pl.ds(row, length)], target.at[pl.ds(start, length)], stores.at[len(pieces)]
        )
        pieces.append((load, store, held, first, count, row))
        row += length
    for piece in pieces:
        piece[0].start()
    for load, store, held, first, count, row in pieces:
        load.wait()
        length = held.shape[1]
        for index in range(count):
            wide[row + index * length : row + (index + 1) * length, :] = f32(held[first + index])
        store.start()
    lane = lax.broadcasted_iota(jnp.int32, (1, 128), 1)
    counts = jnp.where(lane < 8, float(D * D), jnp.where(lane < 10, float(D * FF), float(D)))
    weight_norm = jnp.sqrt(sums_ref[0:1, :] / counts)
    update_norm = jnp.sqrt(sums_ref[1:2, :] / counts)
    trust = weight_norm / (update_norm + epsilon)
    table_ref[...] = jnp.concatenate([weight_norm, update_norm, trust], axis=0)[:, :16]
    groups = [tensors(*group) for group in (grads, weights, firsts, seconds, new_weights, new_firsts, new_seconds)]
    for index, parts in enumerate(zip(*groups)):
        grad, weight, first, second, new_weight, new_first, new_second = [part[0] for part in parts]
        ratio = jnp.sum(jnp.where(lane == index, trust, 0.0), axis=1, keepdims=True)
        master = weight[...]
        first_new, second_new, direction = moments(
            grad[...], first[...], second[...], master, parts[0][1]
        )
        new_first[...] = first_new
        new_second[...] = second_new
        new_weight[...] = master - learn_rate * ratio * direction
    for piece in pieces:
        piece[1].wait()


def update(both, layer, source_rows, sums, grads, weights, firsts, seconds):
    shape = lambda values: jax.ShapeDtypeStruct(values.shape, jnp.float32)
    results = [shape(values) for values in weights]
    size, columns = both.shape[2:]
    split = source_rows // (2 * size)
    total = layer.shape[0] * layer.shape[1]
    wide = lambda rows: jax.ShapeDtypeStruct((rows, columns), jnp.float32)
    dma = pltpu.SemaphoreType.DMA((5,))
    return pl.pallas_call(
        partial(update_kernel, split),
        out_shape=[wide(source_rows), wide(total), wide(total)]
        + [jax.ShapeDtypeStruct((3, 16), jnp.float32)]
        + results * 3,
        in_specs=[ANYWHERE] * 2 + [IN_VMEM] * 21,
        out_specs=[ANYWHERE] * 3 + [IN_VMEM] * 16,
        scratch_shapes=[
            pltpu.VMEM(both.shape, jnp.bfloat16),
            pltpu.VMEM(layer.shape, jnp.bfloat16),
            pltpu.VMEM((source_rows + 2 * total, columns), jnp.float32),
            dma, dma,
        ],
        compiler_params=pltpu.CompilerParams(vmem_limit_bytes=VMEM_LIMIT),
        name="update",
    )(both, layer, sums, *grads, *weights, *firsts, *seconds)


def finish_kernel(
    n, side, units, width, prefix_ref, q_ref, k_ref, v_ref, do_ref, o_ref, row_sums_ref,
    near_ref, x_ref, first_ref, cross_dk_ref, cross_dv_ref, rest_ref,
    feed_ref, cross_wo_ref, weight_ref, norm_ref, source_grad_ref, *refs,
):
    states, refs = refs[:15], refs[15:]
    out_ref, sums_ref, grads, refs = refs[0], refs[1], refs[2:7], refs[7:]
    (
        source_ref, source_sem, dq_ref, dk_ref, dv_ref, query_acc, delta, master_sems, inner, stage, far_recv, group_send, group_recv,
        far_send_sem, far_recv_sem, group_send_sems, group_recv_sems,
        mine, slots, everyone_send, everyone_recv, *scratch,
    ) = refs
    n_dp = 2 * side * side
    p = Place(n, side)
    everyone = Everyone(n_dp, n, mine, slots, everyone_send, everyone_recv)

    me = p.z
    own_heads = (dq_ref, dk_ref, dv_ref)
    size, model = first_ref.shape
    rows = inner.shape[3]
    per_group = 4
    group_rows = per_group * out_ref.shape[2]
    source_groups = cross_dk_ref.shape[0] // (2 * group_rows)

    def make(flow, group):
        if group < source_groups:
            spot = pl.ds((flow * source_groups + group) * group_rows, group_rows)
            return dot(cross_dk_ref[spot, :], source_ref[:, :width], NT) + dot(
                cross_dv_ref[spot, :], source_ref[:, width:], NT
            )
        tokens = x_ref.shape[0]
        start = flow * (tokens // 2) + (group - source_groups) * group_rows
        spot = pl.ds(start, group_rows)
        total = jnp.zeros((group_rows, model), jnp.float32)
        for index, own in enumerate(own_heads):
            total = total + dot(own[spot, :], near_ref[:, index * width : (index + 1) * width], NT)
        here = first_ref[start % size : start % size + group_rows, :]
        return total + jnp.where(me == start // size, here, 0.0)

    fold = Fold(p, make, out_ref, scratch[:7], per_group)
    group_sum = Reduce(p, [cross_wo_ref, weight_ref, norm_ref, source_grad_ref], scratch[7:15])
    inner_sum = Reduce(p, [inner], scratch[15:23])

    source_load = pltpu.make_async_copy(
        rest_ref.at[:, pl.ds(n * width, 2 * width)], source_ref, source_sem
    )
    source_load.start()
    everyone.greet()
    group_sum.core_start()
    far = {"mp": lax.rem(me + n // 2, n)}
    far_copies = [
        push(
            feed_ref.at[:, pl.ds((2 * index + 1) * units, units)],
            far_recv.at[:, pl.ds(index * units, units)],
            far_send_sem.at[index], far_recv_sem.at[index], far,
        )
        for index in range(2)
    ]

    source_load.wait()
    ticks = iter(range(fold.ticks))

    def advance(count):
        for _ in range(count):
            fold.tick(next(ticks))

    advance(1)
    backward_delta(do_ref, o_ref, delta)
    query_acc[...] = jnp.zeros_like(query_acc)
    key_block = 256

    def self_backward(index, heads):
        backward_block(
            True, key_block, index, heads, prefix_ref, q_ref, k_ref, v_ref, do_ref, row_sums_ref, delta,
            query_acc, dk_ref, dv_ref,
        )

    advance(1)
    group_sum.core_finish(stage)
    group_sum.first_start()
    for index in range(x_ref.shape[0] // key_block):
        for heads in ((0, 1), (2, 3)):
            self_backward(index, heads)
            advance(1)
    dq_ref[...] = bf16(query_acc[...])

    per = 256
    for start in range(0, model, per):
        turned = x_ref[:, start : start + per]
        for index, own in enumerate(own_heads):
            block = bf16(dot(turned, own[...], TN))
            for row in range(0, per, rows):
                flat = (start + row) // rows
                y, x, core = flat // (2 * side), flat // 2 % side, flat % 2
                inner[y, x, core, :, index * width : (index + 1) * width] = block[row : row + rows]
    inner_sum.core_start()
    advance(1)
    inner_sum.core_finish(stage)
    inner_sum.first_start()
    advance(2)
    group_sum.first_finish()
    group_sum.second_start()
    advance(1)
    advance(1)
    inner_sum.first_finish()
    inner_sum.second_start()
    advance(1)
    group_sum.second_wait()
    whole = n * width
    for group in range(n):
        group_send[group, :, :width] = bf16(
            group_sum.total(slice(group * width, (group + 1) * width))
        )
        start = whole + 2 * group * width
        group_send[group, :, width : 3 * width] = bf16(
            group_sum.total(slice(start, start + 2 * width))
        )
        group_send[group, :, 3 * width :] = bf16(
            group_sum.total(slice(3 * whole, 3 * whole + norm_ref.shape[4]))
        )
    group_copies = []
    for distance in range(1, n):
        to = lax.rem(me + distance, n)
        group_copies.append(
            push(
                group_send.at[to], group_recv.at[distance - 1],
                group_send_sems.at[distance - 1], group_recv_sems.at[distance - 1], {"mp": to},
            )
        )
    advance(2)

    def optimizer_sums(*masters):
        master_loads = [
            pltpu.make_async_copy(source, target, master_sems.at[index])
            for index, (source, target) in enumerate(zip(states, masters))
        ]
        for load in master_loads:
            load.start()
        grad_inner, grad_outer, grad_expand, grad_shrink, grad_norms = grads
        inner_sum.second_wait()
        for index in range(3):
            grad_inner[0, index] = inner_sum.total(slice(index * width, (index + 1) * width))
        start = 3 * whole + norm_ref.shape[4]
        for index in range(2):
            grad_inner[1, index + 1] = group_sum.total(
                slice(start + index * width, start + (index + 1) * width)
            )
        for load in master_loads:
            load.wait()
        weights, firsts, seconds = (tensors(*masters[index : index + 5]) for index in (0, 5, 10))
        share = 1.0 / n
        mine[...] = jnp.zeros(mine.shape, jnp.float32)
        mine[0:1, :] = square_row([ref[...] * ref[...] for ref, _ in weights], share)
        advance(2)
        for copy in far_copies:
            copy.wait_recv()
        grad_shrink[...] = (f32(feed_ref[:, :units]) + f32(far_recv[:, :units])).T
        grad_expand[...] = f32(feed_ref[:, 2 * units : 3 * units]) + f32(far_recv[:, units:])
        advance(2)
        for distance in range(1, n):
            group_copies[distance - 1].wait_recv()
        received = lambda cols: sum(
            [f32(group_recv[distance - 1, :, cols]) for distance in range(1, n)],
            f32(group_send[me, :, cols]),
        )
        grad_outer[1] = received(slice(0, width)).T
        grad_inner[1, 0] = received(slice(width, 2 * width))
        grad_outer[0] = received(slice(2 * width, 3 * width)).T
        grad_norms[...] = received(slice(3 * width, 3 * width + norm_ref.shape[4])).T[:6, :]

        def direction_square(grad, first, second, weight):
            step = moments(grad[0][...], first[0][...], second[0][...], weight[0][...], weight[1])[2]
            return step * step

        mine[1:2, :] = square_row(
            [direction_square(*group) for group in zip(tensors(*grads), firsts, seconds, weights)], share
        )
        everyone.start()
        advance(4)
        sums_ref[...] = everyone.finish()

    pl.run_scoped(optimizer_sums, *[pltpu.VMEM(source.shape, jnp.float32) for source in states])
    for tick in ticks:
        fold.tick(tick)
    fold.finish()
    for copy in (*far_copies, *group_copies):
        copy.wait_send()
    for batch in (group_sum, inner_sum):
        batch.finish()


def finish(
    n_dp, n_mp, prefix, projections, grad_out, mixed, row_sums, near, tokens, first,
    source_heads, rest, feed_grad, cross_wo, weights, norms, source_grad, states,
):
    side = round((n_dp // 2) ** 0.5)
    total, width = mixed.shape
    size, model = first.shape
    units = feed_grad.shape[1] // 4
    rows = model // n_dp
    low, wide = jnp.bfloat16, jnp.float32
    shape = jax.ShapeDtypeStruct
    dma = pltpu.SemaphoreType.DMA
    by_place = lambda values: values.reshape(side, side, 2, rows, values.shape[1])
    early = [by_place(values) for values in (cross_wo, weights, norms, source_grad)]
    columns = sum(values.shape[4] for values in early)
    bundle = 3 * width + norms.shape[1]
    devices = n_dp * n_mp
    chunk_rows = 64
    chunks = (total + source_heads[0].shape[0]) // (2 * chunk_rows)
    both, sums, *grads = pl.pallas_call(
        partial(finish_kernel, n_mp, side, units, width),
        out_shape=[shape((2, chunks, chunk_rows, model), low), shape((8, 128), wide)]
        + [shape(values.shape, wide) for values in states[:5]],
        in_specs=[pl.BlockSpec(memory_space=pltpu.SMEM)]
        + [IN_VMEM] * 11
        + [ANYWHERE, IN_VMEM]
        + [ANYWHERE] * (4 + len(states)),
        out_specs=[ANYWHERE] + [IN_VMEM] * 6,
        scratch_shapes=[
            pltpu.VMEM((model, 2 * width), low),
            dma,
            *[pltpu.VMEM((total, width), low)] * 3,
            pltpu.VMEM((total, width), wide),
            pltpu.VMEM((8, total), wide),
            dma((len(states),)),
            pltpu.VMEM((side, side, 2, rows, 3 * width), low),
            pltpu.VMEM((2, rows, columns), low),
            pltpu.VMEM((rows, 2 * units), low),
            pltpu.VMEM((n_mp, rows, bundle), low),
            pltpu.VMEM((n_mp - 1, rows, bundle), low),
            dma((2,)), dma((2,)), dma((n_mp - 1,)), dma((n_mp - 1,)),
            pltpu.VMEM((8, 128), wide),
            pltpu.VMEM((devices, 8, 128), wide),
            dma((devices - 1,)), dma((devices - 1,)),
            *Fold.scratch(chunks, chunk_rows, model),
            *Reduce.scratch(side, rows, columns, 4),
            *Reduce.scratch(side, rows, 3 * width, 1),
        ],
        compiler_params=pltpu.CompilerParams(
            collective_id=5, has_side_effects=True, vmem_limit_bytes=VMEM_LIMIT
        ),
        cost_estimate=pl.CostEstimate(flops=10**9, bytes_accessed=1 << 20, transcendentals=0),
        name="finish",
    )(
        prefix, *projections, grad_out, mixed, row_sums, near, tokens, first, *source_heads,
        rest, feed_grad, *early, *states,
    )
    return both, sums, grads


def on_device(
    inputs,
    encoder,
    prefix,
    cotangent,
    inner_weights,
    inner_first,
    inner_second,
    outer_weights,
    outer_first,
    outer_second,
    expand_weights,
    expand_first,
    expand_second,
    shrink_weights,
    shrink_first,
    shrink_second,
    norm_params,
    norm_first,
    norm_second,
):
    n_dp, n_mp = lax.axis_size("dp"), lax.axis_size("mp")
    seq_count, seq_len, model = inputs.shape
    tokens = inputs.reshape(seq_len, model)
    states = encoder.reshape(-1, model)
    rows, width = inner_weights.shape[2:]
    units = expand_weights.shape[1]

    norm_t = jnp.pad(bf16(norm_params).reshape(6, rows).T, ((0, 0), (0, 122)))
    near, bundle, later_block, feed_block, self_q, self_k, self_v, self_mixed, self_sums = front(
        n_dp, n_mp, prefix, inner_weights, bf16(jnp.swapaxes(outer_weights, 1, 2)), norm_t,
        expand_weights, bf16(shrink_weights.T), tokens,
    )
    by_rows = lambda values: values.reshape(model, values.shape[-1])
    near, bundle = by_rows(near), by_rows(bundle)
    hidden_one, normed_one, inverse_one, self_slots, norms, cross_query, home, rest = self_to_cross(
        n_dp, n_mp, self_mixed, bundle, tokens, feed_block, later_block
    )
    rest = by_rows(rest)
    cross_k, cross_v, cross_mixed, cross_sums, home = cross_forward(
        n_mp, cross_query, states, rest, home
    )
    out_rows, grad_second, cross_dmix, shrink_grad, expand_grad, cross_wo_grad, norm_rows = feed(
        n_mp, cross_mixed, rest, home, hidden_one, cotangent.reshape(seq_len, model), norms,
    )
    cross_dq, cross_dk, cross_dv, layer_low, source_grad, *halves = cross_backward(
        n_dp, n_mp, cross_query, cross_k, cross_v, cross_dmix, cross_mixed, cross_sums, prefix, out_rows,
        states, shrink_grad, expand_grad,
    )
    grad_first, self_dmix, weight_grad, norm_grad, feed_grad = cross_to_self(
        n_dp, n_mp, cross_dq, bundle, grad_second, hidden_one, normed_one, inverse_one,
        self_slots, norms, norm_rows, halves,
    )
    flat = lambda values: values.reshape(6, rows)
    weights = [inner_weights, outer_weights, expand_weights, shrink_weights, flat(norm_params)]
    firsts = [inner_first, outer_first, expand_first, shrink_first, flat(norm_first)]
    seconds = [inner_second, outer_second, expand_second, shrink_second, flat(norm_second)]
    both, sums, grads = finish(
        n_dp, n_mp, prefix, (self_q, self_k, self_v), self_dmix, self_mixed, self_sums, near, tokens,
        grad_first, (cross_dk, cross_dv), rest,
        feed_grad, cross_wo_grad, weight_grad, norm_grad, source_grad,
        weights + firsts + seconds,
    )
    encoder_grad, input_grad, layer_out, table, *results = update(
        both, layer_low, states.shape[0], sums, grads, weights, firsts, seconds
    )
    for index in (4, 9, 14):
        results[index] = results[index].reshape(2, 3, rows)
    return (
        layer_out.reshape(seq_count, seq_len, model),
        input_grad.reshape(seq_count, seq_len, model),
        encoder_grad.reshape(seq_count, -1, model),
        *results,
        table,
    )


def solution(mesh):
    placed = (
        P("dp", None, None),
        P("dp", None, None),
        P("dp"),
        P("dp", None, None),
        P(None, None, "dp", "mp"),
        P(None, None, "dp", "mp"),
        P(None, None, "dp", "mp"),
        P(None, "mp", "dp"),
        P(None, "mp", "dp"),
        P(None, "mp", "dp"),
        P("dp", "mp"),
        P("dp", "mp"),
        P("dp", "mp"),
        P("mp", "dp"),
        P("mp", "dp"),
        P("mp", "dp"),
        P(None, None, "dp"),
        P(None, None, "dp"),
        P(None, None, "dp"),
    )
    return jax.shard_map(
        on_device,
        mesh=mesh,
        in_specs=placed,
        out_specs=(
            P("dp", None, None),
            P("dp", None, None),
            P("dp", None, None),
            P(None, None, "dp", "mp"),
            P(None, "mp", "dp"),
            P("dp", "mp"),
            P("mp", "dp"),
            P(None, None, "dp"),
            P(None, None, "dp", "mp"),
            P(None, "mp", "dp"),
            P("dp", "mp"),
            P("mp", "dp"),
            P(None, None, "dp"),
            P(None, None, "dp", "mp"),
            P(None, "mp", "dp"),
            P("dp", "mp"),
            P("mp", "dp"),
            P(None, None, "dp"),
            P(),
        ),
        check_vma=False,
    )
```

```python
from functools import partial

import jax
import jax.numpy as jnp
from jax import lax
from jax.experimental import pallas as pl
from jax.experimental.pallas import tpu as pltpu
from jax.sharding import PartitionSpec as P

D = 1024
HEAD = 64
FF = 4096
STEP = 5

first_decay = 0.5
second_decay = 0.6
learn_rate = 0.5
weight_decay = 0.01
epsilon = 1e-06
norm_eps = 1e-05
mask_fill = -1000000000.0

MESH = pl.DeviceIdType.MESH
ANYWHERE = pl.BlockSpec(memory_space=pl.ANY)
IN_VMEM = pl.BlockSpec(memory_space=pltpu.VMEM)
NN = (((1,), (0,)), ((), ()))
NT = (((1,), (1,)), ((), ()))
TN = (((0,), (0,)), ((), ()))
VMEM_LIMIT = 60 << 20


def dot(left, right, dims=NN):
    return lax.dot_general(left, right, dims, preferred_element_type=jnp.float32)


def bf16(values):
    return values.astype(jnp.bfloat16)


def f32(values):
    return values.astype(jnp.float32)


def layer_norm(values, gain_row, bias_row):
    center = values - jnp.mean(values, axis=-1, keepdims=True)
    spread = jnp.mean(center * center, axis=-1, keepdims=True)
    inverse = lax.rsqrt(spread + norm_eps)
    normed = center * inverse
    return (normed * gain_row + bias_row, normed, inverse)


def norm_back(upstream, normed, inverse, gain_row):
    scaled = upstream * gain_row
    inner = (
        scaled
        - jnp.mean(scaled, axis=-1, keepdims=True)
        - normed * jnp.mean(scaled * normed, axis=-1, keepdims=True)
    )
    return (
        inner * inverse,
        jnp.sum(upstream * normed, axis=0, keepdims=True),
        jnp.sum(upstream, axis=0, keepdims=True),
    )


class Place:
    def __init__(self, n_mp, side):
        self.n, self.side = n_mp, side
        self.z = lax.axis_index("mp")
        dp = lax.axis_index("dp")
        self.core = lax.rem(dp, 2)
        self.x = lax.rem(dp // 2, side)
        self.y = dp // (2 * side)

    def at(self, y, x, core):
        return {"dp": (y * self.side + x) * 2 + core}

    def x_peer(self, distance):
        other = lax.rem(self.x + distance, self.side)
        return other, self.at(self.y, other, self.core)

    def y_peer(self, distance):
        other = lax.rem(self.y + distance, self.side)
        return other, self.at(other, self.x, self.core)

    def sibling(self):
        return self.at(self.y, self.x, 1 - self.core)

    def line(self):
        return [{"mp": lax.rem(self.z + distance, self.n)} for distance in range(1, self.n)]

    def plane(self):
        steps = range(1, self.side)
        return (
            [self.x_peer(step)[1] for step in steps]
            + [self.y_peer(step)[1] for step in steps]
            + [self.sibling()]
        )


def greet(others):
    barrier = pltpu.get_barrier_semaphore()
    for other in others:
        pl.semaphore_signal(barrier, inc=1, device_id=other, device_id_type=MESH)
    pl.semaphore_wait(barrier, len(others))


def push(source, target, send_sem, recv_sem, to):
    copy = pltpu.make_async_remote_copy(
        source, target, send_sem, recv_sem, device_id=to, device_id_type=MESH
    )
    copy.start()
    return copy


def rows_at(index, size):
    return pl.ds(pl.multiple_of(index * size, size), size)


def tokens_to_heads(n, make, blocks, target, send_sems, recv_sems, local_sem):
    me = lax.axis_index("mp")
    size = blocks.shape[1]
    copies = []
    for distance in (*range(1, n), 0):
        to = lax.rem(me + distance, n)
        blocks[to] = bf16(make(to))
        place = target.at[rows_at(me, size)]
        if distance:
            copies.append(
                push(
                    blocks.at[to], place,
                    send_sems.at[distance - 1], recv_sems.at[distance - 1], {"mp": to},
                )
            )
        else:
            copy = pltpu.make_async_copy(blocks.at[to], place, local_sem)
            copy.start()
            copies.append(copy)
    return copies


def load_groups(n, bundle, stride, first, width, target, sems):
    return [
        pltpu.make_async_copy(
            bundle.at[:, pl.ds(group * stride + first, width)], target.at[group], sems.at[group]
        )
        for group in range(n)
    ]


class Give:
    def __init__(self, place, out, sems):
        self.place, self.n, self.me, self.out = place, place.n, place.z, out
        self.sems = {"right": sems[0:2], "left": sems[2:4]}

    @staticmethod
    def sems(n):
        return [pltpu.SemaphoreType.DMA((max(n - 1, 1),))] * 4

    def _copy(self, way, step):
        ahead = 1 if way == "right" else -1
        chunk = lax.rem(self.me - ahead * step + self.n, self.n)
        return pltpu.make_async_remote_copy(
            self.out.at[chunk], self.out.at[chunk],
            self.sems[way][0].at[step], self.sems[way][1].at[step],
            device_id={"mp": lax.rem(self.me + ahead + self.n, self.n)}, device_id_type=MESH,
        )

    def _spots(self):
        return (("right", self.me), ("left", self.n - 1 - self.me))

    def step(self, step):
        for way, spot in self._spots():

            @pl.when((spot >= step) & (spot < self.n - 1))
            def _():
                if step > 0:
                    self._copy(way, step - 1).wait_recv()
                self._copy(way, step).start()

    def finish(self):
        for way, spot in self._spots():

            @pl.when(spot == self.n - 1)
            def _():
                for step in range(self.n - 1):
                    self._copy(way, step).wait_recv()

            for step in range(self.n - 1):

                @pl.when((spot >= step) & (spot < self.n - 1))
                def _():
                    self._copy(way, step).wait_send()


class Spread:
    def __init__(self, place, home, send_sems, recv_sems):
        self.place, self.home, self.send, self.recv = place, home, send_sems, recv_sems
        self.half = home.shape[3] // 2
        self.copies = {"first": [], "second": [], "core": []}
        self.index = 0

    def _push(self, stage, block, to):
        spot = self.index
        self.index += 1
        self.copies[stage].append(push(block, block, self.send.at[spot], self.recv.at[spot], to))

    def first(self):
        p, half = self.place, self.half
        for step in range(1, p.side):
            own = self.home.at[p.y, p.x, p.core]
            self._push("first", own.at[pl.ds(0, half)], p.x_peer(step)[1])
            self._push("first", own.at[pl.ds(half, half)], p.y_peer(step)[1])

    def second(self):
        p, half = self.place, self.half
        for copy in self.copies["first"]:
            copy.wait_recv()
        for step in range(1, p.side):
            self._push(
                "second", self.home.at[p.y, :, p.core, pl.ds(0, half)], p.y_peer(step)[1]
            )
            self._push(
                "second", self.home.at[:, p.x, p.core, pl.ds(half, half)], p.x_peer(step)[1]
            )

    def core(self):
        for copy in self.copies["second"]:
            copy.wait_recv()
        self._push("core", self.home.at[:, :, self.place.core], self.place.sibling())

    def finish(self):
        for copy in self.copies["core"] or self.copies["second"] or self.copies["first"]:
            copy.wait_recv()
        for stage in self.copies.values():
            for copy in stage:
                copy.wait_send()

    @staticmethod
    def sems(side):
        return pltpu.SemaphoreType.DMA((4 * (side - 1) + 1,))


class Reduce:
    def __init__(self, place, sources, scratch):
        self.place, self.sources = place, sources
        self.keep, self.first_a, self.first_b, *rest = scratch
        *rest, self.local, self.send, self.recv = rest
        if rest:
            self.second_a, self.second_b = rest
        self.half = self.keep.shape[2] // 2
        self.copies = {"core": [], "first": [], "second": []}
        self.index = 0

    @staticmethod
    def scratch(side, rows, columns, sources, second=True):
        low, dma = jnp.bfloat16, pltpu.SemaphoreType.DMA
        block = pltpu.VMEM((side, side, rows, columns), low)
        first = pltpu.VMEM((side - 1, side, rows // 2, columns), low)
        rest = pltpu.VMEM((side - 1, rows // 2, columns), low)
        count = sources + 4 * (side - 1)
        seconds = [rest, rest] if second else []
        return [
            block, first, first, *seconds, dma((2, sources)), dma((count,)), dma((count,)),
        ]

    def _push(self, stage, source, target, to, begin=True):
        copy = pltpu.make_async_remote_copy(
            source, target, self.send.at[self.index], self.recv.at[self.index],
            device_id=to, device_id_type=MESH,
        )
        self.index += 1
        self.copies[stage].append(copy)
        if begin:
            copy.start()

    def core_start(self, begin=True):
        p, column = self.place, 0
        self.index, self.copies["core"] = 0, []
        for source in self.sources:
            cols = pl.ds(column, source.shape[4])
            column += source.shape[4]
            self._push(
                "core", source.at[:, :, 1 - p.core], self.keep.at[:, :, :, cols], p.sibling(), begin
            )

    def _load(self, stage, index):
        y, x = index // self.place.side, index % self.place.side
        column, loads = 0, []
        for spot, source in enumerate(self.sources):
            cols = pl.ds(column, source.shape[4])
            column += source.shape[4]
            loads.append(
                pltpu.make_async_copy(
                    source.at[y, x, self.place.core], stage.at[index % 2, :, cols],
                    self.local.at[index % 2, spot],
                )
            )
        return loads

    def core_finish(self, stage):
        side, keep, columns = self.place.side, self.keep, self.keep.shape[3]
        for load in self._load(stage, 0):
            load.start()
        for copy in self.copies["core"]:
            copy.wait_recv()
        for index in range(side * side):
            if index + 1 < side * side:
                for load in self._load(stage, index + 1):
                    load.start()
            for load in self._load(stage, index):
                load.wait()
            y, x = index // side, index % side
            keep[y, x] = bf16(f32(keep[y, x]) + f32(stage[index % 2, :, :columns]))

    def first_start(self, begin=True):
        p, half = self.place, self.half
        self.index, self.copies["first"] = len(self.sources), []
        top, bottom = pl.ds(0, half), pl.ds(half, half)
        for step in range(1, p.side):
            other, to = p.x_peer(step)
            self._push("first", self.keep.at[:, other, top], self.first_a.at[step - 1], to, begin)
            other, to = p.y_peer(step)
            self._push("first", self.keep.at[other, :, bottom], self.first_b.at[step - 1], to, begin)

    def first_finish(self):
        p, half, keep = self.place, self.half, self.keep
        for copy in self.copies["first"]:
            copy.wait_recv()

        def add(index, carry):
            total = f32(keep[index, p.x, :half, :])
            for step in range(p.side - 1):
                total = total + f32(self.first_a[step, index])
            keep[index, p.x, :half, :] = bf16(total)
            total = f32(keep[p.y, index, half:, :])
            for step in range(p.side - 1):
                total = total + f32(self.first_b[step, index])
            keep[p.y, index, half:, :] = bf16(total)
            return carry

        lax.fori_loop(0, p.side, add, 0)

    def halves(self, out_a, out_b):
        p, half, keep = self.place, self.half, self.keep
        for index in range(p.side):
            out_a[index] = keep[index, p.x, :half, :]
            out_b[index] = keep[p.y, index, half:, :]

    def second_start(self):
        p, half = self.place, self.half
        top, bottom = pl.ds(0, half), pl.ds(half, half)
        for step in range(1, p.side):
            other, to = p.y_peer(step)
            self._push("second", self.keep.at[other, p.x, top], self.second_a.at[step - 1], to)
            other, to = p.x_peer(step)
            self._push("second", self.keep.at[p.y, other, bottom], self.second_b.at[step - 1], to)

    def second_wait(self):
        for copy in self.copies["second"]:
            copy.wait_recv()

    def total(self, cols):
        p, half = self.place, self.half
        top, bottom = f32(self.keep[p.y, p.x, :half, cols]), f32(self.keep[p.y, p.x, half:, cols])
        for step in range(p.side - 1):
            top = top + f32(self.second_a[step, :, cols])
            bottom = bottom + f32(self.second_b[step, :, cols])
        return jnp.concatenate([top, bottom], axis=0)

    def finish(self):
        for stage in self.copies.values():
            for copy in stage:
                copy.wait_send()


class Halves:
    def __init__(self, place, part_a, part_b, scratch):
        self.place, self.parts = place, (part_a, part_b)
        self.landed, (self.send, self.recv) = scratch[:2], scratch[2:]

    @staticmethod
    def scratch(side, half, columns):
        dma = pltpu.SemaphoreType.DMA((2 * (side - 1),))
        return [pltpu.VMEM((side - 1, half, columns), jnp.bfloat16)] * 2 + [dma, dma]

    def start(self):
        p = self.place
        self.copies = []
        for step in range(1, p.side):
            for index, (other, to) in enumerate((p.y_peer(step), p.x_peer(step))):
                spot = 2 * (step - 1) + index
                self.copies.append(
                    push(
                        self.parts[index].at[other], self.landed[index].at[step - 1],
                        self.send.at[spot], self.recv.at[spot], to,
                    )
                )

    def total(self):
        for copy in self.copies:
            copy.wait()
        sums = []
        for index, mine in enumerate((self.place.y, self.place.x)):
            total = f32(self.parts[index][mine])
            for step in range(self.place.side - 1):
                total = total + f32(self.landed[index][step])
            sums.append(total)
        return jnp.concatenate(sums, axis=0)


def forward_rows(masked, start, block, prefix_ref, q_ref, k_ref, v_ref, mixed_ref, sums_ref):
    width = q_ref.shape[1]
    keys = k_ref.shape[0]
    if masked:
        keys = max(keys // 2, start + block)
    lane = lax.broadcasted_iota(jnp.int32, (block, width), 1) // HEAD
    span = slice(start, start + block) if masked else rows_at(start, block)
    query = q_ref[span, :] * jnp.bfloat16(HEAD**-0.5)
    key_rows, value_rows = k_ref[:keys, :], v_ref[:keys, :]
    if masked:
        query_ids = start + lax.broadcasted_iota(jnp.int32, (block, keys), 0)
        key_ids = lax.broadcasted_iota(jnp.int32, (block, keys), 1)
        allowed = (key_ids <= query_ids) | (key_ids < prefix_ref[0])
    mixed = jnp.zeros((block, width), jnp.float32)
    slot = lax.broadcasted_iota(jnp.int32, (block, 128), 1)
    table = jnp.zeros((block, 128), jnp.float32)
    for head in range(width // HEAD):
        scores = dot(jnp.where(lane == head, query, jnp.bfloat16(0)), key_rows, NT)
        if masked:
            scores = jnp.where(allowed, scores, mask_fill)
        row_max = jnp.max(scores, axis=1, keepdims=True)
        powered = jnp.exp(scores - row_max)
        totals = jnp.sum(powered, axis=1, keepdims=True)
        part = dot(bf16(powered), value_rows) * (1.0 / totals)
        mixed = jnp.where(lane == head, part, mixed)
        table = jnp.where(slot == head, row_max + jnp.log(totals), table)
    mixed_ref[span, :] = bf16(mixed)
    sums_ref[:, span] = table.T[:8, :]


def backward_delta(do_ref, o_ref, delta):
    width = do_ref.shape[1]
    product = f32(do_ref[...]) * f32(o_ref[...])
    row = lax.broadcasted_iota(jnp.int32, (8, width), 0)
    col = lax.broadcasted_iota(jnp.int32, (8, width), 1) // HEAD
    pick = jnp.where(row == col, 1.0, 0.0).astype(jnp.float32)
    delta[...] = lax.dot_general(
        pick, product, NT, precision=lax.Precision.HIGHEST, preferred_element_type=jnp.float32
    )


def backward_block(
    masked, block, index, heads, prefix_ref, q_ref, k_ref, v_ref, do_ref, sums_ref, delta, acc, dk_ref, dv_ref
):
    total, width = q_ref.shape
    factor = HEAD**-0.5
    rows = slice(index * block, (index + 1) * block)
    first = index * block if masked and index * block >= total // 2 else 0
    count = total - first
    lane = lax.broadcasted_iota(jnp.int32, (block, width), 1) // HEAD
    query, grad_rows = q_ref[first:, :], do_ref[first:, :]
    scaled_keys = k_ref[rows, :] * jnp.bfloat16(factor)
    value_rows = v_ref[rows, :]
    if masked:
        query_ids = first + lax.broadcasted_iota(jnp.int32, (block, count), 1)
        key_ids = index * block + lax.broadcasted_iota(jnp.int32, (block, count), 0)
        allowed = (key_ids <= query_ids) | (key_ids < prefix_ref[0])
    key_grad = jnp.zeros((block, width), jnp.float32)
    value_grad = jnp.zeros((block, width), jnp.float32)
    query_grad = jnp.zeros((count, width), jnp.float32)
    for head in heads:
        own_keys = jnp.where(lane == head, scaled_keys, jnp.bfloat16(0))
        scores = dot(own_keys, query, NT)
        if masked:
            scores = jnp.where(allowed, scores, mask_fill)
        probs = jnp.exp(scores - sums_ref[head : head + 1, first:])
        prob_grad = dot(jnp.where(lane == head, value_rows, jnp.bfloat16(0)), grad_rows, NT)
        score_grad = bf16(probs * (prob_grad - delta[head : head + 1, first:]))
        value_grad = jnp.where(lane == head, dot(bf16(probs), grad_rows), value_grad)
        key_grad = jnp.where(lane == head, dot(score_grad, query), key_grad)
        query_grad = query_grad + dot(score_grad, own_keys, TN)
    acc[first:, :] += query_grad
    mine = (lane >= heads[0]) & (lane <= heads[-1])
    key_grad, value_grad = bf16(key_grad * factor), bf16(value_grad)
    if heads[0] > 0:
        key_grad = jnp.where(mine, key_grad, dk_ref[rows, :])
        value_grad = jnp.where(mine, value_grad, dv_ref[rows, :])
    dk_ref[rows, :] = key_grad
    dv_ref[rows, :] = value_grad


def cross_backward_kernel(
    n, side, q_ref, k_ref, v_ref, do_ref, o_ref, sums_ref, mine_ref, states_ref, shrink_ref, expand_ref,
    slots_ref, dk_ref, dv_ref, all_ref, source_ref, half_a_ref, half_b_ref,
    scaled_keys, key_acc, value_acc, delta, blocks, stage, own_sem, dq_send, dq_recv, *scratch,
):
    p = Place(n, side)
    give = Give(p, all_ref, scratch[:4])
    feed_sum = Reduce(p, [shrink_ref, expand_ref], scratch[4:])
    width = q_ref.shape[1]
    size = blocks.shape[1]
    heads = range(width // HEAD)
    factor = HEAD**-0.5
    own = pltpu.make_async_copy(mine_ref, all_ref.at[p.z], own_sem)
    own.start()
    greet(p.line() + p.plane())
    feed_sum.core_start()
    own.wait()
    give.step(0)
    backward_delta(do_ref, o_ref, delta)
    scaled_keys[...] = k_ref[...] * jnp.bfloat16(factor)
    key_acc[...] = jnp.zeros_like(key_acc)
    value_acc[...] = jnp.zeros_like(value_acc)
    lane = lax.broadcasted_iota(jnp.int32, (size, width), 1) // HEAD
    chunk = 512

    def dq_copy(distance):
        to = lax.rem(p.z + distance, n)
        return pltpu.make_async_remote_copy(
            blocks.at[to], slots_ref.at[p.z], dq_send.at[distance - 1], dq_recv.at[distance - 1],
            device_id={"mp": to}, device_id_type=MESH,
        )

    def one_block(step, carry):
        block = lax.rem(p.z + 1 + step, n)
        span = rows_at(block, size)
        query, grad_rows = q_ref[span, :], do_ref[span, :]
        stacked = lambda values: jnp.concatenate(
            [jnp.where(lane == head, values, jnp.bfloat16(0)) for head in heads], axis=0
        )
        across = lambda ref: jnp.concatenate([ref[head : head + 1, span] for head in heads], axis=1)
        own_query, own_grad = stacked(query), stacked(grad_rows)
        row_sums, row_delta = across(sums_ref), across(delta)
        all_grads = jnp.zeros((len(heads) * size, width), jnp.float32)
        for first in range(0, k_ref.shape[0], chunk):
            rows = slice(first, first + chunk)
            if first == chunk:

                @pl.when(step == 0)
                def _():
                    feed_sum.core_start(False)
                    feed_sum.core_finish(stage)
                    feed_sum.first_start()

            if first == 2 * chunk:

                @pl.when(step == 2)
                def _():
                    give.step(1)

            probs = jnp.exp(dot(scaled_keys[rows, :], own_query, NT) - row_sums)
            prob_grad = dot(v_ref[rows, :], own_grad, NT)
            score_grad = bf16(probs * (prob_grad - row_delta))
            value_acc[rows, :] += dot(bf16(probs), own_grad)
            key_acc[rows, :] += dot(score_grad, own_query)
            all_grads = all_grads + dot(score_grad, scaled_keys[rows, :], TN)
        query_grad = jnp.zeros((size, width), jnp.float32)
        for head in heads:
            query_grad = jnp.where(
                lane == head, all_grads[head * size : (head + 1) * size], query_grad
            )
        blocks[block] = bf16(query_grad)

        @pl.when(step < n - 1)
        def _():
            dq_copy(step + 1).start()

        return carry

    lax.fori_loop(0, n, one_block, 0)
    slots_ref[p.z] = blocks[p.z]
    dk_ref[...] = bf16(key_acc[...] * factor)
    dv_ref[...] = bf16(value_acc[...])
    source_ref[:, :width] = bf16(dot(states_ref[...], dk_ref[...], TN))
    source_ref[:, width:] = bf16(dot(states_ref[...], dv_ref[...], TN))
    for later in range(2, n - 1):
        give.step(later)
    feed_sum.core_start(False)
    feed_sum.first_start(False)
    feed_sum.first_finish()
    feed_sum.halves(half_a_ref, half_b_ref)
    feed_sum.finish()
    for distance in range(1, n):
        dq_copy(distance).wait()
    give.finish()


def cross_backward(n_dp, n, query, key_rows, value_rows, grad_out, mixed, sums, mine, states, shrink, expand):
    total, width = query.shape
    keys, model = states.shape
    side = round((n_dp // 2) ** 0.5)
    rows, columns = model // n_dp, shrink.shape[1] + expand.shape[1]
    half = (side, rows // 2, columns)
    by_place = lambda values: values.reshape(side, side, 2, rows, values.shape[1])
    low, wide = jnp.bfloat16, jnp.float32
    shape = jax.ShapeDtypeStruct
    dma = pltpu.SemaphoreType.DMA
    return pl.pallas_call(
        partial(cross_backward_kernel, n, side),
        out_shape=[
            shape((n, total // n, width), low),
            shape((keys, width), low),
            shape((keys, width), low),
            shape((n,) + mine.shape, low),
            shape((model, 2 * width), low),
            shape(half, low),
            shape(half, low),
        ],
        in_specs=[IN_VMEM] * 8 + [ANYWHERE] * 2,
        out_specs=[IN_VMEM] * 3 + [ANYWHERE] + [IN_VMEM] * 3,
        scratch_shapes=[
            pltpu.VMEM((keys, width), low),
            pltpu.VMEM((keys, width), wide),
            pltpu.VMEM((keys, width), wide),
            pltpu.VMEM((8, total), wide),
            pltpu.VMEM((n, total // n, width), low),
            pltpu.VMEM((2, rows, columns), low),
            dma, dma((n - 1,)), dma((n - 1,)),
            *Give.sems(n),
            *Reduce.scratch(side, rows, columns, 2, second=False),
        ],
        compiler_params=pltpu.CompilerParams(
            vmem_limit_bytes=VMEM_LIMIT, collective_id=6, has_side_effects=True
        ),
        cost_estimate=pl.CostEstimate(flops=40 * total * keys * width, bytes_accessed=1 << 20, transcendentals=0),
        name="cross_backward",
    )(
        query, key_rows, value_rows, grad_out, mixed, sums, mine, states, by_place(shrink), by_place(expand),
    )


def front_kernel(
    n, side, prefix_ref, inner_ref, outer_ref, norm_ref, expand_ref, shrink_ref, x_ref,
    near_ref, home_ref, feed_home_ref, q_ref, k_ref, v_ref, mixed_ref, sums_ref, slots_ref,
    block_near, block_line, block_rest, own_sems, near_send, near_recv, home_send, home_recv,
    line_send, line_recv, far_send, far_recv, mixed_send, mixed_recv,
    block_feed, feed_send, feed_recv, rest_send, rest_recv,
):
    p = Place(n, side)
    width = inner_ref.shape[3]
    units = expand_ref.shape[1]
    for index in range(3):
        block_near[:, index * width : (index + 1) * width] = bf16(inner_ref[0, index])
    block_line[:, :width] = bf16(inner_ref[1, 0])
    block_line[:, width : 2 * width] = outer_ref[0]
    for index in range(2):
        block_rest[:, index * width : (index + 1) * width] = bf16(inner_ref[1, index + 1])
    block_rest[:, 2 * width :] = norm_ref[...]
    norms = block_rest.shape[1] - 2 * width
    whole = n * width
    later = whole + norms
    out_cols = pl.ds(pl.multiple_of(p.z * width, width), width)
    query_cols = pl.ds(pl.multiple_of(later + p.z * width, 128), width)
    spot = home_ref.at[p.y, p.x, p.core]
    near_ref[p.y, p.x, p.core] = block_near[...]
    block_feed[:, :units] = bf16(expand_ref[...])
    block_feed[:, units:] = shrink_ref[...]
    feed_spot = feed_home_ref.at[p.y, p.x, p.core]
    own = [
        pltpu.make_async_copy(source, target, own_sems.at[index])
        for index, (source, target) in enumerate(
            (
                (block_line.at[:, pl.ds(width, width)], spot.at[:, out_cols]),
                (block_line.at[:, pl.ds(0, width)], spot.at[:, query_cols]),
                (block_rest.at[:, pl.ds(2 * width, norms)], spot.at[:, pl.ds(whole, norms)]),
                (block_rest.at[:, pl.ds(0, 2 * width)], spot.at[:, pl.ds(later + whole, 2 * width)]),
                (block_feed, feed_spot.at[:, pl.ds(0, 2 * units)]),
            )
        )
    ]
    for copy in own:
        copy.start()
    greet(p.line() + p.plane())
    near = Spread(p, near_ref, near_send, near_recv)
    first_rest = Spread(p, home_ref.at[:, :, :, :, pl.ds(0, later)], home_send, home_recv)
    rest = Spread(
        p, home_ref.at[:, :, :, :, pl.ds(later, whole + 2 * width)], rest_send, rest_recv
    )
    near.first()
    lines = [
        [
            push(
                block_line.at[:, pl.ds(first, width)], spot.at[:, cols],
                line_send.at[part * (n - 1) + index], line_recv.at[part * (n - 1) + index], other,
            )
            for index, other in enumerate(p.line())
        ]
        for part, (first, cols) in enumerate(((width, out_cols), (0, query_cols)))
    ]
    far = push(
        block_feed.at[:, pl.ds(0, units)], feed_spot.at[:, pl.ds(2 * units, units)], far_send, far_recv,
        {"mp": lax.rem(p.z + n // 2, n)},
    )
    for copy in own:
        copy.wait()
    near.second()
    feed_spread = Spread(
        p, feed_home_ref.at[:, :, :, :, pl.ds(0, 2 * units)], feed_send, feed_recv
    )
    for copy in lines[0]:
        copy.wait_recv()
    first_rest.first()
    near.core()
    for copy in lines[1]:
        copy.wait_recv()
    rest.first()
    near.finish()
    first_rest.second()
    model = x_ref.shape[1]
    weights = near_ref[...].reshape(model, 3 * width)
    for start in range(0, x_ref.shape[0], 256):
        rows = slice(start, start + 256)
        made = bf16(dot(x_ref[rows, :], weights))
        for index, target in enumerate((q_ref, k_ref, v_ref)):
            target[rows, :] = made[:, index * width : (index + 1) * width]
    rest.second()
    feed_spread.first()
    size = x_ref.shape[0] // n

    def mixed_copy(distance):
        to = lax.rem(p.z + distance, n)
        return pltpu.make_async_remote_copy(
            mixed_ref.at[rows_at(to, size)], slots_ref.at[p.z],
            mixed_send.at[distance - 1], mixed_recv.at[distance - 1],
            device_id={"mp": to}, device_id_type=MESH,
        )

    def attend(step, carry):
        block = lax.rem(p.z + 1 + step, n)
        for index in range(n):

            @pl.when(block == index)
            def _():
                forward_rows(
                    True, index * size, size, prefix_ref, q_ref, k_ref, v_ref, mixed_ref, sums_ref
                )

        @pl.when(step < n - 1)
        def _():
            mixed_copy(step + 1).start()

        return carry

    lax.fori_loop(0, n, attend, 0)
    slots_ref[p.z] = mixed_ref[rows_at(p.z, size), :]
    first_rest.core()
    rest.core()
    first_rest.finish()
    rest.finish()
    for distance in range(1, n):
        mixed_copy(distance).wait()
    for copy in (*lines[0], *lines[1]):
        copy.wait_send()
    far.wait()
    feed_spread.finish()


def front(n_dp, n_mp, prefix, inner, outer_t, norm_t, expand, shrink_t, tokens):
    rows, width = inner.shape[2:]
    total = tokens.shape[0]
    side = round((n_dp // 2) ** 0.5)
    line = 2 * width
    columns = n_mp * line + 2 * width + norm_t.shape[1]
    units = expand.shape[1]
    low = jnp.bfloat16
    dma = pltpu.SemaphoreType.DMA
    shape = jax.ShapeDtypeStruct
    return pl.pallas_call(
        partial(front_kernel, n_mp, side),
        out_shape=[
            shape((side, side, 2, rows, 3 * width), low),
            shape((side, side, 2, rows, columns), low),
            shape((side, side, 2, rows, 4 * units), low),
            *[shape((total, width), low)] * 4,
            shape((8, total), jnp.float32),
            shape((n_mp, total // n_mp, width), low),
        ],
        in_specs=[pl.BlockSpec(memory_space=pltpu.SMEM)] + [IN_VMEM] * 6,
        out_specs=[IN_VMEM, ANYWHERE, ANYWHERE] + [IN_VMEM] * 6,
        scratch_shapes=[
            pltpu.VMEM((rows, 3 * width), low),
            pltpu.VMEM((rows, line), low),
            pltpu.VMEM((rows, 2 * width + norm_t.shape[1]), low),
            dma((5,)),
            Spread.sems(side), Spread.sems(side), Spread.sems(side), Spread.sems(side),
            dma((2 * n_mp - 2,)), dma((2 * n_mp - 2,)), dma, dma,
            dma((n_mp - 1,)), dma((n_mp - 1,)),
            pltpu.VMEM((rows, 2 * units), low),
            Spread.sems(side), Spread.sems(side), Spread.sems(side), Spread.sems(side),
        ],
        compiler_params=pltpu.CompilerParams(
            collective_id=0, has_side_effects=True, vmem_limit_bytes=VMEM_LIMIT
        ),
        cost_estimate=pl.CostEstimate(flops=40 * 10**9, bytes_accessed=1 << 20, transcendentals=0),
        name="front",
    )(prefix, inner, outer_t, norm_t, expand, shrink_t, tokens)


def middle_kernel(
    n, side, slots_ref, bundle_ref, x_ref, home_in_ref, shrink_ref, outer_ref, states_ref,
    hidden_ref, normed_ref, inverse_ref, norm_ref, q_ref, k_ref, v_ref, mixed_ref, sums_ref, cross_slots_ref,
    home_ref, rest_ref,
    wo, wq, norm_columns, source, x_rows, blocks,
    wo_sems, wq_sems, load_sems, q_send, q_recv, mixed_send, mixed_recv, far_send, far_recv,
    feed_send, feed_recv, later_send, later_recv, line_send, line_recv,
    expand_send, expand_recv, shrink_send, shrink_recv,
):
    p = Place(n, side)
    me = p.z
    size = x_rows.shape[0]
    width = slots_ref.shape[2]
    whole = n * width
    norms = norm_columns.shape[1]
    later = whole + norms
    loads = [
        pltpu.make_async_copy(x_ref.at[rows_at(me, size)], x_rows, load_sems.at[0]),
        pltpu.make_async_copy(bundle_ref.at[:, pl.ds(whole, norms)], norm_columns, load_sems.at[1]),
        pltpu.make_async_copy(
            bundle_ref.at[:, pl.ds(later + whole, 2 * width)], source, load_sems.at[2]
        ),
        *load_groups(n, bundle_ref, width, 0, width, wo, wo_sems),
        *load_groups(n, bundle_ref, width, later, width, wq, wq_sems),
    ]
    for load in loads:
        load.start()
    units = home_ref.shape[4] // 4
    spot = rest_ref.at[p.y, p.x, p.core, :, pl.ds(pl.multiple_of(width * me, width), width)]
    greet(p.line() + p.plane())
    store = pltpu.make_async_copy(outer_ref.at[1], spot, load_sems.at[3])
    store.start()
    line = [
        push(outer_ref.at[1], spot, line_send.at[index], line_recv.at[index], other)
        for index, other in enumerate(p.line())
    ]
    part = lambda first, count: home_ref.at[:, :, :, :, pl.ds(first * units, count * units)]
    rest = Spread(p, rest_ref, later_send, later_recv)
    own_units = Spread(p, part(0, 2), feed_send, feed_recv)
    far_expand = Spread(p, part(2, 1), expand_send, expand_recv)
    far_shrink = Spread(p, part(3, 1), shrink_send, shrink_recv)
    own_units.second()
    far_expand.first()
    store.wait()
    for load in loads:
        load.wait()
    norms = f32(norm_columns[...]).T[:8, :]
    norm_ref[...] = norms
    branch = f32(x_rows[...])
    for group in range(n):
        branch = branch + dot(slots_ref[group], wo[group], NT)
    hidden, normed, inverse = layer_norm(branch, norms[0:1, :], norms[3:4, :])
    hidden_ref[...] = hidden
    normed_ref[...] = normed
    inverse_ref[...] = jnp.broadcast_to(inverse, inverse_ref.shape)
    low = bf16(hidden)

    def q_copy(distance):
        to = lax.rem(me + distance, n)
        return pltpu.make_async_remote_copy(
            blocks.at[to], q_ref.at[rows_at(me, size)], q_send.at[distance - 1], q_recv.at[distance - 1],
            device_id={"mp": to}, device_id_type=MESH,
        )

    for distance in range(1, n):
        to = lax.rem(me + distance, n)
        blocks[to] = bf16(dot(low, wq[to]))
        q_copy(distance).start()
    far = push(
        shrink_ref, home_ref.at[p.y, p.x, p.core, :, pl.ds(3 * units, units)], far_send, far_recv,
        {"mp": lax.rem(me + n // 2, n)},
    )
    q_ref[rows_at(me, size), :] = bf16(dot(low, wq[me]))
    for copy in line:
        copy.wait_recv()
    rest.first()
    for start in range(0, states_ref.shape[0], 512):
        rows = slice(start, start + 512)
        made = bf16(dot(states_ref[rows, :], source[...]))
        k_ref[rows, :] = made[:, :width]
        v_ref[rows, :] = made[:, width:]
    far_expand.second()

    def mixed_copy(distance):
        to = lax.rem(me + distance, n)
        return pltpu.make_async_remote_copy(
            mixed_ref.at[rows_at(to, size)], cross_slots_ref.at[me],
            mixed_send.at[distance - 1], mixed_recv.at[distance - 1],
            device_id={"mp": to}, device_id_type=MESH,
        )

    for step in range(n):
        if step > 0:
            q_copy(n - step).wait_recv()
        forward_rows(
            False, lax.rem(me + step, n), size, None, q_ref, k_ref, v_ref, mixed_ref, sums_ref
        )
        if step > 0:
            mixed_copy(step).start()
        if step == 0:
            rest.second()
    cross_slots_ref[me] = mixed_ref[rows_at(me, size), :]
    far.wait_recv()
    far_shrink.first()
    rest.core()
    far_shrink.second()
    for distance in range(1, n):
        q_copy(distance).wait_send()
        mixed_copy(distance).wait()
    for copy in line:
        copy.wait_send()
    far.wait_send()
    for spread in (rest, own_units, far_expand, far_shrink):
        spread.finish()


def middle(n_dp, n, slots, bundle, tokens, home, shrink_t, outer_t, states):
    side = round((n_dp // 2) ** 0.5)
    _, size, width = slots.shape
    total, model = tokens.shape
    keys = states.shape[0]
    shape = jax.ShapeDtypeStruct
    dma = pltpu.SemaphoreType.DMA
    low, wide = jnp.bfloat16, jnp.float32
    return pl.pallas_call(
        partial(middle_kernel, n, side),
        out_shape=[
            shape((size, model), wide),
            shape((size, model), wide),
            shape((size, 128), wide),
            shape((8, model), wide),
            shape((total, width), low),
            shape((keys, width), low),
            shape((keys, width), low),
            shape((total, width), low),
            shape((8, total), wide),
            shape((n, size, width), low),
            shape(home.shape, low),
            shape((side, side, 2, outer_t.shape[1], n * width), low),
        ],
        in_specs=[IN_VMEM] + [ANYWHERE] * 3 + [IN_VMEM] * 3,
        out_specs=[IN_VMEM] * 10 + [ANYWHERE] * 2,
        input_output_aliases={3: 10},
        scratch_shapes=[
            pltpu.VMEM((n, model, width), low),
            pltpu.VMEM((n, model, width), low),
            pltpu.VMEM((model, bundle.shape[1] - 2 * n * width - 2 * width), low),
            pltpu.VMEM((model, 2 * width), low),
            pltpu.VMEM((size, model), low),
            pltpu.VMEM((n, size, width), low),
            dma((n,)), dma((n,)), dma((4,)),
            dma((n - 1,)), dma((n - 1,)), dma((n - 1,)), dma((n - 1,)), dma, dma,
            Spread.sems(side), Spread.sems(side), Spread.sems(side), Spread.sems(side),
            dma((n - 1,)), dma((n - 1,)),
            Spread.sems(side), Spread.sems(side), Spread.sems(side), Spread.sems(side),
        ],
        compiler_params=pltpu.CompilerParams(
            collective_id=1, has_side_effects=True, vmem_limit_bytes=VMEM_LIMIT
        ),
        cost_estimate=pl.CostEstimate(flops=10**10, bytes_accessed=1 << 20, transcendentals=0),
        name="middle",
    )(slots, bundle, tokens, home, shrink_t, outer_t, states)


def feed_kernel(
    n, side, slots, rest_ref, home_ref, hidden_one_ref, cot_ref, norm_ref,
    out_ref, second_ref, dmix_ref, shrink_grad_ref, expand_grad_ref, wo_grad_ref, norm_grad_ref,
    wo, weights, hidden_two, normed_two, low_two, low_three, act, slope,
    y_own, y_send, y_recv, d_send, d_recv, cot, blocks,
    load_sem, wo_sems, own_sem, send_out, recv_out, pair_send, pair_recv,
    home_sems, home_send, home_recv,
):
    p = Place(n, side)
    me = p.z
    mate = {"mp": me + 1 - 2 * lax.rem(me, 2)}
    size = cot.shape[0]
    half = size // 2
    width = slots.shape[2]
    hidden_units = act.shape[1]
    chunk = min(512, hidden_units)
    loads = [
        *load_groups(n, rest_ref, width, 0, width, wo, wo_sems),
        pltpu.make_async_copy(cot_ref.at[rows_at(me, size)], cot, load_sem),
    ]
    rows = home_ref.shape[3]
    places = [(y, x) for y in range(side) for x in range(side)]
    spots = [rows_at((y * side + x) * 2 + p.core, rows) for y, x in places]
    homes = [
        pltpu.make_async_copy(home_ref.at[y, x, p.core], weights.at[spot], home_sems.at[index])
        for index, ((y, x), spot) in enumerate(zip(places, spots))
    ]
    for load in loads + homes:
        load.start()
    greet(p.line() + [p.sibling()])
    home_copies = [
        push(
            home_ref.at[y, x, p.core], weights.at[spot],
            home_send.at[index], home_recv.at[index], p.sibling(),
        )
        for index, ((y, x), spot) in enumerate(zip(places, spots))
    ]
    for load in loads[:n]:
        load.wait()
    branch = hidden_one_ref[...]
    for group in range(n):
        branch = branch + dot(slots[group], wo[group], NT)
    hidden, normed, inverse_two = layer_norm(branch, norm_ref[1:2, :], norm_ref[4:5, :])
    hidden_two[...] = hidden
    normed_two[...] = normed
    low_two[:size, :] = bf16(hidden)
    pair = []

    def to_mate(source, target):
        index = len(pair)
        pair.append(push(source, target, pair_send.at[index], pair_recv.at[index], mate))
        return pair[-1]

    hidden_copies = [
        to_mate(low_two.at[pl.ds(start, half)], low_two.at[pl.ds(size + start, half)])
        for start in (0, half)
    ]
    for copy in homes:
        copy.wait()
    for copy in home_copies:
        copy.wait_recv()
    units = hidden_units // 2

    def expand_cols(first, count):
        first += first // units * units
        return slice(first, first + count)

    def shrink_cols(first, count):
        first += (first // units + 1) * units
        return slice(first, first + count)

    def shrink_sum(rows):
        return sum(
            dot(act[rows, first : first + units], weights[:, shrink_cols(first, units)], NT)
            for first in (0, units)
        )

    def expand_sum(rows):
        return sum(
            dot(slope[rows, first : first + units], weights[:, expand_cols(first, units)], NT)
            for first in (0, units)
        )

    def expand_rows(start, count):
        rows = low_two[start : start + count, :]
        for first in range(0, hidden_units, chunk):
            pre = dot(rows, weights[:, expand_cols(first, chunk)])
            cdf = 0.5 + 0.5 * lax.erf(pre * 0.7071067811865476)
            act[start : start + count, first : first + chunk] = bf16(pre * cdf)
            slope[start : start + count, first : first + chunk] = bf16(
                cdf + pre * jnp.exp(-0.5 * pre * pre) * 0.3989422804014327
            )

    expand_rows(0, size)
    y_copies = []
    for index, start in enumerate((0, half)):
        hidden_copies[index].wait_recv()
        expand_rows(size + start, half)
        y_send[start : start + half, :] = bf16(shrink_sum(slice(size + start, size + start + half)))
        y_copies.append(to_mate(y_send.at[pl.ds(start, half)], y_recv.at[pl.ds(start, half)]))
    y_own[...] = shrink_sum(slice(0, size))
    for copy in y_copies:
        copy.wait_recv()
    output, normed, inverse = layer_norm(
        hidden_two[...] + y_own[...] + f32(y_recv[...]), norm_ref[2:3, :], norm_ref[5:6, :]
    )
    out_ref[...] = bf16(output)
    loads[n].wait()
    third, gain_three, bias_three = norm_back(f32(cot[...]), normed, inverse, norm_ref[2:3, :])
    low_three[:size, :] = bf16(third)
    grad_copies = [
        to_mate(low_three.at[pl.ds(start, half)], low_three.at[pl.ds(size + start, half)])
        for start in (0, half)
    ]

    def back_rows(start, count):
        rows = low_three[start : start + count, :]
        for first in range(0, hidden_units, chunk):
            grad = dot(rows, weights[:, shrink_cols(first, chunk)])
            spot = (slice(start, start + count), slice(first, first + chunk))
            slope[spot] = bf16(grad * f32(slope[spot]))

    back_rows(0, size)
    d_copies = []
    for index, start in enumerate((0, half)):
        grad_copies[index].wait_recv()
        back_rows(size + start, half)
        d_send[start : start + half, :] = bf16(expand_sum(slice(size + start, size + start + half)))
        d_copies.append(to_mate(d_send.at[pl.ds(start, half)], d_recv.at[pl.ds(start, half)]))
    y_own[...] = third + expand_sum(slice(0, size))
    for copy in d_copies:
        copy.wait_recv()
    second, gain_two, bias_two = norm_back(
        y_own[...] + f32(d_recv[...]), normed_two[...], inverse_two, norm_ref[1:2, :]
    )
    second_ref[...] = second
    low = bf16(second)
    sent = tokens_to_heads(
        n, lambda group: dot(low, wo[group]), blocks, dmix_ref, send_out, recv_out, own_sem
    )
    norm_grad_ref[...] = jnp.concatenate(
        [gain_two, gain_three, bias_two, bias_three, jnp.zeros((4, norm_grad_ref.shape[1]))], axis=0
    )
    for first in range(0, low_two.shape[1], 256):
        rows = slice(first, first + 256)
        shrink_grad_ref[rows, :] = bf16(dot(low_three[:, rows], act[...], TN))
        expand_grad_ref[rows, :] = bf16(dot(low_two[:, rows], slope[...], TN))
    for group in range(n):
        wo_grad_ref[:, group * width : (group + 1) * width] = bf16(dot(low, slots[group], TN))
    for copy in sent:
        copy.wait()
    for copy in pair + home_copies:
        copy.wait_send()


def feed(n, slots, rest, home, hidden_one, cotangent, norms):
    width = slots.shape[2]
    total = cotangent.shape[0]
    side, model, units = home.shape[0], hidden_one.shape[1], home.shape[4] // 2
    size = total // n
    shape = jax.ShapeDtypeStruct
    dma = pltpu.SemaphoreType.DMA
    low, wide = jnp.bfloat16, jnp.float32
    return pl.pallas_call(
        partial(feed_kernel, n, side),
        out_shape=[
            shape((size, model), low),
            shape((size, model), wide),
            shape((total, width), low),
            shape((model, units), low),
            shape((model, units), low),
            shape((model, model), low),
            shape((8, model), wide),
        ],
        in_specs=[IN_VMEM, ANYWHERE, ANYWHERE, IN_VMEM, ANYWHERE, IN_VMEM],
        out_specs=[IN_VMEM] * 2 + [ANYWHERE] + [IN_VMEM] * 4,
        scratch_shapes=[
            pltpu.VMEM((n, model, width), low),
            pltpu.VMEM((model, 2 * units), low),
            pltpu.VMEM((size, model), wide),
            pltpu.VMEM((size, model), wide),
            pltpu.VMEM((2 * size, model), low),
            pltpu.VMEM((2 * size, model), low),
            pltpu.VMEM((2 * size, units), low),
            pltpu.VMEM((2 * size, units), low),
            pltpu.VMEM((size, model), wide),
            pltpu.VMEM((size, model), low),
            pltpu.VMEM((size, model), low),
            pltpu.VMEM((size, model), low),
            pltpu.VMEM((size, model), low),
            pltpu.VMEM((size, model), low),
            pltpu.VMEM((n, size, width), low),
            dma, dma((n,)), dma,
            dma((n - 1,)), dma((n - 1,)),
            dma((8,)), dma((8,)),
            dma((side * side,)), dma((side * side,)), dma((side * side,)),
        ],
        compiler_params=pltpu.CompilerParams(
            collective_id=2, has_side_effects=True, vmem_limit_bytes=VMEM_LIMIT
        ),
        cost_estimate=pl.CostEstimate(
            flops=80 * 10**9, bytes_accessed=8 * total * width, transcendentals=0
        ),
        name="feed",
    )(slots, rest, home, hidden_one, cotangent, norms)


class Line:
    def __init__(self, place, parts, scratch):
        self.n, self.me, self.parts = place.n, place.z, parts
        self.landed = {"right": scratch[0], "left": scratch[1]}
        self.sems = {"right": scratch[2:4], "left": scratch[4:6]}

    @staticmethod
    def scratch(n, rows, columns):
        return [pltpu.VMEM((n - 1, rows, columns), jnp.bfloat16)] * 2 + [
            pltpu.SemaphoreType.DMA((n - 1,))
        ] * 4

    def _spots(self):
        return (("right", self.me, self.me + 1), ("left", self.n - 1 - self.me, self.me - 1))

    def _copy(self, way, spot, to, step):
        n = self.n
        chunk = n - 1 - step + spot if way == "right" else step - spot
        return pltpu.make_async_remote_copy(
            self.parts.at[lax.rem(chunk + n, n)], self.landed[way].at[step],
            self.sems[way][0].at[step], self.sems[way][1].at[step],
            device_id={"mp": lax.rem(to + n, n)}, device_id_type=MESH,
        )

    def step(self, step):
        n = self.n
        for way, spot, to in self._spots():
            chunk = n - 1 - step + spot if way == "right" else step - spot
            chunk = lax.rem(chunk + n, n)

            if step > 0:

                @pl.when((spot > 0) & (spot <= step) & (spot < n - 1))
                def _():
                    self._copy(way, spot, to, step - 1).wait_recv()
                    self.parts[chunk] = bf16(
                        f32(self.parts[chunk]) + f32(self.landed[way][step - 1])
                    )

            @pl.when((spot <= step) & (spot < n - 1))
            def _():
                self._copy(way, spot, to, step).start()

    def finish(self):
        last = self.n - 2
        for way, spot, to in self._spots():

            @pl.when(spot > 0)
            def _():
                self._copy(way, spot, to, last).wait_recv()
                self.parts[self.me] = bf16(
                    f32(self.parts[self.me]) + f32(self.landed[way][last])
                )

            for step in range(self.n - 1):

                @pl.when((spot <= step) & (spot < self.n - 1))
                def _():
                    self._copy(way, spot, to, step).wait_send()


class Fold:
    def __init__(self, place, make, out, scratch, group, slack=2):
        self.n, self.me, self.make, self.out = place.n, place.z, make, out
        self.parts, self.held, self.down_send, self.down_recv, self.back_send, self.back_recv, self.own = scratch
        self.chunks = self.held.shape[1]
        self.ring = self.parts.shape[1]
        self.group, self.slack = group, slack
        self.ticks = self.chunks + slack * (2 * (self.n - 1) - 1)

    @staticmethod
    def scratch(chunks, rows, columns, ring=12):
        low, dma = jnp.bfloat16, pltpu.SemaphoreType.DMA((2, chunks))
        return [
            pltpu.VMEM((2, ring, rows, columns), low), pltpu.VMEM((2, chunks, rows, columns), low),
            dma, dma, dma, dma, dma,
        ]

    def _flows(self):
        n, me = self.n, self.me
        return (
            (0, me, lax.rem(me + 1, n), lax.rem(me + n - 1, n)),
            (1, n - 1 - me, lax.rem(me + n - 1, n), lax.rem(me + 1, n)),
        )

    def _down(self, flow, chunk, to, first):
        source = self.parts.at[flow, lax.rem(chunk, self.ring)] if first else self.held.at[flow, chunk]
        return pltpu.make_async_remote_copy(
            source, self.held.at[flow, chunk],
            self.down_send.at[flow, chunk], self.down_recv.at[flow, chunk],
            device_id={"mp": to}, device_id_type=MESH,
        )

    def _back(self, flow, chunk, to, first):
        source = (self.held if first else self.out).at[flow, chunk]
        return pltpu.make_async_remote_copy(
            source, self.out.at[flow, chunk],
            self.back_send.at[flow, chunk], self.back_recv.at[flow, chunk],
            device_id={"mp": to}, device_id_type=MESH,
        )

    def _keep(self, flow, chunk):
        return pltpu.make_async_copy(
            self.held.at[flow, chunk], self.out.at[flow, chunk], self.own.at[flow, chunk]
        )

    def tick(self, tick):
        last = self.n - 1
        for flow, spot, ahead, behind in self._flows():
            if tick < self.chunks:
                if tick % self.group == 0:
                    whole = bf16(self.make(flow, tick // self.group))
                    rows = whole.shape[0] // self.group
                    for index in range(self.group):
                        if tick + index >= self.ring:

                            @pl.when(spot == 0)
                            def _():
                                self._down(flow, tick + index - self.ring, ahead, True).wait_send()

                        self.parts[flow, (tick + index) % self.ring] = whole[
                            index * rows : (index + 1) * rows
                        ]

                @pl.when(spot == 0)
                def _():
                    self._down(flow, tick, ahead, True).start()

            chunk = tick - self.slack * spot

            @pl.when((spot > 0) & (chunk >= 0) & (chunk < self.chunks))
            def _():
                self._down(flow, chunk, ahead, False).wait_recv()
                self.held[flow, chunk] = bf16(
                    f32(self.held[flow, chunk]) + f32(self.parts[flow, lax.rem(chunk, self.ring)])
                )

                @pl.when(spot < last)
                def _():
                    self._down(flow, chunk, ahead, False).start()

                @pl.when(spot == last)
                def _():
                    self._back(flow, chunk, behind, True).start()
                    self._keep(flow, chunk).start()

            given = tick - self.slack * (2 * last - spot)

            @pl.when((spot > 0) & (spot < last) & (given >= 0) & (given < self.chunks))
            def _():
                self._back(flow, given, behind, False).wait_recv()
                self._back(flow, given, behind, False).start()

    def finish(self):
        last = self.n - 1
        for flow, spot, ahead, behind in self._flows():

            @pl.when(spot == 0)
            def _():
                def wait(chunk, carry):
                    self._back(flow, chunk, behind, False).wait_recv()
                    return carry

                lax.fori_loop(0, self.chunks, wait, 0)

                def sent(chunk, carry):
                    self._down(flow, chunk, ahead, True).wait_send()
                    return carry

                lax.fori_loop(max(self.chunks - self.ring, 0), self.chunks, sent, 0)

            @pl.when((spot > 0) & (spot < last))
            def _():
                def sent(chunk, carry):
                    self._down(flow, chunk, ahead, False).wait_send()
                    self._back(flow, chunk, behind, False).wait_send()
                    return carry

                lax.fori_loop(0, self.chunks, sent, 0)

            @pl.when(spot == last)
            def _():
                def sent(chunk, carry):
                    self._back(flow, chunk, behind, True).wait_send()
                    self._keep(flow, chunk).wait()
                    return carry

                lax.fori_loop(0, self.chunks, sent, 0)


class Everyone:
    def __init__(self, n_dp, n_mp, mine, slots, send_sems, recv_sems):
        self.n, self.n_mp = n_dp * n_mp, n_mp
        self.me = lax.axis_index("dp") * n_mp + lax.axis_index("mp")
        self.mine, self.slots, self.send, self.recv = mine, slots, send_sems, recv_sems

    def _to(self, distance):
        to = lax.rem(self.me + distance, self.n)
        return {"dp": to // self.n_mp, "mp": lax.rem(to, self.n_mp)}

    def _copy(self, distance):
        return pltpu.make_async_remote_copy(
            self.mine, self.slots.at[self.me], self.send.at[distance - 1], self.recv.at[distance - 1],
            device_id=self._to(distance), device_id_type=MESH,
        )

    def greet(self):
        barrier = pltpu.get_barrier_semaphore()

        def signal(distance, carry):
            pl.semaphore_signal(barrier, inc=1, device_id=self._to(distance), device_id_type=MESH)
            return carry

        lax.fori_loop(1, self.n, signal, 0)
        pl.semaphore_wait(barrier, self.n - 1)

    def start(self):
        def start(distance, carry):
            self._copy(distance).start()
            return carry

        self.slots[self.me] = self.mine[...]
        lax.fori_loop(1, self.n, start, 0)

    def finish(self):
        def wait(distance, carry):
            self._copy(distance).wait()
            return carry

        lax.fori_loop(1, self.n, wait, 0)
        return jnp.sum(self.slots[...], axis=0)


def moments(upstream, first_moment, second_moment, master, decay):
    first_new = first_decay * first_moment + (1.0 - first_decay) * upstream
    second_new = second_decay * second_moment + (1.0 - second_decay) * upstream * upstream
    direction = (
        first_new
        / (1.0 - first_decay**STEP)
        / (jnp.sqrt(second_new / (1.0 - second_decay**STEP)) + epsilon)
        + decay * master
    )
    return (first_new, second_new, direction)


def tensors(inner, outer, expand, shrink, norms):
    found = [inner.at[a, c] for a in range(2) for c in range(3)]
    found += [outer.at[0], outer.at[1], expand, shrink]
    found += [norms.at[pl.ds(row, 1)] for row in range(6)]
    return list(zip(found, [weight_decay] * 10 + [0.0] * 6))


def square_row(squares, share):
    lane = lax.broadcasted_iota(jnp.int32, (1, 128), 1)
    row = jnp.zeros((1, 128), jnp.float32)
    for index, values in enumerate(squares):
        total = jnp.sum(jnp.sum(values, axis=0, keepdims=True), axis=1, keepdims=True)
        row = jnp.where(lane == index, total * share if index >= 10 else total, row)
    return row


def update_kernel(split, *refs):
    (
        both_ref, layer_ref, sums_ref, grads, weights, firsts, seconds,
        states_ref, input_ref, output_ref, table_ref, new_weights, new_firsts, new_seconds,
        both, layer, wide, loads, stores,
    ) = (
        *refs[:3], refs[3:8], refs[8:13], refs[13:18], refs[18:23],
        *refs[23:27], refs[27:32], refs[32:37], refs[37:42], *refs[42:],
    )
    size, columns = both.shape[2], both.shape[3]
    chunks = both.shape[1]
    pieces, row = [], 0
    for source, held, first, count, target, start in (
        (both_ref.at[0], both.at[0], 0, split, states_ref, 0),
        (both_ref.at[1], both.at[1], 0, split, states_ref, split * size),
        (both_ref.at[0], both.at[0], split, chunks - split, input_ref, 0),
        (both_ref.at[1], both.at[1], split, chunks - split, input_ref, (chunks - split) * size),
        (layer_ref, layer, 0, layer_ref.shape[0], output_ref, 0),
    ):
        span = pl.ds(first, count)
        length = count * source.shape[1]
        load = pltpu.make_async_copy(source.at[span], held.at[span], loads.at[len(pieces)])
        store = pltpu.make_async_copy(
            wide.at[pl.ds(row, length)], target.at[pl.ds(start, length)], stores.at[len(pieces)]
        )
        pieces.append((load, store, held, first, count, row))
        row += length
    for piece in pieces:
        piece[0].start()
    for load, store, held, first, count, row in pieces:
        load.wait()
        length = held.shape[1]
        for index in range(count):
            wide[row + index * length : row + (index + 1) * length, :] = f32(held[first + index])
        store.start()
    lane = lax.broadcasted_iota(jnp.int32, (1, 128), 1)
    counts = jnp.where(lane < 8, float(D * D), jnp.where(lane < 10, float(D * FF), float(D)))
    weight_norm = jnp.sqrt(sums_ref[0:1, :] / counts)
    update_norm = jnp.sqrt(sums_ref[1:2, :] / counts)
    trust = weight_norm / (update_norm + epsilon)
    table_ref[...] = jnp.concatenate([weight_norm, update_norm, trust], axis=0)[:, :16]
    groups = [tensors(*group) for group in (grads, weights, firsts, seconds, new_weights, new_firsts, new_seconds)]
    for index, parts in enumerate(zip(*groups)):
        grad, weight, first, second, new_weight, new_first, new_second = [part[0] for part in parts]
        ratio = jnp.sum(jnp.where(lane == index, trust, 0.0), axis=1, keepdims=True)
        master = weight[...]
        first_new, second_new, direction = moments(
            grad[...], first[...], second[...], master, parts[0][1]
        )
        new_first[...] = first_new
        new_second[...] = second_new
        new_weight[...] = master - learn_rate * ratio * direction
    for piece in pieces:
        piece[1].wait()


def update(both, layer, source_rows, sums, grads, weights, firsts, seconds):
    shape = lambda values: jax.ShapeDtypeStruct(values.shape, jnp.float32)
    results = [shape(values) for values in weights]
    size, columns = both.shape[2:]
    split = source_rows // (2 * size)
    total = layer.shape[0] * layer.shape[1]
    wide = lambda rows: jax.ShapeDtypeStruct((rows, columns), jnp.float32)
    dma = pltpu.SemaphoreType.DMA((5,))
    return pl.pallas_call(
        partial(update_kernel, split),
        out_shape=[wide(source_rows), wide(total), wide(total)]
        + [jax.ShapeDtypeStruct((3, 16), jnp.float32)]
        + results * 3,
        in_specs=[ANYWHERE] * 2 + [IN_VMEM] * 21,
        out_specs=[ANYWHERE] * 3 + [IN_VMEM] * 16,
        scratch_shapes=[
            pltpu.VMEM(both.shape, jnp.bfloat16),
            pltpu.VMEM(layer.shape, jnp.bfloat16),
            pltpu.VMEM((source_rows + 2 * total, columns), jnp.float32),
            dma, dma,
        ],
        compiler_params=pltpu.CompilerParams(vmem_limit_bytes=VMEM_LIMIT),
        name="update",
    )(both, layer, sums, *grads, *weights, *firsts, *seconds)


def finish_kernel(
    n, side, units, width, prefix_ref, q_ref, k_ref, v_ref, o_ref, row_sums_ref,
    near_ref, x_ref, cross_dk_ref, cross_dv_ref, dq_slots_ref, mixed_slots_ref, inverse_ref, norms_ref, norm_rows_ref,
    half_a_ref, half_b_ref, bundle_ref, second_hbm, hidden_hbm, normed_hbm, cross_wo_ref, source_grad_ref, *refs,
):
    states, refs = refs[:15], refs[15:]
    out_ref, sums_ref, grads, refs = refs[0], refs[1], refs[2:7], refs[7:]
    (
        source_ref, source_sem, do_ref, first_ref, feed_ref, weight_ref, blocks, early_sems, group_sem,
        own_sem, send_out, recv_out, dq_ref, dk_ref, dv_ref, query_acc, delta, master_sems, inner, stage, far_recv, group_send,
        far_send_sem, far_recv_sem, mine, slots, everyone_send, everyone_recv, *scratch,
    ) = refs
    n_dp = 2 * side * side
    p = Place(n, side)
    everyone = Everyone(n_dp, n, mine, slots, everyone_send, everyone_recv)

    me = p.z
    own_heads = (dq_ref, dk_ref, dv_ref)
    size, model = first_ref.shape
    rows = inner.shape[3]
    per_group = 4
    group_rows = per_group * out_ref.shape[2]
    source_groups = cross_dk_ref.shape[0] // (2 * group_rows)

    def make(flow, group):
        if group < source_groups:
            spot = pl.ds((flow * source_groups + group) * group_rows, group_rows)
            made = source_ref[...].reshape(model, 2 * width)
            return dot(cross_dk_ref[spot, :], made[:, :width], NT) + dot(
                cross_dv_ref[spot, :], made[:, width:], NT
            )
        tokens = x_ref.shape[0]
        start = flow * (tokens // 2) + (group - source_groups) * group_rows
        spot = pl.ds(start, group_rows)
        total = jnp.zeros((group_rows, model), jnp.float32)
        for index, own in enumerate(own_heads):
            total = total + dot(own[spot, :], near_ref[:, index * width : (index + 1) * width], NT)
        here = first_ref[start % size : start % size + group_rows, :]
        return total + jnp.where(me == start // size, here, 0.0)

    fold = Fold(p, make, out_ref, scratch[:7], per_group)
    group_sum = Reduce(p, [cross_wo_ref, source_grad_ref], scratch[7:15])
    weight_sum = Reduce(p, [weight_ref], scratch[15:23])
    inner_sum = Reduce(p, [inner], scratch[23:31])
    halves = Halves(p, half_a_ref, half_b_ref, scratch[31:35])
    line = Line(p, group_send, scratch[35:])

    source_load = pltpu.make_async_copy(
        bundle_ref.at[:, :, :, :, pl.ds(2 * n * width + 128, 2 * width)], source_ref, source_sem
    )
    source_load.start()
    weight_loads = [
        pltpu.make_async_copy(
            bundle_ref.at[:, :, :, :, pl.ds(start, n * width)],
            weight_ref.at[:, :, :, :, pl.ds(index * n * width, n * width)], group_sem.at[index],
        )
        for index, start in enumerate((n * width + 128, 0))
    ]
    for load in weight_loads:
        load.start()
    everyone.greet()
    group_sum.core_start()
    halves.start()
    source_load.wait()
    ticks = iter(range(fold.ticks))

    def advance(count):
        for _ in range(count):
            fold.tick(next(ticks))

    advance(2)

    def store_by_place(target, first, columns, value, start):
        for row in range(0, value.shape[0], rows):
            flat = (start + row) // rows
            y, x, core = flat // (2 * side), flat // 2 % side, flat % 2
            target[y, x, core, :, first : first + columns] = value[row : row + rows]

    def held_weight(group, second):
        cols = pl.ds(pl.multiple_of((n * second + group) * width, width), width)
        return weight_ref[:, :, :, :, cols].reshape(model, width)

    def cross_to_self(rows_f32):
        second_load = pltpu.make_async_copy(second_hbm, first_ref, early_sems.at[0])
        normed_load = pltpu.make_async_copy(normed_hbm, rows_f32, early_sems.at[1])
        hidden_load = pltpu.make_async_copy(hidden_hbm, rows_f32, early_sems.at[2])
        second_load.start()
        normed_load.start()
        second_load.wait()
        for load in weight_loads:
            load.wait()
        upstream = first_ref[...]
        for group in range(n):
            upstream = upstream + dot(dq_slots_ref[group], held_weight(group, 0), NT)
        normed_load.wait()
        first, gain_one, bias_one = norm_back(
            upstream, rows_f32[...], inverse_ref[:, 0:1], norms_ref[0:1, :]
        )
        hidden_load.start()
        first_ref[...] = first
        low = bf16(first)
        sent = tokens_to_heads(
            n, lambda group: dot(low, held_weight(group, 1)), blocks, do_ref, send_out, recv_out, own_sem
        )
        advance(1)
        hidden_load.wait()
        hidden_low = bf16(rows_f32[...])
        for group in range(n):
            at = 2 * group * width
            store_by_place(weight_ref, at, width, bf16(dot(hidden_low, dq_slots_ref[group], TN)), 0)
            store_by_place(
                weight_ref, at + width, width, bf16(dot(low, mixed_slots_ref[group], TN)), 0
            )
        rows_all = jnp.concatenate(
            [
                gain_one, norm_rows_ref[0:2, :], bias_one, norm_rows_ref[2:4, :],
                jnp.zeros((122, model), jnp.float32),
            ],
            axis=0,
        )
        store_by_place(weight_ref, 2 * n * width, 128, bf16(rows_all.T), 0)
        advance(1)
        for copy in sent:
            copy.wait()

    pl.run_scoped(cross_to_self, pltpu.VMEM((size, model), jnp.float32))
    weight_sum.core_start()
    feed_ref[...] = bf16(halves.total())
    far = {"mp": lax.rem(me + n // 2, n)}
    far_copies = [
        push(
            feed_ref.at[:, pl.ds((2 * index + 1) * units, units)],
            far_recv.at[:, pl.ds(index * units, units)],
            far_send_sem.at[index], far_recv_sem.at[index], far,
        )
        for index in range(2)
    ]
    group_sum.core_finish(stage)
    group_sum.first_start()
    advance(1)
    weight_sum.core_finish(stage)
    weight_sum.first_start()
    backward_delta(do_ref, o_ref, delta)
    query_acc[...] = jnp.zeros_like(query_acc)
    key_block = 256

    def self_backward(index, heads):
        backward_block(
            True, key_block, index, heads, prefix_ref, q_ref, k_ref, v_ref, do_ref, row_sums_ref, delta,
            query_acc, dk_ref, dv_ref,
        )

    for index in range(x_ref.shape[0] // key_block):
        for heads in ((0, 1), (2, 3)):
            self_backward(index, heads)
            advance(1)
    dq_ref[...] = bf16(query_acc[...])

    per = 256
    for start in range(0, model, per):
        turned = x_ref[:, start : start + per]
        for index, own in enumerate(own_heads):
            store_by_place(inner, index * width, width, bf16(dot(turned, own[...], TN)), start)
    inner_sum.core_start()
    advance(1)
    inner_sum.core_finish(stage)
    inner_sum.first_start()
    advance(2)
    group_sum.first_finish()
    group_sum.second_start()
    weight_sum.first_finish()
    weight_sum.second_start()
    advance(1)
    advance(1)
    inner_sum.first_finish()
    inner_sum.second_start()
    advance(1)
    group_sum.second_wait()
    weight_sum.second_wait()
    whole = n * width
    for group in range(n):
        group_send[group, :, :width] = bf16(
            group_sum.total(slice(group * width, (group + 1) * width))
        )
        start = 2 * group * width
        group_send[group, :, width : 3 * width] = bf16(
            weight_sum.total(slice(start, start + 2 * width))
        )
        group_send[group, :, 3 * width :] = bf16(
            weight_sum.total(slice(2 * whole, 2 * whole + 128))
        )
    line.step(0)
    advance(2)

    def optimizer_sums(*masters):
        master_loads = [
            pltpu.make_async_copy(source, target, master_sems.at[index])
            for index, (source, target) in enumerate(zip(states, masters))
        ]
        for load in master_loads:
            load.start()
        grad_inner, grad_outer, grad_expand, grad_shrink, grad_norms = grads
        inner_sum.second_wait()
        for index in range(3):
            grad_inner[0, index] = inner_sum.total(slice(index * width, (index + 1) * width))
        start = whole
        for index in range(2):
            grad_inner[1, index + 1] = group_sum.total(
                slice(start + index * width, start + (index + 1) * width)
            )
        line.step(1)
        for load in master_loads:
            load.wait()
        weights, firsts, seconds = (tensors(*masters[index : index + 5]) for index in (0, 5, 10))
        share = 1.0 / n
        mine[...] = jnp.zeros(mine.shape, jnp.float32)
        mine[0:1, :] = square_row([ref[...] * ref[...] for ref, _ in weights], share)
        advance(2)
        line.step(2)
        for copy in far_copies:
            copy.wait_recv()
        grad_shrink[...] = (f32(feed_ref[:, :units]) + f32(far_recv[:, :units])).T
        grad_expand[...] = f32(feed_ref[:, 2 * units : 3 * units]) + f32(far_recv[:, units:])
        advance(2)
        line.finish()
        received = lambda cols: f32(group_send[me, :, cols])
        grad_outer[1] = received(slice(0, width)).T
        grad_inner[1, 0] = received(slice(width, 2 * width))
        grad_outer[0] = received(slice(2 * width, 3 * width)).T
        grad_norms[...] = received(slice(3 * width, 3 * width + 128)).T[:6, :]

        def direction_square(grad, first, second, weight):
            step = moments(grad[0][...], first[0][...], second[0][...], weight[0][...], weight[1])[2]
            return step * step

        mine[1:2, :] = square_row(
            [direction_square(*group) for group in zip(tensors(*grads), firsts, seconds, weights)], share
        )
        everyone.start()
        advance(4)
        sums_ref[...] = everyone.finish()

    pl.run_scoped(optimizer_sums, *[pltpu.VMEM(source.shape, jnp.float32) for source in states])
    for tick in ticks:
        fold.tick(tick)
    fold.finish()
    for copy in far_copies:
        copy.wait_send()
    for batch in (group_sum, weight_sum, inner_sum):
        batch.finish()


def finish(
    n_dp, n_mp, prefix, projections, mixed, row_sums, near, tokens, source_heads, dq_slots, mixed_slots,
    inverse, norms, norm_rows, halves, bundle, second, hidden, normed, cross_wo, source_grad, states,
):
    side = round((n_dp // 2) ** 0.5)
    total, width = mixed.shape
    size, model = second.shape
    rows = model // n_dp
    half, feed_columns = halves[0].shape[1:]
    units = feed_columns // 4
    low, wide = jnp.bfloat16, jnp.float32
    shape = jax.ShapeDtypeStruct
    dma = pltpu.SemaphoreType.DMA
    by_place = lambda values: values.reshape(side, side, 2, rows, values.shape[1])
    early = [by_place(values) for values in (cross_wo, source_grad)]
    columns = sum(values.shape[4] for values in early)
    group_bundle = 3 * width + 128
    devices = n_dp * n_mp
    chunk_rows = 64
    chunks = (total + source_heads[0].shape[0]) // (2 * chunk_rows)
    weight_columns = 2 * n_mp * width + 128
    both, sums, *grads = pl.pallas_call(
        partial(finish_kernel, n_mp, side, units, width),
        out_shape=[shape((2, chunks, chunk_rows, model), low), shape((8, 128), wide)]
        + [shape(values.shape, wide) for values in states[:5]],
        in_specs=[pl.BlockSpec(memory_space=pltpu.SMEM)]
        + [IN_VMEM] * 16
        + [ANYWHERE] * (6 + len(states)),
        out_specs=[ANYWHERE] + [IN_VMEM] * 6,
        scratch_shapes=[
            pltpu.VMEM((side, side, 2, rows, 2 * width), low),
            dma,
            pltpu.VMEM((total, width), low),
            pltpu.VMEM((size, model), wide),
            pltpu.VMEM((rows, feed_columns), low),
            pltpu.VMEM((side, side, 2, rows, weight_columns), low),
            pltpu.VMEM((n_mp, size, width), low),
            dma((3,)), dma((2,)), dma, dma((n_mp - 1,)), dma((n_mp - 1,)),
            *[pltpu.VMEM((total, width), low)] * 3,
            pltpu.VMEM((total, width), wide),
            pltpu.VMEM((8, total), wide),
            dma((len(states),)),
            pltpu.VMEM((side, side, 2, rows, 3 * width), low),
            pltpu.VMEM((2, rows, max(columns, weight_columns)), low),
            pltpu.VMEM((rows, 2 * units), low),
            pltpu.VMEM((n_mp, rows, group_bundle), low),
            dma((2,)), dma((2,)),
            pltpu.VMEM((8, 128), wide),
            pltpu.VMEM((devices, 8, 128), wide),
            dma((devices - 1,)), dma((devices - 1,)),
            *Fold.scratch(chunks, chunk_rows, model),
            *Reduce.scratch(side, rows, columns, 2),
            *Reduce.scratch(side, rows, weight_columns, 1),
            *Reduce.scratch(side, rows, 3 * width, 1),
            *Halves.scratch(side, half, feed_columns),
            *Line.scratch(n_mp, rows, group_bundle),
        ],
        compiler_params=pltpu.CompilerParams(
            collective_id=5, has_side_effects=True, vmem_limit_bytes=VMEM_LIMIT
        ),
        cost_estimate=pl.CostEstimate(flops=10**10, bytes_accessed=1 << 20, transcendentals=0),
        name="finish",
    )(
        prefix, *projections, mixed, row_sums, near, tokens, *source_heads, dq_slots, mixed_slots, inverse,
        norms, norm_rows, *halves, by_place(bundle), second, hidden, normed, *early, *states,
    )
    return both, sums, grads


def on_device(
    inputs,
    encoder,
    prefix,
    cotangent,
    inner_weights,
    inner_first,
    inner_second,
    outer_weights,
    outer_first,
    outer_second,
    expand_weights,
    expand_first,
    expand_second,
    shrink_weights,
    shrink_first,
    shrink_second,
    norm_params,
    norm_first,
    norm_second,
):
    n_dp, n_mp = lax.axis_size("dp"), lax.axis_size("mp")
    seq_count, seq_len, model = inputs.shape
    tokens = inputs.reshape(seq_len, model)
    states = encoder.reshape(-1, model)
    rows, width = inner_weights.shape[2:]
    units = expand_weights.shape[1]

    norm_t = jnp.pad(bf16(norm_params).reshape(6, rows).T, ((0, 0), (0, 122)))
    outer_t = bf16(jnp.swapaxes(outer_weights, 1, 2))
    shrink_t = bf16(shrink_weights.T)
    near, bundle, home, self_q, self_k, self_v, self_mixed, self_sums, self_slots = front(
        n_dp, n_mp, prefix, inner_weights, outer_t, norm_t, expand_weights, shrink_t, tokens
    )
    by_rows = lambda values: values.reshape(model, values.shape[-1])
    near, bundle = by_rows(near), by_rows(bundle)
    (
        hidden_one, normed_one, inverse_one, norms, cross_query, cross_k, cross_v, cross_mixed,
        cross_sums, cross_slots, home, rest,
    ) = middle(n_dp, n_mp, self_slots, bundle, tokens, home, shrink_t, outer_t, states)
    rest = by_rows(rest)
    out_rows, grad_second, cross_dmix, shrink_grad, expand_grad, cross_wo_grad, norm_rows = feed(
        n_mp, cross_slots, rest, home, hidden_one, cotangent.reshape(seq_len, model), norms,
    )
    dq_slots, cross_dk, cross_dv, layer_low, source_grad, *halves = cross_backward(
        n_dp, n_mp, cross_query, cross_k, cross_v, cross_dmix, cross_mixed, cross_sums, out_rows, states,
        shrink_grad, expand_grad,
    )
    flat = lambda values: values.reshape(6, rows)
    weights = [inner_weights, outer_weights, expand_weights, shrink_weights, flat(norm_params)]
    firsts = [inner_first, outer_first, expand_first, shrink_first, flat(norm_first)]
    seconds = [inner_second, outer_second, expand_second, shrink_second, flat(norm_second)]
    both, sums, grads = finish(
        n_dp, n_mp, prefix, (self_q, self_k, self_v), self_mixed, self_sums, near, tokens,
        (cross_dk, cross_dv), dq_slots, self_slots, inverse_one, norms, norm_rows, halves, bundle,
        grad_second, hidden_one, normed_one, cross_wo_grad, source_grad, weights + firsts + seconds,
    )
    encoder_grad, input_grad, layer_out, table, *results = update(
        both, layer_low, states.shape[0], sums, grads, weights, firsts, seconds
    )
    for index in (4, 9, 14):
        results[index] = results[index].reshape(2, 3, rows)
    return (
        layer_out.reshape(seq_count, seq_len, model),
        input_grad.reshape(seq_count, seq_len, model),
        encoder_grad.reshape(seq_count, -1, model),
        *results,
        table,
    )


def solution(mesh):
    placed = (
        P("dp", None, None),
        P("dp", None, None),
        P("dp"),
        P("dp", None, None),
        P(None, None, "dp", "mp"),
        P(None, None, "dp", "mp"),
        P(None, None, "dp", "mp"),
        P(None, "mp", "dp"),
        P(None, "mp", "dp"),
        P(None, "mp", "dp"),
        P("dp", "mp"),
        P("dp", "mp"),
        P("dp", "mp"),
        P("mp", "dp"),
        P("mp", "dp"),
        P("mp", "dp"),
        P(None, None, "dp"),
        P(None, None, "dp"),
        P(None, None, "dp"),
    )
    return jax.shard_map(
        on_device,
        mesh=mesh,
        in_specs=placed,
        out_specs=(
            P("dp", None, None),
            P("dp", None, None),
            P("dp", None, None),
            P(None, None, "dp", "mp"),
            P(None, "mp", "dp"),
            P("dp", "mp"),
            P("mp", "dp"),
            P(None, None, "dp"),
            P(None, None, "dp", "mp"),
            P(None, "mp", "dp"),
            P("dp", "mp"),
            P("mp", "dp"),
            P(None, None, "dp"),
            P(None, None, "dp", "mp"),
            P(None, "mp", "dp"),
            P("dp", "mp"),
            P("mp", "dp"),
            P(None, None, "dp"),
            P(),
        ),
        check_vma=False,
    )
```

```python
from functools import partial

import jax
import jax.numpy as jnp
from jax import lax
from jax.experimental import pallas as pl
from jax.experimental.pallas import tpu as pltpu
from jax.sharding import PartitionSpec as P

D = 1024
HEAD = 64
FF = 4096
STEP = 5

first_decay = 0.5
second_decay = 0.6
learn_rate = 0.5
weight_decay = 0.01
epsilon = 1e-06
norm_eps = 1e-05
mask_fill = -1000000000.0

MESH = pl.DeviceIdType.MESH
ANYWHERE = pl.BlockSpec(memory_space=pl.ANY)
IN_VMEM = pl.BlockSpec(memory_space=pltpu.VMEM)
NN = (((1,), (0,)), ((), ()))
NT = (((1,), (1,)), ((), ()))
TN = (((0,), (0,)), ((), ()))
VMEM_LIMIT = 60 << 20


def dot(left, right, dims=NN):
    return lax.dot_general(left, right, dims, preferred_element_type=jnp.float32)


def bf16(values):
    return values.astype(jnp.bfloat16)


def f32(values):
    return values.astype(jnp.float32)


def layer_norm(values, gain_row, bias_row):
    center = values - jnp.mean(values, axis=-1, keepdims=True)
    spread = jnp.mean(center * center, axis=-1, keepdims=True)
    inverse = lax.rsqrt(spread + norm_eps)
    normed = center * inverse
    return (normed * gain_row + bias_row, normed, inverse)


def norm_back(upstream, normed, inverse, gain_row):
    scaled = upstream * gain_row
    inner = (
        scaled
        - jnp.mean(scaled, axis=-1, keepdims=True)
        - normed * jnp.mean(scaled * normed, axis=-1, keepdims=True)
    )
    return (
        inner * inverse,
        jnp.sum(upstream * normed, axis=0, keepdims=True),
        jnp.sum(upstream, axis=0, keepdims=True),
    )


class Place:
    def __init__(self, n_mp, side):
        self.n, self.side = n_mp, side
        self.z = lax.axis_index("mp")
        dp = lax.axis_index("dp")
        self.core = lax.rem(dp, 2)
        self.x = lax.rem(dp // 2, side)
        self.y = dp // (2 * side)

    def at(self, y, x, core):
        return {"dp": (y * self.side + x) * 2 + core}

    def x_peer(self, distance):
        other = lax.rem(self.x + distance, self.side)
        return other, self.at(self.y, other, self.core)

    def y_peer(self, distance):
        other = lax.rem(self.y + distance, self.side)
        return other, self.at(other, self.x, self.core)

    def sibling(self):
        return self.at(self.y, self.x, 1 - self.core)

    def line(self):
        return [{"mp": lax.rem(self.z + distance, self.n)} for distance in range(1, self.n)]

    def plane(self):
        steps = range(1, self.side)
        return (
            [self.x_peer(step)[1] for step in steps]
            + [self.y_peer(step)[1] for step in steps]
            + [self.sibling()]
        )


def greet(others):
    barrier = pltpu.get_barrier_semaphore()
    for other in others:
        pl.semaphore_signal(barrier, inc=1, device_id=other, device_id_type=MESH)
    pl.semaphore_wait(barrier, len(others))


def push(source, target, send_sem, recv_sem, to):
    copy = pltpu.make_async_remote_copy(
        source, target, send_sem, recv_sem, device_id=to, device_id_type=MESH
    )
    copy.start()
    return copy


def rows_at(index, size):
    return pl.ds(pl.multiple_of(index * size, size), size)


def tokens_to_heads(n, make, blocks, target, send_sems, recv_sems, local_sem):
    me = lax.axis_index("mp")
    size = blocks.shape[1]
    copies = []
    for distance in (*range(1, n), 0):
        to = lax.rem(me + distance, n)
        blocks[to] = bf16(make(to))
        place = target.at[rows_at(me, size)]
        if distance:
            copies.append(
                push(
                    blocks.at[to], place,
                    send_sems.at[distance - 1], recv_sems.at[distance - 1], {"mp": to},
                )
            )
        else:
            copy = pltpu.make_async_copy(blocks.at[to], place, local_sem)
            copy.start()
            copies.append(copy)
    return copies


def load_groups(n, bundle, stride, first, width, target, sems):
    return [
        pltpu.make_async_copy(
            bundle.at[:, pl.ds(group * stride + first, width)], target.at[group], sems.at[group]
        )
        for group in range(n)
    ]


class Give:
    def __init__(self, place, out, sems):
        self.place, self.n, self.me, self.out = place, place.n, place.z, out
        self.half = out.shape[1] // 2
        self.sems = {"right": sems[0:2], "left": sems[2:4]}

    @staticmethod
    def sems(n):
        return [pltpu.SemaphoreType.DMA((2 * (n - 1),))] * 4

    def _copy(self, way, step, part):
        ahead = 1 if way == "right" else -1
        chunk = lax.rem(self.me - ahead * step + self.n, self.n)
        block = self.out.at[chunk, pl.ds(part * self.half, self.half)]
        return pltpu.make_async_remote_copy(
            block, block, self.sems[way][0].at[2 * step + part], self.sems[way][1].at[2 * step + part],
            device_id={"mp": lax.rem(self.me + ahead + self.n, self.n)}, device_id_type=MESH,
        )

    def _spots(self):
        return (("right", self.me), ("left", self.n - 1 - self.me))

    def step(self, step, part):
        for way, spot in self._spots():

            @pl.when((spot >= step) & (spot < self.n - 1))
            def _():
                if step > 0:
                    self._copy(way, step - 1, part).wait_recv()
                self._copy(way, step, part).start()

    def finish(self):
        every = [(step, part) for step in range(self.n - 1) for part in range(2)]
        for way, spot in self._spots():

            @pl.when(spot == self.n - 1)
            def _():
                for step, part in every:
                    self._copy(way, step, part).wait_recv()

            for step, part in every:

                @pl.when((spot >= step) & (spot < self.n - 1))
                def _():
                    self._copy(way, step, part).wait_send()


class Spread:
    def __init__(self, place, home, send_sems, recv_sems):
        self.place, self.home, self.send, self.recv = place, home, send_sems, recv_sems
        self.half = home.shape[3] // 2
        self.copies = {"first": [], "second": [], "core": []}
        self.index = 0

    def _push(self, stage, block, to):
        spot = self.index
        self.index += 1
        self.copies[stage].append(push(block, block, self.send.at[spot], self.recv.at[spot], to))

    def first(self):
        p, half = self.place, self.half
        for step in range(1, p.side):
            own = self.home.at[p.y, p.x, p.core]
            self._push("first", own.at[pl.ds(0, half)], p.x_peer(step)[1])
            self._push("first", own.at[pl.ds(half, half)], p.y_peer(step)[1])

    def second(self):
        p, half = self.place, self.half
        for copy in self.copies["first"]:
            copy.wait_recv()
        for step in range(1, p.side):
            self._push(
                "second", self.home.at[p.y, :, p.core, pl.ds(0, half)], p.y_peer(step)[1]
            )
            self._push(
                "second", self.home.at[:, p.x, p.core, pl.ds(half, half)], p.x_peer(step)[1]
            )

    def core(self):
        for copy in self.copies["second"]:
            copy.wait_recv()
        self._push("core", self.home.at[:, :, self.place.core], self.place.sibling())

    def finish(self):
        for copy in self.copies["core"] or self.copies["second"] or self.copies["first"]:
            copy.wait_recv()
        for stage in self.copies.values():
            for copy in stage:
                copy.wait_send()

    @staticmethod
    def sems(side):
        return pltpu.SemaphoreType.DMA((4 * (side - 1) + 1,))


class Reduce:
    def __init__(self, place, sources, scratch):
        self.place, self.sources = place, sources
        self.keep, self.first_a, self.first_b, *rest = scratch
        *rest, self.local, self.send, self.recv = rest
        if rest:
            self.second_a, self.second_b = rest
        self.half = self.keep.shape[2] // 2
        self.copies = {"core": [], "first": [], "second": []}
        self.index = 0

    @staticmethod
    def scratch(side, rows, columns, sources, second=True):
        low, dma = jnp.bfloat16, pltpu.SemaphoreType.DMA
        block = pltpu.VMEM((side, side, rows, columns), low)
        first = pltpu.VMEM((side - 1, side, rows // 2, columns), low)
        rest = pltpu.VMEM((side - 1, rows // 2, columns), low)
        count = sources + 4 * (side - 1)
        seconds = [rest, rest] if second else []
        return [
            block, first, first, *seconds, dma((2, sources)), dma((count,)), dma((count,)),
        ]

    def _push(self, stage, source, target, to, begin=True):
        copy = pltpu.make_async_remote_copy(
            source, target, self.send.at[self.index], self.recv.at[self.index],
            device_id=to, device_id_type=MESH,
        )
        self.index += 1
        self.copies[stage].append(copy)
        if begin:
            copy.start()

    def core_start(self, begin=True):
        p, column = self.place, 0
        self.index, self.copies["core"] = 0, []
        for source in self.sources:
            cols = pl.ds(column, source.shape[4])
            column += source.shape[4]
            self._push(
                "core", source.at[:, :, 1 - p.core], self.keep.at[:, :, :, cols], p.sibling(), begin
            )

    def _load(self, stage, index):
        y, x = index // self.place.side, index % self.place.side
        column, loads = 0, []
        for spot, source in enumerate(self.sources):
            cols = pl.ds(column, source.shape[4])
            column += source.shape[4]
            loads.append(
                pltpu.make_async_copy(
                    source.at[y, x, self.place.core], stage.at[index % 2, :, cols],
                    self.local.at[index % 2, spot],
                )
            )
        return loads

    def core_finish(self, stage):
        side, keep, columns = self.place.side, self.keep, self.keep.shape[3]
        for load in self._load(stage, 0):
            load.start()
        for copy in self.copies["core"]:
            copy.wait_recv()
        for index in range(side * side):
            if index + 1 < side * side:
                for load in self._load(stage, index + 1):
                    load.start()
            for load in self._load(stage, index):
                load.wait()
            y, x = index // side, index % side
            keep[y, x] = bf16(f32(keep[y, x]) + f32(stage[index % 2, :, :columns]))

    def first_start(self, begin=True):
        p, half = self.place, self.half
        self.index, self.copies["first"] = len(self.sources), []
        top, bottom = pl.ds(0, half), pl.ds(half, half)
        for step in range(1, p.side):
            other, to = p.x_peer(step)
            self._push("first", self.keep.at[:, other, top], self.first_a.at[step - 1], to, begin)
            other, to = p.y_peer(step)
            self._push("first", self.keep.at[other, :, bottom], self.first_b.at[step - 1], to, begin)

    def first_finish(self):
        p, half, keep = self.place, self.half, self.keep
        for copy in self.copies["first"]:
            copy.wait_recv()

        def add(index, carry):
            total = f32(keep[index, p.x, :half, :])
            for step in range(p.side - 1):
                total = total + f32(self.first_a[step, index])
            keep[index, p.x, :half, :] = bf16(total)
            total = f32(keep[p.y, index, half:, :])
            for step in range(p.side - 1):
                total = total + f32(self.first_b[step, index])
            keep[p.y, index, half:, :] = bf16(total)
            return carry

        lax.fori_loop(0, p.side, add, 0)

    def halves(self, out_a, out_b):
        p, half, keep = self.place, self.half, self.keep
        for index in range(p.side):
            out_a[index] = keep[index, p.x, :half, :]
            out_b[index] = keep[p.y, index, half:, :]

    def second_start(self):
        p, half = self.place, self.half
        top, bottom = pl.ds(0, half), pl.ds(half, half)
        for step in range(1, p.side):
            other, to = p.y_peer(step)
            self._push("second", self.keep.at[other, p.x, top], self.second_a.at[step - 1], to)
            other, to = p.x_peer(step)
            self._push("second", self.keep.at[p.y, other, bottom], self.second_b.at[step - 1], to)

    def second_wait(self):
        for copy in self.copies["second"]:
            copy.wait_recv()

    def total(self, cols):
        p, half = self.place, self.half
        top, bottom = f32(self.keep[p.y, p.x, :half, cols]), f32(self.keep[p.y, p.x, half:, cols])
        for step in range(p.side - 1):
            top = top + f32(self.second_a[step, :, cols])
            bottom = bottom + f32(self.second_b[step, :, cols])
        return jnp.concatenate([top, bottom], axis=0)

    def finish(self):
        for stage in self.copies.values():
            for copy in stage:
                copy.wait_send()


class Halves:
    def __init__(self, place, part_a, part_b, scratch):
        self.place, self.parts = place, (part_a, part_b)
        self.landed, (self.send, self.recv) = scratch[:2], scratch[2:]

    @staticmethod
    def scratch(side, half, columns):
        dma = pltpu.SemaphoreType.DMA((2 * (side - 1),))
        return [pltpu.VMEM((side - 1, half, columns), jnp.bfloat16)] * 2 + [dma, dma]

    def start(self):
        p = self.place
        self.copies = []
        for step in range(1, p.side):
            for index, (other, to) in enumerate((p.y_peer(step), p.x_peer(step))):
                spot = 2 * (step - 1) + index
                self.copies.append(
                    push(
                        self.parts[index].at[other], self.landed[index].at[step - 1],
                        self.send.at[spot], self.recv.at[spot], to,
                    )
                )

    def total(self):
        for copy in self.copies:
            copy.wait()
        sums = []
        for index, mine in enumerate((self.place.y, self.place.x)):
            total = f32(self.parts[index][mine])
            for step in range(self.place.side - 1):
                total = total + f32(self.landed[index][step])
            sums.append(total)
        return jnp.concatenate(sums, axis=0)


def forward_rows(masked, start, block, prefix_ref, q_ref, k_ref, v_ref, mixed_ref, sums_ref):
    width = q_ref.shape[1]
    keys = k_ref.shape[0]
    if masked:
        keys = max(keys // 2, start + block)
    lane = lax.broadcasted_iota(jnp.int32, (block, width), 1) // HEAD
    span = slice(start, start + block) if masked else rows_at(start, block)
    query = q_ref[span, :] * jnp.bfloat16(HEAD**-0.5)
    key_rows, value_rows = k_ref[:keys, :], v_ref[:keys, :]
    if masked:
        query_ids = start + lax.broadcasted_iota(jnp.int32, (block, keys), 0)
        key_ids = lax.broadcasted_iota(jnp.int32, (block, keys), 1)
        allowed = (key_ids <= query_ids) | (key_ids < prefix_ref[0])
    mixed = jnp.zeros((block, width), jnp.float32)
    slot = lax.broadcasted_iota(jnp.int32, (block, 128), 1)
    table = jnp.zeros((block, 128), jnp.float32)
    for head in range(width // HEAD):
        scores = dot(jnp.where(lane == head, query, jnp.bfloat16(0)), key_rows, NT)
        if masked:
            scores = jnp.where(allowed, scores, mask_fill)
        row_max = jnp.max(scores, axis=1, keepdims=True)
        powered = jnp.exp(scores - row_max)
        totals = jnp.sum(powered, axis=1, keepdims=True)
        part = dot(bf16(powered), value_rows) * (1.0 / totals)
        mixed = jnp.where(lane == head, part, mixed)
        table = jnp.where(slot == head, row_max + jnp.log(totals), table)
    mixed_ref[span, :] = bf16(mixed)
    sums_ref[:, span] = table.T[:8, :]


def backward_delta(do_ref, o_ref, delta):
    width = do_ref.shape[1]
    product = f32(do_ref[...]) * f32(o_ref[...])
    row = lax.broadcasted_iota(jnp.int32, (8, width), 0)
    col = lax.broadcasted_iota(jnp.int32, (8, width), 1) // HEAD
    pick = jnp.where(row == col, 1.0, 0.0).astype(jnp.float32)
    delta[...] = lax.dot_general(
        pick, product, NT, precision=lax.Precision.HIGHEST, preferred_element_type=jnp.float32
    )


def backward_block(
    masked, block, index, heads, prefix_ref, q_ref, k_ref, v_ref, do_ref, sums_ref, delta, acc, dk_ref, dv_ref
):
    total, width = q_ref.shape
    factor = HEAD**-0.5
    rows = slice(index * block, (index + 1) * block)
    first = index * block if masked and index * block >= total // 2 else 0
    count = total - first
    lane = lax.broadcasted_iota(jnp.int32, (block, width), 1) // HEAD
    query, grad_rows = q_ref[first:, :], do_ref[first:, :]
    scaled_keys = k_ref[rows, :] * jnp.bfloat16(factor)
    value_rows = v_ref[rows, :]
    if masked:
        query_ids = first + lax.broadcasted_iota(jnp.int32, (block, count), 1)
        key_ids = index * block + lax.broadcasted_iota(jnp.int32, (block, count), 0)
        allowed = (key_ids <= query_ids) | (key_ids < prefix_ref[0])
    key_grad = jnp.zeros((block, width), jnp.float32)
    value_grad = jnp.zeros((block, width), jnp.float32)
    query_grad = jnp.zeros((count, width), jnp.float32)
    for head in heads:
        own_keys = jnp.where(lane == head, scaled_keys, jnp.bfloat16(0))
        scores = dot(own_keys, query, NT)
        if masked:
            scores = jnp.where(allowed, scores, mask_fill)
        probs = jnp.exp(scores - sums_ref[head : head + 1, first:])
        prob_grad = dot(jnp.where(lane == head, value_rows, jnp.bfloat16(0)), grad_rows, NT)
        score_grad = bf16(probs * (prob_grad - delta[head : head + 1, first:]))
        value_grad = jnp.where(lane == head, dot(bf16(probs), grad_rows), value_grad)
        key_grad = jnp.where(lane == head, dot(score_grad, query), key_grad)
        query_grad = query_grad + dot(score_grad, own_keys, TN)
    acc[first:, :] += query_grad
    mine = (lane >= heads[0]) & (lane <= heads[-1])
    key_grad, value_grad = bf16(key_grad * factor), bf16(value_grad)
    if heads[0] > 0:
        key_grad = jnp.where(mine, key_grad, dk_ref[rows, :])
        value_grad = jnp.where(mine, value_grad, dv_ref[rows, :])
    dk_ref[rows, :] = key_grad
    dv_ref[rows, :] = value_grad


def cross_backward_kernel(
    n, side, q_ref, k_ref, v_ref, do_ref, o_ref, sums_ref, mine_ref, states_hbm, shrink_ref, expand_ref,
    slots_ref, dk_ref, dv_ref, all_ref, source_ref, half_a_ref, half_b_ref,
    scaled_keys, key_acc, value_acc, delta, blocks, stage, states_ref, states_sem, own_sem, dq_send, dq_recv, *scratch,
):
    p = Place(n, side)
    give = Give(p, all_ref, scratch[:4])
    feed_sum = Reduce(p, [shrink_ref, expand_ref], scratch[4:])
    width = q_ref.shape[1]
    size = blocks.shape[1]
    heads = range(width // HEAD)
    factor = HEAD**-0.5
    own = pltpu.make_async_copy(mine_ref, all_ref.at[p.z], own_sem)
    own.start()
    states_load = pltpu.make_async_copy(states_hbm, states_ref, states_sem)
    states_load.start()
    greet(p.line() + p.plane())
    feed_sum.core_start()
    own.wait()
    give.step(0, 0)
    give.step(0, 1)
    backward_delta(do_ref, o_ref, delta)
    scaled_keys[...] = k_ref[...] * jnp.bfloat16(factor)
    key_acc[...] = jnp.zeros_like(key_acc)
    value_acc[...] = jnp.zeros_like(value_acc)
    lane = lax.broadcasted_iota(jnp.int32, (size, width), 1) // HEAD
    chunk = 512

    def dq_copy(distance):
        to = lax.rem(p.z + distance, n)
        return pltpu.make_async_remote_copy(
            blocks.at[to], slots_ref.at[p.z], dq_send.at[distance - 1], dq_recv.at[distance - 1],
            device_id={"mp": to}, device_id_type=MESH,
        )

    def one_block(step, carry):
        block = lax.rem(p.z + 1 + step, n)
        span = rows_at(block, size)
        query, grad_rows = q_ref[span, :], do_ref[span, :]
        stacked = lambda values: jnp.concatenate(
            [jnp.where(lane == head, values, jnp.bfloat16(0)) for head in heads], axis=0
        )
        across = lambda ref: jnp.concatenate([ref[head : head + 1, span] for head in heads], axis=1)
        own_query, own_grad = stacked(query), stacked(grad_rows)
        row_sums, row_delta = across(sums_ref), across(delta)
        all_grads = jnp.zeros((len(heads) * size, width), jnp.float32)
        for first in range(0, k_ref.shape[0], chunk):
            rows = slice(first, first + chunk)
            if first == 0:
                for later in range(1, n):
                    hop = divmod(later + 1, 2)
                    if hop[0] < n - 1:

                        @pl.when(step == later)
                        def _():
                            give.step(*hop)

            if first == 2 * chunk:

                @pl.when(step == 0)
                def _():
                    feed_sum.core_start(False)
                    feed_sum.core_finish(stage)
                    feed_sum.first_start()


            probs = jnp.exp(dot(scaled_keys[rows, :], own_query, NT) - row_sums)
            prob_grad = dot(v_ref[rows, :], own_grad, NT)
            score_grad = bf16(probs * (prob_grad - row_delta))
            value_acc[rows, :] += dot(bf16(probs), own_grad)
            key_acc[rows, :] += dot(score_grad, own_query)
            all_grads = all_grads + dot(score_grad, scaled_keys[rows, :], TN)
        query_grad = jnp.zeros((size, width), jnp.float32)
        for head in heads:
            query_grad = jnp.where(
                lane == head, all_grads[head * size : (head + 1) * size], query_grad
            )
        blocks[block] = bf16(query_grad)

        @pl.when(step < n - 1)
        def _():
            dq_copy(step + 1).start()

        return carry

    lax.fori_loop(0, n, one_block, 0)
    for later in range(n + 1, 2 * (n - 1)):
        give.step(*divmod(later, 2))
    slots_ref[p.z] = blocks[p.z]
    dk_ref[...] = bf16(key_acc[...] * factor)
    dv_ref[...] = bf16(value_acc[...])
    states_load.wait()
    source_ref[:, :width] = bf16(dot(states_ref[...], dk_ref[...], TN))
    source_ref[:, width:] = bf16(dot(states_ref[...], dv_ref[...], TN))
    feed_sum.core_start(False)
    feed_sum.first_start(False)
    feed_sum.first_finish()
    feed_sum.halves(half_a_ref, half_b_ref)
    feed_sum.finish()
    for distance in range(1, n):
        dq_copy(distance).wait()
    give.finish()


def cross_backward(n_dp, n, query, key_rows, value_rows, grad_out, mixed, sums, mine, states, shrink, expand):
    total, width = query.shape
    keys, model = states.shape
    side = round((n_dp // 2) ** 0.5)
    rows, columns = model // n_dp, shrink.shape[1] + expand.shape[1]
    half = (side, rows // 2, columns)
    by_place = lambda values: values.reshape(side, side, 2, rows, values.shape[1])
    low, wide = jnp.bfloat16, jnp.float32
    shape = jax.ShapeDtypeStruct
    dma = pltpu.SemaphoreType.DMA
    return pl.pallas_call(
        partial(cross_backward_kernel, n, side),
        out_shape=[
            shape((n, total // n, width), low),
            shape((keys, width), low),
            shape((keys, width), low),
            shape((n,) + mine.shape, low),
            shape((model, 2 * width), low),
            shape(half, low),
            shape(half, low),
        ],
        in_specs=[IN_VMEM] * 7 + [ANYWHERE] * 3,
        out_specs=[IN_VMEM] * 3 + [ANYWHERE] + [IN_VMEM] * 3,
        scratch_shapes=[
            pltpu.VMEM((keys, width), low),
            pltpu.VMEM((keys, width), wide),
            pltpu.VMEM((keys, width), wide),
            pltpu.VMEM((8, total), wide),
            pltpu.VMEM((n, total // n, width), low),
            pltpu.VMEM((2, rows, columns), low),
            pltpu.VMEM((keys, model), low),
            dma, dma, dma((n - 1,)), dma((n - 1,)),
            *Give.sems(n),
            *Reduce.scratch(side, rows, columns, 2, second=False),
        ],
        compiler_params=pltpu.CompilerParams(
            vmem_limit_bytes=VMEM_LIMIT, collective_id=6, has_side_effects=True
        ),
        cost_estimate=pl.CostEstimate(flops=40 * total * keys * width, bytes_accessed=1 << 20, transcendentals=0),
        name="cross_backward",
    )(
        query, key_rows, value_rows, grad_out, mixed, sums, mine, states, by_place(shrink), by_place(expand),
    )


def front_kernel(
    n, side, prefix_ref, inner_ref, outer_in_ref, norm_in_ref, expand_ref, shrink_in_ref, x_ref, outer_ref, shrink_ref,
    near_ref, home_ref, feed_home_ref, q_ref, k_ref, v_ref, mixed_ref, sums_ref, slots_ref,
    block_near, block_line, block_rest, own_sems, near_send, near_recv, home_send, home_recv,
    line_send, line_recv, far_send, far_recv, mixed_send, mixed_recv,
    block_feed, feed_send, feed_recv, rest_send, rest_recv,
):
    p = Place(n, side)
    width = inner_ref.shape[3]
    units = expand_ref.shape[1]
    if outer_in_ref.shape[1] == width:
        for index in range(2):
            outer_ref[index] = bf16(outer_in_ref[index].T)
        shrink_ref[...] = bf16(shrink_in_ref[...].T)
        norm_row = jnp.concatenate(
            [norm_in_ref[...], jnp.zeros((122, norm_in_ref.shape[1]), jnp.float32)], axis=0
        ).T
    else:
        outer_ref[...] = bf16(outer_in_ref[...])
        shrink_ref[...] = bf16(shrink_in_ref[...])
        norm_row = norm_in_ref[...]
    for index in range(3):
        block_near[:, index * width : (index + 1) * width] = bf16(inner_ref[0, index])
    block_line[:, :width] = bf16(inner_ref[1, 0])
    block_line[:, width : 2 * width] = outer_ref[0]
    for index in range(2):
        block_rest[:, index * width : (index + 1) * width] = bf16(inner_ref[1, index + 1])
    block_rest[:, 2 * width :] = bf16(norm_row)
    norms = block_rest.shape[1] - 2 * width
    whole = n * width
    later = whole + norms
    out_cols = pl.ds(pl.multiple_of(p.z * width, width), width)
    query_cols = pl.ds(pl.multiple_of(later + p.z * width, 128), width)
    spot = home_ref.at[p.y, p.x, p.core]
    near_ref[p.y, p.x, p.core] = block_near[...]
    block_feed[:, :units] = bf16(expand_ref[...])
    block_feed[:, units:] = shrink_ref[...]
    feed_spot = feed_home_ref.at[p.y, p.x, p.core]
    own = [
        pltpu.make_async_copy(source, target, own_sems.at[index])
        for index, (source, target) in enumerate(
            (
                (block_line.at[:, pl.ds(width, width)], spot.at[:, out_cols]),
                (block_line.at[:, pl.ds(0, width)], spot.at[:, query_cols]),
                (block_rest.at[:, pl.ds(2 * width, norms)], spot.at[:, pl.ds(whole, norms)]),
                (block_rest.at[:, pl.ds(0, 2 * width)], spot.at[:, pl.ds(later + whole, 2 * width)]),
                (block_feed, feed_spot.at[:, pl.ds(0, 2 * units)]),
            )
        )
    ]
    for copy in own:
        copy.start()
    greet(p.line() + p.plane())
    near = Spread(p, near_ref, near_send, near_recv)
    first_rest = Spread(p, home_ref.at[:, :, :, :, pl.ds(0, later)], home_send, home_recv)
    rest = Spread(
        p, home_ref.at[:, :, :, :, pl.ds(later, whole + 2 * width)], rest_send, rest_recv
    )
    near.first()
    lines = [
        [
            push(
                block_line.at[:, pl.ds(first, width)], spot.at[:, cols],
                line_send.at[part * (n - 1) + index], line_recv.at[part * (n - 1) + index], other,
            )
            for index, other in enumerate(p.line())
        ]
        for part, (first, cols) in enumerate(((width, out_cols), (0, query_cols)))
    ]
    far = push(
        block_feed.at[:, pl.ds(0, units)], feed_spot.at[:, pl.ds(2 * units, units)], far_send, far_recv,
        {"mp": lax.rem(p.z + n // 2, n)},
    )
    for copy in own:
        copy.wait()
    near.second()
    feed_spread = Spread(
        p, feed_home_ref.at[:, :, :, :, pl.ds(0, 2 * units)], feed_send, feed_recv
    )
    for copy in lines[0]:
        copy.wait_recv()
    first_rest.first()
    near.core()
    for copy in lines[1]:
        copy.wait_recv()
    rest.first()
    near.finish()
    first_rest.second()
    model = x_ref.shape[1]
    weights = near_ref[...].reshape(model, 3 * width)
    for start in range(0, x_ref.shape[0], 256):
        rows = slice(start, start + 256)
        made = bf16(dot(x_ref[rows, :], weights))
        for index, target in enumerate((q_ref, k_ref, v_ref)):
            target[rows, :] = made[:, index * width : (index + 1) * width]
    rest.second()
    feed_spread.first()
    size = x_ref.shape[0] // n

    def mixed_copy(distance):
        to = lax.rem(p.z + distance, n)
        return pltpu.make_async_remote_copy(
            mixed_ref.at[rows_at(to, size)], slots_ref.at[p.z],
            mixed_send.at[distance - 1], mixed_recv.at[distance - 1],
            device_id={"mp": to}, device_id_type=MESH,
        )

    def attend(step, carry):
        block = lax.rem(p.z + 1 + step, n)
        for index in range(n):

            @pl.when(block == index)
            def _():
                forward_rows(
                    True, index * size, size, prefix_ref, q_ref, k_ref, v_ref, mixed_ref, sums_ref
                )

        @pl.when(step < n - 1)
        def _():
            mixed_copy(step + 1).start()

        return carry

    lax.fori_loop(0, n, attend, 0)
    slots_ref[p.z] = mixed_ref[rows_at(p.z, size), :]
    first_rest.core()
    rest.core()
    first_rest.finish()
    rest.finish()
    for distance in range(1, n):
        mixed_copy(distance).wait()
    for copy in (*lines[0], *lines[1]):
        copy.wait_send()
    far.wait()
    feed_spread.finish()


def front(n_dp, n_mp, prefix, inner, outer, norms, expand, shrink, tokens):
    rows, width = inner.shape[2:]
    norm_columns = 128
    if rows % 128:
        outer, shrink = jnp.swapaxes(outer, 1, 2), shrink.T
        norms = jnp.pad(norms.T, ((0, 0), (0, norm_columns - 6)))
    total = tokens.shape[0]
    side = round((n_dp // 2) ** 0.5)
    line = 2 * width
    columns = n_mp * line + 2 * width + norm_columns
    units = expand.shape[1]
    low = jnp.bfloat16
    dma = pltpu.SemaphoreType.DMA
    shape = jax.ShapeDtypeStruct
    return pl.pallas_call(
        partial(front_kernel, n_mp, side),
        out_shape=[
            shape((2, rows, width), low),
            shape((rows, units), low),
            shape((side, side, 2, rows, 3 * width), low),
            shape((side, side, 2, rows, columns), low),
            shape((side, side, 2, rows, 4 * units), low),
            *[shape((total, width), low)] * 4,
            shape((8, total), jnp.float32),
            shape((n_mp, total // n_mp, width), low),
        ],
        in_specs=[pl.BlockSpec(memory_space=pltpu.SMEM)] + [IN_VMEM] * 6,
        out_specs=[IN_VMEM] * 3 + [ANYWHERE, ANYWHERE] + [IN_VMEM] * 6,
        scratch_shapes=[
            pltpu.VMEM((rows, 3 * width), low),
            pltpu.VMEM((rows, line), low),
            pltpu.VMEM((rows, 2 * width + norm_columns), low),
            dma((5,)),
            Spread.sems(side), Spread.sems(side), Spread.sems(side), Spread.sems(side),
            dma((2 * n_mp - 2,)), dma((2 * n_mp - 2,)), dma, dma,
            dma((n_mp - 1,)), dma((n_mp - 1,)),
            pltpu.VMEM((rows, 2 * units), low),
            Spread.sems(side), Spread.sems(side), Spread.sems(side), Spread.sems(side),
        ],
        compiler_params=pltpu.CompilerParams(
            collective_id=0, has_side_effects=True, vmem_limit_bytes=VMEM_LIMIT
        ),
        cost_estimate=pl.CostEstimate(flops=40 * 10**9, bytes_accessed=1 << 20, transcendentals=0),
        name="front",
    )(prefix, inner, outer, norms, expand, shrink, tokens)


def middle_kernel(
    n, side, slots_ref, bundle_ref, x_ref, home_in_ref, states_hbm, shrink_ref, outer_ref,
    hidden_ref, normed_ref, inverse_ref, norm_ref, q_ref, k_ref, v_ref, mixed_ref, sums_ref, cross_slots_ref,
    home_ref, rest_ref,
    wo, wq, norm_columns, source, x_rows, blocks,
    wo_sems, wq_sems, load_sems, q_send, q_recv, mixed_send, mixed_recv, far_send, far_recv,
    feed_send, feed_recv, later_send, later_recv, line_send, line_recv,
    expand_send, expand_recv, shrink_send, shrink_recv, states_ref, states_sem,
):
    p = Place(n, side)
    me = p.z
    size = x_rows.shape[0]
    width = slots_ref.shape[2]
    whole = n * width
    norms = norm_columns.shape[1]
    later = whole + norms
    loads = [
        pltpu.make_async_copy(x_ref.at[rows_at(me, size)], x_rows, load_sems.at[0]),
        pltpu.make_async_copy(bundle_ref.at[:, pl.ds(whole, norms)], norm_columns, load_sems.at[1]),
        pltpu.make_async_copy(
            bundle_ref.at[:, pl.ds(later + whole, 2 * width)], source, load_sems.at[2]
        ),
        *load_groups(n, bundle_ref, width, 0, width, wo, wo_sems),
        *load_groups(n, bundle_ref, width, later, width, wq, wq_sems),
    ]
    for load in loads:
        load.start()
    states_load = pltpu.make_async_copy(states_hbm, states_ref, states_sem)
    states_load.start()
    units = home_ref.shape[4] // 4
    spot = rest_ref.at[p.y, p.x, p.core, :, pl.ds(pl.multiple_of(width * me, width), width)]
    greet(p.line() + p.plane())
    store = pltpu.make_async_copy(outer_ref.at[1], spot, load_sems.at[3])
    store.start()
    line = [
        push(outer_ref.at[1], spot, line_send.at[index], line_recv.at[index], other)
        for index, other in enumerate(p.line())
    ]
    part = lambda first, count: home_ref.at[:, :, :, :, pl.ds(first * units, count * units)]
    rest = Spread(p, rest_ref, later_send, later_recv)
    own_units = Spread(p, part(0, 2), feed_send, feed_recv)
    far_expand = Spread(p, part(2, 1), expand_send, expand_recv)
    far_shrink = Spread(p, part(3, 1), shrink_send, shrink_recv)
    own_units.second()
    far_expand.first()
    store.wait()
    for load in loads:
        load.wait()
    norms = f32(norm_columns[...]).T[:8, :]
    norm_ref[...] = norms
    branch = f32(x_rows[...])
    for group in range(n):
        branch = branch + dot(slots_ref[group], wo[group], NT)
    hidden, normed, inverse = layer_norm(branch, norms[0:1, :], norms[3:4, :])
    hidden_ref[...] = hidden
    normed_ref[...] = normed
    inverse_ref[...] = jnp.broadcast_to(inverse, inverse_ref.shape)
    low = bf16(hidden)

    def q_copy(distance):
        to = lax.rem(me + distance, n)
        return pltpu.make_async_remote_copy(
            blocks.at[to], q_ref.at[rows_at(me, size)], q_send.at[distance - 1], q_recv.at[distance - 1],
            device_id={"mp": to}, device_id_type=MESH,
        )

    for distance in range(1, n):
        to = lax.rem(me + distance, n)
        blocks[to] = bf16(dot(low, wq[to]))
        q_copy(distance).start()
    far = push(
        shrink_ref, home_ref.at[p.y, p.x, p.core, :, pl.ds(3 * units, units)], far_send, far_recv,
        {"mp": lax.rem(me + n // 2, n)},
    )
    q_ref[rows_at(me, size), :] = bf16(dot(low, wq[me]))
    for copy in line:
        copy.wait_recv()
    rest.first()
    states_load.wait()
    for start in range(0, states_ref.shape[0], 512):
        rows = slice(start, start + 512)
        made = bf16(dot(states_ref[rows, :], source[...]))
        k_ref[rows, :] = made[:, :width]
        v_ref[rows, :] = made[:, width:]
    far_expand.second()

    def mixed_copy(distance):
        to = lax.rem(me + distance, n)
        return pltpu.make_async_remote_copy(
            mixed_ref.at[rows_at(to, size)], cross_slots_ref.at[me],
            mixed_send.at[distance - 1], mixed_recv.at[distance - 1],
            device_id={"mp": to}, device_id_type=MESH,
        )

    for step in range(n):
        if step > 0:
            q_copy(n - step).wait_recv()
        forward_rows(
            False, lax.rem(me + step, n), size, None, q_ref, k_ref, v_ref, mixed_ref, sums_ref
        )
        if step > 0:
            mixed_copy(step).start()
        if step == 0:
            rest.second()
    cross_slots_ref[me] = mixed_ref[rows_at(me, size), :]
    far.wait_recv()
    far_shrink.first()
    rest.core()
    far_shrink.second()
    for distance in range(1, n):
        q_copy(distance).wait_send()
        mixed_copy(distance).wait()
    for copy in line:
        copy.wait_send()
    far.wait_send()
    for spread in (rest, own_units, far_expand, far_shrink):
        spread.finish()


def middle(n_dp, n, slots, bundle, tokens, home, shrink_t, outer_t, states):
    side = round((n_dp // 2) ** 0.5)
    _, size, width = slots.shape
    total, model = tokens.shape
    keys = states.shape[0]
    shape = jax.ShapeDtypeStruct
    dma = pltpu.SemaphoreType.DMA
    low, wide = jnp.bfloat16, jnp.float32
    return pl.pallas_call(
        partial(middle_kernel, n, side),
        out_shape=[
            shape((size, model), wide),
            shape((size, model), wide),
            shape((size, 128), wide),
            shape((8, model), wide),
            shape((total, width), low),
            shape((keys, width), low),
            shape((keys, width), low),
            shape((total, width), low),
            shape((8, total), wide),
            shape((n, size, width), low),
            shape(home.shape, low),
            shape((side, side, 2, outer_t.shape[1], n * width), low),
        ],
        in_specs=[IN_VMEM] + [ANYWHERE] * 4 + [IN_VMEM] * 2,
        out_specs=[IN_VMEM] * 10 + [ANYWHERE] * 2,
        input_output_aliases={3: 10},
        scratch_shapes=[
            pltpu.VMEM((n, model, width), low),
            pltpu.VMEM((n, model, width), low),
            pltpu.VMEM((model, bundle.shape[1] - 2 * n * width - 2 * width), low),
            pltpu.VMEM((model, 2 * width), low),
            pltpu.VMEM((size, model), low),
            pltpu.VMEM((n, size, width), low),
            dma((n,)), dma((n,)), dma((4,)),
            dma((n - 1,)), dma((n - 1,)), dma((n - 1,)), dma((n - 1,)), dma, dma,
            Spread.sems(side), Spread.sems(side), Spread.sems(side), Spread.sems(side),
            dma((n - 1,)), dma((n - 1,)),
            Spread.sems(side), Spread.sems(side), Spread.sems(side), Spread.sems(side),
            pltpu.VMEM((keys, model), low), dma,
        ],
        compiler_params=pltpu.CompilerParams(
            collective_id=1, has_side_effects=True, vmem_limit_bytes=VMEM_LIMIT
        ),
        cost_estimate=pl.CostEstimate(flops=10**10, bytes_accessed=1 << 20, transcendentals=0),
        name="middle",
    )(slots, bundle, tokens, home, states, shrink_t, outer_t)


def feed_kernel(
    n, side, slots, rest_ref, home_ref, hidden_one_ref, cot_ref, norm_ref,
    out_ref, second_ref, dmix_ref, shrink_grad_hbm, expand_grad_hbm, wo_grad_ref, norm_grad_ref,
    wo, weights, hidden_two, normed_two, low_two, low_three, act, slope,
    y_own, y_send, y_recv, d_send, d_recv, cot, blocks,
    load_sem, wo_sems, own_sem, send_out, recv_out, pair_send, pair_recv,
    home_sems, home_send, home_recv, shrink_grad_ref, expand_grad_ref, grad_sems,
):
    p = Place(n, side)
    me = p.z
    mate = {"mp": me + 1 - 2 * lax.rem(me, 2)}
    size = cot.shape[0]
    half = size // 2
    width = slots.shape[2]
    hidden_units = act.shape[1]
    chunk = min(512, hidden_units)
    loads = [
        *load_groups(n, rest_ref, width, 0, width, wo, wo_sems),
        pltpu.make_async_copy(cot_ref.at[rows_at(me, size)], cot, load_sem),
    ]
    rows = home_ref.shape[3]
    places = [(y, x) for y in range(side) for x in range(side)]
    spots = [rows_at((y * side + x) * 2 + p.core, rows) for y, x in places]
    homes = [
        pltpu.make_async_copy(home_ref.at[y, x, p.core], weights.at[spot], home_sems.at[index])
        for index, ((y, x), spot) in enumerate(zip(places, spots))
    ]
    for load in loads + homes:
        load.start()
    greet(p.line() + [p.sibling()])
    home_copies = [
        push(
            home_ref.at[y, x, p.core], weights.at[spot],
            home_send.at[index], home_recv.at[index], p.sibling(),
        )
        for index, ((y, x), spot) in enumerate(zip(places, spots))
    ]
    for load in loads[:n]:
        load.wait()
    branch = hidden_one_ref[...]
    for group in range(n):
        branch = branch + dot(slots[group], wo[group], NT)
    hidden, normed, inverse_two = layer_norm(branch, norm_ref[1:2, :], norm_ref[4:5, :])
    hidden_two[...] = hidden
    normed_two[...] = normed
    low_two[:size, :] = bf16(hidden)
    pair = []

    def to_mate(source, target):
        index = len(pair)
        pair.append(push(source, target, pair_send.at[index], pair_recv.at[index], mate))
        return pair[-1]

    hidden_copies = [
        to_mate(low_two.at[pl.ds(start, half)], low_two.at[pl.ds(size + start, half)])
        for start in (0, half)
    ]
    for copy in homes:
        copy.wait()
    for copy in home_copies:
        copy.wait_recv()
    units = hidden_units // 2

    def expand_cols(first, count):
        first += first // units * units
        return slice(first, first + count)

    def shrink_cols(first, count):
        first += (first // units + 1) * units
        return slice(first, first + count)

    def shrink_sum(rows):
        return sum(
            dot(act[rows, first : first + units], weights[:, shrink_cols(first, units)], NT)
            for first in (0, units)
        )

    def expand_sum(rows):
        return sum(
            dot(slope[rows, first : first + units], weights[:, expand_cols(first, units)], NT)
            for first in (0, units)
        )

    def expand_rows(start, count):
        rows = low_two[start : start + count, :]
        for first in range(0, hidden_units, chunk):
            pre = dot(rows, weights[:, expand_cols(first, chunk)])
            cdf = 0.5 + 0.5 * lax.erf(pre * 0.7071067811865476)
            act[start : start + count, first : first + chunk] = bf16(pre * cdf)
            slope[start : start + count, first : first + chunk] = bf16(
                cdf + pre * jnp.exp(-0.5 * pre * pre) * 0.3989422804014327
            )

    expand_rows(0, size)
    y_copies = []
    for index, start in enumerate((0, half)):
        hidden_copies[index].wait_recv()
        expand_rows(size + start, half)
        y_send[start : start + half, :] = bf16(shrink_sum(slice(size + start, size + start + half)))
        y_copies.append(to_mate(y_send.at[pl.ds(start, half)], y_recv.at[pl.ds(start, half)]))
    y_own[...] = shrink_sum(slice(0, size))
    for copy in y_copies:
        copy.wait_recv()
    output, normed, inverse = layer_norm(
        hidden_two[...] + y_own[...] + f32(y_recv[...]), norm_ref[2:3, :], norm_ref[5:6, :]
    )
    out_ref[...] = bf16(output)
    loads[n].wait()
    third, gain_three, bias_three = norm_back(f32(cot[...]), normed, inverse, norm_ref[2:3, :])
    low_three[:size, :] = bf16(third)
    grad_copies = [
        to_mate(low_three.at[pl.ds(start, half)], low_three.at[pl.ds(size + start, half)])
        for start in (0, half)
    ]

    def back_rows(start, count):
        rows = low_three[start : start + count, :]
        for first in range(0, hidden_units, chunk):
            grad = dot(rows, weights[:, shrink_cols(first, chunk)])
            spot = (slice(start, start + count), slice(first, first + chunk))
            slope[spot] = bf16(grad * f32(slope[spot]))

    back_rows(0, size)
    d_copies = []
    for index, start in enumerate((0, half)):
        grad_copies[index].wait_recv()
        back_rows(size + start, half)
        d_send[start : start + half, :] = bf16(expand_sum(slice(size + start, size + start + half)))
        d_copies.append(to_mate(d_send.at[pl.ds(start, half)], d_recv.at[pl.ds(start, half)]))
    y_own[...] = third + expand_sum(slice(0, size))
    for copy in d_copies:
        copy.wait_recv()
    second, gain_two, bias_two = norm_back(
        y_own[...] + f32(d_recv[...]), normed_two[...], inverse_two, norm_ref[1:2, :]
    )
    second_ref[...] = second
    low = bf16(second)
    sent = tokens_to_heads(
        n, lambda group: dot(low, wo[group]), blocks, dmix_ref, send_out, recv_out, own_sem
    )
    norm_grad_ref[...] = jnp.concatenate(
        [gain_two, gain_three, bias_two, bias_three, jnp.zeros((4, norm_grad_ref.shape[1]))], axis=0
    )
    stores = []
    for first in range(0, low_two.shape[1], 256):
        rows = slice(first, first + 256)
        shrink_grad_ref[rows, :] = bf16(dot(low_three[:, rows], act[...], TN))
        expand_grad_ref[rows, :] = bf16(dot(low_two[:, rows], slope[...], TN))
        for index, (made, target) in enumerate(
            ((shrink_grad_ref, shrink_grad_hbm), (expand_grad_ref, expand_grad_hbm))
        ):
            span = pl.ds(first, 256)
            stores.append(
                pltpu.make_async_copy(made.at[span], target.at[span], grad_sems.at[index, first // 256])
            )
            stores[-1].start()
    for group in range(n):
        wo_grad_ref[:, group * width : (group + 1) * width] = bf16(dot(low, slots[group], TN))
    for copy in sent:
        copy.wait()
    for copy in pair + home_copies:
        copy.wait_send()
    for store in stores:
        store.wait()


def feed(n, slots, rest, home, hidden_one, cotangent, norms):
    width = slots.shape[2]
    total = cotangent.shape[0]
    side, model, units = home.shape[0], hidden_one.shape[1], home.shape[4] // 2
    size = total // n
    shape = jax.ShapeDtypeStruct
    dma = pltpu.SemaphoreType.DMA
    low, wide = jnp.bfloat16, jnp.float32
    return pl.pallas_call(
        partial(feed_kernel, n, side),
        out_shape=[
            shape((size, model), low),
            shape((size, model), wide),
            shape((total, width), low),
            shape((model, units), low),
            shape((model, units), low),
            shape((model, model), low),
            shape((8, model), wide),
        ],
        in_specs=[IN_VMEM, ANYWHERE, ANYWHERE, IN_VMEM, ANYWHERE, IN_VMEM],
        out_specs=[IN_VMEM] * 2 + [ANYWHERE] * 3 + [IN_VMEM] * 2,
        scratch_shapes=[
            pltpu.VMEM((n, model, width), low),
            pltpu.VMEM((model, 2 * units), low),
            pltpu.VMEM((size, model), wide),
            pltpu.VMEM((size, model), wide),
            pltpu.VMEM((2 * size, model), low),
            pltpu.VMEM((2 * size, model), low),
            pltpu.VMEM((2 * size, units), low),
            pltpu.VMEM((2 * size, units), low),
            pltpu.VMEM((size, model), wide),
            pltpu.VMEM((size, model), low),
            pltpu.VMEM((size, model), low),
            pltpu.VMEM((size, model), low),
            pltpu.VMEM((size, model), low),
            pltpu.VMEM((size, model), low),
            pltpu.VMEM((n, size, width), low),
            dma, dma((n,)), dma,
            dma((n - 1,)), dma((n - 1,)),
            dma((8,)), dma((8,)),
            dma((side * side,)), dma((side * side,)), dma((side * side,)),
            pltpu.VMEM((model, units), low), pltpu.VMEM((model, units), low), dma((2, model // 256)),
        ],
        compiler_params=pltpu.CompilerParams(
            collective_id=2, has_side_effects=True, vmem_limit_bytes=VMEM_LIMIT
        ),
        cost_estimate=pl.CostEstimate(
            flops=80 * 10**9, bytes_accessed=8 * total * width, transcendentals=0
        ),
        name="feed",
    )(slots, rest, home, hidden_one, cotangent, norms)


class Line:
    def __init__(self, place, parts, scratch):
        self.n, self.me, self.parts = place.n, place.z, parts
        self.landed = {"right": scratch[0], "left": scratch[1]}
        self.sems = {"right": scratch[2:4], "left": scratch[4:6]}

    @staticmethod
    def scratch(n, rows, columns):
        return [pltpu.VMEM((n - 1, rows, columns), jnp.bfloat16)] * 2 + [
            pltpu.SemaphoreType.DMA((n - 1,))
        ] * 4

    def _spots(self):
        return (("right", self.me, self.me + 1), ("left", self.n - 1 - self.me, self.me - 1))

    def _copy(self, way, spot, to, step):
        n = self.n
        chunk = n - 1 - step + spot if way == "right" else step - spot
        return pltpu.make_async_remote_copy(
            self.parts.at[lax.rem(chunk + n, n)], self.landed[way].at[step],
            self.sems[way][0].at[step], self.sems[way][1].at[step],
            device_id={"mp": lax.rem(to + n, n)}, device_id_type=MESH,
        )

    def step(self, step):
        n = self.n
        for way, spot, to in self._spots():
            chunk = n - 1 - step + spot if way == "right" else step - spot
            chunk = lax.rem(chunk + n, n)

            if step > 0:

                @pl.when((spot > 0) & (spot <= step) & (spot < n - 1))
                def _():
                    self._copy(way, spot, to, step - 1).wait_recv()
                    self.parts[chunk] = bf16(
                        f32(self.parts[chunk]) + f32(self.landed[way][step - 1])
                    )

            @pl.when((spot <= step) & (spot < n - 1))
            def _():
                self._copy(way, spot, to, step).start()

    def finish(self):
        last = self.n - 2
        for way, spot, to in self._spots():

            @pl.when(spot > 0)
            def _():
                self._copy(way, spot, to, last).wait_recv()
                self.parts[self.me] = bf16(
                    f32(self.parts[self.me]) + f32(self.landed[way][last])
                )

            for step in range(self.n - 1):

                @pl.when((spot <= step) & (spot < self.n - 1))
                def _():
                    self._copy(way, spot, to, step).wait_send()


class Fold:
    def __init__(self, place, make, out, scratch, group, slack=2):
        self.n, self.me, self.make, self.out = place.n, place.z, make, out
        self.parts, self.held, self.down_send, self.down_recv, self.back_send, self.back_recv, self.own = scratch
        self.chunks = self.held.shape[1]
        self.ring = self.parts.shape[1]
        self.group, self.slack = group, slack
        self.ticks = self.chunks + slack * (2 * (self.n - 1) - 1)

    @staticmethod
    def scratch(chunks, rows, columns, ring=12):
        low, dma = jnp.bfloat16, pltpu.SemaphoreType.DMA((2, chunks))
        return [
            pltpu.VMEM((2, ring, rows, columns), low), pltpu.VMEM((2, chunks, rows, columns), low),
            dma, dma, dma, dma, dma,
        ]

    def _flows(self):
        n, me = self.n, self.me
        return (
            (0, me, lax.rem(me + 1, n), lax.rem(me + n - 1, n)),
            (1, n - 1 - me, lax.rem(me + n - 1, n), lax.rem(me + 1, n)),
        )

    def _down(self, flow, chunk, to, first):
        source = self.parts.at[flow, lax.rem(chunk, self.ring)] if first else self.held.at[flow, chunk]
        return pltpu.make_async_remote_copy(
            source, self.held.at[flow, chunk],
            self.down_send.at[flow, chunk], self.down_recv.at[flow, chunk],
            device_id={"mp": to}, device_id_type=MESH,
        )

    def _back(self, flow, chunk, to, first):
        source = (self.held if first else self.out).at[flow, chunk]
        return pltpu.make_async_remote_copy(
            source, self.out.at[flow, chunk],
            self.back_send.at[flow, chunk], self.back_recv.at[flow, chunk],
            device_id={"mp": to}, device_id_type=MESH,
        )

    def _keep(self, flow, chunk):
        return pltpu.make_async_copy(
            self.held.at[flow, chunk], self.out.at[flow, chunk], self.own.at[flow, chunk]
        )

    def tick(self, tick):
        last = self.n - 1
        for flow, spot, ahead, behind in self._flows():
            if tick < self.chunks:
                if tick % self.group == 0:
                    whole = bf16(self.make(flow, tick // self.group))
                    rows = whole.shape[0] // self.group
                    for index in range(self.group):
                        if tick + index >= self.ring:

                            @pl.when(spot == 0)
                            def _():
                                self._down(flow, tick + index - self.ring, ahead, True).wait_send()

                        self.parts[flow, (tick + index) % self.ring] = whole[
                            index * rows : (index + 1) * rows
                        ]

                @pl.when(spot == 0)
                def _():
                    self._down(flow, tick, ahead, True).start()

            chunk = tick - self.slack * spot

            @pl.when((spot > 0) & (chunk >= 0) & (chunk < self.chunks))
            def _():
                self._down(flow, chunk, ahead, False).wait_recv()
                self.held[flow, chunk] = bf16(
                    f32(self.held[flow, chunk]) + f32(self.parts[flow, lax.rem(chunk, self.ring)])
                )

                @pl.when(spot < last)
                def _():
                    self._down(flow, chunk, ahead, False).start()

                @pl.when(spot == last)
                def _():
                    self._back(flow, chunk, behind, True).start()
                    self._keep(flow, chunk).start()

            given = tick - self.slack * (2 * last - spot)

            @pl.when((spot > 0) & (spot < last) & (given >= 0) & (given < self.chunks))
            def _():
                self._back(flow, given, behind, False).wait_recv()
                self._back(flow, given, behind, False).start()

    def finish(self):
        last = self.n - 1
        for flow, spot, ahead, behind in self._flows():

            @pl.when(spot == 0)
            def _():
                def wait(chunk, carry):
                    self._back(flow, chunk, behind, False).wait_recv()
                    return carry

                lax.fori_loop(0, self.chunks, wait, 0)

                def sent(chunk, carry):
                    self._down(flow, chunk, ahead, True).wait_send()
                    return carry

                lax.fori_loop(max(self.chunks - self.ring, 0), self.chunks, sent, 0)

            @pl.when((spot > 0) & (spot < last))
            def _():
                def sent(chunk, carry):
                    self._down(flow, chunk, ahead, False).wait_send()
                    self._back(flow, chunk, behind, False).wait_send()
                    return carry

                lax.fori_loop(0, self.chunks, sent, 0)

            @pl.when(spot == last)
            def _():
                def sent(chunk, carry):
                    self._back(flow, chunk, behind, True).wait_send()
                    self._keep(flow, chunk).wait()
                    return carry

                lax.fori_loop(0, self.chunks, sent, 0)


class Everyone:
    def __init__(self, n_dp, n_mp, mine, slots, send_sems, recv_sems):
        self.n, self.n_mp = n_dp * n_mp, n_mp
        self.me = lax.axis_index("dp") * n_mp + lax.axis_index("mp")
        self.mine, self.slots, self.send, self.recv = mine, slots, send_sems, recv_sems

    def _to(self, distance):
        to = lax.rem(self.me + distance, self.n)
        return {"dp": to // self.n_mp, "mp": lax.rem(to, self.n_mp)}

    def _copy(self, distance):
        return pltpu.make_async_remote_copy(
            self.mine, self.slots.at[self.me], self.send.at[distance - 1], self.recv.at[distance - 1],
            device_id=self._to(distance), device_id_type=MESH,
        )

    def greet(self):
        barrier = pltpu.get_barrier_semaphore()

        def signal(distance, carry):
            pl.semaphore_signal(barrier, inc=1, device_id=self._to(distance), device_id_type=MESH)
            return carry

        lax.fori_loop(1, self.n, signal, 0)
        pl.semaphore_wait(barrier, self.n - 1)

    def start(self):
        def start(distance, carry):
            self._copy(distance).start()
            return carry

        self.slots[self.me] = self.mine[...]
        lax.fori_loop(1, self.n, start, 0)

    def finish(self):
        def wait(distance, carry):
            self._copy(distance).wait()
            return carry

        lax.fori_loop(1, self.n, wait, 0)
        return jnp.sum(self.slots[...], axis=0)


def moments(upstream, first_moment, second_moment, master, decay):
    first_new = first_decay * first_moment + (1.0 - first_decay) * upstream
    second_new = second_decay * second_moment + (1.0 - second_decay) * upstream * upstream
    direction = (
        first_new
        / (1.0 - first_decay**STEP)
        / (jnp.sqrt(second_new / (1.0 - second_decay**STEP)) + epsilon)
        + decay * master
    )
    return (first_new, second_new, direction)


def tensors(inner, outer, expand, shrink, norms):
    found = [inner.at[a, c] for a in range(2) for c in range(3)]
    found += [outer.at[0], outer.at[1], expand, shrink]
    found += [norms.at[pl.ds(row, 1)] for row in range(6)]
    return list(zip(found, [weight_decay] * 10 + [0.0] * 6))


def square_row(squares, share):
    lane = lax.broadcasted_iota(jnp.int32, (1, 128), 1)
    row = jnp.zeros((1, 128), jnp.float32)
    for index, values in enumerate(squares):
        total = jnp.sum(jnp.sum(values, axis=0, keepdims=True), axis=1, keepdims=True)
        row = jnp.where(lane == index, total * share if index >= 10 else total, row)
    return row


def update_kernel(split, *refs):
    (
        both_ref, layer_ref, sums_ref, grads, weights, firsts, seconds,
        states_ref, input_ref, output_ref, table_ref, new_weights, new_firsts, new_seconds,
        both, layer, wide, loads, stores,
    ) = (
        *refs[:3], refs[3:8], refs[8:13], refs[13:18], refs[18:23],
        *refs[23:27], refs[27:32], refs[32:37], refs[37:42], *refs[42:],
    )
    size, columns = both.shape[2], both.shape[3]
    chunks = both.shape[1]
    pieces, row = [], 0
    for source, held, first, count, target, start in (
        (both_ref.at[0], both.at[0], 0, split, states_ref, 0),
        (both_ref.at[1], both.at[1], 0, split, states_ref, split * size),
        (both_ref.at[0], both.at[0], split, chunks - split, input_ref, 0),
        (both_ref.at[1], both.at[1], split, chunks - split, input_ref, (chunks - split) * size),
        (layer_ref, layer, 0, layer_ref.shape[0], output_ref, 0),
    ):
        span = pl.ds(first, count)
        length = count * source.shape[1]
        load = pltpu.make_async_copy(source.at[span], held.at[span], loads.at[len(pieces)])
        store = pltpu.make_async_copy(
            wide.at[pl.ds(row, length)], target.at[pl.ds(start, length)], stores.at[len(pieces)]
        )
        pieces.append((load, store, held, first, count, row))
        row += length
    for piece in pieces:
        piece[0].start()
    for load, store, held, first, count, row in pieces:
        load.wait()
        length = held.shape[1]
        for index in range(count):
            wide[row + index * length : row + (index + 1) * length, :] = f32(held[first + index])
        store.start()
    lane = lax.broadcasted_iota(jnp.int32, (1, 128), 1)
    counts = jnp.where(lane < 8, float(D * D), jnp.where(lane < 10, float(D * FF), float(D)))
    weight_norm = jnp.sqrt(sums_ref[0:1, :] / counts)
    update_norm = jnp.sqrt(sums_ref[1:2, :] / counts)
    trust = weight_norm / (update_norm + epsilon)
    table_ref[...] = jnp.concatenate([weight_norm, update_norm, trust], axis=0)[:, :16]
    groups = [tensors(*group) for group in (grads, weights, firsts, seconds, new_weights, new_firsts, new_seconds)]
    for index, parts in enumerate(zip(*groups)):
        grad, weight, first, second, new_weight, new_first, new_second = [part[0] for part in parts]
        ratio = jnp.sum(jnp.where(lane == index, trust, 0.0), axis=1, keepdims=True)
        master = weight[...]
        first_new, second_new, direction = moments(
            grad[...], first[...], second[...], master, parts[0][1]
        )
        new_first[...] = first_new
        new_second[...] = second_new
        new_weight[...] = master - learn_rate * ratio * direction
    for piece in pieces:
        piece[1].wait()


def update(both, layer, source_rows, sums, grads, weights, firsts, seconds):
    shape = lambda values: jax.ShapeDtypeStruct(values.shape, jnp.float32)
    results = [shape(values) for values in weights]
    size, columns = both.shape[2:]
    split = source_rows // (2 * size)
    total = layer.shape[0] * layer.shape[1]
    wide = lambda rows: jax.ShapeDtypeStruct((rows, columns), jnp.float32)
    dma = pltpu.SemaphoreType.DMA((5,))
    return pl.pallas_call(
        partial(update_kernel, split),
        out_shape=[wide(source_rows), wide(total), wide(total)]
        + [jax.ShapeDtypeStruct((3, 16), jnp.float32)]
        + results * 3,
        in_specs=[ANYWHERE] * 2 + [IN_VMEM] * 21,
        out_specs=[ANYWHERE] * 3 + [IN_VMEM] * 16,
        scratch_shapes=[
            pltpu.VMEM(both.shape, jnp.bfloat16),
            pltpu.VMEM(layer.shape, jnp.bfloat16),
            pltpu.VMEM((source_rows + 2 * total, columns), jnp.float32),
            dma, dma,
        ],
        compiler_params=pltpu.CompilerParams(vmem_limit_bytes=VMEM_LIMIT),
        name="update",
    )(both, layer, sums, *grads, *weights, *firsts, *seconds)


def finish_kernel(
    n, side, units, width, prefix_ref, q_hbm, k_hbm, v_hbm, o_hbm, row_sums_ref,
    near_hbm, x_hbm, cross_dk_ref, cross_dv_ref, dq_slots_ref, mixed_slots_ref, inverse_ref, norms_ref, norm_rows_ref,
    half_a_ref, half_b_ref, bundle_ref, second_hbm, hidden_hbm, normed_hbm, cross_wo_ref, source_grad_ref, *refs,
):
    states, refs = refs[:15], refs[15:]
    out_ref, sums_ref, grads, refs = refs[0], refs[1], refs[2:7], refs[7:]
    (
        q_ref, k_ref, v_ref, o_ref, near_ref, x_ref, late_sems, source_ref, source_sem, do_ref, first_ref, feed_ref, weight_ref, blocks, early_sems, group_sem,
        own_sem, send_out, recv_out, dq_ref, dk_ref, dv_ref, query_acc, delta, master_sems, inner, stage, far_recv, group_send,
        far_send_sem, far_recv_sem, mine, slots, everyone_send, everyone_recv, *scratch,
    ) = refs
    n_dp = 2 * side * side
    p = Place(n, side)
    everyone = Everyone(n_dp, n, mine, slots, everyone_send, everyone_recv)

    me = p.z
    own_heads = (dq_ref, dk_ref, dv_ref)
    size, model = first_ref.shape
    rows = inner.shape[3]
    per_group = 4
    group_rows = per_group * out_ref.shape[2]
    source_groups = cross_dk_ref.shape[0] // (2 * group_rows)

    def make(flow, group):
        if group < source_groups:
            spot = pl.ds((flow * source_groups + group) * group_rows, group_rows)
            made = source_ref[...].reshape(model, 2 * width)
            return dot(cross_dk_ref[spot, :], made[:, :width], NT) + dot(
                cross_dv_ref[spot, :], made[:, width:], NT
            )
        tokens = x_ref.shape[0]
        start = flow * (tokens // 2) + (group - source_groups) * group_rows
        spot = pl.ds(start, group_rows)
        total = jnp.zeros((group_rows, model), jnp.float32)
        for index, own in enumerate(own_heads):
            total = total + dot(own[spot, :], near_ref[:, index * width : (index + 1) * width], NT)
        here = first_ref[start % size : start % size + group_rows, :]
        return total + jnp.where(me == start // size, here, 0.0)

    fold = Fold(p, make, out_ref, scratch[:7], per_group)
    group_sum = Reduce(p, [cross_wo_ref, source_grad_ref], scratch[7:15])
    weight_sum = Reduce(p, [weight_ref], scratch[15:23])
    inner_sum = Reduce(p, [inner], scratch[23:31])
    halves = Halves(p, half_a_ref, half_b_ref, scratch[31:35])
    line = Line(p, group_send, scratch[35:])

    source_load = pltpu.make_async_copy(
        bundle_ref.at[:, :, :, :, pl.ds(2 * n * width + 128, 2 * width)], source_ref, source_sem
    )
    source_load.start()
    late_loads = [
        pltpu.make_async_copy(source, target, late_sems.at[index])
        for index, (source, target) in enumerate(
            zip((q_hbm, k_hbm, v_hbm, o_hbm, near_hbm, x_hbm), (q_ref, k_ref, v_ref, o_ref, near_ref, x_ref))
        )
    ]
    for load in late_loads:
        load.start()
    weight_loads = [
        pltpu.make_async_copy(
            bundle_ref.at[:, :, :, :, pl.ds(start, n * width)],
            weight_ref.at[:, :, :, :, pl.ds(index * n * width, n * width)], group_sem.at[index],
        )
        for index, start in enumerate((n * width + 128, 0))
    ]
    for load in weight_loads:
        load.start()
    everyone.greet()
    group_sum.core_start()
    halves.start()
    source_load.wait()
    ticks = iter(range(fold.ticks))

    def advance(count):
        for _ in range(count):
            fold.tick(next(ticks))

    advance(2)

    def store_by_place(target, first, columns, value, start):
        for row in range(0, value.shape[0], rows):
            flat = (start + row) // rows
            y, x, core = flat // (2 * side), flat // 2 % side, flat % 2
            target[y, x, core, :, first : first + columns] = value[row : row + rows]

    def held_weight(group, second):
        cols = pl.ds(pl.multiple_of((n * second + group) * width, width), width)
        return weight_ref[:, :, :, :, cols].reshape(model, width)

    def cross_to_self(rows_f32):
        second_load = pltpu.make_async_copy(second_hbm, first_ref, early_sems.at[0])
        normed_load = pltpu.make_async_copy(normed_hbm, rows_f32, early_sems.at[1])
        hidden_load = pltpu.make_async_copy(hidden_hbm, rows_f32, early_sems.at[2])
        second_load.start()
        normed_load.start()
        second_load.wait()
        for load in weight_loads:
            load.wait()
        upstream = first_ref[...]
        for group in range(n):
            upstream = upstream + dot(dq_slots_ref[group], held_weight(group, 0), NT)
        normed_load.wait()
        first, gain_one, bias_one = norm_back(
            upstream, rows_f32[...], inverse_ref[:, 0:1], norms_ref[0:1, :]
        )
        hidden_load.start()
        first_ref[...] = first
        low = bf16(first)
        sent = tokens_to_heads(
            n, lambda group: dot(low, held_weight(group, 1)), blocks, do_ref, send_out, recv_out, own_sem
        )
        advance(1)
        hidden_load.wait()
        hidden_low = bf16(rows_f32[...])
        for group in range(n):
            at = 2 * group * width
            store_by_place(weight_ref, at, width, bf16(dot(hidden_low, dq_slots_ref[group], TN)), 0)
            store_by_place(
                weight_ref, at + width, width, bf16(dot(low, mixed_slots_ref[group], TN)), 0
            )
        rows_all = jnp.concatenate(
            [
                gain_one, norm_rows_ref[0:2, :], bias_one, norm_rows_ref[2:4, :],
                jnp.zeros((122, model), jnp.float32),
            ],
            axis=0,
        )
        store_by_place(weight_ref, 2 * n * width, 128, bf16(rows_all.T), 0)
        advance(1)
        for copy in sent:
            copy.wait()

    pl.run_scoped(cross_to_self, pltpu.VMEM((size, model), jnp.float32))
    weight_sum.core_start()
    feed_ref[...] = bf16(halves.total())
    far = {"mp": lax.rem(me + n // 2, n)}
    far_copies = [
        push(
            feed_ref.at[:, pl.ds((2 * index + 1) * units, units)],
            far_recv.at[:, pl.ds(index * units, units)],
            far_send_sem.at[index], far_recv_sem.at[index], far,
        )
        for index in range(2)
    ]
    group_sum.core_finish(stage)
    group_sum.first_start()
    advance(1)
    weight_sum.core_finish(stage)
    weight_sum.first_start()
    for load in late_loads:
        load.wait()
    backward_delta(do_ref, o_ref, delta)
    query_acc[...] = jnp.zeros_like(query_acc)
    key_block = 256

    def self_backward(index, heads):
        backward_block(
            True, key_block, index, heads, prefix_ref, q_ref, k_ref, v_ref, do_ref, row_sums_ref, delta,
            query_acc, dk_ref, dv_ref,
        )

    for index in range(x_ref.shape[0] // key_block):
        for heads in ((0, 1), (2, 3)):
            self_backward(index, heads)
            advance(1)
    dq_ref[...] = bf16(query_acc[...])

    per = 256
    for start in range(0, model, per):
        turned = x_ref[:, start : start + per]
        for index, own in enumerate(own_heads):
            store_by_place(inner, index * width, width, bf16(dot(turned, own[...], TN)), start)
    inner_sum.core_start()
    advance(1)
    inner_sum.core_finish(stage)
    inner_sum.first_start()
    advance(2)
    group_sum.first_finish()
    group_sum.second_start()
    weight_sum.first_finish()
    weight_sum.second_start()
    advance(1)
    advance(1)
    inner_sum.first_finish()
    inner_sum.second_start()
    advance(1)
    group_sum.second_wait()
    weight_sum.second_wait()
    whole = n * width
    for group in range(n):
        group_send[group, :, :width] = bf16(
            group_sum.total(slice(group * width, (group + 1) * width))
        )
        start = 2 * group * width
        group_send[group, :, width : 3 * width] = bf16(
            weight_sum.total(slice(start, start + 2 * width))
        )
        group_send[group, :, 3 * width :] = bf16(
            weight_sum.total(slice(2 * whole, 2 * whole + 128))
        )
    line.step(0)
    advance(2)

    def optimizer_sums(*masters):
        master_loads = [
            pltpu.make_async_copy(source, target, master_sems.at[index])
            for index, (source, target) in enumerate(zip(states, masters))
        ]
        for load in master_loads:
            load.start()
        grad_inner, grad_outer, grad_expand, grad_shrink, grad_norms = grads
        inner_sum.second_wait()
        for index in range(3):
            grad_inner[0, index] = inner_sum.total(slice(index * width, (index + 1) * width))
        start = whole
        for index in range(2):
            grad_inner[1, index + 1] = group_sum.total(
                slice(start + index * width, start + (index + 1) * width)
            )
        line.step(1)
        for load in master_loads:
            load.wait()
        weights, firsts, seconds = (tensors(*masters[index : index + 5]) for index in (0, 5, 10))
        share = 1.0 / n
        mine[...] = jnp.zeros(mine.shape, jnp.float32)
        mine[0:1, :] = square_row([ref[...] * ref[...] for ref, _ in weights], share)
        advance(2)
        line.step(2)
        for copy in far_copies:
            copy.wait_recv()
        grad_shrink[...] = (f32(feed_ref[:, :units]) + f32(far_recv[:, :units])).T
        grad_expand[...] = f32(feed_ref[:, 2 * units : 3 * units]) + f32(far_recv[:, units:])
        advance(2)
        line.finish()
        received = lambda cols: f32(group_send[me, :, cols])
        grad_outer[1] = received(slice(0, width)).T
        grad_inner[1, 0] = received(slice(width, 2 * width))
        grad_outer[0] = received(slice(2 * width, 3 * width)).T
        grad_norms[...] = received(slice(3 * width, 3 * width + 128)).T[:6, :]

        def direction_square(grad, first, second, weight):
            step = moments(grad[0][...], first[0][...], second[0][...], weight[0][...], weight[1])[2]
            return step * step

        mine[1:2, :] = square_row(
            [direction_square(*group) for group in zip(tensors(*grads), firsts, seconds, weights)], share
        )
        everyone.start()
        advance(4)
        sums_ref[...] = everyone.finish()

    pl.run_scoped(optimizer_sums, *[pltpu.VMEM(source.shape, jnp.float32) for source in states])
    for tick in ticks:
        fold.tick(tick)
    fold.finish()
    for copy in far_copies:
        copy.wait_send()
    for batch in (group_sum, weight_sum, inner_sum):
        batch.finish()


def finish(
    n_dp, n_mp, prefix, projections, mixed, row_sums, near, tokens, source_heads, dq_slots, mixed_slots,
    inverse, norms, norm_rows, halves, bundle, second, hidden, normed, cross_wo, source_grad, states,
):
    side = round((n_dp // 2) ** 0.5)
    total, width = mixed.shape
    size, model = second.shape
    rows = model // n_dp
    half, feed_columns = halves[0].shape[1:]
    units = feed_columns // 4
    low, wide = jnp.bfloat16, jnp.float32
    shape = jax.ShapeDtypeStruct
    dma = pltpu.SemaphoreType.DMA
    by_place = lambda values: values.reshape(side, side, 2, rows, values.shape[1])
    early = [by_place(values) for values in (cross_wo, source_grad)]
    columns = sum(values.shape[4] for values in early)
    group_bundle = 3 * width + 128
    devices = n_dp * n_mp
    chunk_rows = 64
    chunks = (total + source_heads[0].shape[0]) // (2 * chunk_rows)
    weight_columns = 2 * n_mp * width + 128
    both, sums, *grads = pl.pallas_call(
        partial(finish_kernel, n_mp, side, units, width),
        out_shape=[shape((2, chunks, chunk_rows, model), low), shape((8, 128), wide)]
        + [shape(values.shape, wide) for values in states[:5]],
        in_specs=[pl.BlockSpec(memory_space=pltpu.SMEM)]
        + [ANYWHERE] * 4
        + [IN_VMEM]
        + [ANYWHERE] * 2
        + [IN_VMEM] * 9
        + [ANYWHERE] * (6 + len(states)),
        out_specs=[ANYWHERE] + [IN_VMEM] * 6,
        scratch_shapes=[
            *[pltpu.VMEM((total, width), low)] * 4,
            pltpu.VMEM(near.shape, low),
            pltpu.VMEM(tokens.shape, low),
            dma((6,)),
            pltpu.VMEM((side, side, 2, rows, 2 * width), low),
            dma,
            pltpu.VMEM((total, width), low),
            pltpu.VMEM((size, model), wide),
            pltpu.VMEM((rows, feed_columns), low),
            pltpu.VMEM((side, side, 2, rows, weight_columns), low),
            pltpu.VMEM((n_mp, size, width), low),
            dma((3,)), dma((2,)), dma, dma((n_mp - 1,)), dma((n_mp - 1,)),
            *[pltpu.VMEM((total, width), low)] * 3,
            pltpu.VMEM((total, width), wide),
            pltpu.VMEM((8, total), wide),
            dma((len(states),)),
            pltpu.VMEM((side, side, 2, rows, 3 * width), low),
            pltpu.VMEM((2, rows, max(columns, weight_columns)), low),
            pltpu.VMEM((rows, 2 * units), low),
            pltpu.VMEM((n_mp, rows, group_bundle), low),
            dma((2,)), dma((2,)),
            pltpu.VMEM((8, 128), wide),
            pltpu.VMEM((devices, 8, 128), wide),
            dma((devices - 1,)), dma((devices - 1,)),
            *Fold.scratch(chunks, chunk_rows, model),
            *Reduce.scratch(side, rows, columns, 2),
            *Reduce.scratch(side, rows, weight_columns, 1),
            *Reduce.scratch(side, rows, 3 * width, 1),
            *Halves.scratch(side, half, feed_columns),
            *Line.scratch(n_mp, rows, group_bundle),
        ],
        compiler_params=pltpu.CompilerParams(
            collective_id=5, has_side_effects=True, vmem_limit_bytes=VMEM_LIMIT
        ),
        cost_estimate=pl.CostEstimate(flops=10**10, bytes_accessed=1 << 20, transcendentals=0),
        name="finish",
    )(
        prefix, *projections, mixed, row_sums, near, tokens, *source_heads, dq_slots, mixed_slots, inverse,
        norms, norm_rows, *halves, by_place(bundle), second, hidden, normed, *early, *states,
    )
    return both, sums, grads


def on_device(
    inputs,
    encoder,
    prefix,
    cotangent,
    inner_weights,
    inner_first,
    inner_second,
    outer_weights,
    outer_first,
    outer_second,
    expand_weights,
    expand_first,
    expand_second,
    shrink_weights,
    shrink_first,
    shrink_second,
    norm_params,
    norm_first,
    norm_second,
):
    n_dp, n_mp = lax.axis_size("dp"), lax.axis_size("mp")
    seq_count, seq_len, model = inputs.shape
    tokens = inputs.reshape(seq_len, model)
    states = encoder.reshape(-1, model)
    rows, width = inner_weights.shape[2:]
    units = expand_weights.shape[1]

    flat = lambda values: values.reshape(6, rows)
    outer_t, shrink_t, near, bundle, home, self_q, self_k, self_v, self_mixed, self_sums, self_slots = front(
        n_dp, n_mp, prefix, inner_weights, outer_weights, flat(norm_params), expand_weights, shrink_weights, tokens
    )
    by_rows = lambda values: values.reshape(model, values.shape[-1])
    near, bundle = by_rows(near), by_rows(bundle)
    (
        hidden_one, normed_one, inverse_one, norms, cross_query, cross_k, cross_v, cross_mixed,
        cross_sums, cross_slots, home, rest,
    ) = middle(n_dp, n_mp, self_slots, bundle, tokens, home, shrink_t, outer_t, states)
    rest = by_rows(rest)
    out_rows, grad_second, cross_dmix, shrink_grad, expand_grad, cross_wo_grad, norm_rows = feed(
        n_mp, cross_slots, rest, home, hidden_one, cotangent.reshape(seq_len, model), norms,
    )
    dq_slots, cross_dk, cross_dv, layer_low, source_grad, *halves = cross_backward(
        n_dp, n_mp, cross_query, cross_k, cross_v, cross_dmix, cross_mixed, cross_sums, out_rows, states,
        shrink_grad, expand_grad,
    )
    weights = [inner_weights, outer_weights, expand_weights, shrink_weights, flat(norm_params)]
    firsts = [inner_first, outer_first, expand_first, shrink_first, flat(norm_first)]
    seconds = [inner_second, outer_second, expand_second, shrink_second, flat(norm_second)]
    both, sums, grads = finish(
        n_dp, n_mp, prefix, (self_q, self_k, self_v), self_mixed, self_sums, near, tokens,
        (cross_dk, cross_dv), dq_slots, self_slots, inverse_one, norms, norm_rows, halves, bundle,
        grad_second, hidden_one, normed_one, cross_wo_grad, source_grad, weights + firsts + seconds,
    )
    encoder_grad, input_grad, layer_out, table, *results = update(
        both, layer_low, states.shape[0], sums, grads, weights, firsts, seconds
    )
    for index in (4, 9, 14):
        results[index] = results[index].reshape(2, 3, rows)
    return (
        layer_out.reshape(seq_count, seq_len, model),
        input_grad.reshape(seq_count, seq_len, model),
        encoder_grad.reshape(seq_count, -1, model),
        *results,
        table,
    )


def solution(mesh):
    placed = (
        P("dp", None, None),
        P("dp", None, None),
        P("dp"),
        P("dp", None, None),
        P(None, None, "dp", "mp"),
        P(None, None, "dp", "mp"),
        P(None, None, "dp", "mp"),
        P(None, "mp", "dp"),
        P(None, "mp", "dp"),
        P(None, "mp", "dp"),
        P("dp", "mp"),
        P("dp", "mp"),
        P("dp", "mp"),
        P("mp", "dp"),
        P("mp", "dp"),
        P("mp", "dp"),
        P(None, None, "dp"),
        P(None, None, "dp"),
        P(None, None, "dp"),
    )
    return jax.shard_map(
        on_device,
        mesh=mesh,
        in_specs=placed,
        out_specs=(
            P("dp", None, None),
            P("dp", None, None),
            P("dp", None, None),
            P(None, None, "dp", "mp"),
            P(None, "mp", "dp"),
            P("dp", "mp"),
            P("mp", "dp"),
            P(None, None, "dp"),
            P(None, None, "dp", "mp"),
            P(None, "mp", "dp"),
            P("dp", "mp"),
            P("mp", "dp"),
            P(None, None, "dp"),
            P(None, None, "dp", "mp"),
            P(None, "mp", "dp"),
            P("dp", "mp"),
            P("mp", "dp"),
            P(None, None, "dp"),
            P(),
        ),
        check_vma=False,
    )
```

```python
from functools import partial

import jax
import jax.numpy as jnp
from jax import lax
from jax.experimental import pallas as pl
from jax.experimental.pallas import tpu as pltpu
from jax.sharding import PartitionSpec as P

D = 1024
HEAD = 64
FF = 4096
STEP = 5

first_decay = 0.5
second_decay = 0.6
learn_rate = 0.5
weight_decay = 0.01
epsilon = 1e-06
norm_eps = 1e-05
mask_fill = -1000000000.0

MESH = pl.DeviceIdType.MESH
ANYWHERE = pl.BlockSpec(memory_space=pl.ANY)
IN_VMEM = pl.BlockSpec(memory_space=pltpu.VMEM)
NN = (((1,), (0,)), ((), ()))
NT = (((1,), (1,)), ((), ()))
TN = (((0,), (0,)), ((), ()))
VMEM_LIMIT = 60 << 20


def dot(left, right, dims=NN):
    return lax.dot_general(left, right, dims, preferred_element_type=jnp.float32)


def bf16(values):
    return values.astype(jnp.bfloat16)


def f32(values):
    return values.astype(jnp.float32)


def layer_norm(values, gain_row, bias_row):
    center = values - jnp.mean(values, axis=-1, keepdims=True)
    spread = jnp.mean(center * center, axis=-1, keepdims=True)
    inverse = lax.rsqrt(spread + norm_eps)
    normed = center * inverse
    return (normed * gain_row + bias_row, normed, inverse)


def norm_back(upstream, normed, inverse, gain_row):
    scaled = upstream * gain_row
    inner = (
        scaled
        - jnp.mean(scaled, axis=-1, keepdims=True)
        - normed * jnp.mean(scaled * normed, axis=-1, keepdims=True)
    )
    return (
        inner * inverse,
        jnp.sum(upstream * normed, axis=0, keepdims=True),
        jnp.sum(upstream, axis=0, keepdims=True),
    )


class Place:
    def __init__(self, n_mp, side):
        self.n, self.side = n_mp, side
        self.z = lax.axis_index("mp")
        dp = lax.axis_index("dp")
        self.core = lax.rem(dp, 2)
        self.x = lax.rem(dp // 2, side)
        self.y = dp // (2 * side)

    def at(self, y, x, core):
        return {"dp": (y * self.side + x) * 2 + core}

    def x_peer(self, distance):
        other = lax.rem(self.x + distance, self.side)
        return other, self.at(self.y, other, self.core)

    def y_peer(self, distance):
        other = lax.rem(self.y + distance, self.side)
        return other, self.at(other, self.x, self.core)

    def sibling(self):
        return self.at(self.y, self.x, 1 - self.core)

    def line(self):
        return [{"mp": lax.rem(self.z + distance, self.n)} for distance in range(1, self.n)]

    def plane(self):
        steps = range(1, self.side)
        return (
            [self.x_peer(step)[1] for step in steps]
            + [self.y_peer(step)[1] for step in steps]
            + [self.sibling()]
        )


def greet(others):
    barrier = pltpu.get_barrier_semaphore()
    for other in others:
        pl.semaphore_signal(barrier, inc=1, device_id=other, device_id_type=MESH)
    pl.semaphore_wait(barrier, len(others))


def push(source, target, send_sem, recv_sem, to):
    copy = pltpu.make_async_remote_copy(
        source, target, send_sem, recv_sem, device_id=to, device_id_type=MESH
    )
    copy.start()
    return copy


def rows_at(index, size):
    return pl.ds(pl.multiple_of(index * size, size), size)


def tokens_to_heads(n, make, blocks, target, send_sems, recv_sems, local_sem):
    me = lax.axis_index("mp")
    size = blocks.shape[1]
    copies = []
    for distance in (*range(1, n), 0):
        to = lax.rem(me + distance, n)
        blocks[to] = bf16(make(to))
        place = target.at[rows_at(me, size)]
        if distance:
            copies.append(
                push(
                    blocks.at[to], place,
                    send_sems.at[distance - 1], recv_sems.at[distance - 1], {"mp": to},
                )
            )
        else:
            copy = pltpu.make_async_copy(blocks.at[to], place, local_sem)
            copy.start()
            copies.append(copy)
    return copies


def load_groups(n, bundle, stride, first, width, target, sems):
    return [
        pltpu.make_async_copy(
            bundle.at[:, pl.ds(group * stride + first, width)], target.at[group], sems.at[group]
        )
        for group in range(n)
    ]


class Give:
    def __init__(self, place, out, sems):
        self.place, self.n, self.me, self.out = place, place.n, place.z, out
        self.half = out.shape[1] // 2
        self.sems = {"right": sems[0:2], "left": sems[2:4]}

    @staticmethod
    def sems(n):
        return [pltpu.SemaphoreType.DMA((2 * (n - 1),))] * 4

    def _copy(self, way, step, part):
        ahead = 1 if way == "right" else -1
        chunk = lax.rem(self.me - ahead * step + self.n, self.n)
        block = self.out.at[chunk, pl.ds(part * self.half, self.half)]
        return pltpu.make_async_remote_copy(
            block, block, self.sems[way][0].at[2 * step + part], self.sems[way][1].at[2 * step + part],
            device_id={"mp": lax.rem(self.me + ahead + self.n, self.n)}, device_id_type=MESH,
        )

    def _spots(self):
        return (("right", self.me), ("left", self.n - 1 - self.me))

    def step(self, step, part):
        for way, spot in self._spots():

            @pl.when((spot >= step) & (spot < self.n - 1))
            def _():
                if step > 0:
                    self._copy(way, step - 1, part).wait_recv()
                self._copy(way, step, part).start()

    def finish(self):
        every = [(step, part) for step in range(self.n - 1) for part in range(2)]
        for way, spot in self._spots():

            @pl.when(spot == self.n - 1)
            def _():
                for step, part in every:
                    self._copy(way, step, part).wait_recv()

            for step, part in every:

                @pl.when((spot >= step) & (spot < self.n - 1))
                def _():
                    self._copy(way, step, part).wait_send()


class Spread:
    def __init__(self, place, home, send_sems, recv_sems):
        self.place, self.home, self.send, self.recv = place, home, send_sems, recv_sems
        self.half = home.shape[3] // 2
        self.copies = {"first": [], "second": [], "core": []}
        self.index = 0

    def _push(self, stage, block, to):
        spot = self.index
        self.index += 1
        self.copies[stage].append(push(block, block, self.send.at[spot], self.recv.at[spot], to))

    def first(self):
        p, half = self.place, self.half
        for step in range(1, p.side):
            own = self.home.at[p.y, p.x, p.core]
            self._push("first", own.at[pl.ds(0, half)], p.x_peer(step)[1])
            self._push("first", own.at[pl.ds(half, half)], p.y_peer(step)[1])

    def second(self):
        p, half = self.place, self.half
        for copy in self.copies["first"]:
            copy.wait_recv()
        for step in range(1, p.side):
            self._push(
                "second", self.home.at[p.y, :, p.core, pl.ds(0, half)], p.y_peer(step)[1]
            )
            self._push(
                "second", self.home.at[:, p.x, p.core, pl.ds(half, half)], p.x_peer(step)[1]
            )

    def core(self):
        for copy in self.copies["second"]:
            copy.wait_recv()
        self._push("core", self.home.at[:, :, self.place.core], self.place.sibling())

    def finish(self):
        for copy in self.copies["core"] or self.copies["second"] or self.copies["first"]:
            copy.wait_recv()
        for stage in self.copies.values():
            for copy in stage:
                copy.wait_send()

    @staticmethod
    def sems(side):
        return pltpu.SemaphoreType.DMA((4 * (side - 1) + 1,))


class Reduce:
    def __init__(self, place, sources, scratch):
        self.place, self.sources = place, sources
        self.keep, self.first_a, self.first_b, *rest = scratch
        *rest, self.local, self.send, self.recv = rest
        if rest:
            self.second_a, self.second_b = rest
        self.half = self.keep.shape[2] // 2
        self.copies = {"core": [], "first": [], "second": []}
        self.index = 0

    @staticmethod
    def scratch(side, rows, columns, sources, second=True):
        low, dma = jnp.bfloat16, pltpu.SemaphoreType.DMA
        block = pltpu.VMEM((side, side, rows, columns), low)
        first = pltpu.VMEM((side - 1, side, rows // 2, columns), low)
        rest = pltpu.VMEM((side - 1, rows // 2, columns), low)
        count = sources + 4 * (side - 1)
        seconds = [rest, rest] if second else []
        return [
            block, first, first, *seconds, dma((2, sources)), dma((count,)), dma((count,)),
        ]

    def _push(self, stage, source, target, to, begin=True):
        copy = pltpu.make_async_remote_copy(
            source, target, self.send.at[self.index], self.recv.at[self.index],
            device_id=to, device_id_type=MESH,
        )
        self.index += 1
        self.copies[stage].append(copy)
        if begin:
            copy.start()

    def core_start(self, begin=True):
        p, column = self.place, 0
        self.index, self.copies["core"] = 0, []
        for source in self.sources:
            cols = pl.ds(column, source.shape[4])
            column += source.shape[4]
            self._push(
                "core", source.at[:, :, 1 - p.core], self.keep.at[:, :, :, cols], p.sibling(), begin
            )

    def _load(self, stage, index):
        y, x = index // self.place.side, index % self.place.side
        column, loads = 0, []
        for spot, source in enumerate(self.sources):
            cols = pl.ds(column, source.shape[4])
            column += source.shape[4]
            loads.append(
                pltpu.make_async_copy(
                    source.at[y, x, self.place.core], stage.at[index % 2, :, cols],
                    self.local.at[index % 2, spot],
                )
            )
        return loads

    def core_finish(self, stage):
        side, keep, columns = self.place.side, self.keep, self.keep.shape[3]
        for load in self._load(stage, 0):
            load.start()
        for copy in self.copies["core"]:
            copy.wait_recv()
        for index in range(side * side):
            if index + 1 < side * side:
                for load in self._load(stage, index + 1):
                    load.start()
            for load in self._load(stage, index):
                load.wait()
            y, x = index // side, index % side
            keep[y, x] = bf16(f32(keep[y, x]) + f32(stage[index % 2, :, :columns]))

    def first_start(self, begin=True):
        p, half = self.place, self.half
        self.index, self.copies["first"] = len(self.sources), []
        top, bottom = pl.ds(0, half), pl.ds(half, half)
        for step in range(1, p.side):
            other, to = p.x_peer(step)
            self._push("first", self.keep.at[:, other, top], self.first_a.at[step - 1], to, begin)
            other, to = p.y_peer(step)
            self._push("first", self.keep.at[other, :, bottom], self.first_b.at[step - 1], to, begin)

    def first_finish(self):
        p, half, keep = self.place, self.half, self.keep
        for copy in self.copies["first"]:
            copy.wait_recv()

        def add(index, carry):
            total = f32(keep[index, p.x, :half, :])
            for step in range(p.side - 1):
                total = total + f32(self.first_a[step, index])
            keep[index, p.x, :half, :] = bf16(total)
            total = f32(keep[p.y, index, half:, :])
            for step in range(p.side - 1):
                total = total + f32(self.first_b[step, index])
            keep[p.y, index, half:, :] = bf16(total)
            return carry

        lax.fori_loop(0, p.side, add, 0)

    def halves(self, out_a, out_b):
        p, half, keep = self.place, self.half, self.keep
        for index in range(p.side):
            out_a[index] = keep[index, p.x, :half, :]
            out_b[index] = keep[p.y, index, half:, :]

    def second_start(self):
        p, half = self.place, self.half
        top, bottom = pl.ds(0, half), pl.ds(half, half)
        for step in range(1, p.side):
            other, to = p.y_peer(step)
            self._push("second", self.keep.at[other, p.x, top], self.second_a.at[step - 1], to)
            other, to = p.x_peer(step)
            self._push("second", self.keep.at[p.y, other, bottom], self.second_b.at[step - 1], to)

    def second_wait(self):
        for copy in self.copies["second"]:
            copy.wait_recv()

    def total(self, cols):
        p, half = self.place, self.half
        top, bottom = f32(self.keep[p.y, p.x, :half, cols]), f32(self.keep[p.y, p.x, half:, cols])
        for step in range(p.side - 1):
            top = top + f32(self.second_a[step, :, cols])
            bottom = bottom + f32(self.second_b[step, :, cols])
        return jnp.concatenate([top, bottom], axis=0)

    def finish(self):
        for stage in self.copies.values():
            for copy in stage:
                copy.wait_send()


class Halves:
    def __init__(self, place, part_a, part_b, scratch):
        self.place, self.parts = place, (part_a, part_b)
        self.landed, (self.send, self.recv) = scratch[:2], scratch[2:]

    @staticmethod
    def scratch(side, half, columns):
        dma = pltpu.SemaphoreType.DMA((2 * (side - 1),))
        return [pltpu.VMEM((side - 1, half, columns), jnp.bfloat16)] * 2 + [dma, dma]

    def start(self):
        p = self.place
        self.copies = []
        for step in range(1, p.side):
            for index, (other, to) in enumerate((p.y_peer(step), p.x_peer(step))):
                spot = 2 * (step - 1) + index
                self.copies.append(
                    push(
                        self.parts[index].at[other], self.landed[index].at[step - 1],
                        self.send.at[spot], self.recv.at[spot], to,
                    )
                )

    def total(self):
        for copy in self.copies:
            copy.wait()
        sums = []
        for index, mine in enumerate((self.place.y, self.place.x)):
            total = f32(self.parts[index][mine])
            for step in range(self.place.side - 1):
                total = total + f32(self.landed[index][step])
            sums.append(total)
        return jnp.concatenate(sums, axis=0)


def forward_rows(masked, start, block, prefix_ref, q_ref, k_ref, v_ref, mixed_ref, sums_ref):
    width = q_ref.shape[1]
    keys = k_ref.shape[0]
    if masked:
        keys = max(keys // 2, start + block)
    lane = lax.broadcasted_iota(jnp.int32, (block, width), 1) // HEAD
    span = slice(start, start + block) if masked else rows_at(start, block)
    query = q_ref[span, :] * jnp.bfloat16(HEAD**-0.5)
    key_rows, value_rows = k_ref[:keys, :], v_ref[:keys, :]
    if masked:
        query_ids = start + lax.broadcasted_iota(jnp.int32, (block, keys), 0)
        key_ids = lax.broadcasted_iota(jnp.int32, (block, keys), 1)
        allowed = (key_ids <= query_ids) | (key_ids < prefix_ref[0])
    mixed = jnp.zeros((block, width), jnp.float32)
    slot = lax.broadcasted_iota(jnp.int32, (block, 128), 1)
    table = jnp.zeros((block, 128), jnp.float32)
    for head in range(width // HEAD):
        scores = dot(jnp.where(lane == head, query, jnp.bfloat16(0)), key_rows, NT)
        if masked:
            scores = jnp.where(allowed, scores, mask_fill)
        row_max = jnp.max(scores, axis=1, keepdims=True)
        powered = jnp.exp(scores - row_max)
        totals = jnp.sum(powered, axis=1, keepdims=True)
        part = dot(bf16(powered), value_rows) * (1.0 / totals)
        mixed = jnp.where(lane == head, part, mixed)
        table = jnp.where(slot == head, row_max + jnp.log(totals), table)
    mixed_ref[span, :] = bf16(mixed)
    sums_ref[:, span] = table.T[:8, :]


def backward_delta(do_ref, o_ref, delta):
    width = do_ref.shape[1]
    product = f32(do_ref[...]) * f32(o_ref[...])
    row = lax.broadcasted_iota(jnp.int32, (8, width), 0)
    col = lax.broadcasted_iota(jnp.int32, (8, width), 1) // HEAD
    pick = jnp.where(row == col, 1.0, 0.0).astype(jnp.float32)
    delta[...] = lax.dot_general(
        pick, product, NT, precision=lax.Precision.HIGHEST, preferred_element_type=jnp.float32
    )


def backward_block(
    masked, block, index, heads, prefix_ref, q_ref, k_ref, v_ref, do_ref, sums_ref, delta, acc, dk_ref, dv_ref
):
    total, width = q_ref.shape
    factor = HEAD**-0.5
    rows = slice(index * block, (index + 1) * block)
    first = index * block if masked and index * block >= total // 2 else 0
    count = total - first
    lane = lax.broadcasted_iota(jnp.int32, (block, width), 1) // HEAD
    query, grad_rows = q_ref[first:, :], do_ref[first:, :]
    scaled_keys = k_ref[rows, :] * jnp.bfloat16(factor)
    value_rows = v_ref[rows, :]
    if masked:
        query_ids = first + lax.broadcasted_iota(jnp.int32, (block, count), 1)
        key_ids = index * block + lax.broadcasted_iota(jnp.int32, (block, count), 0)
        allowed = (key_ids <= query_ids) | (key_ids < prefix_ref[0])
    key_grad = jnp.zeros((block, width), jnp.float32)
    value_grad = jnp.zeros((block, width), jnp.float32)
    query_grad = jnp.zeros((count, width), jnp.float32)
    for head in heads:
        own_keys = jnp.where(lane == head, scaled_keys, jnp.bfloat16(0))
        scores = dot(own_keys, query, NT)
        if masked:
            scores = jnp.where(allowed, scores, mask_fill)
        probs = jnp.exp(scores - sums_ref[head : head + 1, first:])
        prob_grad = dot(jnp.where(lane == head, value_rows, jnp.bfloat16(0)), grad_rows, NT)
        score_grad = bf16(probs * (prob_grad - delta[head : head + 1, first:]))
        value_grad = jnp.where(lane == head, dot(bf16(probs), grad_rows), value_grad)
        key_grad = jnp.where(lane == head, dot(score_grad, query), key_grad)
        query_grad = query_grad + dot(score_grad, own_keys, TN)
    acc[first:, :] += query_grad
    mine = (lane >= heads[0]) & (lane <= heads[-1])
    key_grad, value_grad = bf16(key_grad * factor), bf16(value_grad)
    if heads[0] > 0:
        key_grad = jnp.where(mine, key_grad, dk_ref[rows, :])
        value_grad = jnp.where(mine, value_grad, dv_ref[rows, :])
    dk_ref[rows, :] = key_grad
    dv_ref[rows, :] = value_grad


def cross_backward_kernel(
    n, side, q_ref, k_ref, v_ref, do_ref, o_ref, sums_ref, mine_ref, states_hbm, shrink_ref, expand_ref,
    slots_ref, dk_ref, dv_ref, all_ref, source_ref, half_a_ref, half_b_ref,
    scaled_keys, key_acc, value_acc, delta, blocks, stage, states_ref, states_sem, own_sem, dq_send, dq_recv, *scratch,
):
    p = Place(n, side)
    give = Give(p, all_ref, scratch[:4])
    feed_sum = Reduce(p, [shrink_ref, expand_ref], scratch[4:])
    width = q_ref.shape[1]
    size = blocks.shape[1]
    heads = range(width // HEAD)
    factor = HEAD**-0.5
    own = pltpu.make_async_copy(mine_ref, all_ref.at[p.z], own_sem)
    own.start()
    states_load = pltpu.make_async_copy(states_hbm, states_ref, states_sem)
    states_load.start()
    greet(p.line() + p.plane())
    feed_sum.core_start()
    own.wait()
    give.step(0, 0)
    give.step(0, 1)
    backward_delta(do_ref, o_ref, delta)
    scaled_keys[...] = k_ref[...] * jnp.bfloat16(factor)
    key_acc[...] = jnp.zeros_like(key_acc)
    value_acc[...] = jnp.zeros_like(value_acc)
    lane = lax.broadcasted_iota(jnp.int32, (size, width), 1) // HEAD
    chunk = 512

    def dq_copy(distance):
        to = lax.rem(p.z + distance, n)
        return pltpu.make_async_remote_copy(
            blocks.at[to], slots_ref.at[p.z], dq_send.at[distance - 1], dq_recv.at[distance - 1],
            device_id={"mp": to}, device_id_type=MESH,
        )

    def one_block(step, carry):
        block = lax.rem(p.z + 1 + step, n)
        span = rows_at(block, size)
        query, grad_rows = q_ref[span, :], do_ref[span, :]
        stacked = lambda values: jnp.concatenate(
            [jnp.where(lane == head, values, jnp.bfloat16(0)) for head in heads], axis=0
        )
        across = lambda ref: jnp.concatenate([ref[head : head + 1, span] for head in heads], axis=1)
        own_query, own_grad = stacked(query), stacked(grad_rows)
        row_sums, row_delta = across(sums_ref), across(delta)
        all_grads = jnp.zeros((len(heads) * size, width), jnp.float32)
        for first in range(0, k_ref.shape[0], chunk):
            rows = slice(first, first + chunk)
            if first == 0:
                for later in range(1, n):
                    hop = divmod(later + 1, 2)
                    if hop[0] < n - 1:

                        @pl.when(step == later)
                        def _():
                            give.step(*hop)

            if first == 3 * chunk:

                @pl.when(step == 0)
                def _():
                    feed_sum.core_start(False)
                    feed_sum.core_finish(stage)
                    feed_sum.first_start()


            probs = jnp.exp(dot(scaled_keys[rows, :], own_query, NT) - row_sums)
            prob_grad = dot(v_ref[rows, :], own_grad, NT)
            score_grad = bf16(probs * (prob_grad - row_delta))
            value_acc[rows, :] += dot(bf16(probs), own_grad)
            key_acc[rows, :] += dot(score_grad, own_query)
            all_grads = all_grads + dot(score_grad, scaled_keys[rows, :], TN)
        query_grad = jnp.zeros((size, width), jnp.float32)
        for head in heads:
            query_grad = jnp.where(
                lane == head, all_grads[head * size : (head + 1) * size], query_grad
            )
        blocks[block] = bf16(query_grad)

        @pl.when(step < n - 1)
        def _():
            dq_copy(step + 1).start()

        return carry

    lax.fori_loop(0, n, one_block, 0)
    for later in range(n + 1, 2 * (n - 1)):
        give.step(*divmod(later, 2))
    slots_ref[p.z] = blocks[p.z]
    dk_ref[...] = bf16(key_acc[...] * factor)
    dv_ref[...] = bf16(value_acc[...])
    states_load.wait()
    source_ref[:, :width] = bf16(dot(states_ref[...], dk_ref[...], TN))
    source_ref[:, width:] = bf16(dot(states_ref[...], dv_ref[...], TN))
    feed_sum.core_start(False)
    feed_sum.first_start(False)
    feed_sum.first_finish()
    feed_sum.halves(half_a_ref, half_b_ref)
    feed_sum.finish()
    for distance in range(1, n):
        dq_copy(distance).wait()
    give.finish()


def cross_backward(n_dp, n, query, key_rows, value_rows, grad_out, mixed, sums, mine, states, shrink, expand):
    total, width = query.shape
    keys, model = states.shape
    side = round((n_dp // 2) ** 0.5)
    rows, columns = model // n_dp, shrink.shape[1] + expand.shape[1]
    half = (side, rows // 2, columns)
    by_place = lambda values: values.reshape(side, side, 2, rows, values.shape[1])
    low, wide = jnp.bfloat16, jnp.float32
    shape = jax.ShapeDtypeStruct
    dma = pltpu.SemaphoreType.DMA
    return pl.pallas_call(
        partial(cross_backward_kernel, n, side),
        out_shape=[
            shape((n, total // n, width), low),
            shape((keys, width), low),
            shape((keys, width), low),
            shape((n,) + mine.shape, low),
            shape((model, 2 * width), low),
            shape(half, low),
            shape(half, low),
        ],
        in_specs=[IN_VMEM] * 7 + [ANYWHERE] * 3,
        out_specs=[IN_VMEM] * 3 + [ANYWHERE] + [IN_VMEM] * 3,
        scratch_shapes=[
            pltpu.VMEM((keys, width), low),
            pltpu.VMEM((keys, width), wide),
            pltpu.VMEM((keys, width), wide),
            pltpu.VMEM((8, total), wide),
            pltpu.VMEM((n, total // n, width), low),
            pltpu.VMEM((2, rows, columns), low),
            pltpu.VMEM((keys, model), low),
            dma, dma, dma((n - 1,)), dma((n - 1,)),
            *Give.sems(n),
            *Reduce.scratch(side, rows, columns, 2, second=False),
        ],
        compiler_params=pltpu.CompilerParams(
            vmem_limit_bytes=VMEM_LIMIT, collective_id=6, has_side_effects=True
        ),
        cost_estimate=pl.CostEstimate(flops=40 * total * keys * width, bytes_accessed=1 << 20, transcendentals=0),
        name="cross_backward",
    )(
        query, key_rows, value_rows, grad_out, mixed, sums, mine, states, by_place(shrink), by_place(expand),
    )


def front_kernel(
    n, side, prefix_ref, inner_ref, outer_in_ref, norm_in_ref, expand_ref, shrink_in_ref, x_ref, outer_ref, shrink_ref,
    near_ref, home_ref, feed_home_ref, q_ref, k_ref, v_ref, mixed_ref, sums_ref, slots_ref,
    block_near, block_line, block_rest, own_sems, near_send, near_recv, home_send, home_recv,
    line_send, line_recv, far_send, far_recv, mixed_send, mixed_recv,
    block_feed, feed_send, feed_recv, rest_send, rest_recv,
):
    p = Place(n, side)
    width = inner_ref.shape[3]
    units = expand_ref.shape[1]
    if outer_in_ref.shape[1] == width:
        for index in range(2):
            outer_ref[index] = bf16(outer_in_ref[index].T)
        shrink_ref[...] = bf16(shrink_in_ref[...].T)
        norm_row = jnp.concatenate(
            [norm_in_ref[...], jnp.zeros((122, norm_in_ref.shape[1]), jnp.float32)], axis=0
        ).T
    else:
        outer_ref[...] = bf16(outer_in_ref[...])
        shrink_ref[...] = bf16(shrink_in_ref[...])
        norm_row = norm_in_ref[...]
    for index in range(3):
        block_near[:, index * width : (index + 1) * width] = bf16(inner_ref[0, index])
    block_line[:, :width] = bf16(inner_ref[1, 0])
    block_line[:, width : 2 * width] = outer_ref[0]
    for index in range(2):
        block_rest[:, index * width : (index + 1) * width] = bf16(inner_ref[1, index + 1])
    block_rest[:, 2 * width :] = bf16(norm_row)
    norms = block_rest.shape[1] - 2 * width
    whole = n * width
    later = whole + norms
    out_cols = pl.ds(pl.multiple_of(p.z * width, width), width)
    query_cols = pl.ds(pl.multiple_of(later + p.z * width, 128), width)
    spot = home_ref.at[p.y, p.x, p.core]
    near_ref[p.y, p.x, p.core] = block_near[...]
    block_feed[:, :units] = bf16(expand_ref[...])
    block_feed[:, units:] = shrink_ref[...]
    feed_spot = feed_home_ref.at[p.y, p.x, p.core]
    own = [
        pltpu.make_async_copy(source, target, own_sems.at[index])
        for index, (source, target) in enumerate(
            (
                (block_line.at[:, pl.ds(width, width)], spot.at[:, out_cols]),
                (block_line.at[:, pl.ds(0, width)], spot.at[:, query_cols]),
                (block_rest.at[:, pl.ds(2 * width, norms)], spot.at[:, pl.ds(whole, norms)]),
                (block_rest.at[:, pl.ds(0, 2 * width)], spot.at[:, pl.ds(later + whole, 2 * width)]),
                (block_feed, feed_spot.at[:, pl.ds(0, 2 * units)]),
            )
        )
    ]
    for copy in own:
        copy.start()
    greet(p.line() + p.plane())
    near = Spread(p, near_ref, near_send, near_recv)
    first_rest = Spread(p, home_ref.at[:, :, :, :, pl.ds(0, later)], home_send, home_recv)
    rest = Spread(
        p, home_ref.at[:, :, :, :, pl.ds(later, whole + 2 * width)], rest_send, rest_recv
    )
    near.first()
    lines = [
        [
            push(
                block_line.at[:, pl.ds(first, width)], spot.at[:, cols],
                line_send.at[part * (n - 1) + index], line_recv.at[part * (n - 1) + index], other,
            )
            for index, other in enumerate(p.line())
        ]
        for part, (first, cols) in enumerate(((width, out_cols), (0, query_cols)))
    ]
    far = push(
        block_feed.at[:, pl.ds(0, units)], feed_spot.at[:, pl.ds(2 * units, units)], far_send, far_recv,
        {"mp": lax.rem(p.z + n // 2, n)},
    )
    for copy in own:
        copy.wait()
    near.second()
    feed_spread = Spread(
        p, feed_home_ref.at[:, :, :, :, pl.ds(0, 2 * units)], feed_send, feed_recv
    )
    for copy in lines[0]:
        copy.wait_recv()
    first_rest.first()
    near.core()
    for copy in lines[1]:
        copy.wait_recv()
    rest.first()
    near.finish()
    first_rest.second()
    model = x_ref.shape[1]
    weights = near_ref[...].reshape(model, 3 * width)
    for start in range(0, x_ref.shape[0], 256):
        rows = slice(start, start + 256)
        made = bf16(dot(x_ref[rows, :], weights))
        for index, target in enumerate((q_ref, k_ref, v_ref)):
            target[rows, :] = made[:, index * width : (index + 1) * width]
    rest.second()
    feed_spread.first()
    size = x_ref.shape[0] // n

    def mixed_copy(distance):
        to = lax.rem(p.z + distance, n)
        return pltpu.make_async_remote_copy(
            mixed_ref.at[rows_at(to, size)], slots_ref.at[p.z],
            mixed_send.at[distance - 1], mixed_recv.at[distance - 1],
            device_id={"mp": to}, device_id_type=MESH,
        )

    def attend(step, carry):
        block = lax.rem(p.z + 1 + step, n)
        for index in range(n):

            @pl.when(block == index)
            def _():
                forward_rows(
                    True, index * size, size, prefix_ref, q_ref, k_ref, v_ref, mixed_ref, sums_ref
                )

        @pl.when(step < n - 1)
        def _():
            mixed_copy(step + 1).start()

        return carry

    lax.fori_loop(0, n, attend, 0)
    slots_ref[p.z] = mixed_ref[rows_at(p.z, size), :]
    first_rest.core()
    rest.core()
    first_rest.finish()
    rest.finish()
    for distance in range(1, n):
        mixed_copy(distance).wait()
    for copy in (*lines[0], *lines[1]):
        copy.wait_send()
    far.wait()
    feed_spread.finish()


def front(n_dp, n_mp, prefix, inner, outer, norms, expand, shrink, tokens):
    rows, width = inner.shape[2:]
    norm_columns = 128
    if rows % 128:
        outer, shrink = jnp.swapaxes(outer, 1, 2), shrink.T
        norms = jnp.pad(norms.T, ((0, 0), (0, norm_columns - 6)))
    total = tokens.shape[0]
    side = round((n_dp // 2) ** 0.5)
    line = 2 * width
    columns = n_mp * line + 2 * width + norm_columns
    units = expand.shape[1]
    low = jnp.bfloat16
    dma = pltpu.SemaphoreType.DMA
    shape = jax.ShapeDtypeStruct
    return pl.pallas_call(
        partial(front_kernel, n_mp, side),
        out_shape=[
            shape((2, rows, width), low),
            shape((rows, units), low),
            shape((side, side, 2, rows, 3 * width), low),
            shape((side, side, 2, rows, columns), low),
            shape((side, side, 2, rows, 4 * units), low),
            *[shape((total, width), low)] * 4,
            shape((8, total), jnp.float32),
            shape((n_mp, total // n_mp, width), low),
        ],
        in_specs=[pl.BlockSpec(memory_space=pltpu.SMEM)] + [IN_VMEM] * 6,
        out_specs=[IN_VMEM] * 3 + [ANYWHERE, ANYWHERE] + [IN_VMEM] * 6,
        scratch_shapes=[
            pltpu.VMEM((rows, 3 * width), low),
            pltpu.VMEM((rows, line), low),
            pltpu.VMEM((rows, 2 * width + norm_columns), low),
            dma((5,)),
            Spread.sems(side), Spread.sems(side), Spread.sems(side), Spread.sems(side),
            dma((2 * n_mp - 2,)), dma((2 * n_mp - 2,)), dma, dma,
            dma((n_mp - 1,)), dma((n_mp - 1,)),
            pltpu.VMEM((rows, 2 * units), low),
            Spread.sems(side), Spread.sems(side), Spread.sems(side), Spread.sems(side),
        ],
        compiler_params=pltpu.CompilerParams(
            collective_id=0, has_side_effects=True, vmem_limit_bytes=VMEM_LIMIT
        ),
        cost_estimate=pl.CostEstimate(flops=40 * 10**9, bytes_accessed=1 << 20, transcendentals=0),
        name="front",
    )(prefix, inner, outer, norms, expand, shrink, tokens)


def middle_kernel(
    n, side, slots_ref, bundle_ref, x_ref, home_in_ref, states_hbm, shrink_ref, outer_ref,
    hidden_ref, normed_ref, inverse_ref, norm_ref, q_ref, k_ref, v_ref, mixed_ref, sums_ref, cross_slots_ref,
    home_ref, rest_ref,
    wo, wq, norm_columns, source, x_rows, blocks,
    wo_sems, wq_sems, load_sems, q_send, q_recv, mixed_send, mixed_recv, far_send, far_recv,
    feed_send, feed_recv, later_send, later_recv, line_send, line_recv,
    expand_send, expand_recv, shrink_send, shrink_recv, states_ref, states_sem,
):
    p = Place(n, side)
    me = p.z
    size = x_rows.shape[0]
    width = slots_ref.shape[2]
    whole = n * width
    norms = norm_columns.shape[1]
    later = whole + norms
    loads = [
        pltpu.make_async_copy(x_ref.at[rows_at(me, size)], x_rows, load_sems.at[0]),
        pltpu.make_async_copy(bundle_ref.at[:, pl.ds(whole, norms)], norm_columns, load_sems.at[1]),
        pltpu.make_async_copy(
            bundle_ref.at[:, pl.ds(later + whole, 2 * width)], source, load_sems.at[2]
        ),
        *load_groups(n, bundle_ref, width, 0, width, wo, wo_sems),
        *load_groups(n, bundle_ref, width, later, width, wq, wq_sems),
    ]
    for load in loads:
        load.start()
    states_load = pltpu.make_async_copy(states_hbm, states_ref, states_sem)
    states_load.start()
    units = home_ref.shape[4] // 4
    spot = rest_ref.at[p.y, p.x, p.core, :, pl.ds(pl.multiple_of(width * me, width), width)]
    greet(p.line() + p.plane())
    store = pltpu.make_async_copy(outer_ref.at[1], spot, load_sems.at[3])
    store.start()
    line = [
        push(outer_ref.at[1], spot, line_send.at[index], line_recv.at[index], other)
        for index, other in enumerate(p.line())
    ]
    part = lambda first, count: home_ref.at[:, :, :, :, pl.ds(first * units, count * units)]
    rest = Spread(p, rest_ref, later_send, later_recv)
    own_units = Spread(p, part(0, 2), feed_send, feed_recv)
    far_expand = Spread(p, part(2, 1), expand_send, expand_recv)
    far_shrink = Spread(p, part(3, 1), shrink_send, shrink_recv)
    own_units.second()
    far_expand.first()
    store.wait()
    for load in loads:
        load.wait()
    norms = f32(norm_columns[...]).T[:8, :]
    norm_ref[...] = norms
    branch = f32(x_rows[...])
    for group in range(n):
        branch = branch + dot(slots_ref[group], wo[group], NT)
    hidden, normed, inverse = layer_norm(branch, norms[0:1, :], norms[3:4, :])
    hidden_ref[...] = hidden
    normed_ref[...] = normed
    inverse_ref[...] = jnp.broadcast_to(inverse, inverse_ref.shape)
    low = bf16(hidden)

    def q_copy(distance):
        to = lax.rem(me + distance, n)
        return pltpu.make_async_remote_copy(
            blocks.at[to], q_ref.at[rows_at(me, size)], q_send.at[distance - 1], q_recv.at[distance - 1],
            device_id={"mp": to}, device_id_type=MESH,
        )

    for distance in range(1, n):
        to = lax.rem(me + distance, n)
        blocks[to] = bf16(dot(low, wq[to]))
        q_copy(distance).start()
    far = push(
        shrink_ref, home_ref.at[p.y, p.x, p.core, :, pl.ds(3 * units, units)], far_send, far_recv,
        {"mp": lax.rem(me + n // 2, n)},
    )
    q_ref[rows_at(me, size), :] = bf16(dot(low, wq[me]))
    for copy in line:
        copy.wait_recv()
    rest.first()
    states_load.wait()
    for start in range(0, states_ref.shape[0], 512):
        rows = slice(start, start + 512)
        made = bf16(dot(states_ref[rows, :], source[...]))
        k_ref[rows, :] = made[:, :width]
        v_ref[rows, :] = made[:, width:]
    far_expand.second()

    def mixed_copy(distance):
        to = lax.rem(me + distance, n)
        return pltpu.make_async_remote_copy(
            mixed_ref.at[rows_at(to, size)], cross_slots_ref.at[me],
            mixed_send.at[distance - 1], mixed_recv.at[distance - 1],
            device_id={"mp": to}, device_id_type=MESH,
        )

    for step in range(n):
        if step > 0:
            q_copy(n - step).wait_recv()
        forward_rows(
            False, lax.rem(me + step, n), size, None, q_ref, k_ref, v_ref, mixed_ref, sums_ref
        )
        if step > 0:
            mixed_copy(step).start()
        if step == 0:
            rest.second()
    cross_slots_ref[me] = mixed_ref[rows_at(me, size), :]
    far.wait_recv()
    far_shrink.first()
    rest.core()
    far_shrink.second()
    for distance in range(1, n):
        q_copy(distance).wait_send()
        mixed_copy(distance).wait()
    for copy in line:
        copy.wait_send()
    far.wait_send()
    for spread in (rest, own_units, far_expand, far_shrink):
        spread.finish()


def middle(n_dp, n, slots, bundle, tokens, home, shrink_t, outer_t, states):
    side = round((n_dp // 2) ** 0.5)
    _, size, width = slots.shape
    total, model = tokens.shape
    keys = states.shape[0]
    shape = jax.ShapeDtypeStruct
    dma = pltpu.SemaphoreType.DMA
    low, wide = jnp.bfloat16, jnp.float32
    return pl.pallas_call(
        partial(middle_kernel, n, side),
        out_shape=[
            shape((size, model), wide),
            shape((size, model), wide),
            shape((size, 128), wide),
            shape((8, model), wide),
            shape((total, width), low),
            shape((keys, width), low),
            shape((keys, width), low),
            shape((total, width), low),
            shape((8, total), wide),
            shape((n, size, width), low),
            shape(home.shape, low),
            shape((side, side, 2, outer_t.shape[1], n * width), low),
        ],
        in_specs=[IN_VMEM] + [ANYWHERE] * 4 + [IN_VMEM] * 2,
        out_specs=[IN_VMEM] * 10 + [ANYWHERE] * 2,
        input_output_aliases={3: 10},
        scratch_shapes=[
            pltpu.VMEM((n, model, width), low),
            pltpu.VMEM((n, model, width), low),
            pltpu.VMEM((model, bundle.shape[1] - 2 * n * width - 2 * width), low),
            pltpu.VMEM((model, 2 * width), low),
            pltpu.VMEM((size, model), low),
            pltpu.VMEM((n, size, width), low),
            dma((n,)), dma((n,)), dma((4,)),
            dma((n - 1,)), dma((n - 1,)), dma((n - 1,)), dma((n - 1,)), dma, dma,
            Spread.sems(side), Spread.sems(side), Spread.sems(side), Spread.sems(side),
            dma((n - 1,)), dma((n - 1,)),
            Spread.sems(side), Spread.sems(side), Spread.sems(side), Spread.sems(side),
            pltpu.VMEM((keys, model), low), dma,
        ],
        compiler_params=pltpu.CompilerParams(
            collective_id=1, has_side_effects=True, vmem_limit_bytes=VMEM_LIMIT
        ),
        cost_estimate=pl.CostEstimate(flops=10**10, bytes_accessed=1 << 20, transcendentals=0),
        name="middle",
    )(slots, bundle, tokens, home, states, shrink_t, outer_t)


def feed_kernel(
    n, side, slots, rest_ref, home_ref, hidden_one_ref, cot_ref, norm_ref,
    out_ref, second_ref, dmix_ref, shrink_grad_hbm, expand_grad_hbm, wo_grad_ref, norm_grad_ref,
    wo, weights, hidden_two, normed_two, low_two, low_three, act, slope,
    y_own, y_send, y_recv, d_send, d_recv, cot, blocks,
    load_sem, wo_sems, own_sem, send_out, recv_out, pair_send, pair_recv,
    home_sems, home_send, home_recv, shrink_grad_ref, expand_grad_ref, grad_sems,
):
    p = Place(n, side)
    me = p.z
    mate = {"mp": me + 1 - 2 * lax.rem(me, 2)}
    size = cot.shape[0]
    half = size // 2
    width = slots.shape[2]
    hidden_units = act.shape[1]
    chunk = min(512, hidden_units)
    loads = [
        *load_groups(n, rest_ref, width, 0, width, wo, wo_sems),
        pltpu.make_async_copy(cot_ref.at[rows_at(me, size)], cot, load_sem),
    ]
    rows = home_ref.shape[3]
    places = [(y, x) for y in range(side) for x in range(side)]
    spots = [rows_at((y * side + x) * 2 + p.core, rows) for y, x in places]
    homes = [
        pltpu.make_async_copy(home_ref.at[y, x, p.core], weights.at[spot], home_sems.at[index])
        for index, ((y, x), spot) in enumerate(zip(places, spots))
    ]
    for load in loads + homes:
        load.start()
    greet(p.line() + [p.sibling()])
    home_copies = [
        push(
            home_ref.at[y, x, p.core], weights.at[spot],
            home_send.at[index], home_recv.at[index], p.sibling(),
        )
        for index, ((y, x), spot) in enumerate(zip(places, spots))
    ]
    for load in loads[:n]:
        load.wait()
    branch = hidden_one_ref[...]
    for group in range(n):
        branch = branch + dot(slots[group], wo[group], NT)
    hidden, normed, inverse_two = layer_norm(branch, norm_ref[1:2, :], norm_ref[4:5, :])
    hidden_two[...] = hidden
    normed_two[...] = normed
    low_two[:size, :] = bf16(hidden)
    pair = []

    def to_mate(source, target):
        index = len(pair)
        pair.append(push(source, target, pair_send.at[index], pair_recv.at[index], mate))
        return pair[-1]

    hidden_copies = [
        to_mate(low_two.at[pl.ds(start, half)], low_two.at[pl.ds(size + start, half)])
        for start in (0, half)
    ]
    for copy in homes:
        copy.wait()
    for copy in home_copies:
        copy.wait_recv()
    units = hidden_units // 2

    def expand_cols(first, count):
        first += first // units * units
        return slice(first, first + count)

    def shrink_cols(first, count):
        first += (first // units + 1) * units
        return slice(first, first + count)

    def shrink_sum(rows):
        return sum(
            dot(act[rows, first : first + units], weights[:, shrink_cols(first, units)], NT)
            for first in (0, units)
        )

    def expand_sum(rows):
        return sum(
            dot(slope[rows, first : first + units], weights[:, expand_cols(first, units)], NT)
            for first in (0, units)
        )

    def expand_rows(start, count):
        rows = low_two[start : start + count, :]
        for first in range(0, hidden_units, chunk):
            pre = dot(rows, weights[:, expand_cols(first, chunk)])
            cdf = 0.5 + 0.5 * lax.erf(pre * 0.7071067811865476)
            act[start : start + count, first : first + chunk] = bf16(pre * cdf)
            slope[start : start + count, first : first + chunk] = bf16(
                cdf + pre * jnp.exp(-0.5 * pre * pre) * 0.3989422804014327
            )

    expand_rows(0, size)
    y_copies = []
    for index, start in enumerate((0, half)):
        hidden_copies[index].wait_recv()
        expand_rows(size + start, half)
        y_send[start : start + half, :] = bf16(shrink_sum(slice(size + start, size + start + half)))
        y_copies.append(to_mate(y_send.at[pl.ds(start, half)], y_recv.at[pl.ds(start, half)]))
    y_own[...] = shrink_sum(slice(0, size))
    for copy in y_copies:
        copy.wait_recv()
    output, normed, inverse = layer_norm(
        hidden_two[...] + y_own[...] + f32(y_recv[...]), norm_ref[2:3, :], norm_ref[5:6, :]
    )
    out_ref[...] = bf16(output)
    loads[n].wait()
    third, gain_three, bias_three = norm_back(f32(cot[...]), normed, inverse, norm_ref[2:3, :])
    low_three[:size, :] = bf16(third)
    grad_copies = [
        to_mate(low_three.at[pl.ds(start, half)], low_three.at[pl.ds(size + start, half)])
        for start in (0, half)
    ]

    def back_rows(start, count):
        rows = low_three[start : start + count, :]
        for first in range(0, hidden_units, chunk):
            grad = dot(rows, weights[:, shrink_cols(first, chunk)])
            spot = (slice(start, start + count), slice(first, first + chunk))
            slope[spot] = bf16(grad * f32(slope[spot]))

    back_rows(0, size)
    d_copies = []
    for index, start in enumerate((0, half)):
        grad_copies[index].wait_recv()
        back_rows(size + start, half)
        d_send[start : start + half, :] = bf16(expand_sum(slice(size + start, size + start + half)))
        d_copies.append(to_mate(d_send.at[pl.ds(start, half)], d_recv.at[pl.ds(start, half)]))
    y_own[...] = third + expand_sum(slice(0, size))
    for copy in d_copies:
        copy.wait_recv()
    second, gain_two, bias_two = norm_back(
        y_own[...] + f32(d_recv[...]), normed_two[...], inverse_two, norm_ref[1:2, :]
    )
    second_ref[...] = second
    low = bf16(second)
    sent = tokens_to_heads(
        n, lambda group: dot(low, wo[group]), blocks, dmix_ref, send_out, recv_out, own_sem
    )
    norm_grad_ref[...] = jnp.concatenate(
        [gain_two, gain_three, bias_two, bias_three, jnp.zeros((4, norm_grad_ref.shape[1]))], axis=0
    )
    stores = []
    for first in range(0, low_two.shape[1], 256):
        rows = slice(first, first + 256)
        shrink_grad_ref[rows, :] = bf16(dot(low_three[:, rows], act[...], TN))
        expand_grad_ref[rows, :] = bf16(dot(low_two[:, rows], slope[...], TN))
        for index, (made, target) in enumerate(
            ((shrink_grad_ref, shrink_grad_hbm), (expand_grad_ref, expand_grad_hbm))
        ):
            span = pl.ds(first, 256)
            stores.append(
                pltpu.make_async_copy(made.at[span], target.at[span], grad_sems.at[index, first // 256])
            )
            stores[-1].start()
    for group in range(n):
        wo_grad_ref[:, group * width : (group + 1) * width] = bf16(dot(low, slots[group], TN))
    for copy in sent:
        copy.wait()
    for copy in pair + home_copies:
        copy.wait_send()
    for store in stores:
        store.wait()


def feed(n, slots, rest, home, hidden_one, cotangent, norms):
    width = slots.shape[2]
    total = cotangent.shape[0]
    side, model, units = home.shape[0], hidden_one.shape[1], home.shape[4] // 2
    size = total // n
    shape = jax.ShapeDtypeStruct
    dma = pltpu.SemaphoreType.DMA
    low, wide = jnp.bfloat16, jnp.float32
    return pl.pallas_call(
        partial(feed_kernel, n, side),
        out_shape=[
            shape((size, model), low),
            shape((size, model), wide),
            shape((total, width), low),
            shape((model, units), low),
            shape((model, units), low),
            shape((model, model), low),
            shape((8, model), wide),
        ],
        in_specs=[IN_VMEM, ANYWHERE, ANYWHERE, IN_VMEM, ANYWHERE, IN_VMEM],
        out_specs=[IN_VMEM] * 2 + [ANYWHERE] * 3 + [IN_VMEM] * 2,
        scratch_shapes=[
            pltpu.VMEM((n, model, width), low),
            pltpu.VMEM((model, 2 * units), low),
            pltpu.VMEM((size, model), wide),
            pltpu.VMEM((size, model), wide),
            pltpu.VMEM((2 * size, model), low),
            pltpu.VMEM((2 * size, model), low),
            pltpu.VMEM((2 * size, units), low),
            pltpu.VMEM((2 * size, units), low),
            pltpu.VMEM((size, model), wide),
            pltpu.VMEM((size, model), low),
            pltpu.VMEM((size, model), low),
            pltpu.VMEM((size, model), low),
            pltpu.VMEM((size, model), low),
            pltpu.VMEM((size, model), low),
            pltpu.VMEM((n, size, width), low),
            dma, dma((n,)), dma,
            dma((n - 1,)), dma((n - 1,)),
            dma((8,)), dma((8,)),
            dma((side * side,)), dma((side * side,)), dma((side * side,)),
            pltpu.VMEM((model, units), low), pltpu.VMEM((model, units), low), dma((2, model // 256)),
        ],
        compiler_params=pltpu.CompilerParams(
            collective_id=2, has_side_effects=True, vmem_limit_bytes=VMEM_LIMIT
        ),
        cost_estimate=pl.CostEstimate(
            flops=80 * 10**9, bytes_accessed=8 * total * width, transcendentals=0
        ),
        name="feed",
    )(slots, rest, home, hidden_one, cotangent, norms)


class Line:
    def __init__(self, place, parts, scratch):
        self.n, self.me, self.parts = place.n, place.z, parts
        self.landed = {"right": scratch[0], "left": scratch[1]}
        self.sems = {"right": scratch[2:4], "left": scratch[4:6]}

    @staticmethod
    def scratch(n, rows, columns):
        return [pltpu.VMEM((n - 1, rows, columns), jnp.bfloat16)] * 2 + [
            pltpu.SemaphoreType.DMA((n - 1,))
        ] * 4

    def _spots(self):
        return (("right", self.me, self.me + 1), ("left", self.n - 1 - self.me, self.me - 1))

    def _copy(self, way, spot, to, step):
        n = self.n
        chunk = n - 1 - step + spot if way == "right" else step - spot
        return pltpu.make_async_remote_copy(
            self.parts.at[lax.rem(chunk + n, n)], self.landed[way].at[step],
            self.sems[way][0].at[step], self.sems[way][1].at[step],
            device_id={"mp": lax.rem(to + n, n)}, device_id_type=MESH,
        )

    def step(self, step):
        n = self.n
        for way, spot, to in self._spots():
            chunk = n - 1 - step + spot if way == "right" else step - spot
            chunk = lax.rem(chunk + n, n)

            if step > 0:

                @pl.when((spot > 0) & (spot <= step) & (spot < n - 1))
                def _():
                    self._copy(way, spot, to, step - 1).wait_recv()
                    self.parts[chunk] = bf16(
                        f32(self.parts[chunk]) + f32(self.landed[way][step - 1])
                    )

            @pl.when((spot <= step) & (spot < n - 1))
            def _():
                self._copy(way, spot, to, step).start()

    def finish(self):
        last = self.n - 2
        for way, spot, to in self._spots():

            @pl.when(spot > 0)
            def _():
                self._copy(way, spot, to, last).wait_recv()
                self.parts[self.me] = bf16(
                    f32(self.parts[self.me]) + f32(self.landed[way][last])
                )

            for step in range(self.n - 1):

                @pl.when((spot <= step) & (spot < self.n - 1))
                def _():
                    self._copy(way, spot, to, step).wait_send()


class Fold:
    def __init__(self, place, make, out, scratch, group, slack=2):
        self.n, self.me, self.make, self.out = place.n, place.z, make, out
        self.parts, self.held, self.down_send, self.down_recv, self.back_send, self.back_recv, self.own = scratch
        self.chunks = self.held.shape[1]
        self.ring = self.parts.shape[1]
        self.group, self.slack = group, slack
        self.ticks = self.chunks + slack * (2 * (self.n - 1) - 1)

    @staticmethod
    def scratch(chunks, rows, columns, ring=12):
        low, dma = jnp.bfloat16, pltpu.SemaphoreType.DMA((2, chunks))
        return [
            pltpu.VMEM((2, ring, rows, columns), low), pltpu.VMEM((2, chunks, rows, columns), low),
            dma, dma, dma, dma, dma,
        ]

    def _flows(self):
        n, me = self.n, self.me
        return (
            (0, me, lax.rem(me + 1, n), lax.rem(me + n - 1, n)),
            (1, n - 1 - me, lax.rem(me + n - 1, n), lax.rem(me + 1, n)),
        )

    def _down(self, flow, chunk, to, first):
        source = self.parts.at[flow, lax.rem(chunk, self.ring)] if first else self.held.at[flow, chunk]
        return pltpu.make_async_remote_copy(
            source, self.held.at[flow, chunk],
            self.down_send.at[flow, chunk], self.down_recv.at[flow, chunk],
            device_id={"mp": to}, device_id_type=MESH,
        )

    def _back(self, flow, chunk, to, first):
        source = (self.held if first else self.out).at[flow, chunk]
        return pltpu.make_async_remote_copy(
            source, self.out.at[flow, chunk],
            self.back_send.at[flow, chunk], self.back_recv.at[flow, chunk],
            device_id={"mp": to}, device_id_type=MESH,
        )

    def _keep(self, flow, chunk):
        return pltpu.make_async_copy(
            self.held.at[flow, chunk], self.out.at[flow, chunk], self.own.at[flow, chunk]
        )

    def tick(self, tick):
        last = self.n - 1
        for flow, spot, ahead, behind in self._flows():
            if tick < self.chunks:
                if tick % self.group == 0:
                    whole = bf16(self.make(flow, tick // self.group))
                    rows = whole.shape[0] // self.group
                    for index in range(self.group):
                        if tick + index >= self.ring:

                            @pl.when(spot == 0)
                            def _():
                                self._down(flow, tick + index - self.ring, ahead, True).wait_send()

                        self.parts[flow, (tick + index) % self.ring] = whole[
                            index * rows : (index + 1) * rows
                        ]

                @pl.when(spot == 0)
                def _():
                    self._down(flow, tick, ahead, True).start()

            chunk = tick - self.slack * spot

            @pl.when((spot > 0) & (chunk >= 0) & (chunk < self.chunks))
            def _():
                self._down(flow, chunk, ahead, False).wait_recv()
                self.held[flow, chunk] = bf16(
                    f32(self.held[flow, chunk]) + f32(self.parts[flow, lax.rem(chunk, self.ring)])
                )

                @pl.when(spot < last)
                def _():
                    self._down(flow, chunk, ahead, False).start()

                @pl.when(spot == last)
                def _():
                    self._back(flow, chunk, behind, True).start()
                    self._keep(flow, chunk).start()

            given = tick - self.slack * (2 * last - spot)

            @pl.when((spot > 0) & (spot < last) & (given >= 0) & (given < self.chunks))
            def _():
                self._back(flow, given, behind, False).wait_recv()
                self._back(flow, given, behind, False).start()

    def finish(self):
        last = self.n - 1
        for flow, spot, ahead, behind in self._flows():

            @pl.when(spot == 0)
            def _():
                def wait(chunk, carry):
                    self._back(flow, chunk, behind, False).wait_recv()
                    return carry

                lax.fori_loop(0, self.chunks, wait, 0)

                def sent(chunk, carry):
                    self._down(flow, chunk, ahead, True).wait_send()
                    return carry

                lax.fori_loop(max(self.chunks - self.ring, 0), self.chunks, sent, 0)

            @pl.when((spot > 0) & (spot < last))
            def _():
                def sent(chunk, carry):
                    self._down(flow, chunk, ahead, False).wait_send()
                    self._back(flow, chunk, behind, False).wait_send()
                    return carry

                lax.fori_loop(0, self.chunks, sent, 0)

            @pl.when(spot == last)
            def _():
                def sent(chunk, carry):
                    self._back(flow, chunk, behind, True).wait_send()
                    self._keep(flow, chunk).wait()
                    return carry

                lax.fori_loop(0, self.chunks, sent, 0)


class Everyone:
    def __init__(self, n_dp, n_mp, mine, slots, send_sems, recv_sems):
        self.n, self.n_mp = n_dp * n_mp, n_mp
        self.me = lax.axis_index("dp") * n_mp + lax.axis_index("mp")
        self.mine, self.slots, self.send, self.recv = mine, slots, send_sems, recv_sems

    def _to(self, distance):
        to = lax.rem(self.me + distance, self.n)
        return {"dp": to // self.n_mp, "mp": lax.rem(to, self.n_mp)}

    def _copy(self, distance):
        return pltpu.make_async_remote_copy(
            self.mine, self.slots.at[self.me], self.send.at[distance - 1], self.recv.at[distance - 1],
            device_id=self._to(distance), device_id_type=MESH,
        )

    def greet(self):
        barrier = pltpu.get_barrier_semaphore()

        def signal(distance, carry):
            pl.semaphore_signal(barrier, inc=1, device_id=self._to(distance), device_id_type=MESH)
            return carry

        lax.fori_loop(1, self.n, signal, 0)
        pl.semaphore_wait(barrier, self.n - 1)

    def start(self):
        def start(distance, carry):
            self._copy(distance).start()
            return carry

        self.slots[self.me] = self.mine[...]
        lax.fori_loop(1, self.n, start, 0)

    def finish(self):
        def wait(distance, carry):
            self._copy(distance).wait()
            return carry

        lax.fori_loop(1, self.n, wait, 0)
        return jnp.sum(self.slots[...], axis=0)


def moments(upstream, first_moment, second_moment, master, decay):
    first_new = first_decay * first_moment + (1.0 - first_decay) * upstream
    second_new = second_decay * second_moment + (1.0 - second_decay) * upstream * upstream
    direction = (
        first_new
        / (1.0 - first_decay**STEP)
        / (jnp.sqrt(second_new / (1.0 - second_decay**STEP)) + epsilon)
        + decay * master
    )
    return (first_new, second_new, direction)


def tensors(inner, outer, expand, shrink, norms):
    found = [inner.at[a, c] for a in range(2) for c in range(3)]
    found += [outer.at[0], outer.at[1], expand, shrink]
    found += [norms.at[pl.ds(row, 1)] for row in range(6)]
    return list(zip(found, [weight_decay] * 10 + [0.0] * 6))


def square_row(squares, share):
    lane = lax.broadcasted_iota(jnp.int32, (1, 128), 1)
    row = jnp.zeros((1, 128), jnp.float32)
    for index, values in enumerate(squares):
        total = jnp.sum(jnp.sum(values, axis=0, keepdims=True), axis=1, keepdims=True)
        row = jnp.where(lane == index, total * share if index >= 10 else total, row)
    return row


def update_kernel(split, *refs):
    (
        both_ref, layer_ref, sums_ref, grads, weights, firsts, seconds,
        states_ref, input_ref, output_ref, table_ref, new_weights, new_firsts, new_seconds,
        both, layer, wide, loads, stores,
    ) = (
        *refs[:3], refs[3:8], refs[8:13], refs[13:18], refs[18:23],
        *refs[23:27], refs[27:32], refs[32:37], refs[37:42], *refs[42:],
    )
    size, columns = both.shape[2], both.shape[3]
    chunks = both.shape[1]
    pieces, row = [], 0
    for source, held, first, count, target, start in (
        (both_ref.at[0], both.at[0], 0, split, states_ref, 0),
        (both_ref.at[1], both.at[1], 0, split, states_ref, split * size),
        (both_ref.at[0], both.at[0], split, chunks - split, input_ref, 0),
        (both_ref.at[1], both.at[1], split, chunks - split, input_ref, (chunks - split) * size),
        (layer_ref, layer, 0, layer_ref.shape[0], output_ref, 0),
    ):
        span = pl.ds(first, count)
        length = count * source.shape[1]
        load = pltpu.make_async_copy(source.at[span], held.at[span], loads.at[len(pieces)])
        store = pltpu.make_async_copy(
            wide.at[pl.ds(row, length)], target.at[pl.ds(start, length)], stores.at[len(pieces)]
        )
        pieces.append((load, store, held, first, count, row))
        row += length
    for piece in pieces:
        piece[0].start()
    for load, store, held, first, count, row in pieces:
        load.wait()
        length = held.shape[1]
        for index in range(count):
            wide[row + index * length : row + (index + 1) * length, :] = f32(held[first + index])
        store.start()
    lane = lax.broadcasted_iota(jnp.int32, (1, 128), 1)
    counts = jnp.where(lane < 8, float(D * D), jnp.where(lane < 10, float(D * FF), float(D)))
    weight_norm = jnp.sqrt(sums_ref[0:1, :] / counts)
    update_norm = jnp.sqrt(sums_ref[1:2, :] / counts)
    trust = weight_norm / (update_norm + epsilon)
    table_ref[...] = jnp.concatenate([weight_norm, update_norm, trust], axis=0)[:, :16]
    groups = [tensors(*group) for group in (grads, weights, firsts, seconds, new_weights, new_firsts, new_seconds)]
    for index, parts in enumerate(zip(*groups)):
        grad, weight, first, second, new_weight, new_first, new_second = [part[0] for part in parts]
        ratio = jnp.sum(jnp.where(lane == index, trust, 0.0), axis=1, keepdims=True)
        master = weight[...]
        first_new, second_new, direction = moments(
            grad[...], first[...], second[...], master, parts[0][1]
        )
        new_first[...] = first_new
        new_second[...] = second_new
        new_weight[...] = master - learn_rate * ratio * direction
    for piece in pieces:
        piece[1].wait()


def update(both, layer, source_rows, sums, grads, weights, firsts, seconds):
    shape = lambda values: jax.ShapeDtypeStruct(values.shape, jnp.float32)
    results = [shape(values) for values in weights]
    size, columns = both.shape[2:]
    split = source_rows // (2 * size)
    total = layer.shape[0] * layer.shape[1]
    wide = lambda rows: jax.ShapeDtypeStruct((rows, columns), jnp.float32)
    dma = pltpu.SemaphoreType.DMA((5,))
    return pl.pallas_call(
        partial(update_kernel, split),
        out_shape=[wide(source_rows), wide(total), wide(total)]
        + [jax.ShapeDtypeStruct((3, 16), jnp.float32)]
        + results * 3,
        in_specs=[ANYWHERE] * 2 + [IN_VMEM] * 21,
        out_specs=[ANYWHERE] * 3 + [IN_VMEM] * 16,
        scratch_shapes=[
            pltpu.VMEM(both.shape, jnp.bfloat16),
            pltpu.VMEM(layer.shape, jnp.bfloat16),
            pltpu.VMEM((source_rows + 2 * total, columns), jnp.float32),
            dma, dma,
        ],
        compiler_params=pltpu.CompilerParams(vmem_limit_bytes=VMEM_LIMIT),
        name="update",
    )(both, layer, sums, *grads, *weights, *firsts, *seconds)


def finish_kernel(
    n, side, units, width, prefix_ref, q_hbm, k_hbm, v_hbm, o_hbm, row_sums_ref,
    near_hbm, x_hbm, cross_dk_ref, cross_dv_ref, dq_slots_ref, mixed_slots_ref, inverse_ref, norms_ref, norm_rows_ref,
    half_a_ref, half_b_ref, bundle_ref, second_hbm, hidden_hbm, normed_hbm, cross_wo_ref, source_grad_ref, *refs,
):
    states, refs = refs[:15], refs[15:]
    out_ref, sums_ref, grads, refs = refs[0], refs[1], refs[2:7], refs[7:]
    (
        q_ref, k_ref, v_ref, o_ref, near_ref, x_ref, late_sems, source_ref, source_sem, do_ref, first_ref, feed_ref, weight_ref, blocks, early_sems, group_sem,
        own_sem, send_out, recv_out, dq_ref, dk_ref, dv_ref, query_acc, delta, master_sems, inner, stage, far_recv, group_send,
        far_send_sem, far_recv_sem, mine, slots, everyone_send, everyone_recv, *scratch,
    ) = refs
    n_dp = 2 * side * side
    p = Place(n, side)
    everyone = Everyone(n_dp, n, mine, slots, everyone_send, everyone_recv)

    me = p.z
    own_heads = (dq_ref, dk_ref, dv_ref)
    size, model = first_ref.shape
    rows = inner.shape[3]
    per_group = 4
    group_rows = per_group * out_ref.shape[2]
    source_groups = cross_dk_ref.shape[0] // (2 * group_rows)

    def make(flow, group):
        if group < source_groups:
            spot = pl.ds((flow * source_groups + group) * group_rows, group_rows)
            made = source_ref[...].reshape(model, 2 * width)
            return dot(cross_dk_ref[spot, :], made[:, :width], NT) + dot(
                cross_dv_ref[spot, :], made[:, width:], NT
            )
        tokens = x_ref.shape[0]
        start = flow * (tokens // 2) + (group - source_groups) * group_rows
        spot = pl.ds(start, group_rows)
        total = jnp.zeros((group_rows, model), jnp.float32)
        for index, own in enumerate(own_heads):
            total = total + dot(own[spot, :], near_ref[:, index * width : (index + 1) * width], NT)
        here = first_ref[start % size : start % size + group_rows, :]
        return total + jnp.where(me == start // size, here, 0.0)

    fold = Fold(p, make, out_ref, scratch[:7], per_group)
    group_sum = Reduce(p, [cross_wo_ref, source_grad_ref], scratch[7:15])
    weight_sum = Reduce(p, [weight_ref], scratch[15:23])
    inner_sum = Reduce(p, [inner], scratch[23:31])
    halves = Halves(p, half_a_ref, half_b_ref, scratch[31:35])
    line = Line(p, group_send, scratch[35:])

    source_load = pltpu.make_async_copy(
        bundle_ref.at[:, :, :, :, pl.ds(2 * n * width + 128, 2 * width)], source_ref, source_sem
    )
    source_load.start()
    late_loads = [
        pltpu.make_async_copy(source, target, late_sems.at[index])
        for index, (source, target) in enumerate(
            zip((q_hbm, k_hbm, v_hbm, o_hbm, near_hbm, x_hbm), (q_ref, k_ref, v_ref, o_ref, near_ref, x_ref))
        )
    ]
    for load in late_loads:
        load.start()
    weight_loads = [
        pltpu.make_async_copy(
            bundle_ref.at[:, :, :, :, pl.ds(start, n * width)],
            weight_ref.at[:, :, :, :, pl.ds(index * n * width, n * width)], group_sem.at[index],
        )
        for index, start in enumerate((n * width + 128, 0))
    ]
    for load in weight_loads:
        load.start()
    everyone.greet()
    group_sum.core_start()
    halves.start()
    source_load.wait()
    ticks = iter(range(fold.ticks))

    def advance(count):
        for _ in range(count):
            fold.tick(next(ticks))

    advance(2)

    def store_by_place(target, first, columns, value, start):
        for row in range(0, value.shape[0], rows):
            flat = (start + row) // rows
            y, x, core = flat // (2 * side), flat // 2 % side, flat % 2
            target[y, x, core, :, first : first + columns] = value[row : row + rows]

    def held_weight(group, second):
        cols = pl.ds(pl.multiple_of((n * second + group) * width, width), width)
        return weight_ref[:, :, :, :, cols].reshape(model, width)

    def cross_to_self(rows_f32):
        second_load = pltpu.make_async_copy(second_hbm, first_ref, early_sems.at[0])
        normed_load = pltpu.make_async_copy(normed_hbm, rows_f32, early_sems.at[1])
        hidden_load = pltpu.make_async_copy(hidden_hbm, rows_f32, early_sems.at[2])
        second_load.start()
        normed_load.start()
        second_load.wait()
        for load in weight_loads:
            load.wait()
        upstream = first_ref[...]
        for group in range(n):
            upstream = upstream + dot(dq_slots_ref[group], held_weight(group, 0), NT)
        normed_load.wait()
        first, gain_one, bias_one = norm_back(
            upstream, rows_f32[...], inverse_ref[:, 0:1], norms_ref[0:1, :]
        )
        hidden_load.start()
        first_ref[...] = first
        low = bf16(first)
        sent = tokens_to_heads(
            n, lambda group: dot(low, held_weight(group, 1)), blocks, do_ref, send_out, recv_out, own_sem
        )
        advance(1)
        hidden_load.wait()
        hidden_low = bf16(rows_f32[...])
        for group in range(n):
            at = 2 * group * width
            store_by_place(weight_ref, at, width, bf16(dot(hidden_low, dq_slots_ref[group], TN)), 0)
            store_by_place(
                weight_ref, at + width, width, bf16(dot(low, mixed_slots_ref[group], TN)), 0
            )
        rows_all = jnp.concatenate(
            [
                gain_one, norm_rows_ref[0:2, :], bias_one, norm_rows_ref[2:4, :],
                jnp.zeros((122, model), jnp.float32),
            ],
            axis=0,
        )
        store_by_place(weight_ref, 2 * n * width, 128, bf16(rows_all.T), 0)
        advance(1)
        for copy in sent:
            copy.wait()

    pl.run_scoped(cross_to_self, pltpu.VMEM((size, model), jnp.float32))
    weight_sum.core_start()
    feed_ref[...] = bf16(halves.total())
    far = {"mp": lax.rem(me + n // 2, n)}
    far_copies = [
        push(
            feed_ref.at[:, pl.ds((2 * index + 1) * units, units)],
            far_recv.at[:, pl.ds(index * units, units)],
            far_send_sem.at[index], far_recv_sem.at[index], far,
        )
        for index in range(2)
    ]
    group_sum.core_finish(stage)
    group_sum.first_start()
    advance(1)
    weight_sum.core_finish(stage)
    weight_sum.first_start()
    for load in late_loads:
        load.wait()
    backward_delta(do_ref, o_ref, delta)
    query_acc[...] = jnp.zeros_like(query_acc)
    key_block = 256

    def self_backward(index, heads):
        backward_block(
            True, key_block, index, heads, prefix_ref, q_ref, k_ref, v_ref, do_ref, row_sums_ref, delta,
            query_acc, dk_ref, dv_ref,
        )

    for index in range(x_ref.shape[0] // key_block):
        for heads in ((0, 1), (2, 3)):
            self_backward(index, heads)
            advance(1)
    dq_ref[...] = bf16(query_acc[...])

    per = 256
    for start in range(0, model, per):
        turned = x_ref[:, start : start + per]
        for index, own in enumerate(own_heads):
            store_by_place(inner, index * width, width, bf16(dot(turned, own[...], TN)), start)
    inner_sum.core_start()
    advance(1)
    inner_sum.core_finish(stage)
    inner_sum.first_start()
    advance(2)
    group_sum.first_finish()
    group_sum.second_start()
    weight_sum.first_finish()
    weight_sum.second_start()
    advance(1)
    advance(1)
    inner_sum.first_finish()
    inner_sum.second_start()
    advance(1)
    group_sum.second_wait()
    weight_sum.second_wait()
    whole = n * width
    for group in range(n):
        group_send[group, :, :width] = bf16(
            group_sum.total(slice(group * width, (group + 1) * width))
        )
        start = 2 * group * width
        group_send[group, :, width : 3 * width] = bf16(
            weight_sum.total(slice(start, start + 2 * width))
        )
        group_send[group, :, 3 * width :] = bf16(
            weight_sum.total(slice(2 * whole, 2 * whole + 128))
        )
    line.step(0)
    advance(2)

    def optimizer_sums(*masters):
        master_loads = [
            pltpu.make_async_copy(source, target, master_sems.at[index])
            for index, (source, target) in enumerate(zip(states, masters))
        ]
        for load in master_loads:
            load.start()
        grad_inner, grad_outer, grad_expand, grad_shrink, grad_norms = grads
        inner_sum.second_wait()
        for index in range(3):
            grad_inner[0, index] = inner_sum.total(slice(index * width, (index + 1) * width))
        start = whole
        for index in range(2):
            grad_inner[1, index + 1] = group_sum.total(
                slice(start + index * width, start + (index + 1) * width)
            )
        line.step(1)
        for load in master_loads:
            load.wait()
        weights, firsts, seconds = (tensors(*masters[index : index + 5]) for index in (0, 5, 10))
        share = 1.0 / n
        mine[...] = jnp.zeros(mine.shape, jnp.float32)
        mine[0:1, :] = square_row([ref[...] * ref[...] for ref, _ in weights], share)
        advance(2)
        line.step(2)
        for copy in far_copies:
            copy.wait_recv()
        grad_shrink[...] = (f32(feed_ref[:, :units]) + f32(far_recv[:, :units])).T
        grad_expand[...] = f32(feed_ref[:, 2 * units : 3 * units]) + f32(far_recv[:, units:])
        advance(2)
        line.finish()
        received = lambda cols: f32(group_send[me, :, cols])
        grad_outer[1] = received(slice(0, width)).T
        grad_inner[1, 0] = received(slice(width, 2 * width))
        grad_outer[0] = received(slice(2 * width, 3 * width)).T
        grad_norms[...] = received(slice(3 * width, 3 * width + 128)).T[:6, :]

        def direction_square(grad, first, second, weight):
            step = moments(grad[0][...], first[0][...], second[0][...], weight[0][...], weight[1])[2]
            return step * step

        mine[1:2, :] = square_row(
            [direction_square(*group) for group in zip(tensors(*grads), firsts, seconds, weights)], share
        )
        everyone.start()
        advance(4)
        sums_ref[...] = everyone.finish()

    pl.run_scoped(optimizer_sums, *[pltpu.VMEM(source.shape, jnp.float32) for source in states])
    for tick in ticks:
        fold.tick(tick)
    fold.finish()
    for copy in far_copies:
        copy.wait_send()
    for batch in (group_sum, weight_sum, inner_sum):
        batch.finish()


def finish(
    n_dp, n_mp, prefix, projections, mixed, row_sums, near, tokens, source_heads, dq_slots, mixed_slots,
    inverse, norms, norm_rows, halves, bundle, second, hidden, normed, cross_wo, source_grad, states,
):
    side = round((n_dp // 2) ** 0.5)
    total, width = mixed.shape
    size, model = second.shape
    rows = model // n_dp
    half, feed_columns = halves[0].shape[1:]
    units = feed_columns // 4
    low, wide = jnp.bfloat16, jnp.float32
    shape = jax.ShapeDtypeStruct
    dma = pltpu.SemaphoreType.DMA
    by_place = lambda values: values.reshape(side, side, 2, rows, values.shape[1])
    early = [by_place(values) for values in (cross_wo, source_grad)]
    columns = sum(values.shape[4] for values in early)
    group_bundle = 3 * width + 128
    devices = n_dp * n_mp
    chunk_rows = 64
    chunks = (total + source_heads[0].shape[0]) // (2 * chunk_rows)
    weight_columns = 2 * n_mp * width + 128
    both, sums, *grads = pl.pallas_call(
        partial(finish_kernel, n_mp, side, units, width),
        out_shape=[shape((2, chunks, chunk_rows, model), low), shape((8, 128), wide)]
        + [shape(values.shape, wide) for values in states[:5]],
        in_specs=[pl.BlockSpec(memory_space=pltpu.SMEM)]
        + [ANYWHERE] * 4
        + [IN_VMEM]
        + [ANYWHERE] * 2
        + [IN_VMEM] * 9
        + [ANYWHERE] * (6 + len(states)),
        out_specs=[ANYWHERE] + [IN_VMEM] * 6,
        scratch_shapes=[
            *[pltpu.VMEM((total, width), low)] * 4,
            pltpu.VMEM(near.shape, low),
            pltpu.VMEM(tokens.shape, low),
            dma((6,)),
            pltpu.VMEM((side, side, 2, rows, 2 * width), low),
            dma,
            pltpu.VMEM((total, width), low),
            pltpu.VMEM((size, model), wide),
            pltpu.VMEM((rows, feed_columns), low),
            pltpu.VMEM((side, side, 2, rows, weight_columns), low),
            pltpu.VMEM((n_mp, size, width), low),
            dma((3,)), dma((2,)), dma, dma((n_mp - 1,)), dma((n_mp - 1,)),
            *[pltpu.VMEM((total, width), low)] * 3,
            pltpu.VMEM((total, width), wide),
            pltpu.VMEM((8, total), wide),
            dma((len(states),)),
            pltpu.VMEM((side, side, 2, rows, 3 * width), low),
            pltpu.VMEM((2, rows, max(columns, weight_columns)), low),
            pltpu.VMEM((rows, 2 * units), low),
            pltpu.VMEM((n_mp, rows, group_bundle), low),
            dma((2,)), dma((2,)),
            pltpu.VMEM((8, 128), wide),
            pltpu.VMEM((devices, 8, 128), wide),
            dma((devices - 1,)), dma((devices - 1,)),
            *Fold.scratch(chunks, chunk_rows, model),
            *Reduce.scratch(side, rows, columns, 2),
            *Reduce.scratch(side, rows, weight_columns, 1),
            *Reduce.scratch(side, rows, 3 * width, 1),
            *Halves.scratch(side, half, feed_columns),
            *Line.scratch(n_mp, rows, group_bundle),
        ],
        compiler_params=pltpu.CompilerParams(
            collective_id=5, has_side_effects=True, vmem_limit_bytes=VMEM_LIMIT
        ),
        cost_estimate=pl.CostEstimate(flops=10**10, bytes_accessed=1 << 20, transcendentals=0),
        name="finish",
    )(
        prefix, *projections, mixed, row_sums, near, tokens, *source_heads, dq_slots, mixed_slots, inverse,
        norms, norm_rows, *halves, by_place(bundle), second, hidden, normed, *early, *states,
    )
    return both, sums, grads


def on_device(
    inputs,
    encoder,
    prefix,
    cotangent,
    inner_weights,
    inner_first,
    inner_second,
    outer_weights,
    outer_first,
    outer_second,
    expand_weights,
    expand_first,
    expand_second,
    shrink_weights,
    shrink_first,
    shrink_second,
    norm_params,
    norm_first,
    norm_second,
):
    n_dp, n_mp = lax.axis_size("dp"), lax.axis_size("mp")
    seq_count, seq_len, model = inputs.shape
    tokens = inputs.reshape(seq_len, model)
    states = encoder.reshape(-1, model)
    rows, width = inner_weights.shape[2:]
    units = expand_weights.shape[1]

    flat = lambda values: values.reshape(6, rows)
    outer_t, shrink_t, near, bundle, home, self_q, self_k, self_v, self_mixed, self_sums, self_slots = front(
        n_dp, n_mp, prefix, inner_weights, outer_weights, flat(norm_params), expand_weights, shrink_weights, tokens
    )
    by_rows = lambda values: values.reshape(model, values.shape[-1])
    near, bundle = by_rows(near), by_rows(bundle)
    (
        hidden_one, normed_one, inverse_one, norms, cross_query, cross_k, cross_v, cross_mixed,
        cross_sums, cross_slots, home, rest,
    ) = middle(n_dp, n_mp, self_slots, bundle, tokens, home, shrink_t, outer_t, states)
    rest = by_rows(rest)
    out_rows, grad_second, cross_dmix, shrink_grad, expand_grad, cross_wo_grad, norm_rows = feed(
        n_mp, cross_slots, rest, home, hidden_one, cotangent.reshape(seq_len, model), norms,
    )
    dq_slots, cross_dk, cross_dv, layer_low, source_grad, *halves = cross_backward(
        n_dp, n_mp, cross_query, cross_k, cross_v, cross_dmix, cross_mixed, cross_sums, out_rows, states,
        shrink_grad, expand_grad,
    )
    weights = [inner_weights, outer_weights, expand_weights, shrink_weights, flat(norm_params)]
    firsts = [inner_first, outer_first, expand_first, shrink_first, flat(norm_first)]
    seconds = [inner_second, outer_second, expand_second, shrink_second, flat(norm_second)]
    both, sums, grads = finish(
        n_dp, n_mp, prefix, (self_q, self_k, self_v), self_mixed, self_sums, near, tokens,
        (cross_dk, cross_dv), dq_slots, self_slots, inverse_one, norms, norm_rows, halves, bundle,
        grad_second, hidden_one, normed_one, cross_wo_grad, source_grad, weights + firsts + seconds,
    )
    encoder_grad, input_grad, layer_out, table, *results = update(
        both, layer_low, states.shape[0], sums, grads, weights, firsts, seconds
    )
    for index in (4, 9, 14):
        results[index] = results[index].reshape(2, 3, rows)
    return (
        layer_out.reshape(seq_count, seq_len, model),
        input_grad.reshape(seq_count, seq_len, model),
        encoder_grad.reshape(seq_count, -1, model),
        *results,
        table,
    )


def solution(mesh):
    placed = (
        P("dp", None, None),
        P("dp", None, None),
        P("dp"),
        P("dp", None, None),
        P(None, None, "dp", "mp"),
        P(None, None, "dp", "mp"),
        P(None, None, "dp", "mp"),
        P(None, "mp", "dp"),
        P(None, "mp", "dp"),
        P(None, "mp", "dp"),
        P("dp", "mp"),
        P("dp", "mp"),
        P("dp", "mp"),
        P("mp", "dp"),
        P("mp", "dp"),
        P("mp", "dp"),
        P(None, None, "dp"),
        P(None, None, "dp"),
        P(None, None, "dp"),
    )
    return jax.shard_map(
        on_device,
        mesh=mesh,
        in_specs=placed,
        out_specs=(
            P("dp", None, None),
            P("dp", None, None),
            P("dp", None, None),
            P(None, None, "dp", "mp"),
            P(None, "mp", "dp"),
            P("dp", "mp"),
            P("mp", "dp"),
            P(None, None, "dp"),
            P(None, None, "dp", "mp"),
            P(None, "mp", "dp"),
            P("dp", "mp"),
            P("mp", "dp"),
            P(None, None, "dp"),
            P(None, None, "dp", "mp"),
            P(None, "mp", "dp"),
            P("dp", "mp"),
            P("mp", "dp"),
            P(None, None, "dp"),
            P(),
        ),
        check_vma=False,
    )
```
